32 devices in a mesh: seq: 8 (over y, x, core), head: 4 (over z).
Axes of the slice: x: 2, y: 2, z: 4, core: 2. Of those that a mesh axis runs over, the one named last changes fastest.
Arguments:
- x_in: bfloat16 [12288, 768], P(('seq', 'head')), may hold values from -6 to 6
- lengths: int32 [8], P('seq'), may hold values from 1 to 1536, 6144 in all
- cotangent: bfloat16 [12288, 768], P(('seq', 'head')), may hold values from -6 to 6
- w_in: float32 [768, 3224], P('seq', 'head'), may hold values from -0.21875 to 0.21875
- w_out: float32 [1536, 768], P('head', 'seq'), may hold values from -0.15625 to 0.15625
- small_params: float32 [10696], replicated, may hold values from -8 to 1.5, as said below
- row_in: float32 [768], P('seq'), may hold values from 2457.6 to 9830.4
- col_in: float32 [3224], P('head'), may hold values from 2457.6 to 9830.4
- row_out: float32 [1536], P('head'), may hold values from 6144 to 24576
- col_out: float32 [768], P('seq'), may hold values from 6144 to 24576
- small_second: float32 [10696], replicated, may hold values from 245.76 to 12288
Outputs:
- out: bfloat16 [12288, 768], P(('seq', 'head'))
- grad_x: float32 [12288, 768], P(('seq', 'head'))
- grad_in: float32 [768, 3224], P('seq', 'head')
- row_in_new: float32 [768], P('seq')
- col_in_new: float32 [3224], P('head')
- w_in_new: float32 [768, 3224], P('seq', 'head')
- grad_out: float32 [1536, 768], P('head', 'seq')
- row_out_new: float32 [1536], P('head')
- col_out_new: float32 [768], P('seq')
- w_out_new: float32 [1536, 768], P('head', 'seq')
- small_grad: float32 [10696], replicated
- small_second_new: float32 [10696], replicated
- small_new: float32 [10696], replicated
The draws below stay inside these ranges and needn't reach their ends.
Inputs may be any that keep to these rules, and one draw needn't show every extreme that they name: `small_params`: step biases lie in -8 to -3, log rates in 0 to 1.5, skip gains and both norm gains in 0.5 to 1.5, convolution taps within 0.9 and its bias within 0.5 of zero.
All inputs are finite; a program needn't handle non-finite values. No bound on the sum of `lengths` on one device may be relied on, other than what follows from the above.
Results may differ from the reference program's by a relative error of at most 0.0023.
The reference program's roundings to bfloat16 on the way count: a program that leaves them out, or rounds other values in their place, can miss the bound.
Values may be sent and summed in bfloat16 or wider, within the bound.
A program may use at most 128 MiB of HBM per device.

```python
import math
import jax
import jax.numpy as jnp
import numpy as np
from jax import lax

D = 768
HEADS = 24
HEAD_DIM = 64
STATE = 64
CONV = 4
SPAN = 128
STEP = 8
INNER = 1536
CONV_CH = 1664
PROJ = 3224
SMALL = 10696
SEQ_LEN = 1536
SEQS = 8
TOKENS = 12288


def draw_small_params(key, part):
    key = jax.random.fold_in(key, 11)
    subkeys = jax.random.split(key, 7)
    norm_gain = jax.random.uniform(subkeys[0], (D,), jnp.float32, 0.5, 1.5)
    conv_weight = jax.random.uniform(subkeys[1], (CONV * CONV_CH,), jnp.float32, -0.9, 0.9)
    conv_bias = jax.random.uniform(subkeys[2], (CONV_CH,), jnp.float32, -0.5, 0.5)
    step_bias = jax.random.uniform(subkeys[3], (HEADS,), jnp.float32, -7.0, -3.0)
    log_rates = jax.random.uniform(subkeys[4], (HEADS,), jnp.float32, 0.0, 1.5)
    skip_gain = jax.random.uniform(subkeys[5], (HEADS,), jnp.float32, 0.5, 1.5)
    out_gain = jax.random.uniform(subkeys[6], (INNER,), jnp.float32, 0.5, 1.5)
    return jnp.concatenate([norm_gain, conv_weight, conv_bias, step_bias, log_rates, skip_gain, out_gain])


def level_of(rng, dims, pieces, smallest, top_value):
    loudness = 1.0
    for position, blocks in pieces:
        draws = jax.random.uniform(jax.random.fold_in(jax.random.fold_in(rng, 6), position), (blocks,), jnp.float32, smallest / len(pieces), top_value / len(pieces))
        loudness = loudness * jnp.repeat(jnp.exp(draws), dims[position] // blocks).reshape((-1,) + (1,) * (len(dims) - 1 - position))
    return loudness


def profile(count, total, bound, lean):
    portions = [(1 << 20) // math.isqrt(rank ** lean) + 1 for rank in range(2, count + 1)]
    rest, counts = total - bound - (count - 1), [1] * (count - 1)
    while rest > 0:
        movable = [i for i in range(count - 1) if counts[i] < bound]
        pool, left = sum([portions[i] for i in movable]), rest
        for i in movable:
            extra = min(bound - counts[i], max(1, left * portions[i] // pool), rest)
            counts[i] = counts[i] + extra
            rest = rest - extra
    return np.array([bound] + counts)


def ragged_sizes(stream_key, count, total, limit, skew):
    if count == 2:
        one = jax.random.randint(stream_key, (), max(1, total - limit), min(limit, total - 1) + 1)
        return jnp.stack([one, total - one])
    sizes = jnp.asarray(profile(count, total, limit, skew), jnp.int32)
    twos = (count - 1) // 2
    source_of, taker = sizes[1:1 + 2 * twos:2], sizes[2:2 + 2 * twos:2]
    margin = jnp.minimum(source_of - 1, limit - taker)
    moved = jax.random.randint(jax.random.fold_in(stream_key, 1), (twos,), 0, 1 << 20) % (margin + 1)
    sizes = sizes.at[1:1 + 2 * twos:2].set(source_of - moved).at[2:2 + 2 * twos:2].set(taker + moved)
    return sizes[jax.random.permutation(jax.random.fold_in(stream_key, 2), count)]


def centred(own_key, shape, scale, most, pieces=(), kind=jnp.bfloat16):
    loudness = level_of(own_key, shape, pieces, -0.22, 0.18) if pieces else 1.0
    array = jax.random.normal(own_key, shape, jnp.float32) * scale * loudness
    return jnp.minimum(jnp.maximum(array, -most), most).astype(kind)


def setup_inputs(seed: int = 0) -> dict:
    arg_keys = jax.random.split(jax.random.key(seed), 12)
    x_in = centred(arg_keys[0], (TOKENS, D), 1.0, 6.0, ((0, 32),))
    lengths = ragged_sizes(arg_keys[1], SEQS, SEQS * SEQ_LEN // 2, SEQ_LEN, 1).astype(jnp.int32)
    cotangent = centred(arg_keys[2], (TOKENS, D), 1.0, 6.0, ((0, 32),))
    w_in = centred(arg_keys[3], (D, PROJ), D ** -0.5, 0.21875, ((0, 8), (1, 4)), jnp.float32)
    w_out = centred(arg_keys[4], (INNER, D), INNER ** -0.5, 0.15625, ((0, 4), (1, 8)), jnp.float32)
    small_params = draw_small_params(jax.random.fold_in(arg_keys[11], 71), 0)
    row_in = jnp.clip(jnp.exp(math.log(9830.4) - 1.3862944 * jax.random.uniform(arg_keys[6], (D,), jnp.float32) ** level_of(arg_keys[6], (D,), ((0, 8),), -0.2, 0.2)), 2457.6, 9830.4)
    col_in = jnp.clip(jnp.exp(math.log(9830.4) - 1.3862944 * jax.random.uniform(arg_keys[7], (PROJ,), jnp.float32) ** level_of(arg_keys[7], (PROJ,), ((0, 4),), -0.2, 0.2)), 2457.6, 9830.4)
    row_out = jnp.clip(jnp.exp(math.log(24576.0) - 1.3862944 * jax.random.uniform(arg_keys[8], (INNER,), jnp.float32) ** level_of(arg_keys[8], (INNER,), ((0, 4),), -0.2, 0.2)), 6144.0, 24576.0)
    col_out = jnp.clip(jnp.exp(math.log(24576.0) - 1.3862944 * jax.random.uniform(arg_keys[9], (D,), jnp.float32) ** level_of(arg_keys[9], (D,), ((0, 8),), -0.2, 0.2)), 6144.0, 24576.0)
    small_second = jnp.clip(jnp.exp(jax.random.uniform(arg_keys[10], (SMALL,), jnp.float32, math.log(245.76), math.log(12288.0))), 245.76, 12288.0)
    return {"x_in": x_in, "lengths": lengths, "cotangent": cotangent, "w_in": w_in, "w_out": w_out, "small_params": small_params, "row_in": row_in, "col_in": col_in, "row_out": row_out, "col_out": col_out, "small_second": small_second}


EPS = 1e-05
EPS_SQUARE = 1e-30
LEARN_RATE = 0.3
LEARN_SMALL = 3.0
CLIP_RMS = 0.1
PRECISE = lax.Precision.HIGHEST

@jax.custom_vjp
def low(v):
    return lax.optimization_barrier(v.astype(jnp.bfloat16)).astype(jnp.float32)

@jax.custom_vjp
def low_back(v):
    return v

def low_keep(v):
    return (low(v), None)

def low_pass(kept, grad):
    return (grad,)

def back_keep(v):
    return (v, None)

def back_low(kept, grad):
    return (low(grad),)
low.defvjp(low_keep, low_pass)
low_back.defvjp(back_keep, back_low)

def silu_gate(value):
    return value * jax.nn.sigmoid(value)

def unpack(small):
    first = D
    norm_gain = small[:first]
    conv_weight = small[first:first + CONV * CONV_CH].reshape(CONV, CONV_CH)
    first = first + CONV * CONV_CH
    conv_bias = small[first:first + CONV_CH]
    first = first + CONV_CH
    step_bias = small[first:first + HEADS]
    log_rates = small[first + HEADS:first + 2 * HEADS]
    skip_gain = small[first + 2 * HEADS:first + 3 * HEADS]
    out_gain = small[first + 3 * HEADS:first + 3 * HEADS + INNER]
    return (norm_gain, conv_weight, conv_bias, step_bias, log_rates, skip_gain, out_gain)

def norm_rows(values, gain):
    return values * lax.rsqrt(lax.optimization_barrier(jnp.mean(values * values, axis=1, keepdims=True)) + EPS) * gain

def gate_rows(heads_in, gate_vals, gain):
    gated = heads_in * silu_gate(gate_vals)
    return gated * lax.rsqrt(lax.optimization_barrier(jnp.mean(gated * gated, axis=1, keepdims=True)) + EPS) * gain

def conv_rows(padded, weight, bias):
    row_count = padded.shape[0] - (CONV - 1)
    total = jnp.zeros((row_count, padded.shape[1]), jnp.float32) + bias[None, :]
    for offset in range(CONV):
        total = total + weight[offset][None, :] * padded[offset:offset + row_count]
    return silu_gate(total)

def direction_scan(xheads, steps, rates, bmaps, cmaps):
    length = xheads.shape[0]
    head_count = xheads.shape[1]
    head_size = xheads.shape[2]
    state_size = bmaps.shape[1]
    blocks = length // SPAN
    blocks_in = (xheads.reshape(blocks, SPAN, head_count, head_size), steps.reshape(blocks, SPAN, head_count), bmaps.reshape(blocks, SPAN, state_size), cmaps.reshape(blocks, SPAN, state_size))
    causal_mask = jnp.arange(SPAN)[:, None] >= jnp.arange(SPAN)[None, :]

    def advance(carried_state, block_data):
        x_block, step_block, b_block, c_block = block_data
        log_decay = jnp.cumsum(step_block * rates[None, :], axis=0).T
        log_gaps = log_decay[:, :, None] - log_decay[:, None, :]
        decay_table = jnp.exp(jnp.where(causal_mask[None], log_gaps, -10000.0))
        intersection = jnp.dot(c_block, b_block.T, precision=PRECISE)
        mixing = intersection[None] * decay_table * step_block.T[:, None, :]
        within = jnp.einsum('hts,shp->thp', mixing, x_block, precision=PRECISE)
        carried = jnp.einsum('tn,hpn->thp', c_block, carried_state, precision=PRECISE) * jnp.exp(log_decay.T)[:, :, None]
        tail_weight = jnp.exp(log_decay[:, -1:] - log_decay).T * step_block
        renewed = carried_state * jnp.exp(log_decay[:, -1])[:, None, None] + jnp.einsum('sh,shp,sn->hpn', tail_weight, x_block, b_block, precision=PRECISE)
        return (renewed, within + carried)
    state_init = jnp.zeros((head_count, head_size, state_size), jnp.float32)
    _, outputs = lax.scan(jax.checkpoint(advance), state_init, blocks_in)
    return outputs.reshape(length, head_count, head_size)

def mixer_heads(xheads, raw_steps, bmaps, cmaps, step_bias, log_rates, skip_gain, valid_rows):
    steps = jax.nn.softplus(raw_steps + step_bias[None, :]) * valid_rows[:, None]
    rates = -jnp.exp(log_rates)
    forward_part = direction_scan(xheads, steps, rates, bmaps, cmaps)
    backward_part = direction_scan(xheads[::-1], steps[::-1], rates, bmaps[::-1], cmaps[::-1])[::-1]
    return forward_part + backward_part + skip_gain[None, :, None] * xheads

def sequence_out(inputs, length, in_low, out_low, small):
    norm_gain, conv_weight, conv_bias, step_bias, log_rates, skip_gain, out_gain = unpack(small)
    row_count = inputs.shape[0]
    valid_rows = (jnp.arange(row_count) < length).astype(jnp.float32)
    normed = norm_rows(inputs, norm_gain)
    projected = low(low_back(jnp.dot(low(normed), in_low, precision=PRECISE)))
    gate_in = projected[:, :INNER]
    conv_in = projected[:, INNER:INNER + CONV_CH]
    raw_steps = projected[:, INNER + CONV_CH:]
    padded = jnp.concatenate([jnp.zeros((CONV - 1, CONV_CH), jnp.float32), conv_in], axis=0)
    convolved = low(conv_rows(padded, conv_weight, conv_bias))
    xheads = convolved[:, :INNER].reshape(row_count, HEADS, HEAD_DIM)
    bmaps = convolved[:, INNER:INNER + STATE]
    cmaps = convolved[:, INNER + STATE:]
    mixed = mixer_heads(xheads, raw_steps, bmaps, cmaps, step_bias, log_rates, skip_gain, valid_rows)
    heads_out = low(low_back(mixed.reshape(row_count, INNER)))
    gate_normed = gate_rows(heads_out, gate_in, out_gain)
    branch = low_back(jnp.dot(low(gate_normed), out_low, precision=PRECISE)) * valid_rows[:, None]
    return inputs + branch

def factored_update(grad, rows_old, cols_old, weight, decay):
    squares = grad * grad
    rows_new = decay * rows_old + (1.0 - decay) * (lax.optimization_barrier(jnp.mean(squares, axis=1)) + EPS_SQUARE)
    cols_new = decay * cols_old + (1.0 - decay) * (lax.optimization_barrier(jnp.mean(squares, axis=0)) + EPS_SQUARE)
    scaled = grad * lax.rsqrt(rows_new[:, None] * cols_new[None, :] / jnp.mean(rows_new))
    spread = jnp.sqrt(jnp.mean(scaled * scaled))
    return (rows_new, cols_new, weight - LEARN_RATE * scaled / jnp.maximum(1.0, spread / CLIP_RMS))

def reference(x_in, lengths, cotangent, w_in, w_out, small_params, row_in, col_in, row_out, col_out, small_second):

    def forward(x_all, weight_in, weight_out, small):
        in_low = low(weight_in)
        out_low = low(weight_out)
        seqs_in = x_all.reshape(SEQS, SEQ_LEN, D)

        def one_seq(carry, item):
            return (carry, sequence_out(item[0], item[1], in_low, out_low, small))
        _, results = lax.scan(jax.checkpoint(one_seq), jnp.zeros((), jnp.float32), (seqs_in, lengths))
        return results.reshape(TOKENS, D)
    result, pullback = jax.vjp(forward, x_in.astype(jnp.float32), w_in, w_out, small_params)
    grad_x, grad_in, grad_out, small_grad = pullback(cotangent.astype(jnp.float32))
    decay = 1.0 - STEP ** (-0.8)
    row_in_new, col_in_new, w_in_new = factored_update(grad_in, row_in, col_in, w_in, decay)
    row_out_new, col_out_new, w_out_new = factored_update(grad_out, row_out, col_out, w_out, decay)
    small_second_new = decay * small_second + (1.0 - decay) * (small_grad * small_grad + EPS_SQUARE)
    scaled = small_grad * lax.rsqrt(small_second_new)
    spread = jnp.sqrt(jnp.mean(scaled * scaled))
    small_new = small_params - LEARN_SMALL * scaled / jnp.maximum(1.0, spread / CLIP_RMS)
    return (result.astype(jnp.bfloat16), grad_x, grad_in, row_in_new, col_in_new, w_in_new, grad_out, row_out_new, col_out_new, w_out_new, small_grad, small_second_new, small_new)
```

```python
import functools

import jax
import jax.numpy as jnp
import numpy as np
from jax import lax
from jax.experimental import pallas as pl
from jax.experimental.pallas import tpu as pltpu
from jax.sharding import PartitionSpec as P

D = 768
HEADS = 24
HEAD_DIM = 64
STATE = 64
CONV = 4
SPAN = 128
STEP = 8
INNER = 1536
CONV_CH = 1664
PROJ = 3224
WIDE = 3328
LANES = 128
HALO = 16

EPS = 1e-05
EPS_SQUARE = 1e-30
LEARN_RATE = 0.3
LEARN_SMALL = 3.0
CLIP_RMS = 0.1
DECAY = 1.0 - STEP ** (-0.8)
F32 = jnp.float32
BF16 = jnp.bfloat16
HIGHEST = lax.Precision.HIGHEST
MESH = pl.DeviceIdType.MESH
VMEM_BYTES = 60 << 20


def nn(left, right):
    return lax.dot_general(left, right, (((1,), (0,)), ((), ())), preferred_element_type=F32)


def nt(left, right):
    return lax.dot_general(left, right, (((1,), (1,)), ((), ())), preferred_element_type=F32)


def split(value):
    high = value.astype(BF16)
    return high, (value - high.astype(F32)).astype(BF16)


def nn_split(value, exact):
    high, low = split(value)
    return nn(high, exact) + nn(low, exact)


def expand(value, spread):
    return nn_split(value, spread)


def fold(value, spread):
    high, low = split(value)
    return nt(high, spread) + nt(low, spread)


def iota(shape, dim):
    return lax.broadcasted_iota(jnp.int32, shape, dim)


def tri_low():
    return (iota((SPAN, SPAN), 0) >= iota((SPAN, SPAN), 1)).astype(F32)


def tri_high():
    return (iota((SPAN, SPAN), 0) <= iota((SPAN, SPAN), 1)).astype(F32)


def precise(left, right):
    return lax.dot_general(
        left, right, (((1,), (0,)), ((), ())), precision=HIGHEST, preferred_element_type=F32
    )


def sigmoid(value):
    return 1.0 / (1.0 + jnp.exp(-value))


def tiles_of(per_part, index):
    return (per_part * index) // LANES, -(-(per_part * (index + 1)) // LANES)


def tile_count(per_part, parts):
    return max(e - s for s, e in (tiles_of(per_part, i) for i in range(parts)))


def gather_kernel(n_s, n_h, pay, full, lsem, zs, zr, ps, pr, cs, cr):
    s = lax.axis_index("seq")
    h = lax.axis_index("head")
    n_c = n_s // 2
    chip = s // 2
    core = lax.rem(s, 2)
    sib = chip * 2 + (1 - core)
    zpeer = [lax.rem(h + j, n_h) for j in range(1, n_h)]
    cpeer = [lax.rem(chip + j, n_c) for j in range(1, n_c)]
    bar = pltpu.get_barrier_semaphore()
    for z in zpeer:
        pl.semaphore_signal(bar, inc=1, device_id=(s, z), device_id_type=MESH)
    for c in cpeer:
        pl.semaphore_signal(bar, inc=1, device_id=(c * 2 + core, h), device_id_type=MESH)
    pl.semaphore_signal(bar, inc=1, device_id=(sib, h), device_id_type=MESH)
    pl.semaphore_wait(bar, n_h + n_c - 1)

    def rc(src, dst, ss, rs, dev):
        return pltpu.make_async_remote_copy(
            src_ref=src, dst_ref=dst, send_sem=ss, recv_sem=rs, device_id=dev, device_id_type=MESH
        )

    local = pltpu.make_async_copy(pay, full.at[h, s], lsem)
    local.start()
    sends = []

    def go(c):
        c.start()
        sends.append(c)

    for j, z in enumerate(zpeer):
        go(rc(pay, full.at[h, s], zs.at[j], zr.at[h], (s, z)))

    def plane(src, k, slot):
        for j, c in enumerate(cpeer):
            go(rc(src, full.at[k, s], ps.at[slot, j], pr.at[chip, k], (c * 2 + core, h)))
        go(rc(src, full.at[k, s], cs.at[slot, 0], cr.at[chip, k], (sib, h)))

    plane(pay, h, 0)
    order = [h] + zpeer

    def relay(kk, i):
        for j, c in enumerate(cpeer):
            o = c * 2 + core
            rc(pay, full.at[kk, o], zs.at[0], pr.at[c, kk], (s, zpeer[0])).wait_recv()
            go(rc(full.at[kk, o], full.at[kk, o], cs.at[i, j + 1], cr.at[c, kk], (sib, h)))

    for i, k in enumerate(zpeer):
        rc(pay, full.at[k, s], zs.at[i], zr.at[k], (s, k)).wait_recv()
        plane(full.at[k, s], k, i + 1)
        relay(order[i], i)
    relay(order[-1], n_h - 1)
    for kk in order:
        for c in [chip] + cpeer:
            rc(pay, full.at[kk, c * 2 + 1 - core], zs.at[0], cr.at[c, kk], (sib, h)).wait_recv()
    for c in sends:
        c.wait_send()
    local.wait()


def gather(pay, n_s, n_h):
    n_c = n_s // 2
    dma = pltpu.SemaphoreType.DMA
    return pl.pallas_call(
        functools.partial(gather_kernel, n_s, n_h),
        out_shape=jax.ShapeDtypeStruct((n_h, n_s) + pay.shape, pay.dtype),
        in_specs=[pl.BlockSpec(memory_space=pl.ANY)],
        out_specs=pl.BlockSpec(memory_space=pl.ANY),
        scratch_shapes=[
            dma,
            dma((n_h - 1,)),
            dma((n_h,)),
            dma((n_h, n_c - 1)),
            dma((n_c, n_h)),
            dma((n_h, n_c)),
            dma((n_c, n_h)),
        ],
        compiler_params=pltpu.CompilerParams(collective_id=0, has_side_effects=True),
        name="gather_weights",
    )(pay)


def chain_kernel(n_h, dev, dec, out, snd, us, ur, ds, dr):
    s = lax.axis_index("seq")
    h = lax.axis_index("head")
    up = lax.rem(h + 1, n_h)
    down = lax.rem(h + n_h - 1, n_h)
    bar = pltpu.get_barrier_semaphore()
    for z in (up, down):
        pl.semaphore_signal(bar, inc=1, device_id=(s, z), device_id_type=MESH)
    pl.semaphore_wait(bar, 2)
    parts = 4
    width = INNER // parts

    def rc(d, c, sem_s, sem_r, dev_h):
        cols = pl.ds(c * width, width)
        return pltpu.make_async_remote_copy(
            src_ref=snd.at[d, :, cols],
            dst_ref=out.at[d, :, cols],
            send_sem=sem_s.at[c],
            recv_sem=sem_r.at[c],
            device_id=(s, dev_h),
            device_id_type=MESH,
        )

    first = h == 0
    last = h == n_h - 1

    @pl.when(first)
    def _():
        out[0] = jnp.zeros((STATE, INNER), F32)
        snd[0] = dev[0]
        for c in range(parts):
            rc(0, c, us, ur, up).start()

    @pl.when(last)
    def _():
        out[1] = jnp.zeros((STATE, INNER), F32)
        snd[1] = dev[1]
        for c in range(parts):
            rc(1, c, ds, dr, down).start()

    for c in range(parts):
        cols = slice(c * width, (c + 1) * width)

        @pl.when(h > 0)
        def _():
            rc(0, c, us, ur, down).wait_recv()

        @pl.when(jnp.logical_and(h > 0, h < n_h - 1))
        def _():
            snd[0, :, cols] = out[0, :, cols] * dec[0:1, cols] + dev[0, :, cols]
            rc(0, c, us, ur, up).start()

        @pl.when(h < n_h - 1)
        def _():
            rc(1, c, ds, dr, up).wait_recv()

        @pl.when(jnp.logical_and(h > 0, h < n_h - 1))
        def _():
            snd[1, :, cols] = out[1, :, cols] * dec[0:1, cols] + dev[1, :, cols]
            rc(1, c, ds, dr, down).start()

    @pl.when(h < n_h - 1)
    def _():
        for c in range(parts):
            rc(0, c, us, ur, up).wait_send()

    @pl.when(h > 0)
    def _():
        for c in range(parts):
            rc(1, c, ds, dr, down).wait_send()


def chain(dev, dec, n_h, cid):
    dma = pltpu.SemaphoreType.DMA
    vm = pl.BlockSpec(memory_space=pltpu.VMEM)
    return pl.pallas_call(
        functools.partial(chain_kernel, n_h),
        out_shape=jax.ShapeDtypeStruct((2, STATE, INNER), F32),
        in_specs=[vm, vm],
        out_specs=vm,
        scratch_shapes=[pltpu.VMEM((2, STATE, INNER), F32), dma((4,)), dma((4,)), dma((4,)), dma((4,))],
        compiler_params=pltpu.CompilerParams(
            collective_id=cid, has_side_effects=True, vmem_limit_bytes=VMEM_BYTES
        ),
        name="state_chain",
    )(dev, dec)


def head_terms(steps, rates):
    logs = steps * rates
    incl = precise(tri_low(), logs)
    return incl, incl - logs, incl[SPAN - 1 : SPAN]


def front_kernel(
    n_h, cph, oph, wi,
    x, full, gain, taps, heads, left, spread,
    nlow, w_in, w_out, gate, conv_in, conv_low, slope, raw, steps, hst, gst, dev, decb, dec,
    nscr, cf,
):
    rows = nlow.shape[0]
    blocks = rows // SPAN

    def norm_body(i, _):
        at = pl.ds(pl.multiple_of(i * 16, 16), 16)
        v = x[at, :].astype(F32)
        n = v * lax.rsqrt(jnp.mean(v * v, axis=1, keepdims=True) + EPS) * gain[...]
        nscr[at, :] = n.astype(BF16)
        return 0

    lax.fori_loop(0, (rows + HALO) // 16, norm_body, 0)
    nlow[...] = nscr[HALO:, :]
    for per, width, base, dst in ((cph, WIDE, 0, w_in), (oph, INNER, wi, w_out)):
        for tile in range(width // LANES):
            parts = []
            for i in range(n_h):
                t0, t1 = tiles_of(per, i)
                if t0 <= tile < t1:
                    at = base + (tile - t0) * LANES
                    parts.append(full[i, :, at : at + LANES])
            v = parts[0] if len(parts) == 1 else parts[0] + parts[1]
            dst[:, tile * LANES : (tile + 1) * LANES] = v

    def gate_body(j, _):
        at = pl.ds(pl.multiple_of(j * 256, 256), 256)
        gate[:, at] = nn(nscr[HALO:, :], w_in[:, at]).astype(BF16)
        return 0

    lax.fori_loop(0, INNER // 256, gate_body, 0)

    def conv_body(j, _):
        at = pl.ds(pl.multiple_of(j * 256, 256), 256)
        v = nn(nscr[...], w_in[:, pl.ds(pl.multiple_of(INNER + j * 256, 256), 256)]).astype(BF16)
        conv_in[:, at] = v
        cf[:, at] = v.astype(F32)
        return 0

    lax.fori_loop(0, INNER // 256, conv_body, 0)
    v = nn(nscr[...], w_in[:, 2 * INNER : WIDE]).astype(BF16)
    conv_in[:, INNER:] = v[:, :LANES]
    cf[:, INNER:] = v[:, :LANES].astype(F32)
    raw[...] = v[HALO:, LANES:].astype(F32)

    def taps_body(j, _):
        at = pl.ds(pl.multiple_of(j * LANES, LANES), LANES)
        total = jnp.zeros((rows, LANES), F32) + taps[CONV : CONV + 1, at]
        for k in range(CONV):
            total = total + taps[k : k + 1, at] * cf[HALO - CONV + 1 + k : HALO - CONV + 1 + k + rows, at]
        sg = sigmoid(total)
        conv_low[:, at] = (total * sg).astype(BF16)
        slope[:, at] = sg * (1.0 + total * (1.0 - sg))
        return 0

    lax.fori_loop(0, CONV_CH // LANES, taps_body, 0)
    biased = raw[...] + heads[0:1, :]
    soft = jnp.maximum(biased, 0.0) + jnp.log1p(jnp.exp(-jnp.abs(biased)))
    keep = jnp.logical_and(iota((rows, LANES), 0) < left[0], iota((rows, LANES), 1) < HEADS)
    steps[...] = jnp.where(keep, soft, 0.0)
    rates = -jnp.exp(heads[1:2, :])
    for b in range(blocks):
        at = slice(b * SPAN, (b + 1) * SPAN)
        st = steps[at, :]
        incl, excl, total = head_terms(st, rates)
        wf = split(jnp.exp(total - incl) * st)
        wg = split(jnp.exp(excl) * st)
        bt = conv_low[at, INNER:].astype(F32).T[:STATE].astype(BF16)
        bt2 = jnp.concatenate([bt, bt], axis=1)
        tot = jnp.broadcast_to(jnp.exp(total), (8, LANES))
        for g in range(INNER // 256):
            cols = slice(g * 256, (g + 1) * 256)
            sp = spread[:, cols]
            xs = conv_low[at, cols].astype(F32)
            for w, dst in ((wf, hst), (wg, gst)):
                hi, lo = split((nn(w[0], sp) + nn(w[1], sp)) * xs)
                dst[b, :, cols] = nn(bt2, jnp.concatenate([hi, lo], axis=0))
            decb[b, :, cols] = expand(tot, sp)
    hv, gv, dv = hst[0], gst[blocks - 1], decb[0]
    for b in range(1, blocks):
        hv = hv * decb[b, 0:1, :] + hst[b]
        dv = dv * decb[b]
    for b in range(blocks - 2, -1, -1):
        gv = gv * decb[b, 0:1, :] + gst[b]
    dev[0] = hv
    dev[1] = gv
    dec[...] = dv


def front(x, full, gain, taps, heads, left, spread, n_h, cph, oph, wi):
    rows = x.shape[0] - HALO
    blocks = rows // SPAN
    vm = pl.BlockSpec(memory_space=pltpu.VMEM)
    sm = pl.BlockSpec(memory_space=pltpu.SMEM)
    sds = jax.ShapeDtypeStruct
    return pl.pallas_call(
        functools.partial(front_kernel, n_h, cph, oph, wi),
        out_shape=(
            sds((rows, D), BF16),
            sds((D, WIDE), BF16),
            sds((D, INNER), BF16),
            sds((rows, INNER), BF16),
            sds((rows + HALO, CONV_CH), BF16),
            sds((rows, CONV_CH), BF16),
            sds((rows, CONV_CH), F32),
            sds((rows, LANES), F32),
            sds((rows, LANES), F32),
            sds((blocks, STATE, INNER), F32),
            sds((blocks, STATE, INNER), F32),
            sds((2, STATE, INNER), F32),
            sds((blocks, 8, INNER), F32),
            sds((8, INNER), F32),
        ),
        in_specs=[vm, vm, vm, vm, vm, sm, vm],
        out_specs=(vm,) * 14,
        scratch_shapes=[pltpu.VMEM((rows + HALO, D), BF16), pltpu.VMEM((rows + HALO, CONV_CH), F32)],
        compiler_params=pltpu.CompilerParams(vmem_limit_bytes=VMEM_BYTES),
        name="front",
    )(x, full, gain, taps, heads, left, spread)


def half_masks(value):
    low = iota(value.shape, 1) < HEAD_DIM
    zero = jnp.zeros_like(value)
    return jnp.where(low, value, zero), jnp.where(low, zero, value)


def block_entries(blocks, dst, entering, local, decb, reverse):
    order = range(blocks - 1, -1, -1) if reverse else range(blocks)
    v = entering
    for b in order:
        dst[b] = v
        v = v * decb[b, 0:1, :] + local[b]


def middle_kernel(
    x, cot, gate, conv_low, steps, hst, gst, into, decb, w_out, heads, out_gain, left, spread,
    result, dgate, hgrad, gout, dgain, lst, mst, dev,
    hin, gin, el, eg, ho, gg_scr, glow,
):
    rows = x.shape[0]
    blocks = rows // SPAN
    rates = -jnp.exp(heads[1:2, :])
    block_entries(blocks, hin, into[0], hst, decb, False)
    block_entries(blocks, gin, into[1], gst, decb, True)
    row = iota((SPAN, SPAN), 0)
    col = iota((SPAN, SPAN), 1)
    after = row >= col
    twice = 1.0 + (row == col).astype(F32)
    skip8 = jnp.broadcast_to(heads[2:3, :], (8, LANES))

    def block_body(b, _):
        at = pl.ds(pl.multiple_of(b * SPAN, SPAN), SPAN)
        st = steps[at, :]
        incl, excl, total = head_terms(st, rates)
        incl_t, excl_t, st_t = incl.T, excl.T, st.T
        bc = conv_low[at, INNER:].astype(F32)
        cb = pltpu.roll(bc, STATE, 1)
        c_low = half_masks(cb)[0].astype(BF16)
        inter = nt(c_low, bc.astype(BF16)) * twice
        cc = cb[:, :STATE].astype(BF16)
        for dst, val in ((el, jnp.exp(incl)), (eg, jnp.exp(total - excl))):
            hi, lo = split(val)
            for g in range(INNER // 256):
                cols = slice(g * 256, (g + 1) * 256)
                dst[at, cols] = nn(hi, spread[:, cols]) + nn(lo, spread[:, cols])
        for pair in range(HEADS // 2):
            cols = slice(pair * LANES, (pair + 1) * LANES)
            xs = conv_low[at, cols]
            mix = []
            for h in (2 * pair, 2 * pair + 1):
                gap = jnp.where(
                    after,
                    incl[:, h : h + 1] - incl_t[h : h + 1, :],
                    excl_t[h : h + 1, :] - excl[:, h : h + 1],
                )
                mix.append(inter * jnp.exp(gap) * st_t[h : h + 1, :])
            x0, x1 = half_masks(xs)
            y = nn_split(jnp.concatenate(mix, axis=1), jnp.concatenate([x0, x1], axis=0))
            hh, hl = split(hin[b, :, cols])
            gh, gl = split(gin[b, :, cols])
            y = y + el[at, cols] * (nn(cc, hh) + nn(cc, hl))
            y = y + eg[at, cols] * (nn(cc, gh) + nn(cc, gl))
            y = y + expand(skip8, spread[:, cols])[0:1] * xs.astype(F32)
            ho[at, cols] = y.astype(BF16)
        return 0

    lax.fori_loop(0, blocks, block_body, 0)
    keep = (iota((rows, 1), 0) < left[0]).astype(F32)
    bgrad = (cot[...].astype(F32) * keep).astype(BF16)
    for g in range(INNER // 256):
        cols = slice(g * 256, (g + 1) * 256)
        gg_scr[:, cols] = nn(bgrad, w_out[:, cols])
    dgain[...] = jnp.zeros_like(dgain)

    def gate_body(i, _):
        at = pl.ds(pl.multiple_of(i * 16, 16), 16)
        z = gate[at, :].astype(F32)
        hv = ho[at, :].astype(F32)
        sg = sigmoid(z)
        sl = z * sg
        gated = hv * sl
        r = lax.rsqrt(jnp.mean(gated * gated, axis=1, keepdims=True) + EPS)
        unit = gated * r
        glow[at, :] = (unit * out_gain[...]).astype(BF16)
        gr = gg_scr[at, :]
        prod = gr * unit
        dgain[...] += prod[0:8] + prod[8:16]
        gg = gr * out_gain[...]
        dg = r * (gg - unit * jnp.mean(gg * unit, axis=1, keepdims=True))
        hgrad[at, :] = (dg * sl).astype(BF16)
        dgate[at, :] = (dg * hv * (sg * (1.0 + z * (1.0 - sg)))).astype(BF16)
        return 0

    lax.fori_loop(0, rows // 16, gate_body, 0)
    for g in range(D // 256):
        cols = slice(g * 256, (g + 1) * 256)
        branch = nt(glow[...], w_out[cols, :])
        result[:, cols] = (x[:, cols].astype(F32) + keep * branch).astype(BF16)
    bgt = bgrad.T
    for g in range(INNER // 256):
        cols = slice(g * 256, (g + 1) * 256)
        gout[:, cols] = nn(bgt, glow[:, cols])

    def state_body(b, _):
        at = pl.ds(pl.multiple_of(b * SPAN, SPAN), SPAN)
        ct = conv_low[at, INNER:].astype(F32).T[STATE:].astype(BF16)
        ct2 = jnp.concatenate([ct, ct], axis=1)
        for g in range(INNER // 256):
            cols = slice(g * 256, (g + 1) * 256)
            dy = hgrad[at, cols].astype(F32)
            for scale, dst in ((el, lst), (eg, mst)):
                hi, lo = split(scale[at, cols] * dy)
                dst[b, :, cols] = nn(ct2, jnp.concatenate([hi, lo], axis=0))
        return 0

    lax.fori_loop(0, blocks, state_body, 0)
    mv, lv = mst[0], lst[blocks - 1]
    for b in range(1, blocks):
        mv = mv * decb[b, 0:1, :] + mst[b]
    for b in range(blocks - 2, -1, -1):
        lv = lv * decb[b, 0:1, :] + lst[b]
    dev[0] = mv
    dev[1] = lv


def middle(x, cot, gate, conv_low, steps, hst, gst, into, decb, w_out, heads, out_gain, left, spread):
    rows = x.shape[0]
    blocks = rows // SPAN
    vm = pl.BlockSpec(memory_space=pltpu.VMEM)
    sm = pl.BlockSpec(memory_space=pltpu.SMEM)
    sds = jax.ShapeDtypeStruct
    big = pltpu.VMEM((rows, INNER), F32)
    low = pltpu.VMEM((rows, INNER), BF16)
    st = pltpu.VMEM((blocks, STATE, INNER), F32)
    return pl.pallas_call(
        middle_kernel,
        out_shape=(
            sds((rows, D), BF16),
            sds((rows, INNER), BF16),
            sds((rows, INNER), BF16),
            sds((D, INNER), F32),
            sds((8, INNER), F32),
            sds((blocks, STATE, INNER), F32),
            sds((blocks, STATE, INNER), F32),
            sds((2, STATE, INNER), F32),
        ),
        in_specs=[vm] * 12 + [sm, vm],
        out_specs=(vm,) * 8,
        scratch_shapes=[st, st, big, big, low, big, low],
        compiler_params=pltpu.CompilerParams(vmem_limit_bytes=VMEM_BYTES),
        name="middle",
    )(x, cot, gate, conv_low, steps, hst, gst, into, decb, w_out, heads, out_gain, left, spread)


def back_kernel(
    conv_low, hgrad, steps, raw, slope, conv_in, hst, gst, lst, mst, into, adj, decb, heads, left, spread,
    dpre, draw, dheads, dtaps,
    hin, gin, lend, mstart, at_f, at_g, cf,
):
    rows = hgrad.shape[0]
    blocks = rows // SPAN
    rates = -jnp.exp(heads[1:2, :])
    block_entries(blocks, hin, into[0], hst, decb, False)
    block_entries(blocks, gin, into[1], gst, decb, True)
    block_entries(blocks, mstart, adj[0], mst, decb, False)
    block_entries(blocks, lend, adj[1], lst, decb, True)
    row = iota((SPAN, SPAN), 0)
    col = iota((SPAN, SPAN), 1)
    later = col >= row
    twice = 1.0 + (row == col).astype(F32)
    skip8 = jnp.broadcast_to(heads[2:3, :], (8, LANES))
    dheads[...] = jnp.zeros_like(dheads)
    at_f[...] = jnp.zeros_like(at_f)
    at_g[...] = jnp.zeros_like(at_g)

    def block_body(b, _):
        at = pl.ds(pl.multiple_of(b * SPAN, SPAN), SPAN)
        st = steps[at, :]
        incl, excl, total = head_terms(st, rates)
        incl_t, excl_t = incl.T, excl.T
        bc = conv_low[at, INNER:].astype(F32)
        cb = pltpu.roll(bc, STATE, 1)
        b_low = half_masks(bc)[0].astype(BF16)
        inter = nt(b_low, cb.astype(BF16))
        inter2 = inter * twice
        bb = bc[:, :STATE].astype(BF16)
        cc = cb[:, :STATE].astype(BF16)
        scales = [split(v) for v in (st, jnp.exp(incl), jnp.exp(total - excl), jnp.exp(total - incl), jnp.exp(excl))]
        q_t = jnp.zeros((SPAN, SPAN), F32)
        back_f = jnp.zeros((SPAN, LANES), F32)
        back_g = jnp.zeros((SPAN, LANES), F32)
        red_f = jnp.zeros((SPAN, LANES), F32)
        red_g = jnp.zeros((SPAN, LANES), F32)
        red_s = jnp.zeros((SPAN, LANES), F32)
        red_k = jnp.zeros((SPAN, LANES), F32)
        cross_f = jnp.zeros((8, LANES), F32)
        cross_g = jnp.zeros((8, LANES), F32)
        dbc = jnp.zeros((SPAN, LANES), F32)
        zero_state = jnp.zeros((STATE, LANES), BF16)
        for pair in range(HEADS // 2):
            cols = slice(pair * LANES, (pair + 1) * LANES)
            sp = spread[:, cols]
            st_e, el, eg, tl, ex = [nn(hi, sp) + nn(lo, sp) for hi, lo in scales]
            xs = conv_low[at, cols].astype(F32)
            dyl = hgrad[at, cols]
            dy = dyl.astype(F32)
            xst = st_e * xs
            xh, xl = split(xst)
            xh0, xh1 = half_masks(xh)
            xl0, xl1 = half_masks(xl)
            dy2 = jnp.concatenate([dyl, dyl], axis=1)
            kern = []
            for h, xa, xb in ((2 * pair, xh0, xl0), (2 * pair + 1, xh1, xl1)):
                gap = jnp.where(
                    later,
                    incl_t[h : h + 1, :] - incl[:, h : h + 1],
                    excl[:, h : h + 1] - excl_t[h : h + 1, :],
                )
                decay = jnp.exp(gap)
                kern.append(inter2 * decay)
                weigh = nt(jnp.concatenate([xa, xb], axis=1), dy2) * decay
                q_t = q_t + weigh * twice
                pairs = weigh * inter
                up = jnp.where(col > row, pairs, 0.0)
                down = jnp.where(col < row, pairs, 0.0)
                at_f[h : h + 1, :] = jnp.sum(up, axis=0, keepdims=True)
                at_g[h : h + 1, :] = jnp.sum(down, axis=0, keepdims=True)
                here = iota((SPAN, LANES), 1) == h
                back_f = jnp.where(here, jnp.sum(up, axis=1, keepdims=True), back_f)
                back_g = jnp.where(here, jnp.sum(down, axis=1, keepdims=True), back_g)
            dy0, dy1 = half_masks(dyl)
            dxu = nn_split(jnp.concatenate(kern, axis=1), jnp.concatenate([dy0, dy1], axis=0))
            hs, gs, ls, ms = hin[b, :, cols], gin[b, :, cols], lend[b, :, cols], mstart[b, :, cols]
            (hh, hl), (gh, gl), (lh, ll), (mh, ml) = split(hs), split(gs), split(ls), split(ms)
            into_f = el * (nn(cc, hh) + nn(cc, hl))
            into_g = eg * (nn(cc, gh) + nn(cc, gl))
            out_f = tl * (nn(bb, lh) + nn(bb, ll))
            out_g = ex * (nn(bb, mh) + nn(bb, ml))
            dxu = dxu + out_f + out_g
            skip = expand(skip8, sp)[0:1]
            dx = st_e * dxu + skip * dy
            dpre[at, cols] = dx * slope[at, cols]
            red_f = red_f + fold(dy * into_f - xst * out_f, sp)
            red_g = red_g + fold(dy * into_g - xst * out_g, sp)
            red_s = red_s + fold(xs * dxu, sp)
            red_k = red_k + fold(xs * dy, sp)
            dtot = decb[b, :, cols]
            h_end = hs * dtot[0:1] + hst[b, :, cols]
            g_start = gs * dtot[0:1] + gst[b, :, cols]
            cf_row = jnp.sum(ls * h_end, axis=0, keepdims=True)
            cg_row = jnp.sum(ms * g_start, axis=0, keepdims=True)
            cross_f = cross_f + fold(jnp.broadcast_to(cf_row, (8, LANES)), sp)
            cross_g = cross_g + fold(jnp.broadcast_to(cg_row, (8, LANES)), sp)
            lefts, rights = [], []
            for scaled, sh, sl_, lowhalf in (
                (xst * tl, lh, ll, True),
                (xst * ex, mh, ml, True),
                (el * dy, hh, hl, False),
                (eg * dy, gh, gl, False),
            ):
                ah, al = split(scaled)
                for a, s in ((ah, sh), (al, sh), (ah, sl_)):
                    lefts.append(a)
                    rights.append(
                        jnp.concatenate([s, zero_state] if lowhalf else [zero_state, s], axis=0)
                    )
            dbc = dbc + nt(jnp.concatenate(lefts, axis=1), jnp.concatenate(rights, axis=1))
        cb_lo, cb_hi = half_masks(cb)
        dbc = dbc + nn_split(q_t, cb_lo.astype(BF16)) + nn_split(q_t.T, cb_hi.astype(BF16))
        dpre[at, INNER:] = dbc * slope[at, INNER:]
        v_f = red_f + at_f[...].T - back_f
        v_g = red_g + at_g[...].T - back_g
        da = precise(tri_high(), v_f) + precise(tri_low(), v_g) + cross_f[0:1] + cross_g[0:1]
        dst = red_s + da * rates
        keep = jnp.logical_and(
            iota((SPAN, LANES), 0) + b * SPAN < left[0], iota((SPAN, LANES), 1) < HEADS
        )
        dr = jnp.where(keep, dst * sigmoid(raw[at, :] + heads[0:1, :]), 0.0)
        draw[at, :] = dr.astype(BF16)
        dheads[0:1, :] += jnp.sum(dr, axis=0, keepdims=True)
        dheads[1:2, :] += jnp.sum(da * st, axis=0, keepdims=True) * rates
        dheads[2:3, :] += jnp.sum(red_k, axis=0, keepdims=True)
        return 0

    lax.fori_loop(0, blocks, block_body, 0)
    cf[...] = conv_in[...].astype(F32)
    dtaps[...] = jnp.zeros_like(dtaps)

    def taps_body(j, _):
        cols = pl.ds(pl.multiple_of(j * LANES, LANES), LANES)
        dp = dpre[:, cols]
        for k in range(CONV):
            first = HALO - CONV + 1 + k
            dtaps[k : k + 1, cols] = jnp.sum(dp * cf[first : first + rows, cols], axis=0, keepdims=True)
        dtaps[CONV : CONV + 1, cols] = jnp.sum(dp, axis=0, keepdims=True)
        return 0

    lax.fori_loop(0, CONV_CH // LANES, taps_body, 0)


def back(conv_low, hgrad, steps, raw, slope, conv_in, hst, gst, lst, mst, into, adj, decb, heads, left, spread):
    rows = hgrad.shape[0]
    blocks = rows // SPAN
    vm = pl.BlockSpec(memory_space=pltpu.VMEM)
    sm = pl.BlockSpec(memory_space=pltpu.SMEM)
    sds = jax.ShapeDtypeStruct
    st = pltpu.VMEM((blocks, STATE, INNER), F32)
    return pl.pallas_call(
        back_kernel,
        out_shape=(
            sds((rows, CONV_CH), F32),
            sds((rows, LANES), BF16),
            sds((8, LANES), F32),
            sds((8, CONV_CH), F32),
        ),
        in_specs=[vm] * 14 + [sm, vm],
        out_specs=(vm,) * 4,
        scratch_shapes=[
            st, st, st, st,
            pltpu.VMEM((LANES, SPAN), F32),
            pltpu.VMEM((LANES, SPAN), F32),
            pltpu.VMEM((rows + HALO, CONV_CH), F32),
        ],
        compiler_params=pltpu.CompilerParams(vmem_limit_bytes=VMEM_BYTES),
        name="back",
    )(conv_low, hgrad, steps, raw, slope, conv_in, hst, gst, lst, mst, into, adj, decb, heads, left, spread)


def tail_kernel(
    dpre, halo, dgate, draw, nlow, w_in, x, cot, gain, taps,
    grad_x, gin, dgain,
    df, pg, ng,
):
    rows = x.shape[0]
    df[0:rows, :] = dpre[...]
    df[rows : rows + 8, :] = halo[...]

    def taps_body(j, _):
        cols = pl.ds(pl.multiple_of(j * LANES, LANES), LANES)
        total = jnp.zeros((rows, LANES), F32)
        for k in range(CONV):
            first = CONV - 1 - k
            total = total + taps[k : k + 1, cols] * df[first : first + rows, cols]
        pg[:, pl.ds(pl.multiple_of(INNER + j * LANES, LANES), LANES)] = total.astype(BF16)
        return 0

    lax.fori_loop(0, CONV_CH // LANES, taps_body, 0)
    pg[:, 0:INNER] = dgate[...]
    pg[:, INNER + CONV_CH :] = draw[...]
    nt_low = nlow[...].T
    ng[...] = jnp.zeros_like(ng)

    def proj_body(j, _):
        cols = pl.ds(pl.multiple_of(j * 256, 256), 256)
        part = pg[:, cols]
        gin[:, cols] = nn(nt_low, part)
        ng[...] += nt(part, w_in[:, cols])
        return 0

    lax.fori_loop(0, WIDE // 256, proj_body, 0)
    dgain[...] = jnp.zeros_like(dgain)

    def norm_body(i, _):
        at = pl.ds(pl.multiple_of(i * 16, 16), 16)
        v = x[at, :].astype(F32)
        r = lax.rsqrt(jnp.mean(v * v, axis=1, keepdims=True) + EPS)
        unit = v * r
        g = ng[at, :]
        prod = g * unit
        dgain[...] += prod[0:8] + prod[8:16]
        gg = g * gain[...]
        grad_x[at, :] = cot[at, :].astype(F32) + r * (gg - unit * jnp.mean(gg * unit, axis=1, keepdims=True))
        return 0

    lax.fori_loop(0, rows // 16, norm_body, 0)


def tail(dpre, halo, dgate, draw, nlow, w_in, x, cot, gain, taps):
    rows = x.shape[0]
    vm = pl.BlockSpec(memory_space=pltpu.VMEM)
    sds = jax.ShapeDtypeStruct
    return pl.pallas_call(
        tail_kernel,
        out_shape=(sds((rows, D), F32), sds((D, WIDE), F32), sds((8, D), F32)),
        in_specs=[vm] * 10,
        out_specs=(vm,) * 3,
        scratch_shapes=[
            pltpu.VMEM((rows + 8, CONV_CH), F32),
            pltpu.VMEM((rows, WIDE), BF16),
            pltpu.VMEM((rows, D), F32),
        ],
        compiler_params=pltpu.CompilerParams(vmem_limit_bytes=VMEM_BYTES),
        name="tail",
    )(dpre, halo, dgate, draw, nlow, w_in, x, cot, gain, taps)


def shifted(value, axis, steps):
    count = lax.axis_size(axis)
    first, last = (max(0, -steps), min(count, count - steps))
    return lax.ppermute(value, axis, [(source, source + steps) for source in range(first, last)])


def on_device(
    x_in, lengths, cotangent, w_in, w_out, small_params, row_in, col_in, row_out, col_out, small_second
):
    n_s = lax.axis_size("seq")
    n_h = lax.axis_size("head")
    seq_index = lax.axis_index("seq")
    head_index = lax.axis_index("head")
    rows = x_in.shape[0]
    rin, cph = w_in.shape
    oph, cout = w_out.shape
    rp = -(-rin // 16) * 16
    wi = tile_count(cph, n_h) * LANES
    wo = tile_count(oph, n_h) * LANES
    pay = jnp.zeros((rp, wi + wo), BF16)
    pay = lax.dynamic_update_slice(pay, w_in.astype(BF16), (0, lax.rem(cph * head_index, LANES)))
    pay = lax.dynamic_update_slice(pay, w_out.astype(BF16).T, (0, wi + lax.rem(oph * head_index, LANES)))
    full = gather(pay, n_s, n_h)[:, :, :rin].reshape(n_h, D, wi + wo)

    first = D + CONV * CONV_CH
    gain = small_params[:D].reshape(1, D)
    taps = jnp.zeros((8, CONV_CH), F32).at[: CONV + 1].set(
        small_params[D : first + CONV_CH].reshape(CONV + 1, CONV_CH)
    )
    first = first + CONV_CH
    heads = jnp.zeros((8, LANES), F32).at[:3, :HEADS].set(
        small_params[first : first + 3 * HEADS].reshape(3, HEADS)
    )
    out_gain = small_params[first + 3 * HEADS :].reshape(1, INNER)
    left = (lengths[0] - head_index * rows).reshape(1)
    spread = jnp.asarray(
        (np.arange(LANES)[:, None] == np.arange(INNER)[None, :] // HEAD_DIM).astype(np.float32)
    ).astype(BF16)
    x_halo = jnp.concatenate([shifted(x_in[rows - HALO :], "head", 1), x_in], axis=0)
    (nlow, w_full, o_full, gate, conv_in, conv_low, slope, raw, steps, hst, gst, dev, decb, dec) = front(
        x_halo, full, gain, taps, heads, left, spread, n_h, cph, oph, wi
    )
    into = chain(dev, dec, n_h, 1)
    result, dgate, hgrad, gout, og_part, lst, mst, dev2 = middle(
        x_in, cotangent, gate, conv_low, steps, hst, gst, into, decb, o_full, heads, out_gain, left, spread
    )
    adj = chain(dev2, dec, n_h, 2)
    dpre, draw, dheads, dtaps = back(
        conv_low, hgrad, steps, raw, slope, conv_in, hst, gst, lst, mst, into, adj, decb, heads, left, spread
    )
    halo = shifted(dpre[:8], "head", -1)
    grad_x, gin, ng_part = tail(dpre, halo, dgate, draw, nlow, w_full, x_in, cotangent, gain, taps)
    small_part = jnp.concatenate(
        [
            jnp.sum(ng_part, axis=0),
            dtaps[: CONV + 1].reshape(-1),
            dheads[:3, :HEADS].reshape(-1),
            jnp.sum(og_part, axis=0),
        ]
    )
    head_in = lax.psum_scatter(gin[:, :PROJ], "head", scatter_dimension=1, tiled=True)
    head_out = lax.psum_scatter(gout.T, "head", scatter_dimension=0, tiled=True)
    grad_in = lax.psum_scatter(head_in, "seq", scatter_dimension=0, tiled=True)
    grad_out = lax.psum_scatter(head_out, "seq", scatter_dimension=1, tiled=True)
    return (result, grad_x) + finish(
        grad_in, grad_out, small_part, w_in, w_out, small_params, row_in, col_in, row_out, col_out, small_second
    )


def finish(
    grad_in, grad_out, small_part, w_in, w_out, small_params, row_in, col_in, row_out, col_out, small_second
):
    seq_count = lax.axis_size("seq")
    head_count = lax.axis_size("head")
    seq_index = lax.axis_index("seq")
    head_index = lax.axis_index("head")
    square_in = grad_in * grad_in
    square_out = grad_out * grad_out
    rows_in, cols_in = grad_in.shape
    rows_out, cols_out = grad_out.shape
    row_in_part = lax.dynamic_update_slice_in_dim(
        jnp.zeros((D,), F32), jnp.sum(square_in, axis=1), seq_index * rows_in, 0
    )
    col_in_part = lax.dynamic_update_slice_in_dim(
        jnp.zeros((PROJ,), F32), jnp.sum(square_in, axis=0), head_index * cols_in, 0
    )
    row_out_part = lax.dynamic_update_slice_in_dim(
        jnp.zeros((INNER,), F32), jnp.sum(square_out, axis=1), head_index * rows_out, 0
    )
    col_out_part = lax.dynamic_update_slice_in_dim(
        jnp.zeros((D,), F32), jnp.sum(square_out, axis=0), seq_index * cols_out, 0
    )
    old_totals = jnp.stack([jnp.sum(row_in) / head_count, jnp.sum(row_out) / seq_count])
    small_grad, row_in_total, col_in_total, row_out_total, col_out_total, old_total = lax.psum(
        (small_part, row_in_part, col_in_part, row_out_part, col_out_part, old_totals), ("seq", "head")
    )
    decay = DECAY
    row_in_new = decay * row_in + (1.0 - decay) * (
        lax.dynamic_slice_in_dim(row_in_total, seq_index * rows_in, rows_in) / PROJ + EPS_SQUARE
    )
    col_in_new = decay * col_in + (1.0 - decay) * (
        lax.dynamic_slice_in_dim(col_in_total, head_index * cols_in, cols_in) / D + EPS_SQUARE
    )
    mean_in = decay * old_total[0] / D + (1.0 - decay) * (jnp.sum(row_in_total) / (D * PROJ) + EPS_SQUARE)
    row_out_new = decay * row_out + (1.0 - decay) * (
        lax.dynamic_slice_in_dim(row_out_total, head_index * rows_out, rows_out) / D + EPS_SQUARE
    )
    col_out_new = decay * col_out + (1.0 - decay) * (
        lax.dynamic_slice_in_dim(col_out_total, seq_index * cols_out, cols_out) / INNER + EPS_SQUARE
    )
    mean_out = decay * old_total[1] / INNER + (1.0 - decay) * (
        jnp.sum(row_out_total) / (INNER * D) + EPS_SQUARE
    )
    scaled_in = grad_in * lax.rsqrt(row_in_new[:, None] * col_in_new[None, :] / mean_in)
    scaled_out = grad_out * lax.rsqrt(row_out_new[:, None] * col_out_new[None, :] / mean_out)
    update_sums = lax.psum(
        jnp.stack([jnp.sum(scaled_in * scaled_in), jnp.sum(scaled_out * scaled_out)]), ("seq", "head")
    )
    spread_in = jnp.sqrt(update_sums[0] / (D * PROJ))
    spread_out = jnp.sqrt(update_sums[1] / (INNER * D))
    w_in_new = w_in - LEARN_RATE * scaled_in / jnp.maximum(1.0, spread_in / CLIP_RMS)
    w_out_new = w_out - LEARN_RATE * scaled_out / jnp.maximum(1.0, spread_out / CLIP_RMS)
    small_second_new = decay * small_second + (1.0 - decay) * (small_grad * small_grad + EPS_SQUARE)
    scaled_small = small_grad * lax.rsqrt(small_second_new)
    spread_small = jnp.sqrt(jnp.mean(scaled_small * scaled_small))
    small_new = small_params - LEARN_SMALL * scaled_small / jnp.maximum(1.0, spread_small / CLIP_RMS)
    return (
        grad_in, row_in_new, col_in_new, w_in_new, grad_out, row_out_new, col_out_new, w_out_new,
        small_grad, small_second_new, small_new,
    )


def solution(mesh):
    both = P(("seq", "head"), None)
    factors = (P("seq", "head"), P("seq"), P("head"), P("seq", "head"))
    return jax.shard_map(
        on_device,
        mesh=mesh,
        in_specs=(
            both, P("seq"), both, P("seq", "head"), P("head", "seq"), P(), P("seq"), P("head"), P("head"), P("seq"), P(),
        ),
        out_specs=(
            both, both, P("seq", "head"), P("seq"), P("head"), P("seq", "head"), P("head", "seq"), P("head"), P("seq"),
            P("head", "seq"), P(), P(), P(),
        ),
        check_vma=False,
    )
```

```python
import functools

import jax
import jax.numpy as jnp
import numpy as np
from jax import lax
from jax.experimental import pallas as pl
from jax.experimental.pallas import tpu as pltpu
from jax.sharding import PartitionSpec as P

D = 768
HEADS = 24
HEAD_DIM = 64
STATE = 64
CONV = 4
SPAN = 128
STEP = 8
INNER = 1536
CONV_CH = 1664
PROJ = 3224
WIDE = 3328
LANES = 128
HALO = 16

EPS = 1e-05
EPS_SQUARE = 1e-30
LEARN_RATE = 0.3
LEARN_SMALL = 3.0
CLIP_RMS = 0.1
DECAY = 1.0 - STEP ** (-0.8)
F32 = jnp.float32
BF16 = jnp.bfloat16
HIGHEST = lax.Precision.HIGHEST
MESH = pl.DeviceIdType.MESH
VMEM_BYTES = 60 << 20


def nn(left, right):
    return lax.dot_general(left, right, (((1,), (0,)), ((), ())), preferred_element_type=F32)


def nt(left, right):
    return lax.dot_general(left, right, (((1,), (1,)), ((), ())), preferred_element_type=F32)


def split(value):
    high = value.astype(BF16)
    return high, (value - high.astype(F32)).astype(BF16)


def nn_split(value, exact):
    high, low = split(value)
    return nn(high, exact) + nn(low, exact)


def expand(value, spread):
    return nn_split(value, spread)


def fold(value, spread):
    high, low = split(value)
    return nt(high, spread) + nt(low, spread)


def iota(shape, dim):
    return lax.broadcasted_iota(jnp.int32, shape, dim)


def tri_low():
    return (iota((SPAN, SPAN), 0) >= iota((SPAN, SPAN), 1)).astype(F32)


def tri_high():
    return (iota((SPAN, SPAN), 0) <= iota((SPAN, SPAN), 1)).astype(F32)


def precise(left, right):
    return lax.dot_general(
        left, right, (((1,), (0,)), ((), ())), precision=HIGHEST, preferred_element_type=F32
    )


def sigmoid(value):
    return 1.0 / (1.0 + jnp.exp(-value))


def tiles_of(per_part, index):
    return (per_part * index) // LANES, -(-(per_part * (index + 1)) // LANES)


def tile_count(per_part, parts):
    return max(e - s for s, e in (tiles_of(per_part, i) for i in range(parts)))


def gather_kernel(n_s, n_h, pay, full, lsem, zs, zr, ps, pr, cs, cr):
    s = lax.axis_index("seq")
    h = lax.axis_index("head")
    n_c = n_s // 2
    chip = s // 2
    core = lax.rem(s, 2)
    sib = chip * 2 + (1 - core)
    zpeer = [lax.rem(h + j, n_h) for j in range(1, n_h)]
    cpeer = [lax.rem(chip + j, n_c) for j in range(1, n_c)]
    bar = pltpu.get_barrier_semaphore()
    for z in zpeer:
        pl.semaphore_signal(bar, inc=1, device_id=(s, z), device_id_type=MESH)
    for c in cpeer:
        pl.semaphore_signal(bar, inc=1, device_id=(c * 2 + core, h), device_id_type=MESH)
    pl.semaphore_signal(bar, inc=1, device_id=(sib, h), device_id_type=MESH)
    pl.semaphore_wait(bar, n_h + n_c - 1)

    def rc(src, dst, ss, rs, dev):
        return pltpu.make_async_remote_copy(
            src_ref=src, dst_ref=dst, send_sem=ss, recv_sem=rs, device_id=dev, device_id_type=MESH
        )

    local = pltpu.make_async_copy(pay, full.at[h, s], lsem)
    local.start()
    sends = []

    def go(c):
        c.start()
        sends.append(c)

    for j, z in enumerate(zpeer):
        go(rc(pay, full.at[h, s], zs.at[j], zr.at[h], (s, z)))

    def plane(src, k, slot):
        for j, c in enumerate(cpeer):
            go(rc(src, full.at[k, s], ps.at[slot, j], pr.at[chip, k], (c * 2 + core, h)))
        go(rc(src, full.at[k, s], cs.at[slot, 0], cr.at[chip, k], (sib, h)))

    plane(pay, h, 0)
    order = [h] + zpeer

    def relay(kk, i):
        for j, c in enumerate(cpeer):
            o = c * 2 + core
            rc(pay, full.at[kk, o], zs.at[0], pr.at[c, kk], (s, zpeer[0])).wait_recv()
            go(rc(full.at[kk, o], full.at[kk, o], cs.at[i, j + 1], cr.at[c, kk], (sib, h)))

    for i, k in enumerate(zpeer):
        rc(pay, full.at[k, s], zs.at[i], zr.at[k], (s, k)).wait_recv()
        plane(full.at[k, s], k, i + 1)
        relay(order[i], i)
    relay(order[-1], n_h - 1)
    for kk in order:
        for c in [chip] + cpeer:
            rc(pay, full.at[kk, c * 2 + 1 - core], zs.at[0], cr.at[c, kk], (sib, h)).wait_recv()
    for c in sends:
        c.wait_send()
    local.wait()


def gather(pay, n_s, n_h):
    n_c = n_s // 2
    dma = pltpu.SemaphoreType.DMA
    return pl.pallas_call(
        functools.partial(gather_kernel, n_s, n_h),
        out_shape=jax.ShapeDtypeStruct((n_h, n_s) + pay.shape, pay.dtype),
        in_specs=[pl.BlockSpec(memory_space=pl.ANY)],
        out_specs=pl.BlockSpec(memory_space=pl.ANY),
        scratch_shapes=[
            dma,
            dma((n_h - 1,)),
            dma((n_h,)),
            dma((n_h, n_c - 1)),
            dma((n_c, n_h)),
            dma((n_h, n_c)),
            dma((n_c, n_h)),
        ],
        compiler_params=pltpu.CompilerParams(collective_id=0, has_side_effects=True),
        name="gather_weights",
    )(pay)


def chain_kernel(n_h, dev, dec, out, snd, us, ur, ds, dr):
    s = lax.axis_index("seq")
    h = lax.axis_index("head")
    up = lax.rem(h + 1, n_h)
    down = lax.rem(h + n_h - 1, n_h)
    bar = pltpu.get_barrier_semaphore()
    for z in (up, down):
        pl.semaphore_signal(bar, inc=1, device_id=(s, z), device_id_type=MESH)
    pl.semaphore_wait(bar, 2)
    chain_run(n_h, s, h, up, down, dev, dec, out, snd, us, ur, ds, dr)


CHAIN_PARTS = 4


def chain_run(n_h, s, h, up, down, dev, dec, out, snd, us, ur, ds, dr):
    parts = CHAIN_PARTS
    width = STATE // parts
    inner = jnp.logical_and(h > 0, h < n_h - 1)

    def rc(d, c, sem_s, sem_r, dev_h):
        at = pl.ds(c * width, width)
        return pltpu.make_async_remote_copy(
            src_ref=snd.at[d, at],
            dst_ref=out.at[d, at],
            send_sem=sem_s.at[c],
            recv_sem=sem_r.at[c],
            device_id=(s, dev_h),
            device_id_type=MESH,
        )

    @pl.when(h == 0)
    def _():
        out[0] = jnp.zeros((STATE, INNER), F32)
        snd[0] = dev[0]
        for c in range(parts):
            rc(0, c, us, ur, up).start()

    @pl.when(h == n_h - 1)
    def _():
        out[1] = jnp.zeros((STATE, INNER), F32)
        snd[1] = dev[1]
        for c in range(parts):
            rc(1, c, ds, dr, down).start()

    def up_step(c):
        at = slice(c * width, (c + 1) * width)

        @pl.when(h > 0)
        def _():
            rc(0, c, us, ur, down).wait_recv()

        @pl.when(inner)
        def _():
            snd[0, at] = out[0, at] * dec[0:1] + dev[0, at]
            rc(0, c, us, ur, up).start()

    def down_step(c):
        at = slice(c * width, (c + 1) * width)

        @pl.when(h < n_h - 1)
        def _():
            rc(1, c, ds, dr, up).wait_recv()

        @pl.when(inner)
        def _():
            snd[1, at] = out[1, at] * dec[0:1] + dev[1, at]
            rc(1, c, ds, dr, down).start()

    @pl.when(h < n_h // 2)
    def _():
        up_step(0)
        for c in range(parts):
            if c + 1 < parts:
                up_step(c + 1)
            down_step(c)

    @pl.when(h >= n_h // 2)
    def _():
        down_step(0)
        for c in range(parts):
            if c + 1 < parts:
                down_step(c + 1)
            up_step(c)

    @pl.when(h < n_h - 1)
    def _():
        for c in range(parts):
            rc(0, c, us, ur, up).wait_send()

    @pl.when(h > 0)
    def _():
        for c in range(parts):
            rc(1, c, ds, dr, down).wait_send()


def chain(dev, dec, n_h, cid):
    dma = pltpu.SemaphoreType.DMA
    vm = pl.BlockSpec(memory_space=pltpu.VMEM)
    return pl.pallas_call(
        functools.partial(chain_kernel, n_h),
        out_shape=jax.ShapeDtypeStruct((2, STATE, INNER), F32),
        in_specs=[vm, vm],
        out_specs=vm,
        scratch_shapes=[pltpu.VMEM((2, STATE, INNER), F32)] + [dma((CHAIN_PARTS,))] * 4,
        compiler_params=pltpu.CompilerParams(
            collective_id=cid, has_side_effects=True, vmem_limit_bytes=VMEM_BYTES
        ),
        name="state_chain",
    )(dev, dec)


def head_terms(steps, rates):
    logs = steps * rates
    incl = precise(tri_low(), logs)
    return incl, incl - logs, incl[SPAN - 1 : SPAN]


def front_kernel(
    n_h, cph, oph, wi,
    x, full, gain, taps, heads, left, spread,
    nlow, w_in, w_out, gate, conv_in, conv_low, slope, raw, steps, hst, gst, dev, decb, dec,
    nscr, cf,
):
    rows = nlow.shape[0]
    blocks = rows // SPAN

    def norm_body(i, _):
        at = pl.ds(pl.multiple_of(i * 16, 16), 16)
        v = x[at, :].astype(F32)
        n = v * lax.rsqrt(jnp.mean(v * v, axis=1, keepdims=True) + EPS) * gain[...]
        nscr[at, :] = n.astype(BF16)
        return 0

    lax.fori_loop(0, (rows + HALO) // 16, norm_body, 0)
    nlow[...] = nscr[HALO:, :]
    for per, width, base, dst in ((cph, WIDE, 0, w_in), (oph, INNER, wi, w_out)):
        for tile in range(width // LANES):
            parts = []
            for i in range(n_h):
                t0, t1 = tiles_of(per, i)
                if t0 <= tile < t1:
                    at = base + (tile - t0) * LANES
                    parts.append(full[i, :, at : at + LANES])
            v = parts[0] if len(parts) == 1 else parts[0] + parts[1]
            dst[:, tile * LANES : (tile + 1) * LANES] = v

    def gate_body(j, _):
        at = pl.ds(pl.multiple_of(j * 256, 256), 256)
        gate[:, at] = nn(nscr[HALO:, :], w_in[:, at]).astype(BF16)
        return 0

    lax.fori_loop(0, INNER // 256, gate_body, 0)

    def conv_body(j, _):
        at = pl.ds(pl.multiple_of(j * 256, 256), 256)
        v = nn(nscr[...], w_in[:, pl.ds(pl.multiple_of(INNER + j * 256, 256), 256)]).astype(BF16)
        conv_in[:, at] = v
        cf[:, at] = v.astype(F32)
        return 0

    lax.fori_loop(0, INNER // 256, conv_body, 0)
    v = nn(nscr[...], w_in[:, 2 * INNER : WIDE]).astype(BF16)
    conv_in[:, INNER:] = v[:, :LANES]
    cf[:, INNER:] = v[:, :LANES].astype(F32)
    raw[...] = v[HALO:, LANES:].astype(F32)

    def taps_body(j, _):
        at = pl.ds(pl.multiple_of(j * LANES, LANES), LANES)
        total = jnp.zeros((rows, LANES), F32) + taps[CONV : CONV + 1, at]
        for k in range(CONV):
            total = total + taps[k : k + 1, at] * cf[HALO - CONV + 1 + k : HALO - CONV + 1 + k + rows, at]
        sg = sigmoid(total)
        conv_low[:, at] = (total * sg).astype(BF16)
        slope[:, at] = sg * (1.0 + total * (1.0 - sg))
        return 0

    lax.fori_loop(0, CONV_CH // LANES, taps_body, 0)
    biased = raw[...] + heads[0:1, :]
    soft = jnp.maximum(biased, 0.0) + jnp.log1p(jnp.exp(-jnp.abs(biased)))
    keep = jnp.logical_and(iota((rows, LANES), 0) < left[0], iota((rows, LANES), 1) < HEADS)
    steps[...] = jnp.where(keep, soft, 0.0)
    rates = -jnp.exp(heads[1:2, :])
    for b in range(blocks):
        at = slice(b * SPAN, (b + 1) * SPAN)
        st = steps[at, :]
        incl, excl, total = head_terms(st, rates)
        wf = split(jnp.exp(total - incl) * st)
        wg = split(jnp.exp(excl) * st)
        bt = conv_low[at, INNER:].astype(F32).T[:STATE].astype(BF16)
        bt2 = jnp.concatenate([bt, bt], axis=1)
        tot = jnp.broadcast_to(jnp.exp(total), (8, LANES))
        for g in range(INNER // 256):
            cols = slice(g * 256, (g + 1) * 256)
            sp = spread[:, cols]
            xs = conv_low[at, cols].astype(F32)
            for w, dst in ((wf, hst), (wg, gst)):
                hi, lo = split((nn(w[0], sp) + nn(w[1], sp)) * xs)
                dst[b, :, cols] = nn(bt2, jnp.concatenate([hi, lo], axis=0))
            decb[b, :, cols] = expand(tot, sp)
    hv, gv, dv = hst[0], gst[blocks - 1], decb[0]
    for b in range(1, blocks):
        hv = hv * decb[b, 0:1, :] + hst[b]
        dv = dv * decb[b]
    for b in range(blocks - 2, -1, -1):
        gv = gv * decb[b, 0:1, :] + gst[b]
    dev[0] = hv
    dev[1] = gv
    dec[...] = dv


def front(x, full, gain, taps, heads, left, spread, n_h, cph, oph, wi):
    rows = x.shape[0] - HALO
    blocks = rows // SPAN
    vm = pl.BlockSpec(memory_space=pltpu.VMEM)
    sm = pl.BlockSpec(memory_space=pltpu.SMEM)
    sds = jax.ShapeDtypeStruct
    return pl.pallas_call(
        functools.partial(front_kernel, n_h, cph, oph, wi),
        out_shape=(
            sds((rows, D), BF16),
            sds((D, WIDE), BF16),
            sds((D, INNER), BF16),
            sds((rows, INNER), BF16),
            sds((rows + HALO, CONV_CH), BF16),
            sds((rows, CONV_CH), BF16),
            sds((rows, CONV_CH), F32),
            sds((rows, LANES), F32),
            sds((rows, LANES), F32),
            sds((blocks, STATE, INNER), F32),
            sds((blocks, STATE, INNER), F32),
            sds((2, STATE, INNER), F32),
            sds((blocks, 8, INNER), F32),
            sds((8, INNER), F32),
        ),
        in_specs=[vm, vm, vm, vm, vm, sm, vm],
        out_specs=(vm,) * 14,
        scratch_shapes=[pltpu.VMEM((rows + HALO, D), BF16), pltpu.VMEM((rows + HALO, CONV_CH), F32)],
        compiler_params=pltpu.CompilerParams(vmem_limit_bytes=VMEM_BYTES),
        name="front",
    )(x, full, gain, taps, heads, left, spread)


def half_masks(value):
    low = iota(value.shape, 1) < HEAD_DIM
    zero = jnp.zeros_like(value)
    return jnp.where(low, value, zero), jnp.where(low, zero, value)


def block_entries(blocks, dst, entering, local, decb, reverse):
    order = range(blocks - 1, -1, -1) if reverse else range(blocks)
    v = entering
    for b in order:
        dst[b] = v
        v = v * decb[b, 0:1, :] + local[b]


def middle_kernel(
    x, cot, gate, conv_low, steps, hst, gst, into, decb, w_out, heads, out_gain, left, spread,
    result, dgate, hgrad, gout, dgain, lst, mst, dev,
    hin, gin, el, eg, ho, gg_scr, glow,
):
    rows = x.shape[0]
    blocks = rows // SPAN
    rates = -jnp.exp(heads[1:2, :])
    block_entries(blocks, hin, into[0], hst, decb, False)
    block_entries(blocks, gin, into[1], gst, decb, True)
    row = iota((SPAN, SPAN), 0)
    col = iota((SPAN, SPAN), 1)
    after = row >= col
    twice = 1.0 + (row == col).astype(F32)
    skip8 = jnp.broadcast_to(heads[2:3, :], (8, LANES))

    def block_body(b, _):
        at = pl.ds(pl.multiple_of(b * SPAN, SPAN), SPAN)
        st = steps[at, :]
        incl, excl, total = head_terms(st, rates)
        incl_t, excl_t, st_t = incl.T, excl.T, st.T
        bc = conv_low[at, INNER:].astype(F32)
        cb = pltpu.roll(bc, STATE, 1)
        c_low = half_masks(cb)[0].astype(BF16)
        inter = nt(c_low, bc.astype(BF16)) * twice
        cc = cb[:, :STATE].astype(BF16)
        for dst, val in ((el, jnp.exp(incl)), (eg, jnp.exp(total - excl))):
            hi, lo = split(val)
            for g in range(INNER // 256):
                cols = slice(g * 256, (g + 1) * 256)
                dst[at, cols] = nn(hi, spread[:, cols]) + nn(lo, spread[:, cols])
        for pair in range(HEADS // 2):
            cols = slice(pair * LANES, (pair + 1) * LANES)
            xs = conv_low[at, cols]
            mix = []
            for h in (2 * pair, 2 * pair + 1):
                gap = jnp.where(
                    after,
                    incl[:, h : h + 1] - incl_t[h : h + 1, :],
                    excl_t[h : h + 1, :] - excl[:, h : h + 1],
                )
                mix.append(inter * jnp.exp(gap) * st_t[h : h + 1, :])
            x0, x1 = half_masks(xs)
            y = nn_split(jnp.concatenate(mix, axis=1), jnp.concatenate([x0, x1], axis=0))
            hh, hl = split(hin[b, :, cols])
            gh, gl = split(gin[b, :, cols])
            y = y + el[at, cols] * (nn(cc, hh) + nn(cc, hl))
            y = y + eg[at, cols] * (nn(cc, gh) + nn(cc, gl))
            y = y + expand(skip8, spread[:, cols])[0:1] * xs.astype(F32)
            ho[at, cols] = y.astype(BF16)
        return 0

    lax.fori_loop(0, blocks, block_body, 0)
    keep = (iota((rows, 1), 0) < left[0]).astype(F32)
    bgrad = (cot[...].astype(F32) * keep).astype(BF16)
    for g in range(INNER // 256):
        cols = slice(g * 256, (g + 1) * 256)
        gg_scr[:, cols] = nn(bgrad, w_out[:, cols])
    dgain[...] = jnp.zeros_like(dgain)

    def gate_body(i, _):
        at = pl.ds(pl.multiple_of(i * 16, 16), 16)
        z = gate[at, :].astype(F32)
        hv = ho[at, :].astype(F32)
        sg = sigmoid(z)
        sl = z * sg
        gated = hv * sl
        r = lax.rsqrt(jnp.mean(gated * gated, axis=1, keepdims=True) + EPS)
        unit = gated * r
        glow[at, :] = (unit * out_gain[...]).astype(BF16)
        gr = gg_scr[at, :]
        prod = gr * unit
        dgain[...] += prod[0:8] + prod[8:16]
        gg = gr * out_gain[...]
        dg = r * (gg - unit * jnp.mean(gg * unit, axis=1, keepdims=True))
        hgrad[at, :] = (dg * sl).astype(BF16)
        dgate[at, :] = (dg * hv * (sg * (1.0 + z * (1.0 - sg)))).astype(BF16)
        return 0

    lax.fori_loop(0, rows // 16, gate_body, 0)
    for g in range(D // 256):
        cols = slice(g * 256, (g + 1) * 256)
        branch = nt(glow[...], w_out[cols, :])
        result[:, cols] = (x[:, cols].astype(F32) + keep * branch).astype(BF16)
    bgt = bgrad.T
    for g in range(INNER // 256):
        cols = slice(g * 256, (g + 1) * 256)
        gout[:, cols] = nn(bgt, glow[:, cols])

    def state_body(b, _):
        at = pl.ds(pl.multiple_of(b * SPAN, SPAN), SPAN)
        ct = conv_low[at, INNER:].astype(F32).T[STATE:].astype(BF16)
        ct2 = jnp.concatenate([ct, ct], axis=1)
        for g in range(INNER // 256):
            cols = slice(g * 256, (g + 1) * 256)
            dy = hgrad[at, cols].astype(F32)
            for scale, dst in ((el, lst), (eg, mst)):
                hi, lo = split(scale[at, cols] * dy)
                dst[b, :, cols] = nn(ct2, jnp.concatenate([hi, lo], axis=0))
        return 0

    lax.fori_loop(0, blocks, state_body, 0)
    mv, lv = mst[0], lst[blocks - 1]
    for b in range(1, blocks):
        mv = mv * decb[b, 0:1, :] + mst[b]
    for b in range(blocks - 2, -1, -1):
        lv = lv * decb[b, 0:1, :] + lst[b]
    dev[0] = mv
    dev[1] = lv


def middle(x, cot, gate, conv_low, steps, hst, gst, into, decb, w_out, heads, out_gain, left, spread):
    rows = x.shape[0]
    blocks = rows // SPAN
    vm = pl.BlockSpec(memory_space=pltpu.VMEM)
    sm = pl.BlockSpec(memory_space=pltpu.SMEM)
    sds = jax.ShapeDtypeStruct
    big = pltpu.VMEM((rows, INNER), F32)
    low = pltpu.VMEM((rows, INNER), BF16)
    st = pltpu.VMEM((blocks, STATE, INNER), F32)
    return pl.pallas_call(
        middle_kernel,
        out_shape=(
            sds((rows, D), BF16),
            sds((rows, INNER), BF16),
            sds((rows, INNER), BF16),
            sds((D, INNER), F32),
            sds((8, INNER), F32),
            sds((blocks, STATE, INNER), F32),
            sds((blocks, STATE, INNER), F32),
            sds((2, STATE, INNER), F32),
        ),
        in_specs=[vm] * 12 + [sm, vm],
        out_specs=(vm,) * 8,
        scratch_shapes=[st, st, big, big, low, big, low],
        compiler_params=pltpu.CompilerParams(vmem_limit_bytes=VMEM_BYTES),
        name="middle",
    )(x, cot, gate, conv_low, steps, hst, gst, into, decb, w_out, heads, out_gain, left, spread)


def back_kernel(
    conv_low, hgrad, steps, raw, slope, conv_in, hst, gst, lst, mst, into, adj, decb, heads, left, spread,
    dpre, draw, dheads, dtaps,
    hin, gin, lend, mstart, at_f, at_g, cf,
):
    rows = hgrad.shape[0]
    blocks = rows // SPAN
    rates = -jnp.exp(heads[1:2, :])
    block_entries(blocks, hin, into[0], hst, decb, False)
    block_entries(blocks, gin, into[1], gst, decb, True)
    block_entries(blocks, mstart, adj[0], mst, decb, False)
    block_entries(blocks, lend, adj[1], lst, decb, True)
    row = iota((SPAN, SPAN), 0)
    col = iota((SPAN, SPAN), 1)
    later = col >= row
    twice = 1.0 + (row == col).astype(F32)
    skip8 = jnp.broadcast_to(heads[2:3, :], (8, LANES))
    dheads[...] = jnp.zeros_like(dheads)
    at_f[...] = jnp.zeros_like(at_f)
    at_g[...] = jnp.zeros_like(at_g)

    def block_body(b, _):
        at = pl.ds(pl.multiple_of(b * SPAN, SPAN), SPAN)
        st = steps[at, :]
        incl, excl, total = head_terms(st, rates)
        incl_t, excl_t = incl.T, excl.T
        bc = conv_low[at, INNER:].astype(F32)
        cb = pltpu.roll(bc, STATE, 1)
        b_low = half_masks(bc)[0].astype(BF16)
        inter = nt(b_low, cb.astype(BF16))
        inter2 = inter * twice
        bb = bc[:, :STATE].astype(BF16)
        cc = cb[:, :STATE].astype(BF16)
        scales = [split(v) for v in (st, jnp.exp(incl), jnp.exp(total - excl), jnp.exp(total - incl), jnp.exp(excl))]
        q_t = jnp.zeros((SPAN, SPAN), F32)
        back_f = jnp.zeros((SPAN, LANES), F32)
        back_g = jnp.zeros((SPAN, LANES), F32)
        red_f = jnp.zeros((SPAN, LANES), F32)
        red_g = jnp.zeros((SPAN, LANES), F32)
        red_s = jnp.zeros((SPAN, LANES), F32)
        red_k = jnp.zeros((SPAN, LANES), F32)
        cross_f = jnp.zeros((8, LANES), F32)
        cross_g = jnp.zeros((8, LANES), F32)
        dbc = jnp.zeros((SPAN, LANES), F32)
        zero_state = jnp.zeros((STATE, LANES), BF16)
        for pair in range(HEADS // 2):
            cols = slice(pair * LANES, (pair + 1) * LANES)
            sp = spread[:, cols]
            st_e, el, eg, tl, ex = [nn(hi, sp) + nn(lo, sp) for hi, lo in scales]
            xs = conv_low[at, cols].astype(F32)
            dyl = hgrad[at, cols]
            dy = dyl.astype(F32)
            xst = st_e * xs
            xh, xl = split(xst)
            xh0, xh1 = half_masks(xh)
            xl0, xl1 = half_masks(xl)
            dy2 = jnp.concatenate([dyl, dyl], axis=1)
            kern = []
            for h, xa, xb in ((2 * pair, xh0, xl0), (2 * pair + 1, xh1, xl1)):
                gap = jnp.where(
                    later,
                    incl_t[h : h + 1, :] - incl[:, h : h + 1],
                    excl[:, h : h + 1] - excl_t[h : h + 1, :],
                )
                decay = jnp.exp(gap)
                kern.append(inter2 * decay)
                weigh = nt(jnp.concatenate([xa, xb], axis=1), dy2) * decay
                q_t = q_t + weigh * twice
                pairs = weigh * inter
                up = jnp.where(col > row, pairs, 0.0)
                down = jnp.where(col < row, pairs, 0.0)
                at_f[h : h + 1, :] = jnp.sum(up, axis=0, keepdims=True)
                at_g[h : h + 1, :] = jnp.sum(down, axis=0, keepdims=True)
                here = iota((SPAN, LANES), 1) == h
                back_f = jnp.where(here, jnp.sum(up, axis=1, keepdims=True), back_f)
                back_g = jnp.where(here, jnp.sum(down, axis=1, keepdims=True), back_g)
            dy0, dy1 = half_masks(dyl)
            dxu = nn_split(jnp.concatenate(kern, axis=1), jnp.concatenate([dy0, dy1], axis=0))
            hs, gs, ls, ms = hin[b, :, cols], gin[b, :, cols], lend[b, :, cols], mstart[b, :, cols]
            (hh, hl), (gh, gl), (lh, ll), (mh, ml) = split(hs), split(gs), split(ls), split(ms)
            into_f = el * (nn(cc, hh) + nn(cc, hl))
            into_g = eg * (nn(cc, gh) + nn(cc, gl))
            out_f = tl * (nn(bb, lh) + nn(bb, ll))
            out_g = ex * (nn(bb, mh) + nn(bb, ml))
            dxu = dxu + out_f + out_g
            skip = expand(skip8, sp)[0:1]
            dx = st_e * dxu + skip * dy
            dpre[at, cols] = dx * slope[at, cols]
            red_f = red_f + fold(dy * into_f - xst * out_f, sp)
            red_g = red_g + fold(dy * into_g - xst * out_g, sp)
            red_s = red_s + fold(xs * dxu, sp)
            red_k = red_k + fold(xs * dy, sp)
            dtot = decb[b, :, cols]
            h_end = hs * dtot[0:1] + hst[b, :, cols]
            g_start = gs * dtot[0:1] + gst[b, :, cols]
            cf_row = jnp.sum(ls * h_end, axis=0, keepdims=True)
            cg_row = jnp.sum(ms * g_start, axis=0, keepdims=True)
            cross_f = cross_f + fold(jnp.broadcast_to(cf_row, (8, LANES)), sp)
            cross_g = cross_g + fold(jnp.broadcast_to(cg_row, (8, LANES)), sp)
            lefts, rights = [], []
            for scaled, sh, sl_, lowhalf in (
                (xst * tl, lh, ll, True),
                (xst * ex, mh, ml, True),
                (el * dy, hh, hl, False),
                (eg * dy, gh, gl, False),
            ):
                ah, al = split(scaled)
                for a, s in ((ah, sh), (al, sh), (ah, sl_)):
                    lefts.append(a)
                    rights.append(
                        jnp.concatenate([s, zero_state] if lowhalf else [zero_state, s], axis=0)
                    )
            dbc = dbc + nt(jnp.concatenate(lefts, axis=1), jnp.concatenate(rights, axis=1))
        cb_lo, cb_hi = half_masks(cb)
        dbc = dbc + nn_split(q_t, cb_lo.astype(BF16)) + nn_split(q_t.T, cb_hi.astype(BF16))
        dpre[at, INNER:] = dbc * slope[at, INNER:]
        v_f = red_f + at_f[...].T - back_f
        v_g = red_g + at_g[...].T - back_g
        da = precise(tri_high(), v_f) + precise(tri_low(), v_g) + cross_f[0:1] + cross_g[0:1]
        dst = red_s + da * rates
        keep = jnp.logical_and(
            iota((SPAN, LANES), 0) + b * SPAN < left[0], iota((SPAN, LANES), 1) < HEADS
        )
        dr = jnp.where(keep, dst * sigmoid(raw[at, :] + heads[0:1, :]), 0.0)
        draw[at, :] = dr.astype(BF16)
        dheads[0:1, :] += jnp.sum(dr, axis=0, keepdims=True)
        dheads[1:2, :] += jnp.sum(da * st, axis=0, keepdims=True) * rates
        dheads[2:3, :] += jnp.sum(red_k, axis=0, keepdims=True)
        return 0

    lax.fori_loop(0, blocks, block_body, 0)
    cf[...] = conv_in[...].astype(F32)
    dtaps[...] = jnp.zeros_like(dtaps)

    def taps_body(j, _):
        cols = pl.ds(pl.multiple_of(j * LANES, LANES), LANES)
        dp = dpre[:, cols]
        for k in range(CONV):
            first = HALO - CONV + 1 + k
            dtaps[k : k + 1, cols] = jnp.sum(dp * cf[first : first + rows, cols], axis=0, keepdims=True)
        dtaps[CONV : CONV + 1, cols] = jnp.sum(dp, axis=0, keepdims=True)
        return 0

    lax.fori_loop(0, CONV_CH // LANES, taps_body, 0)


def back(conv_low, hgrad, steps, raw, slope, conv_in, hst, gst, lst, mst, into, adj, decb, heads, left, spread):
    rows = hgrad.shape[0]
    blocks = rows // SPAN
    vm = pl.BlockSpec(memory_space=pltpu.VMEM)
    sm = pl.BlockSpec(memory_space=pltpu.SMEM)
    sds = jax.ShapeDtypeStruct
    st = pltpu.VMEM((blocks, STATE, INNER), F32)
    return pl.pallas_call(
        back_kernel,
        out_shape=(
            sds((rows, CONV_CH), F32),
            sds((rows, LANES), BF16),
            sds((8, LANES), F32),
            sds((8, CONV_CH), F32),
        ),
        in_specs=[vm] * 14 + [sm, vm],
        out_specs=(vm,) * 4,
        scratch_shapes=[
            st, st, st, st,
            pltpu.VMEM((LANES, SPAN), F32),
            pltpu.VMEM((LANES, SPAN), F32),
            pltpu.VMEM((rows + HALO, CONV_CH), F32),
        ],
        compiler_params=pltpu.CompilerParams(vmem_limit_bytes=VMEM_BYTES),
        name="back",
    )(conv_low, hgrad, steps, raw, slope, conv_in, hst, gst, lst, mst, into, adj, decb, heads, left, spread)


def tail_kernel(
    dpre, halo, dgate, draw, nlow, w_in, x, cot, gain, taps,
    grad_x, gin, dgain,
    df, pg, ng,
):
    rows = x.shape[0]
    df[0:rows, :] = dpre[...]
    df[rows : rows + 8, :] = halo[...]

    def taps_body(j, _):
        cols = pl.ds(pl.multiple_of(j * LANES, LANES), LANES)
        total = jnp.zeros((rows, LANES), F32)
        for k in range(CONV):
            first = CONV - 1 - k
            total = total + taps[k : k + 1, cols] * df[first : first + rows, cols]
        pg[:, pl.ds(pl.multiple_of(INNER + j * LANES, LANES), LANES)] = total.astype(BF16)
        return 0

    lax.fori_loop(0, CONV_CH // LANES, taps_body, 0)
    pg[:, 0:INNER] = dgate[...]
    pg[:, INNER + CONV_CH :] = draw[...]
    nt_low = nlow[...].T
    ng[...] = jnp.zeros_like(ng)

    def proj_body(j, _):
        cols = pl.ds(pl.multiple_of(j * 256, 256), 256)
        part = pg[:, cols]
        gin[:, cols] = nn(nt_low, part)
        ng[...] += nt(part, w_in[:, cols])
        return 0

    lax.fori_loop(0, WIDE // 256, proj_body, 0)
    dgain[...] = jnp.zeros_like(dgain)

    def norm_body(i, _):
        at = pl.ds(pl.multiple_of(i * 16, 16), 16)
        v = x[at, :].astype(F32)
        r = lax.rsqrt(jnp.mean(v * v, axis=1, keepdims=True) + EPS)
        unit = v * r
        g = ng[at, :]
        prod = g * unit
        dgain[...] += prod[0:8] + prod[8:16]
        gg = g * gain[...]
        grad_x[at, :] = cot[at, :].astype(F32) + r * (gg - unit * jnp.mean(gg * unit, axis=1, keepdims=True))
        return 0

    lax.fori_loop(0, rows // 16, norm_body, 0)


def tail(dpre, halo, dgate, draw, nlow, w_in, x, cot, gain, taps):
    rows = x.shape[0]
    vm = pl.BlockSpec(memory_space=pltpu.VMEM)
    sds = jax.ShapeDtypeStruct
    return pl.pallas_call(
        tail_kernel,
        out_shape=(sds((rows, D), F32), sds((D, WIDE), F32), sds((8, D), F32)),
        in_specs=[vm] * 10,
        out_specs=(vm,) * 3,
        scratch_shapes=[
            pltpu.VMEM((rows + 8, CONV_CH), F32),
            pltpu.VMEM((rows, WIDE), BF16),
            pltpu.VMEM((rows, D), F32),
        ],
        compiler_params=pltpu.CompilerParams(vmem_limit_bytes=VMEM_BYTES),
        name="tail",
    )(dpre, halo, dgate, draw, nlow, w_in, x, cot, gain, taps)


SMALL_ROWS = 88
NORM_ROWS = D // LANES
TAPS_ROWS = CONV_CH // LANES
HEAD_ROW = NORM_ROWS + (CONV + 1) * TAPS_ROWS
GAIN_ROW = HEAD_ROW + 3


def chunk_bounds(per, parts, width):
    return [(per * q) // LANES * LANES for q in range(parts)] + [width]


def peers_of(s, h, n_s, n_h):
    n_c = n_s // 2
    chip = s // 2
    core = lax.rem(s, 2)
    zpeer = [lax.rem(h + j, n_h) for j in range(1, n_h)]
    cpeer = [lax.rem(chip + j, n_c) for j in range(1, n_c)]
    return chip, core, chip * 2 + (1 - core), zpeer, cpeer


def remote(src, dst, send, recv, dev):
    return pltpu.make_async_remote_copy(
        src_ref=src, dst_ref=dst, send_sem=send, recv_sem=recv, device_id=dev, device_id_type=MESH
    )


def scatter_kernel(
    n_s, n_h, cph, oph, rin, wi, wo,
    gin, gout, ngp, dtaps, dheads, ogp,
    outw, small,
    r0, pb, r1, acc, zb, r2, sz, sp,
    s0s, s0r, s1s, s1r, s2s, s2r, szs, szr, sps, spr,
):
    s = lax.axis_index("seq")
    h = lax.axis_index("head")
    n_c = n_s // 2
    chip, core, sib, zpeer, cpeer = peers_of(s, h, n_s, n_h)
    speer = [lax.rem(s + j, n_s) for j in range(1, n_s)]
    ib = chunk_bounds(cph, n_h, WIDE)
    ob = chunk_bounds(oph, n_h, INNER)
    base = [ib[q] + ob[q] for q in range(n_h + 1)]
    bar = pltpu.get_barrier_semaphore()
    for z in zpeer:
        pl.semaphore_signal(bar, inc=1, device_id=(s, z), device_id_type=MESH)
    for p in speer:
        pl.semaphore_signal(bar, inc=1, device_id=(p, h), device_id_type=MESH)
    pl.semaphore_wait(bar, n_h + n_s - 2)
    sends = []

    def go(c):
        c.start()
        sends.append(c)

    def slab(target):
        return pl.ds(pl.multiple_of(rin * target, 8), rin)

    ks = cpeer + [chip]

    def pieces(q):
        wq = ib[q + 1] - ib[q]
        yield 0, gin, slice(ib[q], ib[q + 1]), slice(base[q], base[q] + wq)
        yield 1, gout, slice(ob[q], ob[q + 1]), slice(base[q] + wq, base[q + 1])

    for i in range(NORM_ROWS):
        sz[h, i : i + 1, :] = jnp.sum(ngp[:, i * LANES : (i + 1) * LANES], axis=0, keepdims=True)
    for k in range(CONV + 1):
        for i in range(TAPS_ROWS):
            r = NORM_ROWS + k * TAPS_ROWS + i
            sz[h, r : r + 1, :] = dtaps[k : k + 1, i * LANES : (i + 1) * LANES]
    sz[h, HEAD_ROW : HEAD_ROW + 3, :] = dheads[0:3, :]
    for i in range(INNER // LANES):
        r = GAIN_ROW + i
        sz[h, r : r + 1, :] = jnp.sum(ogp[:, i * LANES : (i + 1) * LANES], axis=0, keepdims=True)
    sz[h, GAIN_ROW + INNER // LANES :, :] = jnp.zeros((SMALL_ROWS - GAIN_ROW - INNER // LANES, LANES), F32)
    for j, z in enumerate(zpeer):
        go(remote(sz.at[h], sz.at[h], szs.at[j], szr.at[h], (s, z)))

    for q in range(n_h):
        for j, k in enumerate(ks):
            for n, src, cols, dst in pieces(q):
                go(
                    remote(
                        src.at[slab(2 * k + 1 - core), cols],
                        r0.at[k, :, dst],
                        s0s.at[q, j, n],
                        s0r.at[q, k, n],
                        (sib, h),
                    )
                )

    def plane_send(q):
        for j, k in enumerate(ks):
            for n, src, cols, dst in pieces(q):
                remote(
                    src.at[slab(2 * k + core), cols], r0.at[k, :, dst], s0s.at[q, j, n], s0r.at[q, k, n], (sib, h)
                ).wait_recv()
                v = src[slab(2 * k + core), cols] + r0[k, :, dst]
                if j < n_c - 1:
                    pb[j, 0:rin, dst] = v.astype(BF16)
                else:
                    acc[:, dst] = v
            if j < n_c - 1:
                at = slice(base[q], base[q + 1])
                go(remote(pb.at[j, :, at], r1.at[chip, :, at], s1s.at[q, j], s1r.at[q, chip], (2 * k + core, h)))

    def plane_recv(q):
        at = slice(base[q], base[q + 1])
        for j, k in enumerate(cpeer):
            remote(pb.at[j, :, at], r1.at[k, :, at], s1s.at[q, j], s1r.at[q, k], (2 * k + core, h)).wait_recv()
            acc[:, at] += r1[k, 0:rin, at].astype(F32)

    def window(q):
        t0, t1 = tiles_of(cph, q)
        span = (t1 - t0) * LANES
        wq = ib[q + 1] - ib[q]
        zb[q, :, 0:wq] = acc[:, base[q] : base[q] + wq]
        if span > wq:
            zb[q, :, wq:span] = acc[:, base[q + 1] : base[q + 1] + span - wq]
        if span < wi:
            zb[q, :, span:wi] = jnp.zeros((rin, wi - span), F32)
        t0, t1 = tiles_of(oph, q)
        span = (t1 - t0) * LANES
        oq = ob[q + 1] - ob[q]
        zb[q, :, wi : wi + oq] = acc[:, base[q] + wq : base[q + 1]]
        if span > oq:
            start = base[q + 1] + ib[q + 2] - ib[q + 1]
            zb[q, :, wi + oq : wi + span] = acc[:, start : start + span - oq]
        if span < wo:
            zb[q, :, wi + span :] = jnp.zeros((rin, wo - span), F32)

        @pl.when(h != q)
        def _():
            remote(zb.at[q], r2.at[h], s2s.at[q], s2r.at[h], (s, q)).start()

    for q in range(n_h):
        plane_send(q)
        if q == 0:
            total = jnp.zeros((SMALL_ROWS, LANES), F32)
            for j, z in enumerate(zpeer):
                remote(sz.at[z], sz.at[z], szs.at[j], szr.at[z], (s, z)).wait_recv()
            for z in range(n_h):
                total = total + sz[z]
            sp[s] = total
            for j, p in enumerate(speer):
                go(remote(sp.at[s], sp.at[s], sps.at[j], spr.at[s], (p, h)))
        if q >= 1:
            plane_recv(q - 1)
        if q >= 2:
            window(q - 2)
    plane_recv(n_h - 1)
    window(n_h - 2)
    window(n_h - 1)
    for j, p in enumerate(speer):
        remote(sp.at[p], sp.at[p], sps.at[j], spr.at[p], (p, h)).wait_recv()
    total = jnp.zeros((SMALL_ROWS, LANES), F32)
    for p in range(n_s):
        total = total + sp[p]
    small[...] = total
    outw[...] = zb[h]
    for z in zpeer:
        remote(zb.at[0], r2.at[z], s2s.at[0], s2r.at[z], (s, z)).wait_recv()
        outw[...] += r2[z]
    for q in range(n_h):

        @pl.when(h != q)
        def _():
            remote(zb.at[q], r2.at[h], s2s.at[q], s2r.at[h], (s, q)).wait_send()

    for c in sends:
        c.wait_send()


def scatter(gin, gout, ngp, dtaps, dheads, ogp, n_s, n_h, cph, oph, rin, wi, wo):
    n_c = n_s // 2
    rp = -(-rin // 16) * 16
    wide = WIDE + INNER
    dma = pltpu.SemaphoreType.DMA
    vm = pl.BlockSpec(memory_space=pltpu.VMEM)
    sds = jax.ShapeDtypeStruct
    return pl.pallas_call(
        functools.partial(scatter_kernel, n_s, n_h, cph, oph, rin, wi, wo),
        out_shape=(sds((rin, wi + wo), F32), sds((SMALL_ROWS, LANES), F32)),
        in_specs=[vm] * 6,
        out_specs=(vm, vm),
        scratch_shapes=[
            pltpu.VMEM((n_c, rin, wide), F32),
            pltpu.VMEM((n_c - 1, rp, wide), BF16),
            pltpu.VMEM((n_c, rp, wide), BF16),
            pltpu.VMEM((rin, wide), F32),
            pltpu.VMEM((n_h, rin, wi + wo), F32),
            pltpu.VMEM((n_h, rin, wi + wo), F32),
            pltpu.VMEM((n_h, SMALL_ROWS, LANES), F32),
            pltpu.VMEM((n_s, SMALL_ROWS, LANES), F32),
            dma((n_h, n_c, 2)),
            dma((n_h, n_c, 2)),
            dma((n_h, n_c)),
            dma((n_h, n_c)),
            dma((n_h,)),
            dma((n_h,)),
            dma((n_h,)),
            dma((n_h,)),
            dma((n_s,)),
            dma((n_s,)),
        ],
        compiler_params=pltpu.CompilerParams(
            collective_id=3, has_side_effects=True, vmem_limit_bytes=VMEM_BYTES
        ),
        name="sum_gradients",
    )(gin, gout, ngp, dtaps, dheads, ogp)


def finish_kernel(
    n_s, n_h, cph, oph, rin, wi, wo,
    gw, small, w_in, w_out, row_in, col_in, row_out, col_out, params, second,
    grad_in, row_in_new, col_in_new, w_in_new, grad_out, row_out_new, col_out_new, w_out_new, second_new, params_new,
    z1, p1, z2, p2, mask,
    z1s, z1r, p1s, p1r, z2s, z2r, p2s, p2r,
):
    s = lax.axis_index("seq")
    h = lax.axis_index("head")
    _, _, _, zpeer, _ = peers_of(s, h, n_s, n_h)
    speer = [lax.rem(s + j, n_s) for j in range(1, n_s)]
    bar = pltpu.get_barrier_semaphore()
    for z in zpeer:
        pl.semaphore_signal(bar, inc=1, device_id=(s, z), device_id_type=MESH)
    for p in speer:
        pl.semaphore_signal(bar, inc=1, device_id=(p, h), device_id_type=MESH)
    sends = []

    def start(buf, me, peers, along_z, snd, rcv):
        for j, p in enumerate(peers):
            c = remote(buf.at[me], buf.at[me], snd.at[j], rcv.at[me], (s, p) if along_z else (p, h))
            c.start()
            sends.append(c)

    def arrive(buf, peers, along_z, snd, rcv):
        for j, p in enumerate(peers):
            remote(buf.at[p], buf.at[p], snd.at[j], rcv.at[p], (s, p) if along_z else (p, h)).wait_recv()
        total = buf[0]
        for i in range(1, buf.shape[0]):
            total = total + buf[i]
        return total

    keep = 1.0 - DECAY
    off_in = lax.rem(cph * h, LANES)
    off_out = lax.rem(oph * h, LANES)
    rows8 = -(-rin // 8) * 8
    g_in = pltpu.roll(gw[:, :wi], lax.rem(wi - off_in, wi), 1)[:, :cph]
    grad_in[...] = g_in
    g_out = pltpu.roll(gw[:, wi:], lax.rem(wo - off_out, wo), 1)[:, :oph]
    padded = jnp.concatenate([g_out, jnp.zeros((LANES - rin, oph), F32)], axis=0)
    grad_out[...] = padded.T[:, :rin]
    sq_in = g_in * g_in
    sq_out = g_out * g_out
    wide_in = jnp.broadcast_to(jnp.sum(sq_in, axis=1, keepdims=True), (rin, LANES))
    wide_out = jnp.broadcast_to(jnp.sum(sq_out, axis=1, keepdims=True), (rin, LANES))
    fill = jnp.zeros((LANES - rin, LANES), F32)
    pick = iota((8, LANES), 0) == 0
    line_in = jnp.concatenate([wide_in, fill], axis=0).T[0:8]
    line_out = jnp.concatenate([wide_out, fill], axis=0).T[0:8]
    z1[h] = jnp.where(pick, line_in, line_out)
    cs_in = jnp.sum(sq_in, axis=0, keepdims=True)
    rs_out = jnp.sum(sq_out, axis=0, keepdims=True)
    pl.semaphore_wait(bar, n_h + n_s - 2)
    start(z1, h, zpeer, True, z1s, z1r)

    g = small[...]
    sec = DECAY * second[...] + keep * (g * g + EPS_SQUARE)
    second_new[...] = sec
    u = g * lax.rsqrt(sec)
    total_small = jnp.sum(u * u, keepdims=True)
    spread_small = jnp.sqrt(total_small / (D + (CONV + 1) * CONV_CH + 3 * HEADS + INNER))
    params_new[...] = params[...] - LEARN_SMALL * u / jnp.maximum(1.0, spread_small / CLIP_RMS)

    ti = iota((8, LANES), 1) < rin
    sums = arrive(z1, zpeer, True, z1s, z1r)
    line_r = DECAY * row_in[...] + keep * (sums[0:1] / PROJ + EPS_SQUARE)
    line_c = DECAY * col_out[...] + keep * (sums[1:2] / INNER + EPS_SQUARE)
    row_in_new[...] = line_r
    col_out_new[...] = line_c
    row_total = jnp.sum(jnp.where(ti[0:1], line_r, 0.0), axis=1, keepdims=True)

    n_ci = -(-cph // LANES)
    n_ro = -(-oph // LANES)
    mask[...] = jnp.zeros_like(mask)
    mask[0:1, 0:cph] = cs_in
    mask[0:1, wi : wi + oph] = rs_out
    p1[s] = jnp.zeros_like(p1[0])
    for i in range(n_ci):
        p1[s, i : i + 1, :] = mask[0:1, i * LANES : (i + 1) * LANES]
    for i in range(n_ro):
        p1[s, n_ci + i : n_ci + i + 1, :] = mask[0:1, wi + i * LANES : wi + (i + 1) * LANES]
    p1[s, n_ci + n_ro : n_ci + n_ro + 1, :] = jnp.broadcast_to(row_total, (1, LANES))
    start(p1, s, speer, False, p1s, p1r)
    up_r = jnp.broadcast_to(line_r, (LANES, LANES)).T[0:rin, 0:1]
    up_c = jnp.broadcast_to(line_c, (LANES, LANES)).T[0:rin, 0:1]
    sums = arrive(p1, speer, False, p1s, p1r)
    for i in range(n_ci):
        mask[0:1, i * LANES : (i + 1) * LANES] = sums[i : i + 1]
    for i in range(n_ro):
        mask[0:1, wi + i * LANES : wi + (i + 1) * LANES] = sums[n_ci + i : n_ci + i + 1]
    line_ci = DECAY * col_in[...] + keep * (mask[0:1, 0:cph] / D + EPS_SQUARE)
    line_ro = DECAY * row_out[...] + keep * (mask[0:1, wi : wi + oph] / D + EPS_SQUARE)
    col_in_new[...] = line_ci
    row_out_new[...] = line_ro
    mean_in = sums[n_ci + n_ro : n_ci + n_ro + 1, 0:1] / D
    u_in = g_in * lax.rsqrt(up_r * line_ci / mean_in)
    u_out = g_out * lax.rsqrt(up_c * line_ro)
    lane = iota((8, LANES), 1)
    z2[h] = jnp.where(
        lane == 0,
        jnp.sum(u_in * u_in, keepdims=True),
        jnp.where(
            lane == 1,
            jnp.sum(u_out * u_out, keepdims=True),
            jnp.where(lane == 2, jnp.sum(line_ro, axis=1, keepdims=True), 0.0),
        ),
    )
    start(z2, h, zpeer, True, z2s, z2r)
    p2[s] = arrive(z2, zpeer, True, z2s, z2r)
    start(p2, s, speer, False, p2s, p2r)
    mean_out = p2[s, 0:1, 2:3] / INNER
    sums = arrive(p2, speer, False, p2s, p2r)
    clip_in = jnp.maximum(1.0, jnp.sqrt(sums[0:1, 0:1] / (D * PROJ)) / CLIP_RMS)
    clip_out = jnp.maximum(1.0, jnp.sqrt(sums[0:1, 1:2] * mean_out / (INNER * D)) / CLIP_RMS)
    w_in_new[...] = w_in[...] - LEARN_RATE * u_in / clip_in
    step_out = LEARN_RATE * (u_out * jnp.sqrt(mean_out)) / clip_out
    padded = jnp.concatenate([step_out, jnp.zeros((LANES - rin, oph), F32)], axis=0)
    w_out_new[...] = w_out[...] - padded.T[:, :rin]
    for c in sends:
        c.wait_send()


def finish(gw, small, w_in, w_out, row_in, col_in, row_out, col_out, params, second, n_s, n_h, wi, wo):
    rin, cph = w_in.shape
    oph, _ = w_out.shape
    dma = pltpu.SemaphoreType.DMA
    vm = pl.BlockSpec(memory_space=pltpu.VMEM)
    sds = jax.ShapeDtypeStruct
    n_rows = -(-(-(-cph // LANES) + -(-oph // LANES) + 1) // 8) * 8
    line = sds((1, LANES), F32)
    return pl.pallas_call(
        functools.partial(finish_kernel, n_s, n_h, cph, oph, rin, wi, wo),
        out_shape=(
            sds((rin, cph), F32),
            line,
            sds((1, cph), F32),
            sds((rin, cph), F32),
            sds((oph, rin), F32),
            sds((1, oph), F32),
            line,
            sds((oph, rin), F32),
            sds((SMALL_ROWS, LANES), F32),
            sds((SMALL_ROWS, LANES), F32),
        ),
        in_specs=[vm] * 10,
        out_specs=(vm,) * 10,
        scratch_shapes=[
            pltpu.VMEM((n_h, 8, LANES), F32),
            pltpu.VMEM((n_s, n_rows, LANES), F32),
            pltpu.VMEM((n_h, 8, LANES), F32),
            pltpu.VMEM((n_s, 8, LANES), F32),
            pltpu.VMEM((8, wi + wo), F32),
            dma((n_h,)),
            dma((n_h,)),
            dma((n_s,)),
            dma((n_s,)),
            dma((n_h,)),
            dma((n_h,)),
            dma((n_s,)),
            dma((n_s,)),
        ],
        compiler_params=pltpu.CompilerParams(
            collective_id=4, has_side_effects=True, vmem_limit_bytes=VMEM_BYTES
        ),
        name="optimizer",
    )(gw, small, w_in, w_out, row_in, col_in, row_out, col_out, params, second)


def to_rows(flat, fill):
    first = D + (CONV + 1) * CONV_CH
    rows = [flat[:first].reshape(-1, LANES)]
    middle = flat[first : first + 3 * HEADS].reshape(3, HEADS)
    rows.append(jnp.pad(middle, ((0, 0), (0, LANES - HEADS)), constant_values=fill))
    rows.append(flat[first + 3 * HEADS :].reshape(-1, LANES))
    rows.append(jnp.full((SMALL_ROWS - GAIN_ROW - INNER // LANES, LANES), fill, F32))
    return jnp.concatenate(rows, axis=0)


def from_rows(rows):
    return jnp.concatenate(
        [
            rows[:HEAD_ROW].reshape(-1),
            rows[HEAD_ROW:GAIN_ROW, :HEADS].reshape(-1),
            rows[GAIN_ROW : GAIN_ROW + INNER // LANES].reshape(-1),
        ]
    )


def shifted(value, axis, steps):
    count = lax.axis_size(axis)
    first, last = (max(0, -steps), min(count, count - steps))
    return lax.ppermute(value, axis, [(source, source + steps) for source in range(first, last)])


def on_device(
    x_in, lengths, cotangent, w_in, w_out, small_params, row_in, col_in, row_out, col_out, small_second
):
    n_s = lax.axis_size("seq")
    n_h = lax.axis_size("head")
    seq_index = lax.axis_index("seq")
    head_index = lax.axis_index("head")
    rows = x_in.shape[0]
    rin, cph = w_in.shape
    oph, cout = w_out.shape
    rp = -(-rin // 16) * 16
    wi = tile_count(cph, n_h) * LANES
    wo = tile_count(oph, n_h) * LANES
    pay = jnp.zeros((rp, wi + wo), BF16)
    pay = lax.dynamic_update_slice(pay, w_in.astype(BF16), (0, lax.rem(cph * head_index, LANES)))
    pay = lax.dynamic_update_slice(pay, w_out.astype(BF16).T, (0, wi + lax.rem(oph * head_index, LANES)))
    full = gather(pay, n_s, n_h)[:, :, :rin].reshape(n_h, D, wi + wo)

    first = D + CONV * CONV_CH
    gain = small_params[:D].reshape(1, D)
    taps = jnp.zeros((8, CONV_CH), F32).at[: CONV + 1].set(
        small_params[D : first + CONV_CH].reshape(CONV + 1, CONV_CH)
    )
    first = first + CONV_CH
    heads = jnp.zeros((8, LANES), F32).at[:3, :HEADS].set(
        small_params[first : first + 3 * HEADS].reshape(3, HEADS)
    )
    out_gain = small_params[first + 3 * HEADS :].reshape(1, INNER)
    left = (lengths[0] - head_index * rows).reshape(1)
    spread = jnp.asarray(
        (np.arange(LANES)[:, None] == np.arange(INNER)[None, :] // HEAD_DIM).astype(np.float32)
    ).astype(BF16)
    x_halo = jnp.concatenate([shifted(x_in[rows - HALO :], "head", 1), x_in], axis=0)
    (nlow, w_full, o_full, gate, conv_in, conv_low, slope, raw, steps, hst, gst, dev, decb, dec) = front(
        x_halo, full, gain, taps, heads, left, spread, n_h, cph, oph, wi
    )
    into = chain(dev, dec, n_h, 1)
    result, dgate, hgrad, gout, og_part, lst, mst, dev2 = middle(
        x_in, cotangent, gate, conv_low, steps, hst, gst, into, decb, o_full, heads, out_gain, left, spread
    )
    adj = chain(dev2, dec, n_h, 2)
    dpre, draw, dheads, dtaps = back(
        conv_low, hgrad, steps, raw, slope, conv_in, hst, gst, lst, mst, into, adj, decb, heads, left, spread
    )
    halo = shifted(dpre[:8], "head", -1)
    grad_x, gin, ng_part = tail(dpre, halo, dgate, draw, nlow, w_full, x_in, cotangent, gain, taps)
    gw, small = scatter(gin, gout, ng_part, dtaps, dheads, og_part, n_s, n_h, cph, oph, rin, wi, wo)
    line = lambda v: jnp.pad(v.reshape(1, -1), ((0, 0), (0, LANES - v.shape[0])))
    (grad_in, row_in_new, col_in_new, w_in_new, grad_out, row_out_new, col_out_new, w_out_new, second_new, params_new) = finish(
        gw, small, w_in, w_out, line(row_in), col_in.reshape(1, -1), row_out.reshape(1, -1), line(col_out),
        to_rows(small_params, 0.0), to_rows(small_second, 1.0), n_s, n_h, wi, wo,
    )
    return (
        result, grad_x, grad_in, row_in_new[0, :rin], col_in_new.reshape(-1), w_in_new, grad_out, row_out_new.reshape(-1),
        col_out_new[0, :rin], w_out_new, from_rows(small), from_rows(second_new), from_rows(params_new),
    )


def solution(mesh):
    both = P(("seq", "head"), None)
    factors = (P("seq", "head"), P("seq"), P("head"), P("seq", "head"))
    return jax.shard_map(
        on_device,
        mesh=mesh,
        in_specs=(
            both, P("seq"), both, P("seq", "head"), P("head", "seq"), P(), P("seq"), P("head"), P("head"), P("seq"), P(),
        ),
        out_specs=(
            both, both, P("seq", "head"), P("seq"), P("head"), P("seq", "head"), P("head", "seq"), P("head"), P("seq"),
            P("head", "seq"), P(), P(), P(),
        ),
        check_vma=False,
    )
```

```python
import functools

import jax
import jax.numpy as jnp
import numpy as np
from jax import lax
from jax.experimental import pallas as pl
from jax.experimental.pallas import tpu as pltpu
from jax.sharding import PartitionSpec as P

D = 768
HEADS = 24
HEAD_DIM = 64
STATE = 64
CONV = 4
SPAN = 128
STEP = 8
INNER = 1536
CONV_CH = 1664
PROJ = 3224
WIDE = 3328
LANES = 128
HALO = 16

EPS = 1e-05
EPS_SQUARE = 1e-30
LEARN_RATE = 0.3
LEARN_SMALL = 3.0
CLIP_RMS = 0.1
DECAY = 1.0 - STEP ** (-0.8)
F32 = jnp.float32
BF16 = jnp.bfloat16
HIGHEST = lax.Precision.HIGHEST
MESH = pl.DeviceIdType.MESH
VMEM_BYTES = 60 << 20


def nn(left, right):
    return lax.dot_general(left, right, (((1,), (0,)), ((), ())), preferred_element_type=F32)


def nt(left, right):
    return lax.dot_general(left, right, (((1,), (1,)), ((), ())), preferred_element_type=F32)


def split(value):
    high = value.astype(BF16)
    return high, (value - high.astype(F32)).astype(BF16)


def nn_split(value, exact):
    high, low = split(value)
    return nn(high, exact) + nn(low, exact)


def expand(value, spread):
    return nn_split(value, spread)


def fold(value, spread):
    high, low = split(value)
    return nt(high, spread) + nt(low, spread)


def iota(shape, dim):
    return lax.broadcasted_iota(jnp.int32, shape, dim)


def tri_low():
    return (iota((SPAN, SPAN), 0) >= iota((SPAN, SPAN), 1)).astype(F32)


def tri_high():
    return (iota((SPAN, SPAN), 0) <= iota((SPAN, SPAN), 1)).astype(F32)


def precise(left, right):
    return lax.dot_general(
        left, right, (((1,), (0,)), ((), ())), precision=HIGHEST, preferred_element_type=F32
    )


def sigmoid(value):
    return 1.0 / (1.0 + jnp.exp(-value))


def tiles_of(per_part, index):
    return (per_part * index) // LANES, -(-(per_part * (index + 1)) // LANES)


def tile_count(per_part, parts):
    return max(e - s for s, e in (tiles_of(per_part, i) for i in range(parts)))


def half_masks(value):
    low = iota(value.shape, 1) < HEAD_DIM
    zero = jnp.zeros_like(value)
    return jnp.where(low, value, zero), jnp.where(low, zero, value)


def head_terms(steps, rates):
    logs = steps * rates
    incl = precise(tri_low(), logs)
    return incl, incl - logs, incl[SPAN - 1 : SPAN]


CHAIN_PARTS = 4


class Chain:
    def __init__(self, n_h, s, h, dev, dec, out, snd, us, ur, ds, dr):
        self.n_h, self.s, self.h = n_h, s, h
        self.dev, self.dec, self.out, self.snd = dev, dec, out, snd
        self.sems = ((us, ur), (ds, dr))
        self.next = (lax.rem(h + 1, n_h), lax.rem(h + n_h - 1, n_h))
        self.inner = jnp.logical_and(h > 0, h < n_h - 1)
        self.first = (h == 0, h == n_h - 1)
        self.last = (h == n_h - 1, h == 0)

    def link(self, d, c):
        width = STATE // CHAIN_PARTS
        at = pl.ds(c * width, width)
        snd, rcv = self.sems[d]
        return remote(self.snd.at[d, at], self.out.at[d, at], snd.at[c], rcv.at[c], (self.s, self.next[d]))

    def begin(self):
        for d in range(2):

            @pl.when(self.first[d])
            def _():
                self.out[d] = jnp.zeros((STATE, INNER), F32)
                self.snd[d] = self.dev[d]
                for c in range(CHAIN_PARTS):
                    self.link(d, c).start()

    def step(self, d, c):
        width = STATE // CHAIN_PARTS
        at = slice(c * width, (c + 1) * width)

        @pl.when(jnp.logical_not(self.first[d]))
        def _():
            self.link(d, c).wait_recv()

        @pl.when(self.inner)
        def _():
            self.snd[d, at] = self.out[d, at] * self.dec[0:1] + self.dev[d, at]
            self.link(d, c).start()

    def at(self, k):
        for c in range(CHAIN_PARTS):

            @pl.when(k == 2 * self.h + c)
            def _():
                self.step(0, c)

            @pl.when(k == 2 * (self.n_h - 1 - self.h) + c)
            def _():
                self.step(1, c)

    def steps(self):
        return 2 * (self.n_h - 1) + CHAIN_PARTS

    def finish(self):
        for d in range(2):

            @pl.when(jnp.logical_not(self.last[d]))
            def _():
                for c in range(CHAIN_PARTS):
                    self.link(d, c).wait_send()


def remote(src, dst, send, recv, dev):
    return pltpu.make_async_remote_copy(
        src_ref=src, dst_ref=dst, send_sem=send, recv_sem=recv, device_id=dev, device_id_type=MESH
    )


def split3(value):
    high = value.astype(BF16)
    rest = value - high.astype(F32)
    mid, low = split(rest)
    return high, mid, low


def flat_rows(flat, rows, fill):
    count = SMALL // LANES
    for i in range(count):
        rows[i : i + 1, :] = flat[pl.ds(i * LANES, LANES)].reshape(1, LANES)
    rows[count:, :] = jnp.full((rows.shape[0] - count, LANES), fill, F32)
    rest = SMALL - count * LANES
    rows[count : count + 1, 0:rest] = flat[pl.ds(count * LANES, rest)].reshape(1, rest)


def piece_map(dp, rin, rp):
    place = iota((dp, D), 0)
    return jnp.logical_and(place // rp * rin + place % rp == iota((dp, D), 1), place % rp < rin).astype(BF16)


def unpack_rows(rows, rin, rp, gain, taps, heads, out_gain):
    dp = gain.shape[1]
    first = D // LANES
    flat_gain = jnp.concatenate([rows[i : i + 1, :] for i in range(first)], axis=1)
    if dp == D:
        gain[...] = flat_gain
    else:
        parts = split3(jnp.broadcast_to(flat_gain, (8, D)))
        gain[...] = sum(nt(p, piece_map(dp, rin, rp)) for p in parts)[0:1]
    taps[...] = jnp.zeros_like(taps)
    for k in range(CONV + 1):
        for i in range(TAPS_ROWS):
            r = first + k * TAPS_ROWS + i
            taps[k : k + 1, i * LANES : (i + 1) * LANES] = rows[r : r + 1, :]
    r = HEAD_ROW
    lane = iota((1, LANES), 1)
    line = rows[r : r + 1, :]
    heads[...] = jnp.zeros_like(heads)
    for n in range(3):
        v = line if n == 0 else pltpu.roll(line, LANES - n * HEADS, 1)
        heads[n : n + 1, :] = jnp.where(lane < HEADS, v, 0.0)
    if out_gain is not None:
        turn = LANES - 3 * HEADS
        for i in range(INNER // LANES):
            here = pltpu.roll(rows[r + i : r + i + 1, :], turn, 1)
            after = pltpu.roll(rows[r + i + 1 : r + i + 2, :], turn, 1)
            out_gain[0:1, i * LANES : (i + 1) * LANES] = jnp.where(lane < turn, here, after)


def fill_spread(spread):
    spread[...] = (iota((LANES, INNER), 0) == iota((LANES, INNER), 1) // HEAD_DIM).astype(BF16)


class Gather:
    def __init__(self, n_s, n_h, s, h, full, lanes, sems):
        self.n_s, self.n_h, self.s, self.h, self.full, self.lanes = n_s, n_h, s, h, full, lanes
        self.zs, self.zr, self.ps, self.pr, self.ds, self.dr, self.cs, self.cr = sems
        self.n_c = n_s // 2
        self.chip = s // 2
        self.core = lax.rem(s, 2)
        self.sib = self.chip * 2 + (1 - self.core)
        self.cpeer = [lax.rem(self.chip + j, self.n_c) for j in range(1, self.n_c)]
        self.square = self.n_c == 4
        self.xn = self.chip + 1 - 2 * lax.rem(self.chip, 2)
        self.yn = lax.rem(self.chip + self.n_c // 2, self.n_c)
        self.diag = 3 - self.chip
        self.inner = jnp.logical_and(h > 0, h < n_h - 1)
        self.order = [h] + [self.nth(j) for j in range(1, n_h)]

    def nth(self, j):
        n_h, h = self.n_h, self.h
        below = jnp.where(j - 1 >= h, j, j - 1)
        mirror = n_h - 1 - h
        above = n_h - 1 - jnp.where(j - 1 >= mirror, j, j - 1)
        return jnp.where(2 * h < n_h, below, above)

    def blk(self, q, c, part=None):
        ref = self.full.at[q, c * 2 + self.core]
        rp = self.full.shape[2]
        if part is None:
            return ref.at[:, self.lanes]
        mid = rp // 2 // 16 * 16
        return ref.at[pl.ds(0, mid) if part == 0 else pl.ds(mid, rp - mid), self.lanes]

    def along(self, q, way):
        ref = self.blk(q, self.chip)
        to = lax.rem(self.h + (1 if way == 0 else self.n_h - 1), self.n_h)
        return remote(ref, ref, self.zs.at[q, way], self.zr.at[q], (self.s, to))

    def begin(self):
        @pl.when(self.h < self.n_h - 1)
        def _():
            self.along(self.h, 0).start()

        @pl.when(self.h > 0)
        def _():
            self.along(self.h, 1).start()

        self.spread_out(0)

    def z_in(self, i):
        q = self.order[i]
        self.along(q, 0).wait_recv()

        @pl.when(jnp.logical_and(q < self.h, self.h < self.n_h - 1))
        def _():
            self.along(q, 0).start()

        @pl.when(jnp.logical_and(q > self.h, self.h > 0))
        def _():
            self.along(q, 1).start()

    def z_done(self):
        for i in range(self.n_h):
            q = self.order[i]

            @pl.when(jnp.logical_and(q <= self.h, self.h < self.n_h - 1))
            def _():
                self.along(q, 0).wait_send()

            @pl.when(jnp.logical_and(q >= self.h, self.h > 0))
            def _():
                self.along(q, 1).wait_send()

    def to_chip(self, i, m, part, q, c):
        ref = self.blk(q, self.chip, part)
        n = 0 if part is None else part
        return remote(ref, ref, self.ps.at[i, m, n], self.pr.at[q, self.chip, n], (c * 2 + self.core, self.h))

    def over(self, i, j, q, c):
        ref = self.blk(q, c)
        return remote(ref, ref, self.cs.at[i, j], self.cr.at[q, c], (self.sib, self.h))

    def spread_out(self, i):
        for c in self.to_chips(i):
            c.start()
        self.over(i, 0, self.order[i], self.chip).start()

    def to_chips(self, i):
        q = self.order[i]
        if self.square:
            near = ((0, self.xn), (1, self.yn))
            return [self.to_chip(i, m, (n + m) % 2, q, c) for n in range(2) for m, c in near]
        return [self.to_chip(i, j, None, q, c) for j, c in enumerate(self.cpeer)]

    def onward(self, i, n):
        q = self.order[i]
        c, to = (self.xn, self.yn) if n == 0 else (self.yn, self.xn)
        ref = self.blk(q, c, n)
        return remote(ref, ref, self.ds.at[i, n], self.dr.at[q, n], (to * 2 + self.core, self.h))

    def got(self, q, c, part):
        ref = self.blk(q, c, part)
        n = 0 if part is None else part
        remote(ref, ref, self.ps.at[0, 0, 0], self.pr.at[q, c, n], (self.sib, self.h)).wait_recv()

    def pass_on(self, i):
        q = self.order[i]
        if self.square:
            for n, c in ((0, self.xn), (1, self.yn)):
                self.got(q, c, n)
                self.onward(i, n).start()
            for n, c in ((1, self.xn), (0, self.yn)):
                self.got(q, c, n)
                self.over(i, 2 - n, q, c).start()
        else:
            for j, c in enumerate(self.cpeer):
                self.got(q, c, None)
                self.over(i, j + 1, q, c).start()

    def last_in(self, i):
        if self.square:
            q = self.order[i]
            for n in range(2):
                ref = self.blk(q, self.diag, n)
                remote(ref, ref, self.ds.at[0, 0], self.dr.at[q, n], (self.sib, self.h)).wait_recv()
            self.over(i, 3, q, self.diag).start()

    def complete(self, i):
        q = self.order[i]
        for c in [self.chip] + self.cpeer:
            ref = self.full.at[q, c * 2 + 1 - self.core].at[:, self.lanes]
            remote(ref, ref, self.cs.at[0, 0], self.cr.at[q, c], (self.sib, self.h)).wait_recv()

    def plan(self, columns):
        n_h = self.n_h

        def run(*steps):
            def all_steps():
                for step in steps:
                    step()

            return all_steps

        plan = [lambda: self.z_in(1), lambda: self.spread_out(1)]
        if n_h > 2:
            plan.append(lambda: pl.when(self.inner)(lambda: self.z_in(2)))
        plan.append(lambda: self.pass_on(0))
        for i in range(2, n_h):
            if i == 2:
                plan.append(lambda: pl.when(jnp.logical_not(self.inner))(lambda: self.z_in(2)))
            else:
                plan.append(lambda i=i: self.z_in(i))
            plan.append(lambda i=i: self.spread_out(i))
            plan.append(run(lambda i=i: self.last_in(i - 2), lambda i=i: self.pass_on(i - 1)))
            plan.append(run(lambda i=i: self.complete(i - 2), lambda i=i: columns(i - 2)))
        plan.append(run(lambda: self.last_in(n_h - 2), lambda: self.pass_on(n_h - 1)))
        plan.append(run(lambda: self.complete(n_h - 2), lambda: columns(n_h - 2)))
        plan.append(run(lambda: self.last_in(n_h - 1), lambda: self.complete(n_h - 1), lambda: columns(n_h - 1)))
        return plan

    def finish(self):
        self.z_done()
        for i in range(self.n_h):
            q = self.order[i]
            chips = [self.chip] + ([self.xn, self.yn, self.diag] if self.square else self.cpeer)
            for c in self.to_chips(i):
                c.wait_send()
            for j, c in enumerate(chips):
                self.over(i, j, q, c).wait_send()
            if self.square:
                for n in range(2):
                    self.onward(i, n).wait_send()


def gather_sems(n_s, n_h):
    dma = pltpu.SemaphoreType.DMA
    n_c = n_s // 2
    return [
        dma((n_h, 2)), dma((n_h,)), dma((n_h, n_c, 2)), dma((n_h, n_c, 2)), dma((n_h, 2)), dma((n_h, 2)), dma((n_h, n_c)),
        dma((n_h, n_c)),
    ]


def fore_kernel(
    n_s, n_h, cph, oph, rin, rp, wi, wo,
    x, cot, w_in, w_out_t, flat, lengths,
    result, w_full_o, nlow_o, conv_in_o, conv_low_o, slope_o, raw, steps, decb, dec, dgate, hgrad, glow, dgain, lst, mst,
    dev2, hin_o, gin_o,
    full, w_full, o_full, xh, shift_in, shift_out, nscr, conv_in, conv_low, slope, cf, gate, hst, gst, dev, into, csnd, incl_r,
    excl_r, incl_t, excl_t, steps_t, inter_s, yb, el, eg, gg_scr, hin, gin, prm, gain, taps, heads, out_gain, spread,
    xs_, xr_, us, ur, dws, dwr, outs, *gsems,
):
    s = lax.axis_index("seq")
    h = lax.axis_index("head")
    n_c = n_s // 2
    rows = x.shape[0]
    dp = x.shape[1]
    blocks = rows // SPAN
    chip = s // 2
    core = lax.rem(s, 2)
    sib = chip * 2 + (1 - core)
    cpeer = [lax.rem(chip + j, n_c) for j in range(1, n_c)]
    left = lengths[0] - h * rows
    g_in = Gather(n_s, n_h, s, h, full, slice(0, wi), gsems[:8])
    g_out = Gather(n_s, n_h, s, h, full, slice(wi, wi + wo), gsems[8:])
    zpeer = [lax.rem(h + j, n_h) for j in range(1, n_h)]
    bar = pltpu.get_barrier_semaphore()
    for z in zpeer:
        pl.semaphore_signal(bar, inc=1, device_id=(s, z), device_id_type=MESH)
    for c in cpeer:
        pl.semaphore_signal(bar, inc=1, device_id=(c * 2 + core, h), device_id_type=MESH)
    pl.semaphore_signal(bar, inc=1, device_id=(sib, h), device_id_type=MESH)

    shift_in[...] = jnp.zeros_like(shift_in)
    shift_in[0:rin, 0:cph] = w_in[...]
    full[h, s, :, 0:wi] = pltpu.roll(shift_in[...], lax.rem(cph * h, LANES), 1).astype(BF16)
    shift_out[...] = jnp.zeros_like(shift_out)
    shift_out[0:rin, 0:oph] = w_out_t[...]
    turned = shift_out[...]
    if oph % LANES:
        turned = pltpu.roll(turned, lax.rem(oph * h, LANES), 1)
    full[h, s, :, wi:] = turned.astype(BF16)
    pl.semaphore_wait(bar, n_h + n_c - 1)

    g_in.begin()
    up = lax.rem(h + 1, n_h)
    halo = remote(x.at[rows - HALO : rows], xh, xs_.at[0], xr_.at[0], (s, up))

    @pl.when(h < n_h - 1)
    def _():
        halo.start()

    flat_rows(flat, prm, 0.0)
    unpack_rows(prm, rin, rp, gain, taps, heads, out_gain)
    fill_spread(spread)

    def norm_rows(src, at, dst):
        v = src[at, :].astype(F32)
        n = v * lax.rsqrt(jnp.sum(v * v, axis=1, keepdims=True) * (1.0 / D) + EPS) * gain[...]
        nscr[dst, :] = n.astype(BF16)

    def norm_body(i, _):
        at = pl.multiple_of(i * 16, 16)
        norm_rows(x, pl.ds(at, 16), pl.ds(at + HALO, 16))
        return 0

    lax.fori_loop(0, rows // 16, norm_body, 0)

    @pl.when(h > 0)
    def _():
        halo.wait_recv()

    @pl.when(h == 0)
    def _():
        xh[...] = jnp.zeros_like(xh)

    norm_rows(xh, slice(0, HALO), slice(0, HALO))

    def leave(src, dst, n):
        return pltpu.make_async_copy(src, dst, outs.at[n])

    leaving = [leave(nscr.at[HALO:], nlow_o, 0)]
    leaving[0].start()

    def project(tile, weights):
        w_full[:, pl.ds(pl.multiple_of(tile * LANES, LANES), LANES)] = weights
        v = nn(nscr[...], weights).astype(BF16)
        first, last = INNER // LANES, WIDE // LANES - 1

        @pl.when(tile < first)
        def _():
            gate[:, pl.ds(pl.multiple_of(tile * LANES, LANES), LANES)] = v[HALO:]

        @pl.when(tile == last)
        def _():
            raw[...] = v[HALO:].astype(F32)

        @pl.when(jnp.logical_and(tile >= first, tile < last))
        def _():
            at = pl.ds(pl.multiple_of((tile - first) * LANES, LANES), LANES)
            conv_in[:, at] = v
            cf[...] = v.astype(F32)
            total = jnp.zeros((rows, LANES), F32) + taps[CONV : CONV + 1, at]
            for k in range(CONV):
                start = HALO - CONV + 1 + k
                total = total + taps[k : k + 1, at] * cf[start : start + rows, :]
            sg = sigmoid(total)
            conv_low[:, at] = (total * sg).astype(BF16)
            slope[:, at] = sg * (1.0 + total * (1.0 - sg))

    def columns(i):
        q = g_in.order[i]
        t0 = (cph * q) // LANES
        lo = (cph * q + LANES - 1) // LANES
        hi = jnp.where(q == n_h - 1, WIDE // LANES, (cph * (q + 1)) // LANES)

        def tile_body(t, _):
            at = pl.ds(pl.multiple_of((t - t0) * LANES, LANES), LANES)
            project(t, full[q, :, :, at].reshape(dp, LANES))
            return 0

        lax.fori_loop(lo, hi, tile_body, 0)

    for step in g_in.plan(columns):
        step()
    g_out.begin()
    for q in range(1, n_h):
        if (cph * q) % LANES:
            tile, t0 = (cph * q) // LANES, (cph * (q - 1)) // LANES
            at = (tile - t0) * LANES
            project(tile, (full[q - 1, :, :, at : at + LANES] + full[q, :, :, 0:LANES]).reshape(dp, LANES))
    for n, (src, dst) in enumerate(((w_full, w_full_o), (conv_in, conv_in_o), (conv_low, conv_low_o), (slope, slope_o))):
        leaving.append(leave(src, dst, n + 1))
        leaving[-1].start()

    biased = raw[...] + heads[0:1, :]
    soft = jnp.maximum(biased, 0.0) + jnp.log1p(jnp.exp(-jnp.abs(biased)))
    keep = jnp.logical_and(iota((rows, LANES), 0) < left, iota((rows, LANES), 1) < HEADS)
    steps[...] = jnp.where(keep, soft, 0.0)
    rates = -jnp.exp(heads[1:2, :])
    for b in range(blocks):
        at = slice(b * SPAN, (b + 1) * SPAN)
        st = steps[at, :]
        incl, excl, total = head_terms(st, rates)
        incl_r[b] = incl
        excl_r[b] = excl
        incl_t[b] = incl.T
        excl_t[b] = excl.T
        steps_t[b] = st.T
        wide = split(jnp.concatenate([jnp.exp(total - incl) * st, jnp.exp(excl) * st], axis=0))
        bc = conv_low[at, INNER:].astype(F32)
        bt = bc.T[:STATE].astype(BF16)
        bt2 = jnp.concatenate([bt, bt], axis=1)
        c_low = half_masks(pltpu.roll(bc, STATE, 1))[0].astype(BF16)
        inter_s[b] = nt(c_low, bc.astype(BF16))
        tot = jnp.broadcast_to(jnp.exp(total), (8, LANES))
        for g in range(INNER // 256):
            cols = slice(g * 256, (g + 1) * 256)
            sp = spread[:, cols]
            xs = conv_low[at, cols].astype(F32)
            w = nn(wide[0], sp) + nn(wide[1], sp)
            for n, dst in ((0, hst), (1, gst)):
                hi, lo = split(w[n * SPAN : (n + 1) * SPAN] * xs)
                dst[b, :, cols] = nn(bt2, jnp.concatenate([hi, lo], axis=0))
            decb[b, :, cols] = expand(tot, sp)
    hv, gv, dv = hst[0], gst[blocks - 1], decb[0]
    for b in range(1, blocks):
        hv = hv * decb[b, 0:1, :] + hst[b]
        dv = dv * decb[b]
    for b in range(blocks - 2, -1, -1):
        gv = gv * decb[b, 0:1, :] + gst[b]
    dev[0] = hv
    dev[1] = gv
    dec[...] = dv
    chain = Chain(n_h, s, h, dev, dec, into, csnd, us, ur, dws, dwr)
    chain.begin()

    row = iota((SPAN, SPAN), 0)
    col = iota((SPAN, SPAN), 1)
    twice = 1.0 + (row == col).astype(F32)
    skip8 = jnp.broadcast_to(heads[2:3, :], (8, LANES))

    def pair_body(pair, _):
        cols = pl.ds(pl.multiple_of(pair * LANES, LANES), LANES)
        after = row >= col
        hot = (iota((LANES, 2 * LANES), 0) == 2 * pair + iota((LANES, 2 * LANES), 1) // LANES).astype(BF16)
        hot3 = jnp.concatenate([hot, hot, hot], axis=0)
        skip = expand(skip8, spread[:, cols])[0:1]
        for b in range(blocks):
            at = slice(b * SPAN, (b + 1) * SPAN)
            both = jnp.concatenate([incl_r[b], excl_r[b]], axis=0)
            wide = nn(jnp.concatenate(split3(both), axis=1), hot3)
            inter = inter_s[b] * twice
            xs = conv_low[at, cols]
            mix = []
            for n in range(2):
                hd = 2 * pair + n
                lanes = slice(n * LANES, (n + 1) * LANES)
                gap = jnp.where(
                    after,
                    wide[0:SPAN, lanes] - incl_t[b, pl.ds(hd, 1), :],
                    excl_t[b, pl.ds(hd, 1), :] - wide[SPAN:, lanes],
                )
                mix.append(inter * jnp.exp(gap) * steps_t[b, pl.ds(hd, 1), :])
            x0, x1 = half_masks(xs)
            y = nn_split(jnp.concatenate(mix, axis=1), jnp.concatenate([x0, x1], axis=0))
            yb[at, cols] = y + skip * xs.astype(F32)
        chain.at(pair)
        for n, step in enumerate(out_plan):
            pl.when(pair == n * 12 // len(out_plan))(step)
        return 0

    out_plan = g_out.plan(lambda i: None)
    lax.fori_loop(0, HEADS // 2, pair_body, 0)
    for k in range(HEADS // 2, chain.steps()):
        chain.at(k)

    for tile in range(INNER // LANES):
        parts = []
        for q in range(n_h):
            t0, t1 = tiles_of(oph, q)
            if t0 <= tile < t1:
                at = wi + (tile - t0) * LANES
                parts.append(full[q, :, :, at : at + LANES])
        v = parts[0] if len(parts) == 1 else parts[0] + parts[1]
        o_full[:, tile * LANES : (tile + 1) * LANES] = v.reshape(dp, LANES)

    hin[0] = into[0]
    gin[blocks] = into[1]
    for b in range(blocks):
        hin[b + 1] = hin[b] * decb[b, 0:1, :] + hst[b]
    for b in range(blocks - 1, -1, -1):
        gin[b] = gin[b + 1] * decb[b, 0:1, :] + gst[b]
    for src, dst, n in ((hin, hin_o, 5), (gin, gin_o, 6)):
        leaving.append(leave(src, dst, n))
        leaving[-1].start()
    keep_row = (iota((rows, 1), 0) < left).astype(F32)
    bgrad = (cot[...].astype(F32) * keep_row).astype(BF16)
    for g in range(INNER // 256):
        cols = slice(g * 256, (g + 1) * 256)
        sp = spread[:, cols]
        gg_scr[:, cols] = nn(bgrad, o_full[:, cols])
        for b in range(blocks):
            at = slice(b * SPAN, (b + 1) * SPAN)
            incl = incl_r[b]
            hi, lo = split(jnp.concatenate([jnp.exp(incl), jnp.exp(incl[SPAN - 1 : SPAN] - excl_r[b])], axis=0))
            wide = nn(hi, sp) + nn(lo, sp)
            el[at, cols] = wide[0:SPAN]
            eg[at, cols] = wide[SPAN:]
            cc = pltpu.roll(conv_low[at, INNER:].astype(F32), STATE, 1)[:, :STATE].astype(BF16)
            cc2 = jnp.concatenate([cc, cc], axis=1)
            yf = nn(cc2, jnp.concatenate(split(hin[b, :, cols]), axis=0))
            yg = nn(cc2, jnp.concatenate(split(gin[b + 1, :, cols]), axis=0))
            yb[at, cols] += wide[0:SPAN] * yf + wide[SPAN:] * yg
    dgain[...] = jnp.zeros_like(dgain)

    def gate_body(i, _):
        at = pl.ds(pl.multiple_of(i * 16, 16), 16)
        z = gate[at, :].astype(F32)
        hv = yb[at, :].astype(BF16).astype(F32)
        sg = sigmoid(z)
        sl = z * sg
        gated = hv * sl
        r = lax.rsqrt(jnp.mean(gated * gated, axis=1, keepdims=True) + EPS)
        unit = gated * r
        glow[at, :] = (unit * out_gain[...]).astype(BF16)
        gr = gg_scr[at, :]
        prod = gr * unit
        dgain[...] += prod[0:8] + prod[8:16]
        gg = gr * out_gain[...]
        dg = r * (gg - unit * jnp.mean(gg * unit, axis=1, keepdims=True))
        hgrad[at, :] = (dg * sl).astype(BF16)
        dgate[at, :] = (dg * hv * (sg * (1.0 + z * (1.0 - sg)))).astype(BF16)
        return 0

    lax.fori_loop(0, rows // 16, gate_body, 0)
    for g in range(dp // 256):
        cols = slice(g * 256, (g + 1) * 256)
        branch = nt(glow[...], o_full[cols, :])
        result[:, cols] = (x[:, cols].astype(F32) + keep_row * branch).astype(BF16)

    def state_body(b, _):
        at = pl.ds(pl.multiple_of(b * SPAN, SPAN), SPAN)
        ct = conv_low[at, INNER:].astype(F32).T[STATE:].astype(BF16)
        ct2 = jnp.concatenate([ct, ct], axis=1)
        for g in range(INNER // 256):
            cols = slice(g * 256, (g + 1) * 256)
            dy = hgrad[at, cols].astype(F32)
            for scale, dst in ((el, lst), (eg, mst)):
                hi, lo = split(scale[at, cols] * dy)
                dst[b, :, cols] = nn(ct2, jnp.concatenate([hi, lo], axis=0))
        return 0

    lax.fori_loop(0, blocks, state_body, 0)
    mv, lv = mst[0], lst[blocks - 1]
    for b in range(1, blocks):
        mv = mv * decb[b, 0:1, :] + mst[b]
    for b in range(blocks - 2, -1, -1):
        lv = lv * decb[b, 0:1, :] + lst[b]
    dev2[0] = mv
    dev2[1] = lv
    chain.finish()

    @pl.when(h < n_h - 1)
    def _():
        halo.wait_send()

    g_in.finish()
    g_out.finish()
    for c in leaving:
        c.wait()


def fore(n_s, n_h, rp, *args):
    x, _, w_in, w_out_t = args[:4]
    rin, cph = w_in.shape
    oph = w_out_t.shape[1]
    rows, dp = x.shape
    blocks = rows // SPAN
    wi = tile_count(cph, n_h) * LANES
    wo = tile_count(oph, n_h) * LANES
    dma = pltpu.SemaphoreType.DMA
    vm = pl.BlockSpec(memory_space=pltpu.VMEM)
    sm = pl.BlockSpec(memory_space=pltpu.SMEM)
    hbm = pl.BlockSpec(memory_space=pl.ANY)
    sds = jax.ShapeDtypeStruct
    vf = lambda *shape: pltpu.VMEM(shape, F32)
    vb = lambda *shape: pltpu.VMEM(shape, BF16)
    tables = vf(blocks, SPAN, LANES)
    act = sds((rows, INNER), BF16)
    states = sds((blocks, STATE, INNER), F32)
    entries = sds((blocks + 1, STATE, INNER), F32)
    outs = [
        (sds((rows, dp), BF16), vm),
        (sds((dp, WIDE), BF16), hbm),
        (sds((rows, dp), BF16), hbm),
        (sds((rows + HALO, CONV_CH), BF16), hbm),
        (sds((rows, CONV_CH), BF16), hbm),
        (sds((rows, CONV_CH), F32), hbm),
        (sds((rows, LANES), F32), vm),
        (sds((rows, LANES), F32), vm),
        (sds((blocks, 8, INNER), F32), vm),
        (sds((8, INNER), F32), vm),
        (act, vm),
        (act, vm),
        (act, vm),
        (sds((8, INNER), F32), vm),
        (states, vm),
        (states, vm),
        (sds((2, STATE, INNER), F32), vm),
        (entries, hbm),
        (entries, hbm),
    ]
    return pl.pallas_call(
        functools.partial(fore_kernel, n_s, n_h, cph, oph, rin, rp, wi, wo),
        out_shape=tuple(o for o, _ in outs),
        in_specs=[vm, vm, vm, vm, vm, sm],
        out_specs=tuple(p for _, p in outs),
        scratch_shapes=[
            vb(n_h, n_s, rp, wi + wo),
            vb(dp, WIDE),
            vb(dp, INNER),
            vb(HALO, dp),
            vf(rp, wi),
            vf(rp, wo),
            vb(rows + HALO, dp),
            vb(rows + HALO, CONV_CH),
            vb(rows, CONV_CH),
            vf(rows, CONV_CH),
            vf(rows + HALO, LANES),
            vb(rows, INNER),
            vf(blocks, STATE, INNER),
            vf(blocks, STATE, INNER),
            vf(2, STATE, INNER),
            vf(2, STATE, INNER),
            vf(2, STATE, INNER),
            tables, tables, tables, tables, tables, tables,
            vf(rows, INNER),
            vf(rows, INNER),
            vf(rows, INNER),
            vf(rows, INNER),
            vf(blocks + 1, STATE, INNER),
            vf(blocks + 1, STATE, INNER),
            vf(FLAT_ROWS, LANES),
            vf(1, dp),
            vf(8, CONV_CH),
            vf(8, LANES),
            vf(1, INNER),
            vb(LANES, INNER),
            dma((1,)),
            dma((1,)),
        ]
        + [dma((CHAIN_PARTS,))] * 4
        + [dma((7,))]
        + gather_sems(n_s, n_h) * 2,
        compiler_params=pltpu.CompilerParams(
            collective_id=1, has_side_effects=True, vmem_limit_bytes=FORE_VMEM
        ),
        name="fore",
    )(*args)


FORE_VMEM = 63 << 20
SMALL = 10696
FLAT_ROWS = 88
TAPS_ROWS = CONV_CH // LANES
HEAD_ROW = D // LANES + (CONV + 1) * TAPS_ROWS


CHUNK = 256
OUT_CHUNK = 384
N_IN = WIDE // CHUNK
N_OUT = INNER // OUT_CHUNK
X_CHUNK = INNER // CHUNK
SLOTS = 4
THIRD = 6
HOP = 2


def rear_kernel(
    n_s, n_h, cph, oph, rin, rp, in_slots,
    x, cot, flat, lengths, w_full_i, nlow, dgate_i, glow, conv_low, hgrad, steps, raw, slope_i, conv_in_i,
    hin_i, gin_i, lst_i, mst_i, dev, decb, dec, ogp, w_in, w_out_t, row_in, col_in, row_out, col_out, second_i,
    grad_x, grad_in, row_in_new, col_in_new, w_in_new, grad_out, row_out_new, col_out_new, w_out_new, small, second_new,
    params_new,
    w_full, slope, conv_in, hin, gin, lst, mst, prm, sec_rows, gain, taps, heads, spread,
    adj, csnd, nt_p, bt_p, pg, ng, dpre, halo, dfs, cfs, incl_r, excl_r, incl_t, excl_t, q_t, at_f, at_g, back_f, back_g,
    red, cross, dbc, dheads, dtaps, ngain, inter_s,
    sb, r0, vs, pbi, r1i, acci, r2i, pbo, r1o, acco, r2o, win,
    sz, spl, z1, p1, z2, p2, line,
    us, ur, ds, dr, hs, hr, s0s, s0r, s1s, s1r, s2s, s2r, o0s, o0r, o1s, o1r, o2s, o2r,
    load, szs, szr, sps, spr, z1s, z1r, p1s, p1r, z2s, z2r, p2s, p2r,
):
    s = lax.axis_index("seq")
    h = lax.axis_index("head")
    n_c = n_s // 2
    rows = x.shape[0]
    dp = x.shape[1]
    half = n_c * rp
    blocks = rows // SPAN
    chip = s // 2
    core = lax.rem(s, 2)
    sib = chip * 2 + (1 - core)
    up = lax.rem(h + 1, n_h)
    down = lax.rem(h + n_h - 1, n_h)
    zpeer = [lax.rem(h + j, n_h) for j in range(1, n_h)]
    cpeer = [lax.rem(chip + j, n_c) for j in range(1, n_c)]
    speer = [lax.rem(s + j, n_s) for j in range(1, n_s)]
    bar = pltpu.get_barrier_semaphore()
    for z in zpeer:
        pl.semaphore_signal(bar, inc=1, device_id=(s, z), device_id_type=MESH)
    for p in speer:
        pl.semaphore_signal(bar, inc=1, device_id=(p, h), device_id_type=MESH)
    pl.semaphore_wait(bar, n_h + n_s - 2)

    chain = Chain(n_h, s, h, dev, dec, adj, csnd, us, ur, ds, dr)
    chain.begin()
    pairs_of = (
        (dgate_i, pg.at[:, 0:INNER]), (w_full_i, w_full), (slope_i, slope), (hin_i, hin), (gin_i, gin), (lst_i, lst), (mst_i, mst),
        (conv_in_i, conv_in),
    )
    loads = [pltpu.make_async_copy(src, dst, load.at[n]) for n, (src, dst) in enumerate(pairs_of)]
    for c in loads:
        c.start()
    left = lengths[0] - h * rows

    def over_in(i):
        own = pl.ds(0, CHUNK)
        return remote(
            sb.at[lax.rem(i, 2), :, own], r0.at[lax.rem(i, SLOTS), :, own], s0s.at[i], s0r.at[i], (sib, h)
        )

    def over_out(i):
        return remote(sb.at[lax.rem(i, 2)], r0.at[lax.rem(i, SLOTS)], o0s.at[i], o0r.at[i], (sib, h))

    def first_in(i):
        @pl.when(i >= 2)
        def _():
            over_in(i - 2).wait_send()

        @pl.when(i < 2)
        def _():
            over_out(i + N_OUT - 2).wait_send()

        cols = pl.ds(pl.multiple_of(i * CHUNK, CHUNK), CHUNK)
        part = pg[:, cols]
        sb[lax.rem(i, 2), :, 0:CHUNK] = nn(nt_p[1 - core], part)
        over_in(i).start()
        ng[...] += nt(part, w_full[:, cols])

    def second_in(i):
        cols = pl.ds(pl.multiple_of(i * CHUNK, CHUNK), CHUNK)
        mine = nn(nt_p[core], pg[:, cols])
        over_in(i).wait_recv()
        vs[:, :, 0:CHUNK] = (mine + r0[lax.rem(i, SLOTS), :, 0:CHUNK]).reshape(n_c, rp, CHUNK)
        for j, k in enumerate(cpeer):
            pbi[i, j] = vs[k, :, 0:CHUNK].astype(BF16)
            remote(pbi.at[i, j], r1i.at[i, chip], s1s.at[i, j], s1r.at[i, chip], (2 * k + core, h)).start()
        acci[i] = vs[chip, :, 0:CHUNK]

    def owners(i, wide, per):
        one = (wide * i) // per
        two = (wide * i + wide - 1) // per
        return one, jnp.minimum(two, n_h - 1)

    def third_in(i):
        total = acci[i]
        for j, k in enumerate(cpeer):
            remote(pbi.at[i, j], r1i.at[i, k], s1s.at[i, j], s1r.at[i, k], (2 * k + core, h)).wait_recv()
            total = total + r1i[i, k].astype(F32)
        acci[i] = total

    def links(i, wide, per, acc, rec, snd, rcv):
        one, two = owners(i, wide, per)
        for n, q, real in ((0, one, None), (1, two, two != one))[: rec.shape[1]]:
            for way, to in ((0, up), (1, down)):
                sends_it = h < q if way == 0 else h > q
                if real is not None:
                    sends_it = jnp.logical_and(real, sends_it)
                begins = h == 0 if way == 0 else h == n_h - 1
                dst = rec.at[i, n, way]
                make = lambda src, n=n, way=way, to=to, dst=dst: remote(
                    src, dst, snd.at[i, n, way], rcv.at[i, n, way], (s, to)
                )
                yield way, sends_it, begins, make, n

    def along(i, way, *stream):
        acc, rec = stream[2], stream[3]
        for w, sends_it, begins, make, n in links(i, *stream):
            if w != way:
                continue

            @pl.when(jnp.logical_and(sends_it, begins))
            def _():
                make(acc.at[i]).start()

            @pl.when(jnp.logical_and(sends_it, jnp.logical_not(begins)))
            def _():
                make(acc.at[i]).wait_recv()
                rec[i, n, way] += acc[i]
                make(rec.at[i, n, way]).start()

    def drain_z(i, *stream):
        for _, sends_it, _, make, n in links(i, *stream):

            @pl.when(sends_it)
            def _():
                make(stream[2].at[i]).wait_send()

    in_stream = (CHUNK, cph, acci, r2i, s2s, s2r)
    out_stream = (OUT_CHUNK, oph, acco, r2o, o2s, o2r)

    def drain_in(i):
        for j, k in enumerate(cpeer):
            remote(pbi.at[i, j], r1i.at[i, chip], s1s.at[i, j], s1r.at[i, chip], (2 * k + core, h)).wait_send()
        drain_z(i, *in_stream)

    def first_out(i):
        @pl.when(i >= 2)
        def _():
            over_out(i - 2).wait_send()

        cols = pl.ds(pl.multiple_of(i * OUT_CHUNK, LANES), OUT_CHUNK)
        sb[lax.rem(i, 2)] = nn(bt_p[1 - core], glow[:, cols])
        over_out(i).start()

    def second_out(i):
        cols = pl.ds(pl.multiple_of(i * OUT_CHUNK, LANES), OUT_CHUNK)
        mine = nn(bt_p[core], glow[:, cols])
        over_out(i).wait_recv()
        vs[...] = (mine + r0[lax.rem(i, SLOTS)]).reshape(n_c, rp, OUT_CHUNK)
        for j, k in enumerate(cpeer):
            pbo[i, j] = vs[k].astype(BF16)
            remote(pbo.at[i, j], r1o.at[i, chip], o1s.at[i, j], o1r.at[i, chip], (2 * k + core, h)).start()
        acco[i] = vs[chip]

    def third_out(i):
        total = acco[i]
        for j, k in enumerate(cpeer):
            remote(pbo.at[i, j], r1o.at[i, k], o1s.at[i, j], o1r.at[i, k], (2 * k + core, h)).wait_recv()
            total = total + r1o[i, k].astype(F32)
        acco[i] = total

    def drain_out(i):
        for j, k in enumerate(cpeer):
            remote(pbo.at[i, j], r1o.at[i, chip], o1s.at[i, j], o1r.at[i, chip], (2 * k + core, h)).wait_send()
        drain_z(i, *out_stream)

    def among(k, first, count):
        return jnp.logical_and(k >= first, k < first + count)

    def stage_at(k):
        @pl.when(k < N_OUT)
        def _():
            first_out(k)

        @pl.when(jnp.logical_and(k >= N_OUT, k < N_OUT + N_IN))
        def _():
            first_in(k - N_OUT)

        @pl.when(jnp.logical_and(k >= 1, k < N_OUT + 1))
        def _():
            second_out(k - 1)

        @pl.when(jnp.logical_and(k >= N_OUT + 1, k < N_OUT + N_IN + 1))
        def _():
            second_in(k - 1 - N_OUT)

        @pl.when(among(k, THIRD, N_OUT))
        def _():
            third_out(k - THIRD)

        @pl.when(among(k, N_OUT + THIRD, N_IN))
        def _():
            third_in(k - THIRD - N_OUT)

        for way, lag in ((0, THIRD + HOP * h), (1, THIRD + HOP * (n_h - 1 - h))):

            @pl.when(among(k, lag, N_OUT))
            def _():
                along(k - lag, way, *out_stream)

            @pl.when(among(k, N_OUT + lag, N_IN))
            def _():
                along(k - lag - N_OUT, way, *in_stream)

    last_stage = N_OUT + N_IN - 1 + THIRD + HOP * (n_h - 2)

    keep_row = (iota((rows, 1), 0) < left).astype(F32)
    for src, dst in ((nlow[...], nt_p), ((cot[...].astype(F32) * keep_row).astype(BF16), bt_p)):
        turned = src.T
        for q in range(n_s):
            dst[q % 2, (q // 2) * rp : (q // 2 + 1) * rp, :] = turned[q * rp : (q + 1) * rp]
    flat_rows(flat, prm, 0.0)
    flat_rows(second_i, sec_rows, 1.0)
    unpack_rows(prm, rin, rp, gain, taps, heads, None)
    fill_spread(spread)
    ng[...] = jnp.zeros_like(ng)
    dheads[...] = jnp.zeros_like(dheads)
    dtaps[...] = jnp.zeros_like(dtaps)
    rates = -jnp.exp(heads[1:2, :])
    row = iota((SPAN, SPAN), 0)
    col = iota((SPAN, SPAN), 1)
    twice = 1.0 + (row == col).astype(F32)
    for ref in (q_t, at_f, at_g, back_f, back_g, red, cross, dbc):
        ref[...] = jnp.zeros_like(ref)
    for b in range(blocks):
        at = slice(b * SPAN, (b + 1) * SPAN)
        incl, excl, total = head_terms(steps[at, :], rates)
        incl_r[b] = incl
        excl_r[b] = excl
        incl_t[b] = incl.T
        excl_t[b] = excl.T
        bc = conv_low[at, INNER:].astype(F32)
        cb = pltpu.roll(bc, STATE, 1)
        inter_s[b] = nt(half_masks(bc)[0].astype(BF16), cb.astype(BF16))

    def pair_body(pair, _):
        cols = pl.ds(pl.multiple_of(pair * LANES, LANES), LANES)
        sp = spread[:, cols]
        later = col >= row
        hot = (iota((LANES, 2 * LANES), 0) == 2 * pair + iota((LANES, 2 * LANES), 1) // LANES).astype(BF16)
        hot3 = jnp.concatenate([hot, hot, hot], axis=0)
        for b in range(blocks):
            at = slice(b * SPAN, (b + 1) * SPAN)
            both = jnp.concatenate([incl_r[b], excl_r[b]], axis=0)
            wide = nn(jnp.concatenate(split3(both), axis=1), hot3)
            inter = inter_s[b]
            inter2 = inter * twice
            hi, lo = split(steps[at, :])
            xs = conv_low[at, cols].astype(F32)
            dyl = hgrad[at, cols]
            xh, xl = split((nn(hi, sp) + nn(lo, sp)) * xs)
            xhs = half_masks(xh)
            xls = half_masks(xl)
            dy2 = jnp.concatenate([dyl, dyl], axis=1)
            kern = []
            qt = q_t[b]
            for n in range(2):
                hd = 2 * pair + n
                lanes = slice(n * LANES, (n + 1) * LANES)
                gap = jnp.where(
                    later,
                    incl_t[b, pl.ds(hd, 1), :] - wide[0:SPAN, lanes],
                    wide[SPAN:, lanes] - excl_t[b, pl.ds(hd, 1), :],
                )
                decay = jnp.exp(gap)
                kern.append(inter2 * decay)
                weigh = nt(jnp.concatenate([xhs[n], xls[n]], axis=1), dy2) * decay
                qt = qt + weigh * twice
                pairs = weigh * inter
                above = jnp.where(col > row, pairs, 0.0)
                below = jnp.where(col < row, pairs, 0.0)
                at_f[b, pl.ds(hd, 1), :] = jnp.sum(above, axis=0, keepdims=True)
                at_g[b, pl.ds(hd, 1), :] = jnp.sum(below, axis=0, keepdims=True)
                here = iota((SPAN, LANES), 1) == hd
                back_f[b] = jnp.where(here, jnp.sum(above, axis=1, keepdims=True), back_f[b])
                back_g[b] = jnp.where(here, jnp.sum(below, axis=1, keepdims=True), back_g[b])
            q_t[b] = qt
            dys = half_masks(dyl)
            dpre[at, cols] = nn_split(jnp.concatenate(kern, axis=1), jnp.concatenate(dys, axis=0))
        chain.at(pair)

        @pl.when(pair < N_OUT + X_CHUNK)
        def _():
            stage_at(pair)

        return 0

    pairs_n = HEADS // 2
    for c in loads[:2]:
        c.wait()
    lax.fori_loop(0, pairs_n, pair_body, 0)
    for k in range(pairs_n, chain.steps()):
        chain.at(k)
    for c in loads[2:]:
        c.wait()

    @pl.when(h == n_h - 1)
    def _():
        halo[...] = jnp.zeros_like(halo)

    def halo_copy(g, size):
        cols = pl.ds(pl.multiple_of(g * CHUNK, CHUNK), size)
        return remote(dpre.at[0:8, cols], halo.at[:, cols], hs.at[g], hr.at[g], (s, down))

    def halo_send(g, size):
        @pl.when(h > 0)
        def _():
            halo_copy(g, size).start()

    def conv_back(g, size):
        cols = pl.ds(pl.multiple_of(g * CHUNK, CHUNK), size)
        own = slice(0, size)
        dp_ = dpre[:, cols]
        dfs[0:rows, own] = dp_
        cfs[:, own] = conv_in[:, cols].astype(F32)
        for k in range(CONV):
            first = HALO - CONV + 1 + k
            dtaps[k : k + 1, cols] = jnp.sum(dp_ * cfs[first : first + rows, own], axis=0, keepdims=True)
        dtaps[CONV : CONV + 1, cols] = jnp.sum(dp_, axis=0, keepdims=True)

        @pl.when(h < n_h - 1)
        def _():
            halo_copy(g, size).wait_recv()

        dfs[rows : rows + 8, own] = halo[:, cols]
        total = jnp.zeros((rows, size), F32)
        for k in range(CONV):
            first = CONV - 1 - k
            total = total + taps[k : k + 1, cols] * dfs[first : first + rows, own]
        pg[:, pl.ds(pl.multiple_of(INNER + g * CHUNK, CHUNK), size)] = total.astype(BF16)

    skip8 = jnp.broadcast_to(heads[2:3, :], (8, LANES))

    def group_compute(g):
        cols = pl.ds(pl.multiple_of(g * CHUNK, CHUNK), CHUNK)
        sp = spread[:, cols]
        skip = expand(skip8, sp)[0:1]
        ms, ls = [adj[0, :, cols]], [adj[1, :, cols]]
        for b in range(blocks - 1):
            ms.append(ms[-1] * decb[b, 0:1, cols] + mst[b, :, cols])
        for b in range(blocks - 1, 0, -1):
            ls.insert(0, ls[0] * decb[b, 0:1, cols] + lst[b, :, cols])
        zero_state = jnp.zeros((STATE, CHUNK), BF16)
        for b in range(blocks):
            at = slice(b * SPAN, (b + 1) * SPAN)
            incl, excl = incl_r[b], excl_r[b]
            total = incl[SPAN - 1 : SPAN]
            st = steps[at, :]
            terms = jnp.concatenate(
                [st, jnp.exp(incl), jnp.exp(total - excl), jnp.exp(total - incl), jnp.exp(excl)], axis=0
            )
            hi, lo = split(terms)
            wide = nn(hi, sp) + nn(lo, sp)
            st_e, el, eg, tl, ex = [wide[n * SPAN : (n + 1) * SPAN] for n in range(5)]
            bc = conv_low[at, INNER:].astype(F32)
            cb = pltpu.roll(bc, STATE, 1)
            bb = bc[:, :STATE].astype(BF16)
            cc = cb[:, :STATE].astype(BF16)
            bb2 = jnp.concatenate([bb, bb], axis=1)
            cc2 = jnp.concatenate([cc, cc], axis=1)
            xs = conv_low[at, cols].astype(F32)
            dy = hgrad[at, cols].astype(F32)
            xst = st_e * xs
            parts = [split(v) for v in (hin[b, :, cols], gin[b + 1, :, cols], ls[b], ms[b])]
            into_f = el * nn(cc2, jnp.concatenate(parts[0], axis=0))
            into_g = eg * nn(cc2, jnp.concatenate(parts[1], axis=0))
            out_f = tl * nn(bb2, jnp.concatenate(parts[2], axis=0))
            out_g = ex * nn(bb2, jnp.concatenate(parts[3], axis=0))
            dxu = dpre[at, cols] + out_f + out_g
            dpre[at, cols] = (st_e * dxu + skip * dy) * slope[at, cols]
            stack = jnp.concatenate([dy * into_f - xst * out_f, dy * into_g - xst * out_g, xs * dxu, xs * dy], axis=0)
            red[b] += fold(stack, sp)
            pair_f = jnp.sum(ls[b] * hin[b + 1, :, cols], axis=0, keepdims=True)
            pair_g = jnp.sum(ms[b] * gin[b, :, cols], axis=0, keepdims=True)
            cross[b] += fold(jnp.broadcast_to(pair_f + pair_g, (8, CHUNK)), sp)
            lefts, rights = [], []
            for scaled, (sh, sl), low in (
                (xst * tl, parts[2], True),
                (xst * ex, parts[3], True),
                (el * dy, parts[0], False),
                (eg * dy, parts[1], False),
            ):
                ah, al = split(scaled)
                for a, v in ((ah, sh), (al, sh), (ah, sl)):
                    lefts.append(a)
                    rights.append(jnp.concatenate([v, zero_state] if low else [zero_state, v], axis=0))
            dbc[b] += nt(jnp.concatenate(lefts, axis=1), jnp.concatenate(rights, axis=1))

    def group_body(g, _):
        group_compute(g)
        halo_send(g, CHUNK)

        @pl.when(g >= 1)
        def _():
            conv_back(g - 1, CHUNK)
            stage_at(N_OUT + X_CHUNK + g - 1)

        return 0

    lax.fori_loop(0, X_CHUNK, group_body, 0)

    for b in range(blocks):
        at = slice(b * SPAN, (b + 1) * SPAN)
        bc = conv_low[at, INNER:].astype(F32)
        cb_lo, cb_hi = half_masks(pltpu.roll(bc, STATE, 1))
        qt = q_t[b]
        d = dbc[b] + nn_split(qt, cb_lo.astype(BF16)) + nn_split(qt.T, cb_hi.astype(BF16))
        dpre[at, INNER:] = d * slope[at, INNER:]
    halo_send(X_CHUNK, LANES)
    conv_back(X_CHUNK - 1, CHUNK)
    stage_at(N_OUT + 2 * X_CHUNK - 1)
    for b in range(blocks):
        at = slice(b * SPAN, (b + 1) * SPAN)
        st = steps[at, :]
        rd = red[b]
        v_f = rd[0:SPAN] + at_f[b].T - back_f[b]
        v_g = rd[SPAN : 2 * SPAN] + at_g[b].T - back_g[b]
        da = precise(tri_high(), v_f) + precise(tri_low(), v_g) + cross[b, 0:1]
        dstep = rd[2 * SPAN : 3 * SPAN] + da * rates
        keep = jnp.logical_and(iota((SPAN, LANES), 0) + b * SPAN < left, iota((SPAN, LANES), 1) < HEADS)
        draw = jnp.where(keep, dstep * sigmoid(raw[at, :] + heads[0:1, :]), 0.0)
        pg[at, INNER + CONV_CH :] = draw.astype(BF16)
        dheads[0:1, :] += jnp.sum(draw, axis=0, keepdims=True)
        dheads[1:2, :] += jnp.sum(da * st, axis=0, keepdims=True) * rates
        dheads[2:3, :] += jnp.sum(rd[3 * SPAN :], axis=0, keepdims=True)
    conv_back(X_CHUNK, LANES)
    stage_at(N_OUT + N_IN - 1)
    stage_at(N_OUT + N_IN)

    ngain[...] = jnp.zeros_like(ngain)

    def norm_body(i, _):
        at = pl.ds(pl.multiple_of(i * 16, 16), 16)
        v = x[at, :].astype(F32)
        r = lax.rsqrt(jnp.sum(v * v, axis=1, keepdims=True) * (1.0 / D) + EPS)
        unit = v * r
        g = ng[at, :]
        prod = g * unit
        ngain[...] += prod[0:8] + prod[8:16]
        gg = g * gain[...]
        mean = jnp.sum(gg * unit, axis=1, keepdims=True) * (1.0 / D)
        grad_x[at, :] = cot[at, :].astype(F32) + r * (gg - unit * mean)
        return 0

    lax.fori_loop(0, rows // 16, norm_body, 0)

    sends = []

    def start(buf, me, peers, along_z, snd, rcv):
        for j, p in enumerate(peers):
            c = remote(buf.at[me], buf.at[me], snd.at[j], rcv.at[me], (s, p) if along_z else (p, h))
            c.start()
            sends.append(c)

    def arrive(buf, peers, along_z, snd, rcv):
        for j, p in enumerate(peers):
            remote(buf.at[p], buf.at[p], snd.at[j], rcv.at[p], (s, p) if along_z else (p, h)).wait_recv()
        total = buf[0]
        for i in range(1, buf.shape[0]):
            total = total + buf[i]
        return total

    first = D // LANES
    gsum = ngain[...]
    if dp != D:
        gsum = sum(nn(p, piece_map(dp, rin, rp)) for p in split3(gsum))
    for i in range(first):
        sz[h, i : i + 1, :] = jnp.sum(gsum[:, i * LANES : (i + 1) * LANES], axis=0, keepdims=True)
    for k in range(CONV + 1):
        for i in range(TAPS_ROWS):
            t = first + k * TAPS_ROWS + i
            sz[h, t : t + 1, :] = dtaps[k : k + 1, i * LANES : (i + 1) * LANES]
    lane1 = iota((1, LANES), 1)
    turn = 3 * HEADS
    before = dheads[0:1, :]
    for n in range(1, 3):
        before = jnp.where(lane1 < n * HEADS, before, pltpu.roll(dheads[n : n + 1, :], n * HEADS, 1))
    for i in range(INNER // LANES):
        tile = jnp.sum(ogp[:, i * LANES : (i + 1) * LANES], axis=0, keepdims=True)
        tile = pltpu.roll(tile, turn, 1)
        sz[h, HEAD_ROW + i : HEAD_ROW + i + 1, :] = jnp.where(lane1 < turn, before, tile)
        before = tile
    t = HEAD_ROW + INNER // LANES
    sz[h, t : t + 1, :] = jnp.where(lane1 < turn, before, 0.0)
    sz[h, t + 1 :, :] = jnp.zeros((FLAT_ROWS - t - 1, LANES), F32)
    start(sz, h, zpeer, True, szs, szr)

    def stage_body(k, _):
        stage_at(k)
        return 0

    lax.fori_loop(N_OUT + N_IN + 1, last_stage + 1, stage_body, 0)

    def window(slots, dst, wide, per, acc, rec, snd, rcv):
        c0 = (per * h) // wide
        c1 = (per * (h + 1) + wide - 1) // wide
        for c in range(slots):
            index = jnp.minimum(c0 + c, acc.shape[0] - 1)
            at = slice(c * wide, (c + 1) * wide)
            dst[:, at] = acc[index]
            n = jnp.where(owners(index, wide, per)[0] == h, 0, 1) if rec.shape[1] > 1 else 0
            for way, there in ((0, h > 0), (1, h < n_h - 1)):

                @pl.when(jnp.logical_and(c0 + c < c1, there))
                def _():
                    remote(acc.at[index], rec.at[index, n, way], snd.at[0, 0, 0], rcv.at[index, n, way], (s, up)).wait_recv()
                    dst[:, at] += rec[index, n, way]

    wi = in_slots * CHUNK
    window(in_slots, win, *in_stream)
    g_in = pltpu.roll(win[...], lax.rem(wi - lax.rem(cph * h, CHUNK), wi), 1)[0:rin, :cph]
    window(1, win, *out_stream)
    g_out = win[0:rin, 0:OUT_CHUNK]
    if oph != OUT_CHUNK:
        g_out = pltpu.roll(g_out, lax.rem(OUT_CHUNK - lax.rem(oph * h, OUT_CHUNK), OUT_CHUNK), 1)[:, :oph]
    grad_in[...] = g_in
    grad_out[...] = g_out

    decay_keep = 1.0 - DECAY
    sq_in = g_in * g_in
    sq_out = g_out * g_out
    fill = jnp.zeros((LANES - rin, LANES), F32)
    line_in = jnp.concatenate(
        [jnp.broadcast_to(jnp.sum(sq_in, axis=1, keepdims=True), (rin, LANES)), fill], axis=0
    ).T[0:8]
    line_out = jnp.concatenate(
        [jnp.broadcast_to(jnp.sum(sq_out, axis=1, keepdims=True), (rin, LANES)), fill], axis=0
    ).T[0:8]
    z1[h] = jnp.where(iota((8, LANES), 0) == 0, line_in, line_out)
    start(z1, h, zpeer, True, z1s, z1r)
    cs_in = jnp.sum(sq_in, axis=0, keepdims=True)
    rs_out = jnp.sum(sq_out, axis=0, keepdims=True)
    n_ci = -(-cph // LANES)
    n_ro = -(-oph // LANES)
    line[...] = jnp.zeros_like(line)
    line[0:1, 0:cph] = cs_in
    line[0:1, n_ci * LANES : n_ci * LANES + oph] = rs_out
    p1[s] = jnp.zeros_like(p1[0])
    for i in range(n_ci + n_ro):
        p1[s, i : i + 1, :] = line[0:1, i * LANES : (i + 1) * LANES]
    start(p1, s, speer, False, p1s, p1r)
    spl[s] = arrive(sz, zpeer, True, szs, szr)
    start(spl, s, speer, False, sps, spr)
    sums = arrive(z1, zpeer, True, z1s, z1r)
    line_r = DECAY * row_in[...].reshape(1, rin) + decay_keep * (sums[0:1, 0:rin] / PROJ + EPS_SQUARE)
    line_c = DECAY * col_out[...].reshape(1, rin) + decay_keep * (sums[1:2, 0:rin] / INNER + EPS_SQUARE)
    row_in_new[...] = line_r.reshape(rin)
    col_out_new[...] = line_c.reshape(rin)
    fill_line = jnp.zeros((1, LANES - rin), F32)
    up_r = jnp.broadcast_to(jnp.concatenate([line_r, fill_line], axis=1), (LANES, LANES)).T[0:rin, 0:1]
    up_c = jnp.broadcast_to(jnp.concatenate([line_c, fill_line], axis=1), (LANES, LANES)).T[0:rin, 0:1]
    sums = arrive(p1, speer, False, p1s, p1r)
    for i in range(n_ci + n_ro):
        line[0:1, i * LANES : (i + 1) * LANES] = sums[i : i + 1]
    line_ci = DECAY * col_in[...].reshape(1, cph) + decay_keep * (line[0:1, 0:cph] / D + EPS_SQUARE)
    line_ro = DECAY * row_out[...].reshape(1, oph) + decay_keep * (
        line[0:1, n_ci * LANES : n_ci * LANES + oph] / D + EPS_SQUARE
    )
    col_in_new[...] = line_ci.reshape(cph)
    row_out_new[...] = line_ro.reshape(oph)
    u_in = g_in * lax.rsqrt(up_r * line_ci)
    u_out = g_out * lax.rsqrt(up_c * line_ro)
    lane = iota((8, LANES), 1)
    values = (
        jnp.sum(u_in * u_in, keepdims=True),
        jnp.sum(u_out * u_out, keepdims=True),
        jnp.sum(line_ro, axis=1, keepdims=True),
        jnp.sum(line_r, axis=1, keepdims=True) / n_h,
    )
    note = jnp.zeros((8, LANES), F32)
    for n, v in enumerate(values):
        note = jnp.where(lane == n, v, note)
    z2[h] = note
    start(z2, h, zpeer, True, z2s, z2r)

    g = arrive(spl, speer, False, sps, spr)
    sec = DECAY * sec_rows[...] + decay_keep * (g * g + EPS_SQUARE)
    u = g * lax.rsqrt(sec)
    spread_small = jnp.sqrt(jnp.sum(u * u, keepdims=True) / SMALL)
    par = prm[...] - LEARN_SMALL * u / jnp.maximum(1.0, spread_small / CLIP_RMS)

    p2[s] = arrive(z2, zpeer, True, z2s, z2r)
    start(p2, s, speer, False, p2s, p2r)
    mean_out = p2[s, 0:1, 2:3] / INNER
    whole, rest = SMALL // LANES, SMALL % LANES
    for v, dst in ((g, small), (sec, second_new), (par, params_new)):
        for i in range(whole):
            dst[pl.ds(i * LANES, LANES)] = v[i : i + 1].reshape(LANES)
        dst[pl.ds(whole * LANES, rest)] = v[whole : whole + 1, 0:rest].reshape(rest)

    chain.finish()

    @pl.when(h > 0)
    def _():
        for g in range(X_CHUNK):
            halo_copy(g, CHUNK).wait_send()
        halo_copy(X_CHUNK, LANES).wait_send()

    for i in (N_IN - 2, N_IN - 1):
        over_in(i).wait_send()

    def drain_body(i, _):
        drain_in(i)

        @pl.when(i < N_OUT)
        def _():
            drain_out(i)

        return 0

    lax.fori_loop(0, N_IN, drain_body, 0)
    sums = arrive(p2, speer, False, p2s, p2r)
    mean_in = sums[0:1, 3:4] / D
    clip_in = jnp.maximum(1.0, jnp.sqrt(sums[0:1, 0:1] * mean_in / (D * PROJ)) / CLIP_RMS)
    clip_out = jnp.maximum(1.0, jnp.sqrt(sums[0:1, 1:2] * mean_out / (INNER * D)) / CLIP_RMS)
    w_in_new[...] = w_in[...] - u_in * (LEARN_RATE * jnp.sqrt(mean_in) / clip_in)
    w_out_new[...] = w_out_t[...] - u_out * (LEARN_RATE * jnp.sqrt(mean_out) / clip_out)
    for c in sends:
        c.wait_send()


def rear(n_s, n_h, rp, *args):
    x = args[0]
    w_in, w_out_t = args[22], args[23]
    rin, cph = w_in.shape
    oph = w_out_t.shape[1]
    rows, dp = x.shape
    n_c = n_s // 2
    half = n_c * rp
    blocks = rows // SPAN
    in_slots = max(-(-cph * (q + 1) // CHUNK) - cph * q // CHUNK for q in range(n_h))
    out_dup = 1 if oph % OUT_CHUNK == 0 else 2
    n_line = -(-cph // LANES) + -(-oph // LANES)
    n_rows = -(-(n_line + 1) // 8) * 8
    dma = pltpu.SemaphoreType.DMA
    vm = pl.BlockSpec(memory_space=pltpu.VMEM)
    sm = pl.BlockSpec(memory_space=pltpu.SMEM)
    hbm = pl.BlockSpec(memory_space=pl.ANY)
    sds = jax.ShapeDtypeStruct
    vf = lambda *shape: pltpu.VMEM(shape, F32)
    vb = lambda *shape: pltpu.VMEM(shape, BF16)
    tables = vf(blocks, SPAN, LANES)
    specs = [vm] * len(args)
    specs[3] = sm
    for i in (4, 6, 12, 13, 14, 15, 16, 17):
        specs[i] = hbm
    return pl.pallas_call(
        functools.partial(rear_kernel, n_s, n_h, cph, oph, rin, rp, in_slots),
        out_shape=(
            sds((rows, dp), F32),
            sds((rin, cph), F32),
            sds((rin,), F32),
            sds((cph,), F32),
            sds((rin, cph), F32),
            sds((rin, oph), F32),
            sds((oph,), F32),
            sds((rin,), F32),
            sds((rin, oph), F32),
            sds((SMALL,), F32),
            sds((SMALL,), F32),
            sds((SMALL,), F32),
        ),
        in_specs=specs,
        out_specs=(vm,) * 12,
        scratch_shapes=[
            vb(dp, WIDE),
            vf(rows, CONV_CH),
            vb(rows + HALO, CONV_CH),
            vf(blocks + 1, STATE, INNER),
            vf(blocks + 1, STATE, INNER),
            vf(blocks, STATE, INNER),
            vf(blocks, STATE, INNER),
            vf(FLAT_ROWS, LANES),
            vf(FLAT_ROWS, LANES),
            vf(1, dp),
            vf(8, CONV_CH),
            vf(8, LANES),
            vb(LANES, INNER),
            vf(2, STATE, INNER),
            vf(2, STATE, INNER),
            vb(2, half, rows),
            vb(2, half, rows),
            vb(rows, WIDE),
            vf(rows, dp),
            vf(rows, CONV_CH),
            vf(8, CONV_CH),
            vf(rows + 8, CHUNK),
            vf(rows + HALO, CHUNK),
            tables, tables, tables, tables, tables, tables, tables, tables, tables,
            vf(blocks, 4 * SPAN, LANES),
            vf(blocks, 8, LANES),
            tables,
            vf(8, LANES),
            vf(8, CONV_CH),
            vf(8, dp),
            tables,
            vf(2, half, OUT_CHUNK),
            vf(SLOTS, half, OUT_CHUNK),
            vf(n_c, rp, OUT_CHUNK),
            vb(N_IN, n_c - 1, rp, CHUNK),
            vb(N_IN, n_c, rp, CHUNK),
            vf(N_IN, rp, CHUNK),
            vf(N_IN, 2, 2, rp, CHUNK),
            vb(N_OUT, n_c - 1, rp, OUT_CHUNK),
            vb(N_OUT, n_c, rp, OUT_CHUNK),
            vf(N_OUT, rp, OUT_CHUNK),
            vf(N_OUT, out_dup, 2, rp, OUT_CHUNK),
            vf(rp, in_slots * CHUNK),
            vf(n_h, FLAT_ROWS, LANES),
            vf(n_s, FLAT_ROWS, LANES),
            vf(n_h, 8, LANES),
            vf(n_s, n_rows, LANES),
            vf(n_h, 8, LANES),
            vf(n_s, 8, LANES),
            vf(8, n_line * LANES),
        ]
        + [dma((CHAIN_PARTS,))] * 4
        + [dma((X_CHUNK + 1,))] * 2
        + [dma((N_IN,)), dma((N_IN,)), dma((N_IN, n_c)), dma((N_IN, n_c)), dma((N_IN, 2, 2)), dma((N_IN, 2, 2))]
        + [dma((N_OUT,)), dma((N_OUT,)), dma((N_OUT, n_c)), dma((N_OUT, n_c)), dma((N_OUT, out_dup, 2)), dma((N_OUT, out_dup, 2))]
        + [dma((8,))]
        + [dma((n_h,)), dma((n_h,)), dma((n_s,)), dma((n_s,))] * 3,
        compiler_params=pltpu.CompilerParams(
            collective_id=2, has_side_effects=True, vmem_limit_bytes=REAR_VMEM
        ),
        name="rear",
    )(*args)


REAR_VMEM = 63 << 20


def on_device(
    x_in, lengths, cotangent, w_in, w_out, small_params, row_in, col_in, row_out, col_out, small_second
):
    n_s = lax.axis_size("seq")
    n_h = lax.axis_size("head")
    rin = w_in.shape[0]
    rp = -(-rin // 16) * 16
    dp = n_s * rp
    def pad(v, axis, fill=0):
        if rp == rin:
            return v
        shape = v.shape[:axis] + (n_s, rin) + v.shape[axis + 1 :]
        widths = [(0, 0)] * len(shape)
        widths[axis + 1] = (0, rp - rin)
        v = jnp.pad(v.reshape(shape), widths, constant_values=fill)
        return v.reshape(v.shape[:axis] + (dp,) + v.shape[axis + 2 :])

    def cut(v, axis):
        if rp == rin:
            return v
        shape = v.shape[:axis] + (n_s, rp) + v.shape[axis + 1 :]
        v = lax.slice_in_dim(v.reshape(shape), 0, rin, axis=axis + 1)
        return v.reshape(v.shape[:axis] + (D,) + v.shape[axis + 2 :])

    x = pad(x_in, 1)
    cot = pad(cotangent, 1)
    w_out_t = w_out.T
    (
        result, w_full, nlow, conv_in, conv_low, slope, raw, steps, decb, dec, dgate, hgrad, glow, og_part, lst, mst, dev2, hin,
        gin,
    ) = fore(n_s, n_h, rp, x, cot, w_in, w_out_t, small_params, lengths)
    (
        grad_x, grad_in, row_in_new, col_in_new, w_in_new, grad_out, row_out_new, col_out_new, w_out_new, small,
        second_new, params_new,
    ) = rear(
        n_s, n_h, rp,
        x, cot, small_params, lengths, w_full, nlow, dgate, glow, conv_low, hgrad, steps, raw, slope, conv_in, hin, gin, lst, mst,
        dev2, decb, dec, og_part, w_in, w_out_t, row_in, col_in, row_out, col_out, small_second,
    )
    return (
        cut(result, 1), cut(grad_x, 1), grad_in, row_in_new, col_in_new, w_in_new, grad_out.T, row_out_new, col_out_new,
        w_out_new.T, small, second_new, params_new,
    )


def solution(mesh):
    both = P(("seq", "head"), None)
    factors = (P("seq", "head"), P("seq"), P("head"), P("seq", "head"))
    return jax.shard_map(
        on_device,
        mesh=mesh,
        in_specs=(
            both, P("seq"), both, P("seq", "head"), P("head", "seq"), P(), P("seq"), P("head"), P("head"), P("seq"), P(),
        ),
        out_specs=(
            both, both, P("seq", "head"), P("seq"), P("head"), P("seq", "head"), P("head", "seq"), P("head"), P("seq"),
            P("head", "seq"), P(), P(), P(),
        ),
        check_vma=False,
    )
```

```python
import functools

import jax
import jax.numpy as jnp
import numpy as np
from jax import lax
from jax.experimental import pallas as pl
from jax.experimental.pallas import tpu as pltpu
from jax.sharding import PartitionSpec as P

D = 768
HEADS = 24
HEAD_DIM = 64
STATE = 64
CONV = 4
SPAN = 128
STEP = 8
INNER = 1536
CONV_CH = 1664
PROJ = 3224
WIDE = 3328
LANES = 128
HALO = 16

EPS = 1e-05
EPS_SQUARE = 1e-30
LEARN_RATE = 0.3
LEARN_SMALL = 3.0
CLIP_RMS = 0.1
DECAY = 1.0 - STEP ** (-0.8)
F32 = jnp.float32
BF16 = jnp.bfloat16
HIGHEST = lax.Precision.HIGHEST
MESH = pl.DeviceIdType.MESH
VMEM_BYTES = 60 << 20


def nn(left, right):
    return lax.dot_general(left, right, (((1,), (0,)), ((), ())), preferred_element_type=F32)


def nt(left, right):
    return lax.dot_general(left, right, (((1,), (1,)), ((), ())), preferred_element_type=F32)


def split(value):
    high = value.astype(BF16)
    return high, (value - high.astype(F32)).astype(BF16)


def stacked(value):
    return jnp.concatenate(split(value), axis=0)


def halves_sum(value):
    rows = value.shape[0] // 2
    return value[:rows] + value[rows:]


def nn_split(value, exact):
    return halves_sum(nn(stacked(value), exact))


def expand(value, spread):
    return nn_split(value, spread)


def fold(value, spread):
    return halves_sum(nt(stacked(value), spread))


def iota(shape, dim):
    return lax.broadcasted_iota(jnp.int32, shape, dim)


def tri_low():
    return (iota((SPAN, SPAN), 0) >= iota((SPAN, SPAN), 1)).astype(F32)


def tri_high():
    return (iota((SPAN, SPAN), 0) <= iota((SPAN, SPAN), 1)).astype(F32)


def precise(left, right):
    return lax.dot_general(
        left, right, (((1,), (0,)), ((), ())), precision=HIGHEST, preferred_element_type=F32
    )


def sigmoid(value):
    return 1.0 / (1.0 + jnp.exp(-value))


def tiles_of(per_part, index):
    return (per_part * index) // LANES, -(-(per_part * (index + 1)) // LANES)


def tile_count(per_part, parts):
    return max(e - s for s, e in (tiles_of(per_part, i) for i in range(parts)))


def half_masks(value):
    low = iota(value.shape, 1) < HEAD_DIM
    zero = jnp.zeros_like(value)
    return jnp.where(low, value, zero), jnp.where(low, zero, value)


def head_terms(steps, rates):
    logs = steps * rates
    incl = precise(tri_low(), logs)
    return incl, incl - logs, incl[SPAN - 1 : SPAN]


CHAIN_PARTS = 4


class Chain:
    def __init__(self, n_h, s, h, dev, dec, out, snd, us, ur, ds, dr):
        self.n_h, self.s, self.h = n_h, s, h
        self.dev, self.dec, self.out, self.snd = dev, dec, out, snd
        self.sems = ((us, ur), (ds, dr))
        self.next = (lax.rem(h + 1, n_h), lax.rem(h + n_h - 1, n_h))
        self.inner = jnp.logical_and(h > 0, h < n_h - 1)
        self.first = (h == 0, h == n_h - 1)
        self.last = (h == n_h - 1, h == 0)

    def link(self, d, c):
        width = STATE // CHAIN_PARTS
        at = pl.ds(c * width, width)
        snd, rcv = self.sems[d]
        return remote(self.snd.at[d, at], self.out.at[d, at], snd.at[c], rcv.at[c], (self.s, self.next[d]))

    def begin(self):
        for d in range(2):

            @pl.when(self.first[d])
            def _():
                self.out[d] = jnp.zeros((STATE, INNER), F32)
                self.snd[d] = self.dev[d]
                for c in range(CHAIN_PARTS):
                    self.link(d, c).start()

    def step(self, d, c):
        width = STATE // CHAIN_PARTS
        at = slice(c * width, (c + 1) * width)

        @pl.when(jnp.logical_not(self.first[d]))
        def _():
            self.link(d, c).wait_recv()

        @pl.when(self.inner)
        def _():
            self.snd[d, at] = self.out[d, at] * self.dec[0:1] + self.dev[d, at]
            self.link(d, c).start()

    def at(self, k, stride=2):
        for c in range(CHAIN_PARTS):

            @pl.when(k == stride * self.h + c)
            def _():
                self.step(0, c)

            @pl.when(k == stride * (self.n_h - 1 - self.h) + c)
            def _():
                self.step(1, c)

    def steps(self, stride=2):
        return stride * (self.n_h - 1) + CHAIN_PARTS

    def finish(self):
        for d in range(2):

            @pl.when(jnp.logical_not(self.last[d]))
            def _():
                for c in range(CHAIN_PARTS):
                    self.link(d, c).wait_send()


def remote(src, dst, send, recv, dev):
    return pltpu.make_async_remote_copy(
        src_ref=src, dst_ref=dst, send_sem=send, recv_sem=recv, device_id=dev, device_id_type=MESH
    )


def split3(value):
    high = value.astype(BF16)
    rest = value - high.astype(F32)
    mid, low = split(rest)
    return high, mid, low


def flat_rows(flat, rows, fill):
    count = SMALL // LANES
    for i in range(count):
        rows[i : i + 1, :] = flat[pl.ds(i * LANES, LANES)].reshape(1, LANES)
    rows[count:, :] = jnp.full((rows.shape[0] - count, LANES), fill, F32)
    rest = SMALL - count * LANES
    rows[count : count + 1, 0:rest] = flat[pl.ds(count * LANES, rest)].reshape(1, rest)


def piece_map(dp, rin, rp):
    place = iota((dp, D), 0)
    return jnp.logical_and(place // rp * rin + place % rp == iota((dp, D), 1), place % rp < rin).astype(BF16)


def unpack_rows(rows, rin, rp, gain, taps, heads, out_gain):
    dp = gain.shape[1]
    first = D // LANES
    flat_gain = jnp.concatenate([rows[i : i + 1, :] for i in range(first)], axis=1)
    if dp == D:
        gain[...] = flat_gain
    else:
        parts = split3(jnp.broadcast_to(flat_gain, (8, D)))
        gain[...] = sum(nt(p, piece_map(dp, rin, rp)) for p in parts)[0:1]
    taps[...] = jnp.zeros_like(taps)
    for k in range(CONV + 1):
        for i in range(TAPS_ROWS):
            r = first + k * TAPS_ROWS + i
            taps[k : k + 1, i * LANES : (i + 1) * LANES] = rows[r : r + 1, :]
    r = HEAD_ROW
    lane = iota((1, LANES), 1)
    line = rows[r : r + 1, :]
    heads[...] = jnp.zeros_like(heads)
    for n in range(3):
        v = line if n == 0 else pltpu.roll(line, LANES - n * HEADS, 1)
        heads[n : n + 1, :] = jnp.where(lane < HEADS, v, 0.0)
    if out_gain is not None:
        turn = LANES - 3 * HEADS
        for i in range(INNER // LANES):
            here = pltpu.roll(rows[r + i : r + i + 1, :], turn, 1)
            after = pltpu.roll(rows[r + i + 1 : r + i + 2, :], turn, 1)
            out_gain[0:1, i * LANES : (i + 1) * LANES] = jnp.where(lane < turn, here, after)


def fill_spread(spread):
    spread[...] = (iota((LANES, INNER), 0) == iota((LANES, INNER), 1) // HEAD_DIM).astype(BF16)


def run_all(*steps):
    def run():
        for step in steps:
            step()

    return run


class Gather:
    def __init__(self, n_s, n_h, s, h, full, base, count, parts, sems):
        self.n_s, self.n_h, self.s, self.h, self.full = n_s, n_h, s, h, full
        self.base, self.count, self.parts = base, count, parts
        self.zs, self.zr, self.ps, self.pr, self.ds, self.dr, self.cs, self.cr = sems
        self.n_c = n_s // 2
        self.chip = s // 2
        self.core = lax.rem(s, 2)
        self.sib = self.chip * 2 + (1 - self.core)
        self.cpeer = [lax.rem(self.chip + j, self.n_c) for j in range(1, self.n_c)]
        self.square = self.n_c == 4
        self.xn = self.chip + 1 - 2 * lax.rem(self.chip, 2)
        self.yn = lax.rem(self.chip + self.n_c // 2, self.n_c)
        self.diag = 3 - self.chip
        place = jnp.clip(h - base, 0, count - 1)
        self.order = [base + place] + [base + self.nth(j, place, count) for j in range(1, count)]
        self.items = [(q, p) for q in self.order for p in range(len(parts))]

    def nth(self, j, place, count):
        below = jnp.where(j - 1 >= place, j, j - 1)
        mirror = count - 1 - place
        above = count - 1 - jnp.where(j - 1 >= mirror, j, j - 1)
        return jnp.where(2 * place < count, below, above)

    def when(self, item, work):
        q, p = item
        only = self.parts[p][1]
        if only is None:
            work()
        else:
            pl.when(q == only)(work)

    def blk(self, item, c, part=None, other=False):
        q, p = item
        core = 1 - self.core if other else self.core
        ref = self.full.at[q, c * 2 + core]
        rp = self.full.shape[2]
        lanes = self.parts[p][0]
        if part is None:
            return ref.at[:, lanes]
        mid = rp // 2 // 16 * 16
        return ref.at[pl.ds(0, mid) if part == 0 else pl.ds(mid, rp - mid), lanes]

    def along(self, item, way):
        ref = self.blk(item, self.chip)
        to = lax.rem(self.h + (1 if way == 0 else self.n_h - 1), self.n_h)
        q, p = item
        return remote(ref, ref, self.zs.at[q - self.base, p, way], self.zr.at[q - self.base, p], (self.s, to))

    def begin(self):
        for p in range(len(self.parts)):
            item = (self.h, p)
            mine = jnp.logical_and(self.h >= self.base, self.h < self.base + self.count)
            if self.parts[p][1] is not None:
                mine = jnp.logical_and(mine, self.h == self.parts[p][1])
            for way, there in ((0, self.h < self.n_h - 1), (1, self.h > 0)):
                pl.when(jnp.logical_and(mine, there))(lambda item=item, way=way: self.along(item, way).start())

    def z_in(self, i):
        item = self.items[i]
        q = item[0]

        def take():
            self.along(item, 0).wait_recv()
            up = jnp.logical_and(q < self.h, self.h < self.n_h - 1)
            down = jnp.logical_and(q > self.h, self.h > 0)
            pl.when(up)(lambda: self.along(item, 0).start())
            pl.when(down)(lambda: self.along(item, 1).start())

        self.when(item, lambda: pl.when(q != self.h)(take))

    def z_done(self, i):
        item = self.items[i]
        q = item[0]
        up = jnp.logical_and(q <= self.h, self.h < self.n_h - 1)
        down = jnp.logical_and(q >= self.h, self.h > 0)
        self.when(item, lambda: pl.when(up)(lambda: self.along(item, 0).wait_send()))
        self.when(item, lambda: pl.when(down)(lambda: self.along(item, 1).wait_send()))

    def to_chip(self, i, m, part, c):
        item = self.items[i]
        q, p = item
        ref = self.blk(item, self.chip, part)
        n = 0 if part is None else part
        return remote(ref, ref, self.ps.at[q - self.base, p, m, n], self.pr.at[q - self.base, p, self.chip, n], (c * 2 + self.core, self.h))

    def to_chips(self, i):
        if self.square:
            near = ((0, self.xn), (1, self.yn))
            return [self.to_chip(i, m, (n + m) % 2, c) for n in range(2) for m, c in near]
        return [self.to_chip(i, j, None, c) for j, c in enumerate(self.cpeer)]

    def over(self, i, j, c):
        item = self.items[i]
        q, p = item
        ref = self.blk(item, c)
        return remote(ref, ref, self.cs.at[q - self.base, p, j], self.cr.at[q - self.base, p, c], (self.sib, self.h))

    def onward(self, i, n):
        item = self.items[i]
        q, p = item
        c, to = (self.xn, self.yn) if n == 0 else (self.yn, self.xn)
        ref = self.blk(item, c, n)
        return remote(ref, ref, self.ds.at[q - self.base, p, n], self.dr.at[q - self.base, p, n], (to * 2 + self.core, self.h))

    def spread_out(self, i):
        def work():
            for c in self.to_chips(i):
                c.start()
            self.over(i, 0, self.chip).start()

        self.when(self.items[i], work)

    def got(self, i, c, part):
        item = self.items[i]
        q, p = item
        ref = self.blk(item, c, part)
        n = 0 if part is None else part
        remote(ref, ref, self.ps.at[q - self.base, p, 0, 0], self.pr.at[q - self.base, p, c, n], (self.sib, self.h)).wait_recv()

    def pass_on(self, i):
        def work():
            if self.square:
                for n, c in ((0, self.xn), (1, self.yn)):
                    self.got(i, c, n)
                    self.onward(i, n).start()
                for n, c in ((1, self.xn), (0, self.yn)):
                    self.got(i, c, n)
                    self.over(i, 2 - n, c).start()
            else:
                for j, c in enumerate(self.cpeer):
                    self.got(i, c, None)
                    self.over(i, j + 1, c).start()

        self.when(self.items[i], work)

    def last_in(self, i):
        if not self.square:
            return
        item = self.items[i]
        q, p = item

        def work():
            for n in range(2):
                ref = self.blk(item, self.diag, n)
                remote(ref, ref, self.ds.at[q - self.base, p, 0], self.dr.at[q - self.base, p, n], (self.sib, self.h)).wait_recv()
            self.over(i, 3, self.diag).start()

        self.when(item, work)

    def complete(self, i):
        item = self.items[i]
        q, p = item

        def work():
            for c in [self.chip] + self.cpeer:
                ref = self.blk(item, c, other=True)
                remote(ref, ref, self.cs.at[q - self.base, p, 0], self.cr.at[q - self.base, p, c], (self.sib, self.h)).wait_recv()

        self.when(item, work)

    def plan(self, columns):
        count, parts = len(self.items), len(self.parts)
        plan = []
        for i in range(count + 3):
            if i < count:
                plan.append(run_all(lambda i=i: self.z_in(i), lambda i=i: self.spread_out(i)))
            if 1 <= i <= count:
                plan.append(lambda i=i: self.pass_on(i - 1))
            if 2 <= i <= count + 1:
                plan.append(lambda i=i: self.last_in(i - 2))
            if 3 <= i:
                plan.append(lambda i=i: self.complete(i - 3))
                if (i - 3) % parts == parts - 1 and columns is not None:
                    plan.append(lambda i=i: columns(self.order[(i - 3) // parts]))
        return plan

    def finish(self):
        for i in range(len(self.items)):
            self.z_done(i)
            chips = [self.chip] + ([self.xn, self.yn, self.diag] if self.square else self.cpeer)

            def work():
                for c in self.to_chips(i):
                    c.wait_send()
                for j, c in enumerate(chips):
                    self.over(i, j, c).wait_send()
                if self.square:
                    for n in range(2):
                        self.onward(i, n).wait_send()

            self.when(self.items[i], work)


def gather_sems(n_s, count, parts):
    dma = pltpu.SemaphoreType.DMA
    n_c = n_s // 2
    n = 2 if n_c == 4 else 1
    return [
        dma((count, parts, 2)), dma((count, parts)), dma((count, parts, n_c, n)), dma((count, parts, n_c, n)),
        dma((count, parts, 2)), dma((count, parts, 2)), dma((count, parts, n_c)), dma((count, parts, n_c)),
    ]


def own_tiles(per_part, parts, width):
    return [(per_part * q) // LANES for q in range(parts)] + [width // LANES]


def payload_parts(per_part, parts, width):
    first = own_tiles(per_part, parts, width)
    counts = [first[q + 1] - first[q] for q in range(parts)]
    common = max(counts[:-1])
    mid = (common + 1) // 2
    ranges = [(slice(0, mid * LANES), None), (slice(mid * LANES, common * LANES), None)]
    if counts[-1] > common:
        ranges.append((slice(common * LANES, counts[-1] * LANES), parts - 1))
    return ranges, max(counts) * LANES


def fore_kernel(
    n_s, n_h, cph, oph, rin, rp, wi, wo, wide_in,
    x, cot, w_in, w_out_t, flat, lengths,
    result, w_full_o, nlow_o, conv_in_o, conv_low_o, slope_o, raw, steps, decb, dec, dgate, hgrad, glow, dgain, lst, mst,
    dev2, hin_o, gin_o,
    full, w_full, o_full, xh, shift_in, edge_out, edge_in, shift_out, nscr, conv_in, conv_low, slope, cf, gate, hst, gst, dev, into, csnd, incl_r,
    excl_r, incl_t, excl_t, steps_t, inter_s, yb, el, eg, gg_scr, hin, gin, prm, gain, taps, heads, out_gain, spread, logs3, el_eg, cc2,
    xs_, xr_, es_, er_, us, ur, dws, dwr, outs, *gsems,
):
    s = lax.axis_index("seq")
    h = lax.axis_index("head")
    n_c = n_s // 2
    rows = x.shape[0]
    dp = x.shape[1]
    blocks = rows // SPAN
    chip = s // 2
    core = lax.rem(s, 2)
    sib = chip * 2 + (1 - core)
    cpeer = [lax.rem(chip + j, n_c) for j in range(1, n_c)]
    left = lengths[0] - h * rows
    parts, _ = payload_parts(cph, n_h, WIDE)
    sems = [gsems[8 * n : 8 * n + 8] for n in range(3)]
    half_h = n_h // 2
    g_high = Gather(n_s, n_h, s, h, full, half_h, n_h - half_h, parts, sems[0])
    g_low = Gather(n_s, n_h, s, h, full, 0, half_h, parts[:2], sems[1])
    g_out = Gather(n_s, n_h, s, h, full, 0, n_h, [(slice(wi, wi + wo), None)], sems[2])
    zpeer = [lax.rem(h + j, n_h) for j in range(1, n_h)]
    bar = pltpu.get_barrier_semaphore()
    for z in zpeer:
        pl.semaphore_signal(bar, inc=1, device_id=(s, z), device_id_type=MESH)
    for c in cpeer:
        pl.semaphore_signal(bar, inc=1, device_id=(c * 2 + core, h), device_id_type=MESH)
    pl.semaphore_signal(bar, inc=1, device_id=(sib, h), device_id_type=MESH)

    shift_in[...] = jnp.zeros_like(shift_in)
    shift_in[0:rin, 0:cph] = w_in[...]
    placed = pltpu.roll(shift_in[...], lax.rem(cph * h, LANES), 1)
    shift_in[...] = placed
    full[h, s, :, 0:wi] = placed[:, 0:wi].astype(BF16)
    first_tile = own_tiles(cph, n_h, WIDE)
    up = lax.rem(h + 1, n_h)
    for q in range(n_h - 1):
        at = (first_tile[q + 1] - first_tile[q]) * LANES

        @pl.when(h == q)
        def _():
            edge_out[...] = shift_in[:, at : at + LANES].astype(BF16)

    edge = remote(edge_out, edge_in, es_.at[0], er_.at[0], (s, up))
    shift_out[...] = jnp.zeros_like(shift_out)
    shift_out[0:rin, 0:oph] = w_out_t[...]
    turned = shift_out[...]
    if oph % LANES:
        turned = pltpu.roll(turned, lax.rem(oph * h, LANES), 1)
    full[h, s, :, wi:] = turned.astype(BF16)
    pl.semaphore_wait(bar, n_h + n_c - 1)


    @pl.when(h < n_h - 1)
    def _():
        edge.start()

    @pl.when(h > 0)
    def _():
        edge.wait_recv()
        full[h, s, :, 0:LANES] += edge_in[...]

    g_high.begin()
    halo = remote(x.at[rows - HALO : rows], xh, xs_.at[0], xr_.at[0], (s, up))

    @pl.when(h < n_h - 1)
    def _():
        halo.start()

    high_plan = g_high.plan(lambda q: columns(q))
    high_plan[0]()

    flat_rows(flat, prm, 0.0)
    unpack_rows(prm, rin, rp, gain, taps, heads, out_gain)
    fill_spread(spread)

    def norm_rows(src, at, dst):
        v = src[at, :].astype(F32)
        n = v * lax.rsqrt(jnp.sum(v * v, axis=1, keepdims=True) * (1.0 / D) + EPS) * gain[...]
        nscr[dst, :] = n.astype(BF16)

    def norm_body(i, _):
        at = pl.multiple_of(i * 16, 16)
        norm_rows(x, pl.ds(at, 16), pl.ds(at + HALO, 16))
        return 0

    lax.fori_loop(0, rows // 16, norm_body, 0, unroll=4)

    @pl.when(h > 0)
    def _():
        halo.wait_recv()

    @pl.when(h == 0)
    def _():
        xh[...] = jnp.zeros_like(xh)

    norm_rows(xh, slice(0, HALO), slice(0, HALO))

    def leave(src, dst, n):
        return pltpu.make_async_copy(src, dst, outs.at[n])

    leaving = [leave(nscr.at[HALO:], nlow_o, 0)]
    leaving[0].start()

    def project(tile, weights):
        w_full[:, pl.ds(pl.multiple_of(tile * LANES, LANES), LANES)] = weights
        v = nn(nscr[...], weights).astype(BF16)
        first, last = INNER // LANES, WIDE // LANES - 1

        @pl.when(tile < first)
        def _():
            gate[:, pl.ds(pl.multiple_of(tile * LANES, LANES), LANES)] = v[HALO:]

        @pl.when(tile == last)
        def _():
            raw[...] = v[HALO:].astype(F32)

        @pl.when(jnp.logical_and(tile >= first, tile < last))
        def _():
            at = pl.ds(pl.multiple_of((tile - first) * LANES, LANES), LANES)
            conv_in[:, at] = v
            cf[...] = v.astype(F32)
            total = jnp.zeros((rows, LANES), F32) + taps[CONV : CONV + 1, at]
            for k in range(CONV):
                start = HALO - CONV + 1 + k
                total = total + taps[k : k + 1, at] * cf[start : start + rows, :]
            sg = sigmoid(total)
            conv_low[:, at] = (total * sg).astype(BF16)
            slope[:, at] = sg * (1.0 + total * (1.0 - sg))

    def tile_of(q, t):
        t0 = (cph * q) // LANES
        at = pl.ds(pl.multiple_of((t - t0) * LANES, LANES), LANES)
        project(t, full[q, :, :, at].reshape(dp, LANES))

    def columns(q):
        hi = jnp.where(q == n_h - 1, WIDE // LANES, (cph * (q + 1)) // LANES)

        def tile_body(t, _):
            tile_of(q, t)
            return 0

        lax.fori_loop((cph * q) // LANES, hi, tile_body, 0)

    for step in high_plan[1:]:
        step()
    g_low.begin()
    g_out.begin()
    for n, (src, dst) in enumerate(((conv_in, conv_in_o), (conv_low, conv_low_o), (slope, slope_o))):
        leaving.append(leave(src, dst, n + 1))
        leaving[-1].start()

    biased = raw[...] + heads[0:1, :]
    soft = jnp.maximum(biased, 0.0) + jnp.log1p(jnp.exp(-jnp.abs(biased)))
    keep = jnp.logical_and(iota((rows, LANES), 0) < left, iota((rows, LANES), 1) < HEADS)
    steps[...] = jnp.where(keep, soft, 0.0)
    rates = -jnp.exp(heads[1:2, :])
    for b in range(blocks):
        at = slice(b * SPAN, (b + 1) * SPAN)
        st = steps[at, :]
        incl, excl, total = head_terms(st, rates)
        incl_r[b] = incl
        excl_r[b] = excl
        incl_t[b] = incl.T
        excl_t[b] = excl.T
        steps_t[b] = st.T
        logs3[b] = jnp.concatenate(split3(jnp.concatenate([incl, excl], axis=0)), axis=1)
        el_eg[b] = stacked(jnp.concatenate([jnp.exp(incl), jnp.exp(total - excl)], axis=0))
        wide = stacked(jnp.concatenate([jnp.exp(total - incl) * st, jnp.exp(excl) * st], axis=0))
        bc = conv_low[at, INNER:].astype(F32)
        bt = bc.T[:STATE].astype(BF16)
        bt2 = jnp.concatenate([bt, bt], axis=1)
        cb = pltpu.roll(bc, STATE, 1)
        c_low = half_masks(cb)[0].astype(BF16)
        inter_s[b] = nt(c_low, bc.astype(BF16)) * (1.0 + (iota((SPAN, SPAN), 0) == iota((SPAN, SPAN), 1)).astype(F32))
        cc = cb[:, :STATE].astype(BF16)
        cc2[b] = jnp.concatenate([cc, cc], axis=1)
        tot = jnp.broadcast_to(jnp.exp(total), (8, LANES))
        for g in range(INNER // 256):
            cols = slice(g * 256, (g + 1) * 256)
            sp = spread[:, cols]
            xs = conv_low[at, cols].astype(F32)
            w = halves_sum(nn(wide, sp))
            for n, dst in ((0, hst), (1, gst)):
                hi, lo = split(w[n * SPAN : (n + 1) * SPAN] * xs)
                dst[b, :, cols] = nn(bt2, jnp.concatenate([hi, lo], axis=0))
            decb[b, :, cols] = expand(tot, sp)
    hv, gv, dv = hst[0], gst[blocks - 1], decb[0]
    for b in range(1, blocks):
        hv = hv * decb[b, 0:1, :] + hst[b]
        dv = dv * decb[b]
    for b in range(blocks - 2, -1, -1):
        gv = gv * decb[b, 0:1, :] + gst[b]
    dev[0] = hv
    dev[1] = gv
    dec[...] = dv
    chain = Chain(n_h, s, h, dev, dec, into, csnd, us, ur, dws, dwr)
    chain.begin()

    row = iota((SPAN, SPAN), 0)
    col = iota((SPAN, SPAN), 1)
    skip8 = jnp.broadcast_to(heads[2:3, :], (8, LANES))

    def pair_body(pair, _):
        cols = pl.ds(pl.multiple_of(pair * LANES, LANES), LANES)
        after = row >= col
        hot = (iota((LANES, 2 * LANES), 0) == 2 * pair + iota((LANES, 2 * LANES), 1) // LANES).astype(BF16)
        hot3 = jnp.concatenate([hot, hot, hot], axis=0)
        skip = expand(skip8, spread[:, cols])[0:1]
        wide_all = nn(logs3[...].reshape(blocks * 2 * SPAN, 3 * LANES), hot3)
        for b in range(blocks):
            at = slice(b * SPAN, (b + 1) * SPAN)
            wide = wide_all[b * 2 * SPAN : (b + 1) * 2 * SPAN]
            inter = inter_s[b]
            xs = conv_low[at, cols]
            mix = []
            for n in range(2):
                hd = 2 * pair + n
                lanes = slice(n * LANES, (n + 1) * LANES)
                gap = jnp.where(
                    after,
                    wide[0:SPAN, lanes] - incl_t[b, pl.ds(hd, 1), :],
                    excl_t[b, pl.ds(hd, 1), :] - wide[SPAN:, lanes],
                )
                mix.append(inter * jnp.exp(gap) * steps_t[b, pl.ds(hd, 1), :])
            x0, x1 = half_masks(xs)
            y = nn_split(jnp.concatenate(mix, axis=1), jnp.concatenate([x0, x1], axis=0))
            yb[at, cols] = y + skip * xs.astype(F32)
        chain.at(pair, 3)
        for n, step in enumerate(behind):
            pl.when(pair == n * pairs_n // len(behind))(step)
        return 0

    low_plan = g_low.plan(None)
    out_plan = g_out.plan(None)
    behind = []
    for n in range(max(len(low_plan), len(out_plan))):
        behind += low_plan[n : n + 1] + out_plan[n : n + 1]
    pairs_n = HEADS // 2
    lax.fori_loop(0, pairs_n, pair_body, 0)

    def gate_tiles(q):
        def tile_body(t, _):
            tile_of(q, t)
            chain.at(pairs_n + t, 3)
            return 0

        lax.fori_loop((cph * q) // LANES, (cph * (q + 1)) // LANES, tile_body, 0)

    for q in range(half_h):
        gate_tiles(q)
    for t in range((cph * half_h) // LANES, max(chain.steps(3) - pairs_n, 0)):
        chain.at(pairs_n + t, 3)
    leaving.append(leave(w_full, w_full_o, 4))
    leaving[-1].start()

    for tile in range(INNER // LANES):
        parts = []
        for q in range(n_h):
            t0, t1 = tiles_of(oph, q)
            if t0 <= tile < t1:
                at = wi + (tile - t0) * LANES
                parts.append(full[q, :, :, at : at + LANES])
        v = parts[0] if len(parts) == 1 else parts[0] + parts[1]
        o_full[:, tile * LANES : (tile + 1) * LANES] = v.reshape(dp, LANES)

    hin[0] = into[0]
    gin[blocks] = into[1]
    for b in range(blocks):
        hin[b + 1] = hin[b] * decb[b, 0:1, :] + hst[b]
    for b in range(blocks - 1, -1, -1):
        gin[b] = gin[b + 1] * decb[b, 0:1, :] + gst[b]
    for src, dst, n in ((hin, hin_o, 5), (gin, gin_o, 6)):
        leaving.append(leave(src, dst, n))
        leaving[-1].start()
    keep_row = (iota((rows, 1), 0) < left).astype(F32)
    bgrad = (cot[...].astype(F32) * keep_row).astype(BF16)
    for g in range(INNER // 256):
        cols = slice(g * 256, (g + 1) * 256)
        sp = spread[:, cols]
        gg_scr[:, cols] = nn(bgrad, o_full[:, cols])
        wide_all = nn(el_eg[...].reshape(blocks * 4 * SPAN, LANES), sp)
        for b in range(blocks):
            at = slice(b * SPAN, (b + 1) * SPAN)
            wide = halves_sum(wide_all[b * 4 * SPAN : (b + 1) * 4 * SPAN])
            el[at, cols] = wide[0:SPAN]
            eg[at, cols] = wide[SPAN:]
            yf = nn(cc2[b], stacked(hin[b, :, cols]))
            yg = nn(cc2[b], stacked(gin[b + 1, :, cols]))
            yb[at, cols] += wide[0:SPAN] * yf + wide[SPAN:] * yg
    dgain[...] = jnp.zeros_like(dgain)

    def gate_body(i, _):
        at = pl.ds(pl.multiple_of(i * 16, 16), 16)
        z = gate[at, :].astype(F32)
        hv = yb[at, :].astype(BF16).astype(F32)
        sg = sigmoid(z)
        sl = z * sg
        gated = hv * sl
        r = lax.rsqrt(jnp.mean(gated * gated, axis=1, keepdims=True) + EPS)
        unit = gated * r
        glow[at, :] = (unit * out_gain[...]).astype(BF16)
        gr = gg_scr[at, :]
        prod = gr * unit
        dgain[...] += prod[0:8] + prod[8:16]
        gg = gr * out_gain[...]
        dg = r * (gg - unit * jnp.mean(gg * unit, axis=1, keepdims=True))
        hgrad[at, :] = (dg * sl).astype(BF16)
        dgate[at, :] = (dg * hv * (sg * (1.0 + z * (1.0 - sg)))).astype(BF16)
        return 0

    lax.fori_loop(0, rows // 16, gate_body, 0, unroll=2)
    for g in range(dp // 256):
        cols = slice(g * 256, (g + 1) * 256)
        branch = nt(glow[...], o_full[cols, :])
        result[:, cols] = (x[:, cols].astype(F32) + keep_row * branch).astype(BF16)

    def state_body(b, _):
        at = pl.ds(pl.multiple_of(b * SPAN, SPAN), SPAN)
        ct = conv_low[at, INNER:].astype(F32).T[STATE:].astype(BF16)
        ct2 = jnp.concatenate([ct, ct], axis=1)
        for g in range(INNER // 256):
            cols = slice(g * 256, (g + 1) * 256)
            dy = hgrad[at, cols].astype(F32)
            for scale, dst in ((el, lst), (eg, mst)):
                hi, lo = split(scale[at, cols] * dy)
                dst[b, :, cols] = nn(ct2, jnp.concatenate([hi, lo], axis=0))
        return 0

    lax.fori_loop(0, blocks, state_body, 0)
    mv, lv = mst[0], lst[blocks - 1]
    for b in range(1, blocks):
        mv = mv * decb[b, 0:1, :] + mst[b]
    for b in range(blocks - 2, -1, -1):
        lv = lv * decb[b, 0:1, :] + lst[b]
    dev2[0] = mv
    dev2[1] = lv
    chain.finish()

    @pl.when(h < n_h - 1)
    def _():
        halo.wait_send()

    g_high.finish()
    g_low.finish()
    g_out.finish()

    @pl.when(h < n_h - 1)
    def _():
        edge.wait_send()

    for c in leaving:
        c.wait()


def fore(n_s, n_h, rp, *args):
    x, _, w_in, w_out_t = args[:4]
    rin, cph = w_in.shape
    oph = w_out_t.shape[1]
    rows, dp = x.shape
    blocks = rows // SPAN
    parts, wi = payload_parts(cph, n_h, WIDE)
    wide_in = max(tile_count(cph, n_h) * LANES, wi)
    wo = tile_count(oph, n_h) * LANES
    dma = pltpu.SemaphoreType.DMA
    vm = pl.BlockSpec(memory_space=pltpu.VMEM)
    sm = pl.BlockSpec(memory_space=pltpu.SMEM)
    hbm = pl.BlockSpec(memory_space=pl.ANY)
    sds = jax.ShapeDtypeStruct
    vf = lambda *shape: pltpu.VMEM(shape, F32)
    vb = lambda *shape: pltpu.VMEM(shape, BF16)
    tables = vf(blocks, SPAN, LANES)
    act = sds((rows, INNER), BF16)
    states = sds((blocks, STATE, INNER), F32)
    entries = sds((blocks + 1, STATE, INNER), F32)
    outs = [
        (sds((rows, dp), BF16), vm),
        (sds((dp, WIDE), BF16), hbm),
        (sds((rows, dp), BF16), hbm),
        (sds((rows + HALO, CONV_CH), BF16), hbm),
        (sds((rows, CONV_CH), BF16), hbm),
        (sds((rows, CONV_CH), F32), hbm),
        (sds((rows, LANES), F32), vm),
        (sds((rows, LANES), F32), vm),
        (sds((blocks, 8, INNER), F32), vm),
        (sds((8, INNER), F32), vm),
        (act, vm),
        (act, vm),
        (act, vm),
        (sds((8, INNER), F32), vm),
        (states, vm),
        (states, vm),
        (sds((2, STATE, INNER), F32), vm),
        (entries, hbm),
        (entries, hbm),
    ]
    return pl.pallas_call(
        functools.partial(fore_kernel, n_s, n_h, cph, oph, rin, rp, wi, wo, wide_in),
        out_shape=tuple(o for o, _ in outs),
        in_specs=[vm, vm, vm, vm, vm, sm],
        out_specs=tuple(p for _, p in outs),
        scratch_shapes=[
            vb(n_h, n_s, rp, wi + wo),
            vb(dp, WIDE),
            vb(dp, INNER),
            vb(HALO, dp),
            vf(rp, wide_in),
            vb(rp, LANES),
            vb(rp, LANES),
            vf(rp, wo),
            vb(rows + HALO, dp),
            vb(rows + HALO, CONV_CH),
            vb(rows, CONV_CH),
            vf(rows, CONV_CH),
            vf(rows + HALO, LANES),
            vb(rows, INNER),
            vf(blocks, STATE, INNER),
            vf(blocks, STATE, INNER),
            vf(2, STATE, INNER),
            vf(2, STATE, INNER),
            vf(2, STATE, INNER),
            tables, tables, tables, tables, tables, tables,
            vf(rows, INNER),
            vf(rows, INNER),
            vf(rows, INNER),
            vf(rows, INNER),
            vf(blocks + 1, STATE, INNER),
            vf(blocks + 1, STATE, INNER),
            vf(FLAT_ROWS, LANES),
            vf(1, dp),
            vf(8, CONV_CH),
            vf(8, LANES),
            vf(1, INNER),
            vb(LANES, INNER),
            vb(blocks, 2 * SPAN, 3 * LANES),
            vb(blocks, 4 * SPAN, LANES),
            vb(blocks, SPAN, LANES),
            dma((1,)),
            dma((1,)),
            dma((1,)),
            dma((1,)),
        ]
        + [dma((CHAIN_PARTS,))] * 4
        + [dma((7,))]
        + gather_sems(n_s, n_h - n_h // 2, len(parts))
        + gather_sems(n_s, n_h // 2, 2)
        + gather_sems(n_s, n_h, 1),
        compiler_params=pltpu.CompilerParams(
            collective_id=1, has_side_effects=True, vmem_limit_bytes=FORE_VMEM
        ),
        name="fore",
    )(*args)


FORE_VMEM = 63 << 20
SMALL = 10696
FLAT_ROWS = 128
TAPS_ROWS = CONV_CH // LANES
HEAD_ROW = D // LANES + (CONV + 1) * TAPS_ROWS


CHUNK = 256
OUT_CHUNK = 384
N_IN = WIDE // CHUNK
N_OUT = INNER // OUT_CHUNK
X_CHUNK = INNER // CHUNK
SLOTS = 4
THIRD = 6
THIRD_LATE = 3
HOP = 2
EARLY = N_OUT + X_CHUNK
LATE = HEADS // 2 + 3


def rear_kernel(
    n_s, n_h, cph, oph, rin, rp, in_slots,
    x, cot, flat, lengths, w_full_i, nlow, dgate_i, glow, conv_low, hgrad, steps, raw, slope_i, conv_in_i,
    hin_i, gin_i, lst_i, mst_i, dev, decb, dec, ogp, w_in, w_out_t, row_in, col_in, row_out, col_out, second_i,
    grad_x, grad_in, row_in_new, col_in_new, w_in_new, grad_out, row_out_new, col_out_new, w_out_new, small, second_new,
    params_new,
    w_full, slope, conv_in, hin, gin, lst, mst, prm, sec_rows, gain, taps, heads, spread,
    adj, csnd, nt_p, bt_p, pg, ng, dpre, halo, dfs, cfs, incl_r, excl_r, incl_t, excl_t, q_t, at_f, at_g, back_f, back_g,
    logs3, steps2, terms2, bb2, cc2, red, cross, dbc, dheads, dtaps, ngain, inter_s,
    sb, r0, vs, pbi, r1i, acci, r2i, pbo, r1o, acco, r2o, win,
    sz, szin, spl, sout, z1, p1, z2, p2, line,
    us, ur, ds, dr, hs, hr, s0s, s0r, s1s, s1r, s2s, s2r, o0s, o0r, o1s, o1r, o2s, o2r,
    load, sos, sor, szs, szr, sps, spr, z1s, z1r, p1s, p1r, z2s, z2r, p2s, p2r,
):
    s = lax.axis_index("seq")
    h = lax.axis_index("head")
    n_c = n_s // 2
    rows = x.shape[0]
    dp = x.shape[1]
    half = n_c * rp
    blocks = rows // SPAN
    chip = s // 2
    core = lax.rem(s, 2)
    sib = chip * 2 + (1 - core)
    up = lax.rem(h + 1, n_h)
    down = lax.rem(h + n_h - 1, n_h)
    zpeer = [lax.rem(h + j, n_h) for j in range(1, n_h)]
    cpeer = [lax.rem(chip + j, n_c) for j in range(1, n_c)]
    speer = [lax.rem(s + j, n_s) for j in range(1, n_s)]
    bar = pltpu.get_barrier_semaphore()
    for z in zpeer:
        pl.semaphore_signal(bar, inc=1, device_id=(s, z), device_id_type=MESH)
    for p in speer:
        pl.semaphore_signal(bar, inc=1, device_id=(p, h), device_id_type=MESH)
    pl.semaphore_wait(bar, n_h + n_s - 2)

    chain = Chain(n_h, s, h, dev, dec, adj, csnd, us, ur, ds, dr)
    chain.begin()
    pairs_of = (
        (dgate_i, pg.at[:, 0:INNER]), (w_full_i, w_full), (slope_i, slope), (hin_i, hin), (gin_i, gin), (lst_i, lst), (mst_i, mst),
        (conv_in_i, conv_in),
    )
    loads = [pltpu.make_async_copy(src, dst, load.at[n]) for n, (src, dst) in enumerate(pairs_of)]
    for c in loads:
        c.start()
    left = lengths[0] - h * rows

    def over_in(i):
        own = pl.ds(0, CHUNK)
        return remote(
            sb.at[lax.rem(i, 2), :, own], r0.at[lax.rem(i, SLOTS), :, own], s0s.at[i], s0r.at[i], (sib, h)
        )

    def over_out(i):
        return remote(sb.at[lax.rem(i, 2)], r0.at[lax.rem(i, SLOTS)], o0s.at[i], o0r.at[i], (sib, h))

    def first_in(i):
        @pl.when(i >= 2)
        def _():
            over_in(i - 2).wait_send()

        @pl.when(i < 2)
        def _():
            over_out(i + N_OUT - 2).wait_send()

        cols = pl.ds(pl.multiple_of(i * CHUNK, CHUNK), CHUNK)
        part = pg[:, cols]
        sb[lax.rem(i, 2), :, 0:CHUNK] = nn(nt_p[1 - core], part)
        over_in(i).start()

    def normed_part(first, size, part, fresh):
        third = dp // 3 // LANES * LANES if dp % (3 * LANES) == 0 else dp // 4
        at = slice(part * third, (part + 1) * third)
        v = nt(pg[:, first : first + size], w_full[at, first : first + size])
        ng[:, at] = v if fresh else ng[:, at] + v

    normed_parts = 3 if dp % (3 * LANES) == 0 else 4

    def second_in(i):
        cols = pl.ds(pl.multiple_of(i * CHUNK, CHUNK), CHUNK)
        mine = nn(nt_p[core], pg[:, cols])
        over_in(i).wait_recv()
        vs[:, :, 0:CHUNK] = (mine + r0[lax.rem(i, SLOTS), :, 0:CHUNK]).reshape(n_c, rp, CHUNK)
        for j, k in enumerate(cpeer):
            pbi[i, j] = vs[k, :, 0:CHUNK].astype(BF16)
            remote(pbi.at[i, j], r1i.at[i, n_c - 2 - j], s1s.at[i, j], s1r.at[i, n_c - 2 - j], (2 * k + core, h)).start()
        acci[i] = vs[chip, :, 0:CHUNK]

    def owners(i, wide, per):
        one = (wide * i) // per
        two = (wide * i + wide - 1) // per
        return one, jnp.minimum(two, n_h - 1)

    def third_in(i):
        total = acci[i]
        for j, k in enumerate(cpeer):
            remote(pbi.at[i, j], r1i.at[i, j], s1s.at[i, j], s1r.at[i, j], (2 * k + core, h)).wait_recv()
            total = total + r1i[i, j].astype(F32)
        acci[i] = total

    def links(i, wide, per, acc, rec, snd, rcv):
        one, two = owners(i, wide, per)
        for n, q, real in ((0, one, None), (1, two, two != one))[: rec.shape[1]]:
            for way, to in ((0, up), (1, down)):
                sends_it = h < q if way == 0 else h > q
                if real is not None:
                    sends_it = jnp.logical_and(real, sends_it)
                begins = h == 0 if way == 0 else h == n_h - 1
                dst = rec.at[i, n, way]
                make = lambda src, n=n, way=way, to=to, dst=dst: remote(
                    src, dst, snd.at[i, n, way], rcv.at[i, n, way], (s, to)
                )
                yield way, sends_it, begins, make, n

    def along(i, way, *stream):
        acc, rec = stream[2], stream[3]
        for w, sends_it, begins, make, n in links(i, *stream):
            if w != way:
                continue

            @pl.when(jnp.logical_and(sends_it, begins))
            def _():
                make(acc.at[i]).start()

            @pl.when(jnp.logical_and(sends_it, jnp.logical_not(begins)))
            def _():
                make(acc.at[i]).wait_recv()
                rec[i, n, way] += acc[i]
                make(rec.at[i, n, way]).start()

    def drain_z(i, *stream):
        for _, sends_it, _, make, n in links(i, *stream):

            @pl.when(sends_it)
            def _():
                make(stream[2].at[i]).wait_send()

    in_stream = (CHUNK, cph, acci, r2i, s2s, s2r)
    out_stream = (OUT_CHUNK, oph, acco, r2o, o2s, o2r)

    def drain_in(i):
        for j, k in enumerate(cpeer):
            remote(pbi.at[i, j], r1i.at[i, n_c - 2 - j], s1s.at[i, j], s1r.at[i, n_c - 2 - j], (2 * k + core, h)).wait_send()
        drain_z(i, *in_stream)

    def first_out(i):
        @pl.when(i >= 2)
        def _():
            over_out(i - 2).wait_send()

        cols = pl.ds(pl.multiple_of(i * OUT_CHUNK, LANES), OUT_CHUNK)
        sb[lax.rem(i, 2)] = nn(bt_p[1 - core], glow[:, cols])
        over_out(i).start()

    def second_out(i):
        cols = pl.ds(pl.multiple_of(i * OUT_CHUNK, LANES), OUT_CHUNK)
        mine = nn(bt_p[core], glow[:, cols])
        over_out(i).wait_recv()
        vs[...] = (mine + r0[lax.rem(i, SLOTS)]).reshape(n_c, rp, OUT_CHUNK)
        for j, k in enumerate(cpeer):
            pbo[i, j] = vs[k].astype(BF16)
            remote(pbo.at[i, j], r1o.at[i, n_c - 2 - j], o1s.at[i, j], o1r.at[i, n_c - 2 - j], (2 * k + core, h)).start()
        acco[i] = vs[chip]

    def third_out(i):
        total = acco[i]
        for j, k in enumerate(cpeer):
            remote(pbo.at[i, j], r1o.at[i, j], o1s.at[i, j], o1r.at[i, j], (2 * k + core, h)).wait_recv()
            total = total + r1o[i, j].astype(F32)
        acco[i] = total

    def drain_out(i):
        for j, k in enumerate(cpeer):
            remote(pbo.at[i, j], r1o.at[i, n_c - 2 - j], o1s.at[i, j], o1r.at[i, n_c - 2 - j], (2 * k + core, h)).wait_send()
        drain_z(i, *out_stream)

    def among(k, first, count):
        return jnp.logical_and(k >= first, k < first + count)

    def early_at(t):
        return among(t, 0, EARLY), t

    def late_at(t):
        spaced = LATE + 2 * (X_CHUNK - 2)
        last = t > spaced
        item = jnp.where(last, EARLY + X_CHUNK - 2 + t - spaced, EARLY + (t - LATE) // 2)
        ok = jnp.logical_or(last, (t - LATE) % 2 == 0)
        return jnp.logical_and(among(t, LATE, spaced + 3 - LATE), ok), item

    def tick(t, phase):
        def stage(at, lag, on_out, on_in):
            ok, item = at(t - lag)
            if on_out is not None:
                pl.when(jnp.logical_and(ok, item < N_OUT))(lambda: on_out(item))
                ok = jnp.logical_and(ok, item >= N_OUT)
            pl.when(ok)(lambda: on_in(item - N_OUT))

        if phase == 0:
            stage(early_at, 1, second_out, second_in)
        if phase < 2:
            stage(early_at, THIRD, third_out if phase == 0 else None, third_in)
        if phase > 0:
            stage(late_at, 1, None, second_in)
            stage(late_at, THIRD_LATE, None, third_in)
        for at, third, last in ((early_at, THIRD, 2), (late_at, THIRD_LATE, 3)):
            if at is late_at and phase == 0:
                continue
            for way, far in ((0, h), (1, n_h - 1 - h)):
                stage(
                    at,
                    third + HOP * far,
                    (lambda i, way=way: along(i, way, *out_stream)) if at is early_at else None,
                    lambda i, way=way: along(i, way, *in_stream),
                )

    last_tick = LATE + 2 * (X_CHUNK - 2) + 2 + THIRD_LATE + HOP * (n_h - 2)

    keep_row = (iota((rows, 1), 0) < left).astype(F32)
    for src, dst in ((nlow[...], nt_p), ((cot[...].astype(F32) * keep_row).astype(BF16), bt_p)):
        turned = src.T
        for q in range(n_s):
            dst[q % 2, (q // 2) * rp : (q // 2 + 1) * rp, :] = turned[q * rp : (q + 1) * rp]
    flat_rows(flat, prm, 0.0)
    flat_rows(second_i, sec_rows, 1.0)
    unpack_rows(prm, rin, rp, gain, taps, heads, None)
    fill_spread(spread)
    dheads[...] = jnp.zeros_like(dheads)
    dtaps[...] = jnp.zeros_like(dtaps)
    rates = -jnp.exp(heads[1:2, :])
    row = iota((SPAN, SPAN), 0)
    col = iota((SPAN, SPAN), 1)
    twice = 1.0 + (row == col).astype(F32)
    for ref in (q_t, at_f, at_g, back_f, back_g, red, cross, dbc):
        ref[...] = jnp.zeros_like(ref)
    for b in range(blocks):
        at = slice(b * SPAN, (b + 1) * SPAN)
        incl, excl, total = head_terms(steps[at, :], rates)
        incl_r[b] = incl
        excl_r[b] = excl
        incl_t[b] = incl.T
        excl_t[b] = excl.T
        logs3[b] = jnp.concatenate(split3(jnp.concatenate([incl, excl], axis=0)), axis=1)
        st = steps[at, :]
        steps2[b] = stacked(st)
        terms2[b] = stacked(
            jnp.concatenate([st, jnp.exp(incl), jnp.exp(total - excl), jnp.exp(total - incl), jnp.exp(excl)], axis=0)
        )
        bc = conv_low[at, INNER:].astype(F32)
        cb = pltpu.roll(bc, STATE, 1)
        inter_s[b] = nt(half_masks(bc)[0].astype(BF16), cb.astype(BF16))
        bb, cc = bc[:, :STATE].astype(BF16), cb[:, :STATE].astype(BF16)
        bb2[b] = jnp.concatenate([bb, bb], axis=1)
        cc2[b] = jnp.concatenate([cc, cc], axis=1)

    def pair_body(pair, _):
        cols = pl.ds(pl.multiple_of(pair * LANES, LANES), LANES)
        sp = spread[:, cols]
        later = col >= row
        hot = (iota((LANES, 2 * LANES), 0) == 2 * pair + iota((LANES, 2 * LANES), 1) // LANES).astype(BF16)
        hot3 = jnp.concatenate([hot, hot, hot], axis=0)
        wide_all = nn(logs3[...].reshape(blocks * 2 * SPAN, 3 * LANES), hot3)
        step_all = nn(steps2[...].reshape(blocks * 2 * SPAN, LANES), sp)
        for b in range(blocks):
            at = slice(b * SPAN, (b + 1) * SPAN)
            both = slice(b * 2 * SPAN, (b + 1) * 2 * SPAN)
            wide = wide_all[both]
            inter = inter_s[b]
            inter2 = inter * twice
            xs = conv_low[at, cols].astype(F32)
            dyl = hgrad[at, cols]
            xh, xl = split(halves_sum(step_all[both]) * xs)
            xhs = half_masks(xh)
            xls = half_masks(xl)
            dy2 = jnp.concatenate([dyl, dyl], axis=1)
            kern = []
            qt = q_t[b]
            for n in range(2):
                hd = 2 * pair + n
                lanes = slice(n * LANES, (n + 1) * LANES)
                gap = jnp.where(
                    later,
                    incl_t[b, pl.ds(hd, 1), :] - wide[0:SPAN, lanes],
                    wide[SPAN:, lanes] - excl_t[b, pl.ds(hd, 1), :],
                )
                decay = jnp.exp(gap)
                kern.append(inter2 * decay)
                weigh = nt(jnp.concatenate([xhs[n], xls[n]], axis=1), dy2) * decay
                qt = qt + weigh
                pairs = weigh * inter
                above = jnp.where(col > row, pairs, 0.0)
                below = jnp.where(col < row, pairs, 0.0)
                at_f[b, pl.ds(hd, 1), :] = jnp.sum(above, axis=0, keepdims=True)
                at_g[b, pl.ds(hd, 1), :] = jnp.sum(below, axis=0, keepdims=True)
                here = iota((SPAN, LANES), 1) == hd
                back_f[b] = jnp.where(here, jnp.sum(above, axis=1, keepdims=True), back_f[b])
                back_g[b] = jnp.where(here, jnp.sum(below, axis=1, keepdims=True), back_g[b])
            q_t[b] = qt
            dys = half_masks(dyl)
            dpre[at, cols] = nn_split(jnp.concatenate(kern, axis=1), jnp.concatenate(dys, axis=0))
        chain.at(pair)

        pl.when(pair < N_OUT)(lambda: first_out(pair))
        pl.when(among(pair, N_OUT, X_CHUNK))(lambda: first_in(pair - N_OUT))
        tick(pair, 0)
        for part in range(normed_parts):
            pl.when(pair == N_OUT + 2 + part)(lambda part=part: normed_part(0, INNER, part, True))
        return 0

    pairs_n = HEADS // 2
    for c in loads[:2]:
        c.wait()
    lax.fori_loop(0, pairs_n, pair_body, 0)
    for k in range(pairs_n, chain.steps()):
        chain.at(k)
    for c in loads[2:]:
        c.wait()

    @pl.when(h == n_h - 1)
    def _():
        halo[...] = jnp.zeros_like(halo)

    def halo_copy(g, size):
        cols = pl.ds(pl.multiple_of(g * CHUNK, CHUNK), size)
        return remote(dpre.at[0:8, cols], halo.at[:, cols], hs.at[g], hr.at[g], (s, down))

    def halo_send(g, size):
        @pl.when(h > 0)
        def _():
            halo_copy(g, size).start()

    def conv_back(g, size):
        cols = pl.ds(pl.multiple_of(g * CHUNK, CHUNK), size)
        own = slice(0, size)
        dp_ = dpre[:, cols]
        dfs[0:rows, own] = dp_
        cfs[:, own] = conv_in[:, cols].astype(F32)
        for k in range(CONV):
            first = HALO - CONV + 1 + k
            dtaps[k : k + 1, cols] = jnp.sum(dp_ * cfs[first : first + rows, own], axis=0, keepdims=True)
        dtaps[CONV : CONV + 1, cols] = jnp.sum(dp_, axis=0, keepdims=True)

        @pl.when(h < n_h - 1)
        def _():
            halo_copy(g, size).wait_recv()

        dfs[rows : rows + 8, own] = halo[:, cols]
        total = jnp.zeros((rows, size), F32)
        for k in range(CONV):
            first = CONV - 1 - k
            total = total + taps[k : k + 1, cols] * dfs[first : first + rows, own]
        pg[:, pl.ds(pl.multiple_of(INNER + g * CHUNK, CHUNK), size)] = total.astype(BF16)

    skip8 = jnp.broadcast_to(heads[2:3, :], (8, LANES))

    def group_compute(g):
        cols = pl.ds(pl.multiple_of(g * CHUNK, CHUNK), CHUNK)
        sp = spread[:, cols]
        skip = expand(skip8, sp)[0:1]
        ms, ls = [adj[0, :, cols]], [adj[1, :, cols]]
        for b in range(blocks - 1):
            ms.append(ms[-1] * decb[b, 0:1, cols] + mst[b, :, cols])
        for b in range(blocks - 1, 0, -1):
            ls.insert(0, ls[0] * decb[b, 0:1, cols] + lst[b, :, cols])
        zero_state = jnp.zeros((STATE, CHUNK), BF16)
        for b in range(blocks):
            at = slice(b * SPAN, (b + 1) * SPAN)
            wide = halves_sum(nn(terms2[b], sp))
            st_e, el, eg, tl, ex = [wide[n * SPAN : (n + 1) * SPAN] for n in range(5)]
            xs = conv_low[at, cols].astype(F32)
            dy = hgrad[at, cols].astype(F32)
            xst = st_e * xs
            parts = [split(v) for v in (hin[b, :, cols], gin[b + 1, :, cols], ls[b], ms[b])]
            into_f = el * nn(cc2[b], jnp.concatenate(parts[0], axis=0))
            into_g = eg * nn(cc2[b], jnp.concatenate(parts[1], axis=0))
            out_f = tl * nn(bb2[b], jnp.concatenate(parts[2], axis=0))
            out_g = ex * nn(bb2[b], jnp.concatenate(parts[3], axis=0))
            dxu = dpre[at, cols] + out_f + out_g
            dpre[at, cols] = (st_e * dxu + skip * dy) * slope[at, cols]
            stack = jnp.concatenate([dy * into_f - xst * out_f, dy * into_g - xst * out_g, xs * dxu, xs * dy], axis=0)
            red[b] += fold(stack, sp)
            pair_f = jnp.sum(ls[b] * hin[b + 1, :, cols], axis=0, keepdims=True)
            pair_g = jnp.sum(ms[b] * gin[b, :, cols], axis=0, keepdims=True)
            cross[b] += fold(jnp.broadcast_to(pair_f + pair_g, (8, CHUNK)), sp)
            acc_bc = dbc[b]
            for scaled, (sh, sl), low in (
                (xst * tl, parts[2], True),
                (xst * ex, parts[3], True),
                (el * dy, parts[0], False),
                (eg * dy, parts[1], False),
            ):
                place = lambda v, low=low: jnp.concatenate([v, zero_state] if low else [zero_state, v], axis=0)
                two = stacked(scaled)
                acc_bc = acc_bc + halves_sum(nt(two, place(sh))) + nt(two[:SPAN], place(sl))
            dbc[b] = acc_bc

    def group_body(g, _):
        group_compute(g)
        halo_send(g, CHUNK)
        tick(pairs_n + 2 * g, 1)

        @pl.when(g >= 1)
        def _():
            conv_back(g - 1, CHUNK)
            first_in(X_CHUNK + g - 1)

        tick(pairs_n + 2 * g + 1, 1)

        @pl.when(g == 4)
        def _():
            for part in range(normed_parts):
                normed_part(INNER, 4 * CHUNK, part, False)

        return 0

    lax.fori_loop(0, X_CHUNK, group_body, 0)

    for b in range(blocks):
        at = slice(b * SPAN, (b + 1) * SPAN)
        bc = conv_low[at, INNER:].astype(F32)
        cb_lo, cb_hi = half_masks(pltpu.roll(bc, STATE, 1))
        qt = q_t[b] * twice
        d = dbc[b] + nn_split(qt, cb_lo.astype(BF16)) + nn_split(qt.T, cb_hi.astype(BF16))
        dpre[at, INNER:] = d * slope[at, INNER:]
    halo_send(X_CHUNK, LANES)
    conv_back(X_CHUNK - 1, CHUNK)
    first_in(2 * X_CHUNK - 1)
    tick(pairs_n + 2 * X_CHUNK, 2)
    for b in range(blocks):
        at = slice(b * SPAN, (b + 1) * SPAN)
        st = steps[at, :]
        rd = red[b]
        v_f = rd[0:SPAN] + at_f[b].T - back_f[b]
        v_g = rd[SPAN : 2 * SPAN] + at_g[b].T - back_g[b]
        da = precise(tri_high(), v_f) + precise(tri_low(), v_g) + cross[b, 0:1]
        dstep = rd[2 * SPAN : 3 * SPAN] + da * rates
        keep = jnp.logical_and(iota((SPAN, LANES), 0) + b * SPAN < left, iota((SPAN, LANES), 1) < HEADS)
        draw = jnp.where(keep, dstep * sigmoid(raw[at, :] + heads[0:1, :]), 0.0)
        pg[at, INNER + CONV_CH :] = draw.astype(BF16)
        dheads[0:1, :] += jnp.sum(draw, axis=0, keepdims=True)
        dheads[1:2, :] += jnp.sum(da * st, axis=0, keepdims=True) * rates
        dheads[2:3, :] += jnp.sum(rd[3 * SPAN :], axis=0, keepdims=True)
    conv_back(X_CHUNK, LANES)
    first_in(N_IN - 1)
    tick(pairs_n + 2 * X_CHUNK + 1, 2)
    for part in range(normed_parts):
        normed_part(INNER + 4 * CHUNK, 3 * CHUNK, part, False)
    tick(pairs_n + 2 * X_CHUNK + 2, 2)

    ngain[...] = jnp.zeros_like(ngain)

    def norm_body(i, _):
        at = pl.ds(pl.multiple_of(i * 16, 16), 16)
        v = x[at, :].astype(F32)
        r = lax.rsqrt(jnp.sum(v * v, axis=1, keepdims=True) * (1.0 / D) + EPS)
        unit = v * r
        g = ng[at, :]
        prod = g * unit
        ngain[...] += prod[0:8] + prod[8:16]
        gg = g * gain[...]
        mean = jnp.sum(gg * unit, axis=1, keepdims=True) * (1.0 / D)
        grad_x[at, :] = cot[at, :].astype(F32) + r * (gg - unit * mean)
        return 0

    lax.fori_loop(0, rows // 16, norm_body, 0, unroll=4)

    sends = []

    def start(buf, me, peers, along_z, snd, rcv):
        for j, p in enumerate(peers):
            c = remote(buf.at[me], buf.at[me], snd.at[j], rcv.at[me], (s, p) if along_z else (p, h))
            c.start()
            sends.append(c)

    def arrive(buf, peers, along_z, snd, rcv):
        for j, p in enumerate(peers):
            remote(buf.at[p], buf.at[p], snd.at[j], rcv.at[p], (s, p) if along_z else (p, h)).wait_recv()
        total = buf[0]
        for i in range(1, buf.shape[0]):
            total = total + buf[i]
        return total

    first = D // LANES
    gsum = ngain[...]
    if dp != D:
        gsum = sum(nn(p, piece_map(dp, rin, rp)) for p in split3(gsum))
    for i in range(first):
        sz[h, i : i + 1, :] = jnp.sum(gsum[:, i * LANES : (i + 1) * LANES], axis=0, keepdims=True)
    for k in range(CONV + 1):
        for i in range(TAPS_ROWS):
            t = first + k * TAPS_ROWS + i
            sz[h, t : t + 1, :] = dtaps[k : k + 1, i * LANES : (i + 1) * LANES]
    lane1 = iota((1, LANES), 1)
    turn = 3 * HEADS
    before = dheads[0:1, :]
    for n in range(1, 3):
        before = jnp.where(lane1 < n * HEADS, before, pltpu.roll(dheads[n : n + 1, :], n * HEADS, 1))
    for i in range(INNER // LANES):
        tile = jnp.sum(ogp[:, i * LANES : (i + 1) * LANES], axis=0, keepdims=True)
        tile = pltpu.roll(tile, turn, 1)
        sz[h, HEAD_ROW + i : HEAD_ROW + i + 1, :] = jnp.where(lane1 < turn, before, tile)
        before = tile
    t = HEAD_ROW + INNER // LANES
    sz[h, t : t + 1, :] = jnp.where(lane1 < turn, before, 0.0)
    sz[h, t + 1 :, :] = jnp.zeros((FLAT_ROWS - t - 1, LANES), F32)

    def tick_body(t, _):
        tick(t, 2)
        return 0

    lax.fori_loop(pairs_n + 2 * X_CHUNK + 3, last_tick + 1, tick_body, 0)
    share = FLAT_ROWS // n_h
    part = pl.ds(pl.multiple_of(share * h, 8), share)

    def share_out(j, q):
        rows_of = pl.ds(pl.multiple_of(share * q, 8), share)
        return remote(sz.at[h, rows_of], szin.at[h], szs.at[j], szr.at[h], (s, q))

    for j, q in enumerate(zpeer):
        share_out(j, q).start()
    szin[h] = sz[h, part]

    def window(slots, dst, wide, per, acc, rec, snd, rcv):
        c0 = (per * h) // wide
        c1 = (per * (h + 1) + wide - 1) // wide
        for c in range(slots):
            index = jnp.minimum(c0 + c, acc.shape[0] - 1)
            at = slice(c * wide, (c + 1) * wide)
            dst[:, at] = acc[index]
            n = jnp.where(owners(index, wide, per)[0] == h, 0, 1) if rec.shape[1] > 1 else 0
            for way, there in ((0, h > 0), (1, h < n_h - 1)):

                @pl.when(jnp.logical_and(c0 + c < c1, there))
                def _():
                    remote(acc.at[index], rec.at[index, n, way], snd.at[0, 0, 0], rcv.at[index, n, way], (s, up)).wait_recv()
                    dst[:, at] += rec[index, n, way]

    wi = in_slots * CHUNK
    window(in_slots, win, *in_stream)
    g_in = pltpu.roll(win[...], lax.rem(wi - lax.rem(cph * h, CHUNK), wi), 1)[0:rin, :cph]
    window(1, win, *out_stream)
    g_out = win[0:rin, 0:OUT_CHUNK]
    if oph != OUT_CHUNK:
        g_out = pltpu.roll(g_out, lax.rem(OUT_CHUNK - lax.rem(oph * h, OUT_CHUNK), OUT_CHUNK), 1)[:, :oph]
    grad_in[...] = g_in
    grad_out[...] = g_out

    decay_keep = 1.0 - DECAY
    sq_in = g_in * g_in
    sq_out = g_out * g_out
    fill = jnp.zeros((LANES - rin, LANES), F32)
    line_in = jnp.concatenate(
        [jnp.broadcast_to(jnp.sum(sq_in, axis=1, keepdims=True), (rin, LANES)), fill], axis=0
    ).T[0:8]
    line_out = jnp.concatenate(
        [jnp.broadcast_to(jnp.sum(sq_out, axis=1, keepdims=True), (rin, LANES)), fill], axis=0
    ).T[0:8]
    z1[h] = jnp.where(iota((8, LANES), 0) == 0, line_in, line_out)
    start(z1, h, zpeer, True, z1s, z1r)
    cs_in = jnp.sum(sq_in, axis=0, keepdims=True)
    rs_out = jnp.sum(sq_out, axis=0, keepdims=True)
    n_ci = -(-cph // LANES)
    n_ro = -(-oph // LANES)
    line[...] = jnp.zeros_like(line)
    line[0:1, 0:cph] = cs_in
    line[0:1, n_ci * LANES : n_ci * LANES + oph] = rs_out
    p1[s] = jnp.zeros_like(p1[0])
    for i in range(n_ci + n_ro):
        p1[s, i : i + 1, :] = line[0:1, i * LANES : (i + 1) * LANES]
    start(p1, s, speer, False, p1s, p1r)
    spl[s] = arrive(szin, zpeer, True, szs, szr)
    start(spl, s, speer, False, sps, spr)
    sums = arrive(z1, zpeer, True, z1s, z1r)
    line_r = DECAY * row_in[...].reshape(1, rin) + decay_keep * (sums[0:1, 0:rin] / PROJ + EPS_SQUARE)
    line_c = DECAY * col_out[...].reshape(1, rin) + decay_keep * (sums[1:2, 0:rin] / INNER + EPS_SQUARE)
    row_in_new[...] = line_r.reshape(rin)
    col_out_new[...] = line_c.reshape(rin)
    fill_line = jnp.zeros((1, LANES - rin), F32)
    up_r = jnp.broadcast_to(jnp.concatenate([line_r, fill_line], axis=1), (LANES, LANES)).T[0:rin, 0:1]
    up_c = jnp.broadcast_to(jnp.concatenate([line_c, fill_line], axis=1), (LANES, LANES)).T[0:rin, 0:1]
    sums = arrive(p1, speer, False, p1s, p1r)
    for i in range(n_ci + n_ro):
        line[0:1, i * LANES : (i + 1) * LANES] = sums[i : i + 1]
    line_ci = DECAY * col_in[...].reshape(1, cph) + decay_keep * (line[0:1, 0:cph] / D + EPS_SQUARE)
    line_ro = DECAY * row_out[...].reshape(1, oph) + decay_keep * (
        line[0:1, n_ci * LANES : n_ci * LANES + oph] / D + EPS_SQUARE
    )
    col_in_new[...] = line_ci.reshape(cph)
    row_out_new[...] = line_ro.reshape(oph)
    u_in = g_in * lax.rsqrt(up_r * line_ci)
    u_out = g_out * lax.rsqrt(up_c * line_ro)
    lane = iota((8, LANES), 1)
    values = (
        jnp.sum(u_in * u_in, keepdims=True),
        jnp.sum(u_out * u_out, keepdims=True),
        jnp.sum(line_ro, axis=1, keepdims=True),
        jnp.sum(line_r, axis=1, keepdims=True) / n_h,
    )
    note = jnp.zeros((8, LANES), F32)
    for n, v in enumerate(values):
        note = jnp.where(lane == n, v, note)
    z2[h] = note
    start(z2, h, zpeer, True, z2s, z2r)

    sout[h] = arrive(spl, speer, False, sps, spr)
    start(sout, h, zpeer, True, sos, sor)
    p2[s] = arrive(z2, zpeer, True, z2s, z2r)
    start(p2, s, speer, False, p2s, p2r)
    mean_out = p2[s, 0:1, 2:3] / INNER
    for j, p in enumerate(zpeer):
        remote(sout.at[p], sout.at[p], sos.at[j], sor.at[p], (s, p)).wait_recv()
    g = jnp.concatenate([sout[q] for q in range(n_h)], axis=0)
    sec = DECAY * sec_rows[...] + decay_keep * (g * g + EPS_SQUARE)
    u = g * lax.rsqrt(sec)
    spread_small = jnp.sqrt(jnp.sum(u * u, keepdims=True) / SMALL)
    par = prm[...] - LEARN_SMALL * u / jnp.maximum(1.0, spread_small / CLIP_RMS)

    whole, rest = SMALL // LANES, SMALL % LANES
    for v, dst in ((g, small), (sec, second_new), (par, params_new)):
        for i in range(whole):
            dst[pl.ds(i * LANES, LANES)] = v[i : i + 1].reshape(LANES)
        dst[pl.ds(whole * LANES, rest)] = v[whole : whole + 1, 0:rest].reshape(rest)

    chain.finish()

    @pl.when(h > 0)
    def _():
        for g in range(X_CHUNK):
            halo_copy(g, CHUNK).wait_send()
        halo_copy(X_CHUNK, LANES).wait_send()

    for i in (N_IN - 2, N_IN - 1):
        over_in(i).wait_send()

    def drain_body(i, _):
        drain_in(i)

        @pl.when(i < N_OUT)
        def _():
            drain_out(i)

        return 0

    lax.fori_loop(0, N_IN, drain_body, 0)
    sums = arrive(p2, speer, False, p2s, p2r)
    mean_in = sums[0:1, 3:4] / D
    clip_in = jnp.maximum(1.0, jnp.sqrt(sums[0:1, 0:1] * mean_in / (D * PROJ)) / CLIP_RMS)
    clip_out = jnp.maximum(1.0, jnp.sqrt(sums[0:1, 1:2] * mean_out / (INNER * D)) / CLIP_RMS)
    w_in_new[...] = w_in[...] - u_in * (LEARN_RATE * jnp.sqrt(mean_in) / clip_in)
    w_out_new[...] = w_out_t[...] - u_out * (LEARN_RATE * jnp.sqrt(mean_out) / clip_out)
    for j, q in enumerate(zpeer):
        share_out(j, q).wait_send()
    for c in sends:
        c.wait_send()


def rear(n_s, n_h, rp, *args):
    x = args[0]
    w_in, w_out_t = args[22], args[23]
    rin, cph = w_in.shape
    oph = w_out_t.shape[1]
    rows, dp = x.shape
    n_c = n_s // 2
    half = n_c * rp
    blocks = rows // SPAN
    in_slots = max(-(-cph * (q + 1) // CHUNK) - cph * q // CHUNK for q in range(n_h))
    out_dup = 1 if oph % OUT_CHUNK == 0 else 2
    n_line = -(-cph // LANES) + -(-oph // LANES)
    n_rows = -(-(n_line + 1) // 8) * 8
    dma = pltpu.SemaphoreType.DMA
    vm = pl.BlockSpec(memory_space=pltpu.VMEM)
    sm = pl.BlockSpec(memory_space=pltpu.SMEM)
    hbm = pl.BlockSpec(memory_space=pl.ANY)
    sds = jax.ShapeDtypeStruct
    vf = lambda *shape: pltpu.VMEM(shape, F32)
    vb = lambda *shape: pltpu.VMEM(shape, BF16)
    tables = vf(blocks, SPAN, LANES)
    specs = [vm] * len(args)
    specs[3] = sm
    for i in (4, 6, 12, 13, 14, 15, 16, 17):
        specs[i] = hbm
    return pl.pallas_call(
        functools.partial(rear_kernel, n_s, n_h, cph, oph, rin, rp, in_slots),
        out_shape=(
            sds((rows, dp), F32),
            sds((rin, cph), F32),
            sds((rin,), F32),
            sds((cph,), F32),
            sds((rin, cph), F32),
            sds((rin, oph), F32),
            sds((oph,), F32),
            sds((rin,), F32),
            sds((rin, oph), F32),
            sds((SMALL,), F32),
            sds((SMALL,), F32),
            sds((SMALL,), F32),
        ),
        in_specs=specs,
        out_specs=(vm,) * 12,
        scratch_shapes=[
            vb(dp, WIDE),
            vf(rows, CONV_CH),
            vb(rows + HALO, CONV_CH),
            vf(blocks + 1, STATE, INNER),
            vf(blocks + 1, STATE, INNER),
            vf(blocks, STATE, INNER),
            vf(blocks, STATE, INNER),
            vf(FLAT_ROWS, LANES),
            vf(FLAT_ROWS, LANES),
            vf(1, dp),
            vf(8, CONV_CH),
            vf(8, LANES),
            vb(LANES, INNER),
            vf(2, STATE, INNER),
            vf(2, STATE, INNER),
            vb(2, half, rows),
            vb(2, half, rows),
            vb(rows, WIDE),
            vf(rows, dp),
            vf(rows, CONV_CH),
            vf(8, CONV_CH),
            vf(rows + 8, CHUNK),
            vf(rows + HALO, CHUNK),
            tables, tables, tables, tables, tables, tables, tables, tables, tables,
            vb(blocks, 2 * SPAN, 3 * LANES),
            vb(blocks, 2 * SPAN, LANES),
            vb(blocks, 10 * SPAN, LANES),
            vb(blocks, SPAN, LANES),
            vb(blocks, SPAN, LANES),
            vf(blocks, 4 * SPAN, LANES),
            vf(blocks, 8, LANES),
            tables,
            vf(8, LANES),
            vf(8, CONV_CH),
            vf(8, dp),
            tables,
            vf(2, half, OUT_CHUNK),
            vf(SLOTS, half, OUT_CHUNK),
            vf(n_c, rp, OUT_CHUNK),
            vb(N_IN, n_c - 1, rp, CHUNK),
            vb(N_IN, n_c - 1, rp, CHUNK),
            vf(N_IN, rp, CHUNK),
            vf(N_IN, 2, 2, rp, CHUNK),
            vb(N_OUT, n_c - 1, rp, OUT_CHUNK),
            vb(N_OUT, n_c - 1, rp, OUT_CHUNK),
            vf(N_OUT, rp, OUT_CHUNK),
            vf(N_OUT, out_dup, 2, rp, OUT_CHUNK),
            vf(rp, in_slots * CHUNK),
            vf(n_h, FLAT_ROWS, LANES),
            vf(n_h, FLAT_ROWS // n_h, LANES),
            vf(n_s, FLAT_ROWS // n_h, LANES),
            vf(n_h, FLAT_ROWS // n_h, LANES),
            vf(n_h, 8, LANES),
            vf(n_s, n_rows, LANES),
            vf(n_h, 8, LANES),
            vf(n_s, 8, LANES),
            vf(8, n_line * LANES),
        ]
        + [dma((CHAIN_PARTS,))] * 4
        + [dma((X_CHUNK + 1,))] * 2
        + [dma((N_IN,)), dma((N_IN,)), dma((N_IN, n_c)), dma((N_IN, n_c)), dma((N_IN, 2, 2)), dma((N_IN, 2, 2))]
        + [dma((N_OUT,)), dma((N_OUT,)), dma((N_OUT, n_c)), dma((N_OUT, n_c)), dma((N_OUT, out_dup, 2)), dma((N_OUT, out_dup, 2))]
        + [dma((8,)), dma((n_h,)), dma((n_h,))]
        + [dma((n_h,)), dma((n_h,)), dma((n_s,)), dma((n_s,))] * 3,
        compiler_params=pltpu.CompilerParams(
            collective_id=2, has_side_effects=True, vmem_limit_bytes=REAR_VMEM
        ),
        name="rear",
    )(*args)


REAR_VMEM = (63 << 20) + (1 << 19)


def results_kernel(*refs):
    count = len(refs) // 2
    for n in range(count):
        refs[count + n][...] = refs[n][...]


def results(*arrays):
    vm = pl.BlockSpec(memory_space=pltpu.VMEM)
    return pl.pallas_call(
        results_kernel,
        out_shape=tuple(jax.ShapeDtypeStruct(a.shape, a.dtype) for a in arrays),
        in_specs=[vm] * len(arrays),
        out_specs=(vm,) * len(arrays),
        compiler_params=pltpu.CompilerParams(vmem_limit_bytes=63 << 20),
        name="results",
    )(*arrays)


def on_device(
    x_in, lengths, cotangent, w_in, w_out, small_params, row_in, col_in, row_out, col_out, small_second
):
    n_s = lax.axis_size("seq")
    n_h = lax.axis_size("head")
    rin = w_in.shape[0]
    rp = -(-rin // 16) * 16
    dp = n_s * rp
    def pad(v, axis, fill=0):
        if rp == rin:
            return v
        shape = v.shape[:axis] + (n_s, rin) + v.shape[axis + 1 :]
        widths = [(0, 0)] * len(shape)
        widths[axis + 1] = (0, rp - rin)
        v = jnp.pad(v.reshape(shape), widths, constant_values=fill)
        return v.reshape(v.shape[:axis] + (dp,) + v.shape[axis + 2 :])

    def cut(v, axis):
        if rp == rin:
            return v
        shape = v.shape[:axis] + (n_s, rp) + v.shape[axis + 1 :]
        v = lax.slice_in_dim(v.reshape(shape), 0, rin, axis=axis + 1)
        return v.reshape(v.shape[:axis] + (D,) + v.shape[axis + 2 :])

    x = pad(x_in, 1)
    cot = pad(cotangent, 1)
    w_out_t = w_out.T
    (
        result, w_full, nlow, conv_in, conv_low, slope, raw, steps, decb, dec, dgate, hgrad, glow, og_part, lst, mst, dev2, hin,
        gin,
    ) = fore(n_s, n_h, rp, x, cot, w_in, w_out_t, small_params, lengths)
    (
        grad_x, grad_in, row_in_new, col_in_new, w_in_new, grad_out, row_out_new, col_out_new, w_out_new, small,
        second_new, params_new,
    ) = rear(
        n_s, n_h, rp,
        x, cot, small_params, lengths, w_full, nlow, dgate, glow, conv_low, hgrad, steps, raw, slope, conv_in, hin, gin, lst, mst,
        dev2, decb, dec, og_part, w_in, w_out_t, row_in, col_in, row_out, col_out, small_second,
    )
    (
        result, grad_x, grad_in, row_in_new, col_in_new, w_in_new, grad_out, row_out_new, col_out_new, w_out_new, small,
        second_new, params_new,
    ) = results(
        result, grad_x, grad_in, row_in_new, col_in_new, w_in_new, grad_out, row_out_new, col_out_new, w_out_new, small,
        second_new, params_new,
    )
    return (
        cut(result, 1), cut(grad_x, 1), grad_in, row_in_new, col_in_new, w_in_new, grad_out.T, row_out_new, col_out_new,
        w_out_new.T, small, second_new, params_new,
    )


def solution(mesh):
    both = P(("seq", "head"), None)
    factors = (P("seq", "head"), P("seq"), P("head"), P("seq", "head"))
    return jax.shard_map(
        on_device,
        mesh=mesh,
        in_specs=(
            both, P("seq"), both, P("seq", "head"), P("head", "seq"), P(), P("seq"), P("head"), P("head"), P("seq"), P(),
        ),
        out_specs=(
            both, both, P("seq", "head"), P("seq"), P("head"), P("seq", "head"), P("head", "seq"), P("head"), P("seq"),
            P("head", "seq"), P(), P(), P(),
        ),
        check_vma=False,
    )
```

```python
import functools

import jax
import jax.numpy as jnp
import numpy as np
from jax import lax
from jax.experimental import pallas as pl
from jax.experimental.pallas import tpu as pltpu
from jax.sharding import PartitionSpec as P

D = 768
HEADS = 24
HEAD_DIM = 64
STATE = 64
CONV = 4
SPAN = 128
STEP = 8
INNER = 1536
CONV_CH = 1664
PROJ = 3224
WIDE = 3328
LANES = 128
HALO = 16

EPS = 1e-05
EPS_SQUARE = 1e-30
LEARN_RATE = 0.3
LEARN_SMALL = 3.0
CLIP_RMS = 0.1
DECAY = 1.0 - STEP ** (-0.8)
F32 = jnp.float32
BF16 = jnp.bfloat16
HIGHEST = lax.Precision.HIGHEST
MESH = pl.DeviceIdType.MESH
VMEM_BYTES = 60 << 20


def nn(left, right):
    return lax.dot_general(left, right, (((1,), (0,)), ((), ())), preferred_element_type=F32)


def nt(left, right):
    return lax.dot_general(left, right, (((1,), (1,)), ((), ())), preferred_element_type=F32)


def split(value):
    high = value.astype(BF16)
    return high, (value - high.astype(F32)).astype(BF16)


def stacked(value):
    return jnp.concatenate(split(value), axis=0)


def halves_sum(value):
    rows = value.shape[0] // 2
    return value[:rows] + value[rows:]


def nn_split(value, exact):
    return halves_sum(nn(stacked(value), exact))


def expand(value, spread):
    return nn_split(value, spread)


def fold(value, spread):
    return halves_sum(nt(stacked(value), spread))


def iota(shape, dim):
    return lax.broadcasted_iota(jnp.int32, shape, dim)


def tri_low():
    return (iota((SPAN, SPAN), 0) >= iota((SPAN, SPAN), 1)).astype(F32)


def tri_high():
    return (iota((SPAN, SPAN), 0) <= iota((SPAN, SPAN), 1)).astype(F32)


def precise(left, right):
    return lax.dot_general(
        left, right, (((1,), (0,)), ((), ())), precision=HIGHEST, preferred_element_type=F32
    )


def sigmoid(value):
    return 1.0 / (1.0 + jnp.exp(-value))


def tiles_of(per_part, index):
    return (per_part * index) // LANES, -(-(per_part * (index + 1)) // LANES)


def tile_count(per_part, parts):
    return max(e - s for s, e in (tiles_of(per_part, i) for i in range(parts)))


def half_masks(value):
    low = iota(value.shape, 1) < HEAD_DIM
    zero = jnp.zeros_like(value)
    return jnp.where(low, value, zero), jnp.where(low, zero, value)


def head_terms(steps, rates):
    logs = steps * rates
    incl = precise(tri_low(), logs)
    return incl, incl - logs, incl[SPAN - 1 : SPAN]


CHAIN_PARTS = 6


class Chain:
    def __init__(self, n_h, s, h, dev, dec, out, snd, us, ur, ds, dr):
        self.n_h, self.s, self.h = n_h, s, h
        self.dev, self.dec, self.out, self.snd = dev, dec, out, snd
        self.sems = ((us, ur), (ds, dr))
        self.next = (lax.rem(h + 1, n_h), lax.rem(h + n_h - 1, n_h))
        self.inner = jnp.logical_and(h > 0, h < n_h - 1)
        self.first = (h == 0, h == n_h - 1)
        self.last = (h == n_h - 1, h == 0)

    def link(self, d, c):
        width = INNER // CHAIN_PARTS
        at = pl.ds(c * width, width)
        snd, rcv = self.sems[d]
        return remote(self.snd.at[d, :, at], self.out.at[d, :, at], snd.at[c], rcv.at[c], (self.s, self.next[d]))

    def begin(self, parts):
        width = INNER // CHAIN_PARTS
        for d in range(2):

            @pl.when(self.first[d])
            def _():
                for c in parts:
                    at = slice(c * width, (c + 1) * width)
                    self.out[d, :, at] = jnp.zeros((STATE, width), F32)
                    self.snd[d, :, at] = self.dev[d, :, at]
                    self.link(d, c).start()

    def step(self, d, c):
        width = INNER // CHAIN_PARTS
        at = slice(c * width, (c + 1) * width)

        @pl.when(jnp.logical_not(self.first[d]))
        def _():
            self.link(d, c).wait_recv()

        @pl.when(self.inner)
        def _():
            self.snd[d, :, at] = self.out[d, :, at] * self.dec[0:1, at] + self.dev[d, :, at]
            self.link(d, c).start()

    def at(self, k, stride=2):
        for c in range(CHAIN_PARTS):

            @pl.when(k == stride * self.h + c)
            def _():
                self.step(0, c)

            @pl.when(k == stride * (self.n_h - 1 - self.h) + c)
            def _():
                self.step(1, c)

    def steps(self, stride=2):
        return stride * (self.n_h - 1) + CHAIN_PARTS

    def finish(self):
        for d in range(2):

            @pl.when(jnp.logical_not(self.last[d]))
            def _():
                for c in range(CHAIN_PARTS):
                    self.link(d, c).wait_send()


def remote(src, dst, send, recv, dev):
    return pltpu.make_async_remote_copy(
        src_ref=src, dst_ref=dst, send_sem=send, recv_sem=recv, device_id=dev, device_id_type=MESH
    )


def split3(value):
    high = value.astype(BF16)
    rest = value - high.astype(F32)
    mid, low = split(rest)
    return high, mid, low


def flat_rows(flat, rows, fill):
    count = SMALL // LANES
    for i in range(count):
        rows[i : i + 1, :] = flat[pl.ds(i * LANES, LANES)].reshape(1, LANES)
    rows[count:, :] = jnp.full((rows.shape[0] - count, LANES), fill, F32)
    rest = SMALL - count * LANES
    rows[count : count + 1, 0:rest] = flat[pl.ds(count * LANES, rest)].reshape(1, rest)


def piece_map(dp, rin, rp):
    place = iota((dp, D), 0)
    return jnp.logical_and(place // rp * rin + place % rp == iota((dp, D), 1), place % rp < rin).astype(BF16)


def unpack_rows(rows, rin, rp, gain, taps, heads, out_gain):
    dp = gain.shape[1]
    first = D // LANES
    flat_gain = jnp.concatenate([rows[i : i + 1, :] for i in range(first)], axis=1)
    if dp == D:
        gain[...] = flat_gain
    else:
        parts = split3(jnp.broadcast_to(flat_gain, (8, D)))
        gain[...] = sum(nt(p, piece_map(dp, rin, rp)) for p in parts)[0:1]
    taps[...] = jnp.zeros_like(taps)
    for k in range(CONV + 1):
        for i in range(TAPS_ROWS):
            r = first + k * TAPS_ROWS + i
            taps[k : k + 1, i * LANES : (i + 1) * LANES] = rows[r : r + 1, :]
    r = HEAD_ROW
    lane = iota((1, LANES), 1)
    line = rows[r : r + 1, :]
    heads[...] = jnp.zeros_like(heads)
    for n in range(3):
        v = line if n == 0 else pltpu.roll(line, LANES - n * HEADS, 1)
        heads[n : n + 1, :] = jnp.where(lane < HEADS, v, 0.0)
    if out_gain is not None:
        turn = LANES - 3 * HEADS
        for i in range(INNER // LANES):
            here = pltpu.roll(rows[r + i : r + i + 1, :], turn, 1)
            after = pltpu.roll(rows[r + i + 1 : r + i + 2, :], turn, 1)
            out_gain[0:1, i * LANES : (i + 1) * LANES] = jnp.where(lane < turn, here, after)


def fill_spread(spread):
    spread[...] = (iota((LANES, INNER), 0) == iota((LANES, INNER), 1) // HEAD_DIM).astype(BF16)


def run_all(*steps):
    def run():
        for step in steps:
            step()

    return run


class Gather:
    def __init__(self, n_s, n_h, s, h, full, base, count, parts, sems, gap=3):
        self.gap = gap
        self.n_s, self.n_h, self.s, self.h, self.full = n_s, n_h, s, h, full
        self.base, self.count, self.parts = base, count, parts
        self.zs, self.zr, self.ps, self.pr, self.ds, self.dr, self.cs, self.cr = sems
        self.n_c = n_s // 2
        self.chip = s // 2
        self.core = lax.rem(s, 2)
        self.sib = self.chip * 2 + (1 - self.core)
        self.cpeer = [lax.rem(self.chip + j, self.n_c) for j in range(1, self.n_c)]
        self.square = self.n_c == 4
        self.xn = self.chip + 1 - 2 * lax.rem(self.chip, 2)
        self.yn = lax.rem(self.chip + self.n_c // 2, self.n_c)
        self.diag = 3 - self.chip
        place = jnp.clip(h - base, 0, count - 1)
        self.order = [base + place] + [base + self.nth(j, place, count) for j in range(1, count)]
        self.items = [(q, p) for q in self.order for p in range(len(parts))]

    def nth(self, j, place, count):
        below = jnp.where(j - 1 >= place, j, j - 1)
        mirror = count - 1 - place
        above = count - 1 - jnp.where(j - 1 >= mirror, j, j - 1)
        return jnp.where(2 * place < count, below, above)

    def when(self, item, work):
        q, p = item
        only = self.parts[p][1]
        if only is None:
            work()
        else:
            pl.when(q == only)(work)

    def blk(self, item, c, part=None, other=False):
        q, p = item
        core = 1 - self.core if other else self.core
        ref = self.full.at[q, c * 2 + core]
        rp = self.full.shape[2]
        lanes = self.parts[p][0]
        if part is None:
            return ref.at[:, lanes]
        mid = rp // 2 // 16 * 16
        return ref.at[pl.ds(0, mid) if part == 0 else pl.ds(mid, rp - mid), lanes]

    def along(self, item, way):
        ref = self.blk(item, self.chip)
        to = lax.rem(self.h + (1 if way == 0 else self.n_h - 1), self.n_h)
        q, p = item
        return remote(ref, ref, self.zs.at[q - self.base, p, way], self.zr.at[q - self.base, p], (self.s, to))

    def begin(self, chosen=None):
        for p in range(len(self.parts)) if chosen is None else chosen:
            item = (self.h, p)
            mine = jnp.logical_and(self.h >= self.base, self.h < self.base + self.count)
            if self.parts[p][1] is not None:
                mine = jnp.logical_and(mine, self.h == self.parts[p][1])
            for way, there in ((0, self.h < self.n_h - 1), (1, self.h > 0)):
                pl.when(jnp.logical_and(mine, there))(lambda item=item, way=way: self.along(item, way).start())

    def z_in(self, i):
        item = self.items[i]
        q = item[0]

        def take():
            self.along(item, 0).wait_recv()
            up = jnp.logical_and(q < self.h, self.h < self.n_h - 1)
            down = jnp.logical_and(q > self.h, self.h > 0)
            pl.when(up)(lambda: self.along(item, 0).start())
            pl.when(down)(lambda: self.along(item, 1).start())

        self.when(item, lambda: pl.when(q != self.h)(take))

    def z_done(self, i):
        item = self.items[i]
        q = item[0]
        up = jnp.logical_and(q <= self.h, self.h < self.n_h - 1)
        down = jnp.logical_and(q >= self.h, self.h > 0)
        self.when(item, lambda: pl.when(up)(lambda: self.along(item, 0).wait_send()))
        self.when(item, lambda: pl.when(down)(lambda: self.along(item, 1).wait_send()))

    def to_chip(self, i, m, part, c):
        item = self.items[i]
        q, p = item
        ref = self.blk(item, self.chip, part)
        n = 0 if part is None else part
        return remote(ref, ref, self.ps.at[q - self.base, p, m, n], self.pr.at[q - self.base, p, self.chip, n], (c * 2 + self.core, self.h))

    def to_chips(self, i):
        if self.square:
            near = ((0, self.xn), (1, self.yn))
            return [self.to_chip(i, m, (n + m) % 2, c) for n in range(2) for m, c in near]
        return [self.to_chip(i, j, None, c) for j, c in enumerate(self.cpeer)]

    def over(self, i, j, c):
        item = self.items[i]
        q, p = item
        ref = self.blk(item, c)
        return remote(ref, ref, self.cs.at[q - self.base, p, j], self.cr.at[q - self.base, p, c], (self.sib, self.h))

    def onward(self, i, n):
        item = self.items[i]
        q, p = item
        c, to = (self.xn, self.yn) if n == 0 else (self.yn, self.xn)
        ref = self.blk(item, c, n)
        return remote(ref, ref, self.ds.at[q - self.base, p, n], self.dr.at[q - self.base, p, n], (to * 2 + self.core, self.h))

    def spread_out(self, i):
        def work():
            for c in self.to_chips(i):
                c.start()
            self.over(i, 0, self.chip).start()

        self.when(self.items[i], work)

    def got(self, i, c, part):
        item = self.items[i]
        q, p = item
        ref = self.blk(item, c, part)
        n = 0 if part is None else part
        remote(ref, ref, self.ps.at[q - self.base, p, 0, 0], self.pr.at[q - self.base, p, c, n], (self.sib, self.h)).wait_recv()

    def pass_on(self, i):
        def work():
            if self.square:
                for n, c in ((0, self.xn), (1, self.yn)):
                    self.got(i, c, n)
                    self.onward(i, n).start()
                for n, c in ((1, self.xn), (0, self.yn)):
                    self.got(i, c, n)
                    self.over(i, 2 - n, c).start()
            else:
                for j, c in enumerate(self.cpeer):
                    self.got(i, c, None)
                    self.over(i, j + 1, c).start()

        self.when(self.items[i], work)

    def last_in(self, i):
        if not self.square:
            return
        item = self.items[i]
        q, p = item

        def work():
            for n in range(2):
                ref = self.blk(item, self.diag, n)
                remote(ref, ref, self.ds.at[q - self.base, p, 0], self.dr.at[q - self.base, p, n], (self.sib, self.h)).wait_recv()
            self.over(i, 3, self.diag).start()

        self.when(item, work)

    def complete(self, i):
        item = self.items[i]
        q, p = item

        def work():
            for c in [self.chip] + self.cpeer:
                ref = self.blk(item, c, other=True)
                remote(ref, ref, self.cs.at[q - self.base, p, 0], self.cr.at[q - self.base, p, c], (self.sib, self.h)).wait_recv()

        self.when(item, work)

    def plan(self, columns):
        count, parts = len(self.items), len(self.parts)
        gap = self.gap
        plan = []
        for i in range(count + 3 * gap):
            if i < count:
                plan.append(run_all(lambda i=i: self.z_in(i), lambda i=i: self.spread_out(i)))
            if gap <= i < count + gap:
                plan.append(lambda i=i: self.pass_on(i - gap))
            if 2 * gap <= i < count + 2 * gap:
                plan.append(lambda i=i: self.last_in(i - 2 * gap))
        for i in range(count):
            plan.append(lambda i=i: self.complete(i))
            if i % parts == parts - 1 and columns is not None:
                plan.append(lambda i=i: columns(self.order[i // parts]))
        return plan

    def finish(self):
        for i in range(len(self.items)):
            self.z_done(i)
            chips = [self.chip] + ([self.xn, self.yn, self.diag] if self.square else self.cpeer)

            def work():
                for c in self.to_chips(i):
                    c.wait_send()
                for j, c in enumerate(chips):
                    self.over(i, j, c).wait_send()
                if self.square:
                    for n in range(2):
                        self.onward(i, n).wait_send()

            self.when(self.items[i], work)


def gather_sems(n_s, count, parts):
    dma = pltpu.SemaphoreType.DMA
    n_c = n_s // 2
    n = 2 if n_c == 4 else 1
    return [
        dma((count, parts, 2)), dma((count, parts)), dma((count, parts, n_c, n)), dma((count, parts, n_c, n)),
        dma((count, parts, 2)), dma((count, parts, 2)), dma((count, parts, n_c)), dma((count, parts, n_c)),
    ]


def own_tiles(per_part, parts, width):
    return [(per_part * q) // LANES for q in range(parts)] + [width // LANES]


def payload_parts(per_part, parts, width):
    first = own_tiles(per_part, parts, width)
    counts = [first[q + 1] - first[q] for q in range(parts)]
    common = max(counts[:-1])
    mid = (common + 1) // 2
    ranges = [(slice(mid * LANES, common * LANES), None), (slice(0, mid * LANES), None)]
    if counts[-1] > common:
        ranges.append((slice(common * LANES, counts[-1] * LANES), parts - 1))
    return ranges, max(counts) * LANES


def fore_kernel(
    n_s, n_h, cph, oph, rin, rp, wi, wo, wide_in,
    x, cot, w_in, w_out_t, flat, lengths,
    result, w_full_o, nlow_o, conv_in_o, conv_low_o, slope_o, raw, steps, decb, dec, dgate, hgrad, glow, dgain, lst, mst,
    dev2, hin_o, gin_o,
    full, w_full, o_full, xh, shift_in, edge_out, edge_in, shift_out, nscr, conv_in, conv_low, slope, cf, gate, hst, gst, dev, into, csnd, incl_r,
    excl_r, incl_t, excl_t, steps_t, inter_s, yb, el, eg, gg_scr, hin, gin, prm, gain, taps, heads, out_gain, spread, logs3, el_eg, cc2, tot2, wfg, bts,
    xs_, xr_, es_, er_, us, ur, dws, dwr, outs, *gsems,
):
    s = lax.axis_index("seq")
    h = lax.axis_index("head")
    n_c = n_s // 2
    rows = x.shape[0]
    dp = x.shape[1]
    blocks = rows // SPAN
    chip = s // 2
    core = lax.rem(s, 2)
    sib = chip * 2 + (1 - core)
    cpeer = [lax.rem(chip + j, n_c) for j in range(1, n_c)]
    left = lengths[0] - h * rows
    parts, _ = payload_parts(cph, n_h, WIDE)
    sems = [gsems[8 * n : 8 * n + 8] for n in range(3)]
    half_h = n_h // 2
    g_high = Gather(n_s, n_h, s, h, full, half_h, n_h - half_h, parts, sems[0])
    g_low = Gather(n_s, n_h, s, h, full, 0, half_h, parts[:2], sems[1])
    g_out = Gather(n_s, n_h, s, h, full, 0, n_h, [(slice(wi, wi + wo), None)], sems[2])
    zpeer = [lax.rem(h + j, n_h) for j in range(1, n_h)]
    bar = pltpu.get_barrier_semaphore()
    for z in zpeer:
        pl.semaphore_signal(bar, inc=1, device_id=(s, z), device_id_type=MESH)
    for c in cpeer:
        pl.semaphore_signal(bar, inc=1, device_id=(c * 2 + core, h), device_id_type=MESH)
    pl.semaphore_signal(bar, inc=1, device_id=(sib, h), device_id_type=MESH)

    shift_in[...] = jnp.zeros_like(shift_in)
    shift_in[0:rin, 0:cph] = w_in[...]
    placed = pltpu.roll(shift_in[...], lax.rem(cph * h, LANES), 1)
    shift_in[...] = placed
    full[h, s, :, 0:wi] = placed[:, 0:wi].astype(BF16)
    first_tile = own_tiles(cph, n_h, WIDE)
    up = lax.rem(h + 1, n_h)
    for q in range(n_h - 1):
        at = (first_tile[q + 1] - first_tile[q]) * LANES

        @pl.when(h == q)
        def _():
            edge_out[...] = shift_in[:, at : at + LANES].astype(BF16)

    edge = remote(edge_out, edge_in, es_.at[0], er_.at[0], (s, up))
    shift_out[...] = jnp.zeros_like(shift_out)
    shift_out[0:rin, 0:oph] = w_out_t[...]
    turned = shift_out[...]
    if oph % LANES:
        turned = pltpu.roll(turned, lax.rem(oph * h, LANES), 1)
    full[h, s, :, wi:] = turned.astype(BF16)
    pl.semaphore_wait(bar, n_h + n_c - 1)


    @pl.when(h < n_h - 1)
    def _():
        edge.start()

    g_high.begin([0])

    @pl.when(h > 0)
    def _():
        edge.wait_recv()
        full[h, s, :, 0:LANES] += edge_in[...]

    g_high.begin(range(1, len(parts)))
    halo = remote(x.at[rows - HALO : rows], xh, xs_.at[0], xr_.at[0], (s, up))

    @pl.when(h < n_h - 1)
    def _():
        halo.start()

    high_plan = g_high.plan(lambda q: columns(q))
    high_plan[0]()

    flat_rows(flat, prm, 0.0)
    unpack_rows(prm, rin, rp, gain, taps, heads, out_gain)
    fill_spread(spread)

    def norm_rows(src, at, dst):
        v = src[at, :].astype(F32)
        n = v * lax.rsqrt(jnp.sum(v * v, axis=1, keepdims=True) * (1.0 / D) + EPS) * gain[...]
        nscr[dst, :] = n.astype(BF16)

    def norm_body(i, _):
        at = pl.multiple_of(i * 16, 16)
        norm_rows(x, pl.ds(at, 16), pl.ds(at + HALO, 16))
        return 0

    lax.fori_loop(0, rows // 16, norm_body, 0, unroll=4)

    @pl.when(h > 0)
    def _():
        halo.wait_recv()

    @pl.when(h == 0)
    def _():
        xh[...] = jnp.zeros_like(xh)

    norm_rows(xh, slice(0, HALO), slice(0, HALO))

    def leave(src, dst, n):
        return pltpu.make_async_copy(src, dst, outs.at[n])

    leaving = [leave(nscr.at[HALO:], nlow_o, 0)]
    leaving[0].start()

    def project(tile, weights):
        w_full[:, pl.ds(pl.multiple_of(tile * LANES, LANES), LANES)] = weights
        v = nn(nscr[...], weights).astype(BF16)
        first, last = INNER // LANES, WIDE // LANES - 1

        @pl.when(tile < first)
        def _():
            gate[:, pl.ds(pl.multiple_of(tile * LANES, LANES), LANES)] = v[HALO:]

        @pl.when(tile == last)
        def _():
            raw[...] = v[HALO:].astype(F32)

        @pl.when(jnp.logical_and(tile >= first, tile < last))
        def _():
            at = pl.ds(pl.multiple_of((tile - first) * LANES, LANES), LANES)
            conv_in[:, at] = v
            cf[...] = v.astype(F32)
            total = jnp.zeros((rows, LANES), F32) + taps[CONV : CONV + 1, at]
            for k in range(CONV):
                start = HALO - CONV + 1 + k
                total = total + taps[k : k + 1, at] * cf[start : start + rows, :]
            sg = sigmoid(total)
            conv_low[:, at] = (total * sg).astype(BF16)
            slope[:, at] = sg * (1.0 + total * (1.0 - sg))

    def tile_of(q, t):
        t0 = (cph * q) // LANES
        at = pl.ds(pl.multiple_of((t - t0) * LANES, LANES), LANES)
        project(t, full[q, :, :, at].reshape(dp, LANES))

    def columns(q):
        hi = jnp.where(q == n_h - 1, WIDE // LANES, (cph * (q + 1)) // LANES)

        def tile_body(t, _):
            tile_of(q, t)
            return 0

        lax.fori_loop((cph * q) // LANES, hi, tile_body, 0)

    for n, step in enumerate(high_plan[1:]):
        step()
        if n == 9:
            g_low.begin()
            g_out.begin()
    for n, (src, dst) in enumerate(((conv_in, conv_in_o), (conv_low, conv_low_o), (slope, slope_o))):
        leaving.append(leave(src, dst, n + 1))
        leaving[-1].start()

    biased = raw[...] + heads[0:1, :]
    soft = jnp.maximum(biased, 0.0) + jnp.log1p(jnp.exp(-jnp.abs(biased)))
    keep = jnp.logical_and(iota((rows, LANES), 0) < left, iota((rows, LANES), 1) < HEADS)
    steps[...] = jnp.where(keep, soft, 0.0)
    rates = -jnp.exp(heads[1:2, :])
    for b in range(blocks):
        at = slice(b * SPAN, (b + 1) * SPAN)
        st = steps[at, :]
        incl, excl, total = head_terms(st, rates)
        incl_r[b] = incl
        excl_r[b] = excl
        incl_t[b] = incl.T
        excl_t[b] = excl.T
        steps_t[b] = st.T
        logs3[b] = jnp.concatenate(split3(jnp.concatenate([incl, excl], axis=0)), axis=1)
        el_eg[b] = stacked(jnp.concatenate([jnp.exp(incl), jnp.exp(total - excl)], axis=0))
        wide = stacked(jnp.concatenate([jnp.exp(total - incl) * st, jnp.exp(excl) * st], axis=0))
        bc = conv_low[at, INNER:].astype(F32)
        bt = bc.T[:STATE].astype(BF16)
        bt2 = jnp.concatenate([bt, bt], axis=1)
        cb = pltpu.roll(bc, STATE, 1)
        c_low = half_masks(cb)[0].astype(BF16)
        inter_s[b] = nt(c_low, bc.astype(BF16)) * (1.0 + (iota((SPAN, SPAN), 0) == iota((SPAN, SPAN), 1)).astype(F32))
        cc = cb[:, :STATE].astype(BF16)
        cc2[b] = jnp.concatenate([cc, cc], axis=1)
        tot2[b] = stacked(jnp.broadcast_to(jnp.exp(total), (8, LANES)))
        wfg[b] = wide
        bts[b] = bt2
    chain = Chain(n_h, s, h, dev, dec, into, csnd, us, ur, dws, dwr)
    for g in range(CHAIN_PARTS):
        cols = slice(g * 256, (g + 1) * 256)
        sp = spread[:, cols]
        weights_all = nn(wfg[...].reshape(blocks * 4 * SPAN, LANES), sp)
        totals = nn(tot2[...].reshape(blocks * 16, LANES), sp)
        for b in range(blocks):
            at = slice(b * SPAN, (b + 1) * SPAN)
            xs = conv_low[at, cols].astype(F32)
            w = halves_sum(weights_all[b * 4 * SPAN : (b + 1) * 4 * SPAN])
            for n, dst in ((0, hst), (1, gst)):
                dst[b, :, cols] = nn(bts[b], stacked(w[n * SPAN : (n + 1) * SPAN] * xs))
            decb[b, :, cols] = halves_sum(totals[b * 16 : (b + 1) * 16])
        hv, gv, dv = hst[0, :, cols], gst[blocks - 1, :, cols], decb[0, :, cols]
        for b in range(1, blocks):
            hv = hv * decb[b, 0:1, cols] + hst[b, :, cols]
            dv = dv * decb[b, :, cols]
        for b in range(blocks - 2, -1, -1):
            gv = gv * decb[b, 0:1, cols] + gst[b, :, cols]
        dev[0, :, cols] = hv
        dev[1, :, cols] = gv
        dec[:, cols] = dv
        chain.begin([g])

    row = iota((SPAN, SPAN), 0)
    col = iota((SPAN, SPAN), 1)
    skip8 = jnp.broadcast_to(heads[2:3, :], (8, LANES))

    def pair_body(pair, _):
        cols = pl.ds(pl.multiple_of(pair * LANES, LANES), LANES)
        after = row >= col
        hot = (iota((LANES, 2 * LANES), 0) == 2 * pair + iota((LANES, 2 * LANES), 1) // LANES).astype(BF16)
        hot3 = jnp.concatenate([hot, hot, hot], axis=0)
        skip = expand(skip8, spread[:, cols])[0:1]
        wide_all = nn(logs3[...].reshape(blocks * 2 * SPAN, 3 * LANES), hot3)
        for b in range(blocks):
            at = slice(b * SPAN, (b + 1) * SPAN)
            wide = wide_all[b * 2 * SPAN : (b + 1) * 2 * SPAN]
            inter = inter_s[b]
            xs = conv_low[at, cols]
            mix = []
            for n in range(2):
                hd = 2 * pair + n
                lanes = slice(n * LANES, (n + 1) * LANES)
                gap = jnp.where(
                    after,
                    wide[0:SPAN, lanes] - incl_t[b, pl.ds(hd, 1), :],
                    excl_t[b, pl.ds(hd, 1), :] - wide[SPAN:, lanes],
                )
                mix.append(inter * jnp.exp(gap) * steps_t[b, pl.ds(hd, 1), :])
            x0, x1 = half_masks(xs)
            y = nn_split(jnp.concatenate(mix, axis=1), jnp.concatenate([x0, x1], axis=0))
            yb[at, cols] = y + skip * xs.astype(F32)
        chain.at(pair, 3)
        for n, step in enumerate(behind):
            pl.when(pair == n * pairs_n // len(behind))(step)
        return 0

    low_plan = g_low.plan(None)
    out_plan = g_out.plan(None)
    pairs_n = HEADS // 2
    gates_n = INNER // LANES
    behind = []
    for n in range(max(len(low_plan), len(out_plan))):
        behind += low_plan[n : n + 1] + out_plan[n : n + 1]
    out_plan = []
    lax.fori_loop(0, pairs_n, pair_body, 0)

    def gate_tiles(q):
        def tile_body(t, _):
            tile_of(q, t)
            chain.at(pairs_n + t, 3)
            for n, step in enumerate(out_plan):
                pl.when(t == n * gates_n // len(out_plan))(step)
            return 0

        lax.fori_loop((cph * q) // LANES, (cph * (q + 1)) // LANES, tile_body, 0)

    for q in range(half_h):
        gate_tiles(q)
    for t in range((cph * half_h) // LANES, max(chain.steps(3) - pairs_n, 0)):
        chain.at(pairs_n + t, 3)
    leaving.append(leave(w_full, w_full_o, 4))
    leaving[-1].start()

    for tile in range(INNER // LANES):
        parts = []
        for q in range(n_h):
            t0, t1 = tiles_of(oph, q)
            if t0 <= tile < t1:
                at = wi + (tile - t0) * LANES
                parts.append(full[q, :, :, at : at + LANES])
        v = parts[0] if len(parts) == 1 else parts[0] + parts[1]
        o_full[:, tile * LANES : (tile + 1) * LANES] = v.reshape(dp, LANES)

    hin[0] = into[0]
    gin[blocks] = into[1]
    for b in range(blocks):
        hin[b + 1] = hin[b] * decb[b, 0:1, :] + hst[b]
    for b in range(blocks - 1, -1, -1):
        gin[b] = gin[b + 1] * decb[b, 0:1, :] + gst[b]
    for src, dst, n in ((hin, hin_o, 5), (gin, gin_o, 6)):
        leaving.append(leave(src, dst, n))
        leaving[-1].start()
    keep_row = (iota((rows, 1), 0) < left).astype(F32)
    bgrad = (cot[...].astype(F32) * keep_row).astype(BF16)
    for g in range(INNER // 256):
        cols = slice(g * 256, (g + 1) * 256)
        sp = spread[:, cols]
        gg_scr[:, cols] = nn(bgrad, o_full[:, cols])
        wide_all = nn(el_eg[...].reshape(blocks * 4 * SPAN, LANES), sp)
        for b in range(blocks):
            at = slice(b * SPAN, (b + 1) * SPAN)
            wide = halves_sum(wide_all[b * 4 * SPAN : (b + 1) * 4 * SPAN])
            el[at, cols] = wide[0:SPAN]
            eg[at, cols] = wide[SPAN:]
            yf = nn(cc2[b], stacked(hin[b, :, cols]))
            yg = nn(cc2[b], stacked(gin[b + 1, :, cols]))
            yb[at, cols] += wide[0:SPAN] * yf + wide[SPAN:] * yg
    dgain[...] = jnp.zeros_like(dgain)

    def gate_body(i, _):
        at = pl.ds(pl.multiple_of(i * 16, 16), 16)
        z = gate[at, :].astype(F32)
        hv = yb[at, :].astype(BF16).astype(F32)
        sg = sigmoid(z)
        sl = z * sg
        gated = hv * sl
        r = lax.rsqrt(jnp.mean(gated * gated, axis=1, keepdims=True) + EPS)
        unit = gated * r
        glow[at, :] = (unit * out_gain[...]).astype(BF16)
        gr = gg_scr[at, :]
        prod = gr * unit
        dgain[...] += prod[0:8] + prod[8:16]
        gg = gr * out_gain[...]
        dg = r * (gg - unit * jnp.mean(gg * unit, axis=1, keepdims=True))
        hgrad[at, :] = (dg * sl).astype(BF16)
        dgate[at, :] = (dg * hv * (sg * (1.0 + z * (1.0 - sg)))).astype(BF16)
        return 0

    lax.fori_loop(0, rows // 16, gate_body, 0, unroll=2)
    for g in range(dp // 256):
        cols = slice(g * 256, (g + 1) * 256)
        branch = nt(glow[...], o_full[cols, :])
        result[:, cols] = (x[:, cols].astype(F32) + keep_row * branch).astype(BF16)

    def state_body(b, _):
        at = pl.ds(pl.multiple_of(b * SPAN, SPAN), SPAN)
        ct = conv_low[at, INNER:].astype(F32).T[STATE:].astype(BF16)
        ct2 = jnp.concatenate([ct, ct], axis=1)
        for g in range(INNER // 256):
            cols = slice(g * 256, (g + 1) * 256)
            dy = hgrad[at, cols].astype(F32)
            for scale, dst in ((el, lst), (eg, mst)):
                hi, lo = split(scale[at, cols] * dy)
                dst[b, :, cols] = nn(ct2, jnp.concatenate([hi, lo], axis=0))
        return 0

    lax.fori_loop(0, blocks, state_body, 0)
    mv, lv = mst[0], lst[blocks - 1]
    for b in range(1, blocks):
        mv = mv * decb[b, 0:1, :] + mst[b]
    for b in range(blocks - 2, -1, -1):
        lv = lv * decb[b, 0:1, :] + lst[b]
    dev2[0] = mv
    dev2[1] = lv
    chain.finish()

    @pl.when(h < n_h - 1)
    def _():
        halo.wait_send()

    g_high.finish()
    g_low.finish()
    g_out.finish()

    @pl.when(h < n_h - 1)
    def _():
        edge.wait_send()

    for c in leaving:
        c.wait()


def fore(n_s, n_h, rp, *args):
    x, _, w_in, w_out_t = args[:4]
    rin, cph = w_in.shape
    oph = w_out_t.shape[1]
    rows, dp = x.shape
    blocks = rows // SPAN
    parts, wi = payload_parts(cph, n_h, WIDE)
    wide_in = max(tile_count(cph, n_h) * LANES, wi)
    wo = tile_count(oph, n_h) * LANES
    dma = pltpu.SemaphoreType.DMA
    vm = pl.BlockSpec(memory_space=pltpu.VMEM)
    sm = pl.BlockSpec(memory_space=pltpu.SMEM)
    hbm = pl.BlockSpec(memory_space=pl.ANY)
    sds = jax.ShapeDtypeStruct
    vf = lambda *shape: pltpu.VMEM(shape, F32)
    vb = lambda *shape: pltpu.VMEM(shape, BF16)
    tables = vf(blocks, SPAN, LANES)
    act = sds((rows, INNER), BF16)
    states = sds((blocks, STATE, INNER), F32)
    entries = sds((blocks + 1, STATE, INNER), F32)
    outs = [
        (sds((rows, dp), BF16), vm),
        (sds((dp, WIDE), BF16), hbm),
        (sds((rows, dp), BF16), hbm),
        (sds((rows + HALO, CONV_CH), BF16), hbm),
        (sds((rows, CONV_CH), BF16), hbm),
        (sds((rows, CONV_CH), F32), hbm),
        (sds((rows, LANES), F32), vm),
        (sds((rows, LANES), F32), vm),
        (sds((blocks, 8, INNER), F32), vm),
        (sds((8, INNER), F32), vm),
        (act, vm),
        (act, vm),
        (act, vm),
        (sds((8, INNER), F32), vm),
        (states, vm),
        (states, vm),
        (sds((2, STATE, INNER), F32), vm),
        (entries, hbm),
        (entries, hbm),
    ]
    return pl.pallas_call(
        functools.partial(fore_kernel, n_s, n_h, cph, oph, rin, rp, wi, wo, wide_in),
        out_shape=tuple(o for o, _ in outs),
        in_specs=[vm, vm, vm, vm, vm, sm],
        out_specs=tuple(p for _, p in outs),
        scratch_shapes=[
            vb(n_h, n_s, rp, wi + wo),
            vb(dp, WIDE),
            vb(dp, INNER),
            vb(HALO, dp),
            vf(rp, wide_in),
            vb(rp, LANES),
            vb(rp, LANES),
            vf(rp, wo),
            vb(rows + HALO, dp),
            vb(rows + HALO, CONV_CH),
            vb(rows, CONV_CH),
            vf(rows, CONV_CH),
            vf(rows + HALO, LANES),
            vb(rows, INNER),
            vf(blocks, STATE, INNER),
            vf(blocks, STATE, INNER),
            vf(2, STATE, INNER),
            vf(2, STATE, INNER),
            vf(2, STATE, INNER),
            tables, tables, tables, tables, tables, tables,
            vf(rows, INNER),
            vf(rows, INNER),
            vf(rows, INNER),
            vf(rows, INNER),
            vf(blocks + 1, STATE, INNER),
            vf(blocks + 1, STATE, INNER),
            vf(FLAT_ROWS, LANES),
            vf(1, dp),
            vf(8, CONV_CH),
            vf(8, LANES),
            vf(1, INNER),
            vb(LANES, INNER),
            vb(blocks, 2 * SPAN, 3 * LANES),
            vb(blocks, 4 * SPAN, LANES),
            vb(blocks, SPAN, LANES),
            vb(blocks, 16, LANES),
            vb(blocks, 4 * SPAN, LANES),
            vb(blocks, STATE, 2 * SPAN),
            dma((1,)),
            dma((1,)),
            dma((1,)),
            dma((1,)),
        ]
        + [dma((CHAIN_PARTS,))] * 4
        + [dma((7,))]
        + gather_sems(n_s, n_h - n_h // 2, len(parts))
        + gather_sems(n_s, n_h // 2, 2)
        + gather_sems(n_s, n_h, 1),
        compiler_params=pltpu.CompilerParams(
            collective_id=1, has_side_effects=True, vmem_limit_bytes=FORE_VMEM
        ),
        name="fore",
    )(*args)


FORE_VMEM = 63 << 20
SMALL = 10696
FLAT_ROWS = 128
TAPS_ROWS = CONV_CH // LANES
HEAD_ROW = D // LANES + (CONV + 1) * TAPS_ROWS


CHUNK = 256
OUT_CHUNK = 384
N_IN = WIDE // CHUNK
N_OUT = INNER // OUT_CHUNK
X_CHUNK = INNER // CHUNK
SLOTS = 4
THIRD = 6
THIRD_LATE = 3
HOP = 2
EARLY = N_OUT + X_CHUNK
LATE = HEADS // 2 + 3


def rear_kernel(
    n_s, n_h, cph, oph, rin, rp, in_slots,
    x, cot, flat, lengths, w_full_i, nlow, dgate_i, glow, conv_low, hgrad, steps, raw, slope_i, conv_in_i,
    hin_i, gin_i, lst_i, mst_i, dev, decb, dec, ogp, w_in, w_out_t, row_in, col_in, row_out, col_out, second_i,
    grad_x, grad_in, row_in_new, col_in_new, w_in_new, grad_out, row_out_new, col_out_new, w_out_new, small, second_new,
    params_new,
    w_full, slope, conv_in, hin, gin, lst, mst, prm, sec_rows, gain, taps, heads, spread,
    adj, csnd, nt_p, bt_p, pg, ng, dpre, halo, dfs, cfs, incl_r, excl_r, incl_t, excl_t, q_t, at_f, at_g, back_f, back_g,
    logs3, steps2, terms2, bb2, cc2, red, cross, dbc, dheads, dtaps, ngain, inter_s,
    sb, r0, vs, pbi, r1i, acci, r2i, pbo, r1o, acco, r2o, win, zb, r2b,
    sz, szin, spl, sout, z1, p1, z2, p2, line,
    us, ur, ds, dr, hs, hr, s0s, s0r, s1s, s1r, s2s, s2r, o0s, o0r, o1s, o1r, o2s, o2r,
    load, zbs, zbr, sos, sor, szs, szr, sps, spr, z1s, z1r, p1s, p1r, z2s, z2r, p2s, p2r,
):
    s = lax.axis_index("seq")
    h = lax.axis_index("head")
    n_c = n_s // 2
    rows = x.shape[0]
    dp = x.shape[1]
    half = n_c * rp
    blocks = rows // SPAN
    chip = s // 2
    core = lax.rem(s, 2)
    sib = chip * 2 + (1 - core)
    up = lax.rem(h + 1, n_h)
    down = lax.rem(h + n_h - 1, n_h)
    zpeer = [lax.rem(h + j, n_h) for j in range(1, n_h)]
    cpeer = [lax.rem(chip + j, n_c) for j in range(1, n_c)]
    speer = [lax.rem(s + j, n_s) for j in range(1, n_s)]
    bar = pltpu.get_barrier_semaphore()
    for z in zpeer:
        pl.semaphore_signal(bar, inc=1, device_id=(s, z), device_id_type=MESH)
    for p in speer:
        pl.semaphore_signal(bar, inc=1, device_id=(p, h), device_id_type=MESH)
    chain = Chain(n_h, s, h, dev, dec, adj, csnd, us, ur, ds, dr)
    pairs_of = (
        (dgate_i, pg.at[:, 0:INNER]), (w_full_i, w_full), (slope_i, slope), (hin_i, hin), (gin_i, gin), (lst_i, lst), (mst_i, mst),
        (conv_in_i, conv_in),
    )
    loads = [pltpu.make_async_copy(src, dst, load.at[n]) for n, (src, dst) in enumerate(pairs_of)]
    for c in loads:
        c.start()
    left = lengths[0] - h * rows
    flat_rows(flat, prm, 0.0)
    flat_rows(second_i, sec_rows, 1.0)
    unpack_rows(prm, rin, rp, gain, taps, heads, None)
    fill_spread(spread)
    pl.semaphore_wait(bar, n_h + n_s - 2)
    chain.begin(range(CHAIN_PARTS))

    def over_in(i):
        own = pl.ds(0, CHUNK)
        return remote(
            sb.at[lax.rem(i, 2), :, own], r0.at[lax.rem(i, SLOTS), :, own], s0s.at[i], s0r.at[i], (sib, h)
        )

    def over_out(i):
        return remote(sb.at[lax.rem(i, 2)], r0.at[lax.rem(i, SLOTS)], o0s.at[i], o0r.at[i], (sib, h))

    def first_in(i):
        @pl.when(i >= 2)
        def _():
            over_in(i - 2).wait_send()

        @pl.when(i < 2)
        def _():
            over_out(i + N_OUT - 2).wait_send()

        cols = pl.ds(pl.multiple_of(i * CHUNK, CHUNK), CHUNK)
        part = pg[:, cols]
        sb[lax.rem(i, 2), :, 0:CHUNK] = nn(nt_p[1 - core], part)
        over_in(i).start()

    def normed_part(first, size, part, fresh):
        third = dp // 3 // LANES * LANES if dp % (3 * LANES) == 0 else dp // 4
        at = slice(part * third, (part + 1) * third)
        v = nt(pg[:, first : first + size], w_full[at, first : first + size])
        ng[:, at] = v if fresh else ng[:, at] + v

    normed_parts = 3 if dp % (3 * LANES) == 0 else 4

    def second_in(i):
        cols = pl.ds(pl.multiple_of(i * CHUNK, CHUNK), CHUNK)
        mine = nn(nt_p[core], pg[:, cols])
        over_in(i).wait_recv()
        vs[:, :, 0:CHUNK] = (mine + r0[lax.rem(i, SLOTS), :, 0:CHUNK]).reshape(n_c, rp, CHUNK)
        for j, k in enumerate(cpeer):
            pbi[i, j] = vs[k, :, 0:CHUNK].astype(BF16)
            remote(pbi.at[i, j], r1i.at[i, n_c - 2 - j], s1s.at[i, j], s1r.at[i, n_c - 2 - j], (2 * k + core, h)).start()
        acci[i] = vs[chip, :, 0:CHUNK]

    def owners(i, wide, per):
        one = (wide * i) // per
        two = (wide * i + wide - 1) // per
        return one, jnp.minimum(two, n_h - 1)

    def third_in(i):
        total = acci[i]
        for j, k in enumerate(cpeer):
            remote(pbi.at[i, j], r1i.at[i, j], s1s.at[i, j], s1r.at[i, j], (2 * k + core, h)).wait_recv()
            total = total + r1i[i, j].astype(F32)
        acci[i] = total

    def links(i, wide, per, acc, rec, snd, rcv):
        one, two = owners(i, wide, per)
        for n, q, real in ((0, one, None), (1, two, two != one))[: rec.shape[1]]:
            for way, to in ((0, up), (1, down)):
                sends_it = h < q if way == 0 else h > q
                if real is not None:
                    sends_it = jnp.logical_and(real, sends_it)
                begins = h == 0 if way == 0 else h == n_h - 1
                dst = rec.at[i, n, way]
                make = lambda src, n=n, way=way, to=to, dst=dst: remote(
                    src, dst, snd.at[i, n, way], rcv.at[i, n, way], (s, to)
                )
                yield way, sends_it, begins, make, n

    def along(i, way, *stream):
        acc, rec = stream[2], stream[3]
        for w, sends_it, begins, make, n in links(i, *stream):
            if w != way:
                continue

            @pl.when(jnp.logical_and(sends_it, begins))
            def _():
                make(acc.at[i]).start()

            @pl.when(jnp.logical_and(sends_it, jnp.logical_not(begins)))
            def _():
                make(acc.at[i]).wait_recv()
                rec[i, n, way] += acc[i]
                make(rec.at[i, n, way]).start()

    def straight(i):
        z = i - X_CHUNK
        zb[z] = acci[i].astype(BF16)
        for n, q, real in straight_to(i):
            pl.when(real)(lambda n=n, q=q: remote(zb.at[z], r2b.at[h, z], zbs.at[z, n], zbr.at[h, z], (s, q)).start())

    def straight_to(i):
        one, two = owners(i, CHUNK, cph)
        return ((0, one, one != h), (1, two, jnp.logical_and(two != one, two != h)))

    def drain_straight(i):
        z = i - X_CHUNK
        for n, q, real in straight_to(i):
            pl.when(real)(lambda n=n, q=q: remote(zb.at[z], r2b.at[h, z], zbs.at[z, n], zbr.at[h, z], (s, q)).wait_send())

    def drain_z(i, *stream):
        for _, sends_it, _, make, n in links(i, *stream):

            @pl.when(sends_it)
            def _():
                make(stream[2].at[i]).wait_send()

    in_stream = (CHUNK, cph, acci, r2i, s2s, s2r)
    out_stream = (OUT_CHUNK, oph, acco, r2o, o2s, o2r)

    def drain_in(i):
        for j, k in enumerate(cpeer):
            remote(pbi.at[i, j], r1i.at[i, n_c - 2 - j], s1s.at[i, j], s1r.at[i, n_c - 2 - j], (2 * k + core, h)).wait_send()
        pl.when(i < X_CHUNK)(lambda: drain_z(i, *in_stream))
        pl.when(i >= X_CHUNK)(lambda: drain_straight(i))

    def first_out(i):
        @pl.when(i >= 2)
        def _():
            over_out(i - 2).wait_send()

        cols = pl.ds(pl.multiple_of(i * OUT_CHUNK, LANES), OUT_CHUNK)
        sb[lax.rem(i, 2)] = nn(bt_p[1 - core], glow[:, cols])
        over_out(i).start()

    def second_out(i):
        cols = pl.ds(pl.multiple_of(i * OUT_CHUNK, LANES), OUT_CHUNK)
        mine = nn(bt_p[core], glow[:, cols])
        over_out(i).wait_recv()
        vs[...] = (mine + r0[lax.rem(i, SLOTS)]).reshape(n_c, rp, OUT_CHUNK)
        for j, k in enumerate(cpeer):
            pbo[i, j] = vs[k].astype(BF16)
            remote(pbo.at[i, j], r1o.at[i, n_c - 2 - j], o1s.at[i, j], o1r.at[i, n_c - 2 - j], (2 * k + core, h)).start()
        acco[i] = vs[chip]

    def third_out(i):
        total = acco[i]
        for j, k in enumerate(cpeer):
            remote(pbo.at[i, j], r1o.at[i, j], o1s.at[i, j], o1r.at[i, j], (2 * k + core, h)).wait_recv()
            total = total + r1o[i, j].astype(F32)
        acco[i] = total

    def drain_out(i):
        for j, k in enumerate(cpeer):
            remote(pbo.at[i, j], r1o.at[i, n_c - 2 - j], o1s.at[i, j], o1r.at[i, n_c - 2 - j], (2 * k + core, h)).wait_send()
        drain_z(i, *out_stream)

    def among(k, first, count):
        return jnp.logical_and(k >= first, k < first + count)

    def early_at(t):
        return among(t, 0, EARLY), t

    def late_at(t):
        spaced = LATE + 2 * (X_CHUNK - 2)
        last = t > spaced
        item = jnp.where(last, EARLY + X_CHUNK - 2 + t - spaced, EARLY + (t - LATE) // 2)
        ok = jnp.logical_or(last, (t - LATE) % 2 == 0)
        return jnp.logical_and(among(t, LATE, spaced + 3 - LATE), ok), item

    def tick(t, phase):
        def stage(at, lag, on_out, on_in):
            ok, item = at(t - lag)
            if on_out is not None:
                pl.when(jnp.logical_and(ok, item < N_OUT))(lambda: on_out(item))
                ok = jnp.logical_and(ok, item >= N_OUT)
            pl.when(ok)(lambda: on_in(item - N_OUT))

        if phase == 0:
            stage(early_at, 1, second_out, second_in)
        if phase < 2:
            stage(early_at, THIRD, third_out if phase == 0 else None, third_in)
        if phase > 0:
            stage(late_at, 1, None, second_in)
            stage(late_at, THIRD_LATE, None, lambda i: (third_in(i), straight(i))[0])
        for way, far in ((0, h), (1, n_h - 1 - h)):
            stage(
                early_at,
                THIRD + HOP * far,
                lambda i, way=way: along(i, way, *out_stream),
                lambda i, way=way: along(i, way, *in_stream),
            )

    last_tick = max(LATE + 2 * (X_CHUNK - 2) + 2 + THIRD_LATE, EARLY - 1 + THIRD + HOP * (n_h - 2))

    keep_row = (iota((rows, 1), 0) < left).astype(F32)
    for src, dst in ((nlow[...], nt_p), ((cot[...].astype(F32) * keep_row).astype(BF16), bt_p)):
        turned = src.T
        for q in range(n_s):
            dst[q % 2, (q // 2) * rp : (q // 2 + 1) * rp, :] = turned[q * rp : (q + 1) * rp]
    dheads[...] = jnp.zeros_like(dheads)
    dtaps[...] = jnp.zeros_like(dtaps)
    rates = -jnp.exp(heads[1:2, :])
    row = iota((SPAN, SPAN), 0)
    col = iota((SPAN, SPAN), 1)
    twice = 1.0 + (row == col).astype(F32)
    for ref in (q_t, at_f, at_g, back_f, back_g, red, cross, dbc):
        ref[...] = jnp.zeros_like(ref)
    for b in range(blocks):
        at = slice(b * SPAN, (b + 1) * SPAN)
        incl, excl, total = head_terms(steps[at, :], rates)
        incl_r[b] = incl
        excl_r[b] = excl
        incl_t[b] = incl.T
        excl_t[b] = excl.T
        logs3[b] = jnp.concatenate(split3(jnp.concatenate([incl, excl], axis=0)), axis=1)
        st = steps[at, :]
        steps2[b] = stacked(st)
        terms2[b] = stacked(
            jnp.concatenate([st, jnp.exp(incl), jnp.exp(total - excl), jnp.exp(total - incl), jnp.exp(excl)], axis=0)
        )
        bc = conv_low[at, INNER:].astype(F32)
        cb = pltpu.roll(bc, STATE, 1)
        inter_s[b] = nt(half_masks(bc)[0].astype(BF16), cb.astype(BF16))
        bb, cc = bc[:, :STATE].astype(BF16), cb[:, :STATE].astype(BF16)
        bb2[b] = jnp.concatenate([bb, bb], axis=1)
        cc2[b] = jnp.concatenate([cc, cc], axis=1)

    def pair_body(pair, _):
        cols = pl.ds(pl.multiple_of(pair * LANES, LANES), LANES)
        sp = spread[:, cols]
        later = col >= row
        hot = (iota((LANES, 2 * LANES), 0) == 2 * pair + iota((LANES, 2 * LANES), 1) // LANES).astype(BF16)
        hot3 = jnp.concatenate([hot, hot, hot], axis=0)
        wide_all = nn(logs3[...].reshape(blocks * 2 * SPAN, 3 * LANES), hot3)
        step_all = nn(steps2[...].reshape(blocks * 2 * SPAN, LANES), sp)
        for b in range(blocks):
            at = slice(b * SPAN, (b + 1) * SPAN)
            both = slice(b * 2 * SPAN, (b + 1) * 2 * SPAN)
            wide = wide_all[both]
            inter = inter_s[b]
            inter2 = inter * twice
            xs = conv_low[at, cols].astype(F32)
            dyl = hgrad[at, cols]
            xh, xl = split(halves_sum(step_all[both]) * xs)
            xhs = half_masks(xh)
            xls = half_masks(xl)
            dy2 = jnp.concatenate([dyl, dyl], axis=1)
            kern = []
            qt = q_t[b]
            for n in range(2):
                hd = 2 * pair + n
                lanes = slice(n * LANES, (n + 1) * LANES)
                gap = jnp.where(
                    later,
                    incl_t[b, pl.ds(hd, 1), :] - wide[0:SPAN, lanes],
                    wide[SPAN:, lanes] - excl_t[b, pl.ds(hd, 1), :],
                )
                decay = jnp.exp(gap)
                kern.append(inter2 * decay)
                weigh = nt(jnp.concatenate([xhs[n], xls[n]], axis=1), dy2) * decay
                qt = qt + weigh
                pairs = weigh * inter
                above = jnp.where(col > row, pairs, 0.0)
                below = jnp.where(col < row, pairs, 0.0)
                at_f[b, pl.ds(hd, 1), :] = jnp.sum(above, axis=0, keepdims=True)
                at_g[b, pl.ds(hd, 1), :] = jnp.sum(below, axis=0, keepdims=True)
                here = iota((SPAN, LANES), 1) == hd
                back_f[b] = jnp.where(here, jnp.sum(above, axis=1, keepdims=True), back_f[b])
                back_g[b] = jnp.where(here, jnp.sum(below, axis=1, keepdims=True), back_g[b])
            q_t[b] = qt
            dys = half_masks(dyl)
            dpre[at, cols] = nn_split(jnp.concatenate(kern, axis=1), jnp.concatenate(dys, axis=0))
        chain.at(pair)

        pl.when(pair < N_OUT)(lambda: first_out(pair))
        pl.when(among(pair, N_OUT, X_CHUNK))(lambda: first_in(pair - N_OUT))
        tick(pair, 0)
        for part in range(normed_parts):
            pl.when(pair == N_OUT + 2 + part)(lambda part=part: normed_part(0, INNER, part, True))
        return 0

    pairs_n = HEADS // 2
    for c in loads[:2]:
        c.wait()
    lax.fori_loop(0, pairs_n, pair_body, 0)
    for k in range(pairs_n, chain.steps()):
        chain.at(k)
    for c in loads[2:]:
        c.wait()

    @pl.when(h == n_h - 1)
    def _():
        halo[...] = jnp.zeros_like(halo)

    def halo_copy(g, size):
        cols = pl.ds(pl.multiple_of(g * CHUNK, CHUNK), size)
        return remote(dpre.at[0:8, cols], halo.at[:, cols], hs.at[g], hr.at[g], (s, down))

    def halo_send(g, size):
        @pl.when(h > 0)
        def _():
            halo_copy(g, size).start()

    def conv_back(g, size):
        cols = pl.ds(pl.multiple_of(g * CHUNK, CHUNK), size)
        own = slice(0, size)
        dp_ = dpre[:, cols]
        dfs[0:rows, own] = dp_
        cfs[:, own] = conv_in[:, cols].astype(F32)
        for k in range(CONV):
            first = HALO - CONV + 1 + k
            dtaps[k : k + 1, cols] = jnp.sum(dp_ * cfs[first : first + rows, own], axis=0, keepdims=True)
        dtaps[CONV : CONV + 1, cols] = jnp.sum(dp_, axis=0, keepdims=True)

        @pl.when(h < n_h - 1)
        def _():
            halo_copy(g, size).wait_recv()

        dfs[rows : rows + 8, own] = halo[:, cols]
        total = jnp.zeros((rows, size), F32)
        for k in range(CONV):
            first = CONV - 1 - k
            total = total + taps[k : k + 1, cols] * dfs[first : first + rows, own]
        pg[:, pl.ds(pl.multiple_of(INNER + g * CHUNK, CHUNK), size)] = total.astype(BF16)

    skip8 = jnp.broadcast_to(heads[2:3, :], (8, LANES))

    def group_compute(g):
        cols = pl.ds(pl.multiple_of(g * CHUNK, CHUNK), CHUNK)
        sp = spread[:, cols]
        skip = expand(skip8, sp)[0:1]
        ms, ls = [adj[0, :, cols]], [adj[1, :, cols]]
        for b in range(blocks - 1):
            ms.append(ms[-1] * decb[b, 0:1, cols] + mst[b, :, cols])
        for b in range(blocks - 1, 0, -1):
            ls.insert(0, ls[0] * decb[b, 0:1, cols] + lst[b, :, cols])
        zero_state = jnp.zeros((STATE, CHUNK), BF16)
        for b in range(blocks):
            at = slice(b * SPAN, (b + 1) * SPAN)
            wide = halves_sum(nn(terms2[b], sp))
            st_e, el, eg, tl, ex = [wide[n * SPAN : (n + 1) * SPAN] for n in range(5)]
            xs = conv_low[at, cols].astype(F32)
            dy = hgrad[at, cols].astype(F32)
            xst = st_e * xs
            parts = [split(v) for v in (hin[b, :, cols], gin[b + 1, :, cols], ls[b], ms[b])]
            into_f = el * nn(cc2[b], jnp.concatenate(parts[0], axis=0))
            into_g = eg * nn(cc2[b], jnp.concatenate(parts[1], axis=0))
            out_f = tl * nn(bb2[b], jnp.concatenate(parts[2], axis=0))
            out_g = ex * nn(bb2[b], jnp.concatenate(parts[3], axis=0))
            dxu = dpre[at, cols] + out_f + out_g
            dpre[at, cols] = (st_e * dxu + skip * dy) * slope[at, cols]
            stack = jnp.concatenate([dy * into_f - xst * out_f, dy * into_g - xst * out_g, xs * dxu, xs * dy], axis=0)
            red[b] += fold(stack, sp)
            pair_f = jnp.sum(ls[b] * hin[b + 1, :, cols], axis=0, keepdims=True)
            pair_g = jnp.sum(ms[b] * gin[b, :, cols], axis=0, keepdims=True)
            cross[b] += fold(jnp.broadcast_to(pair_f + pair_g, (8, CHUNK)), sp)
            acc_bc = dbc[b]
            for scaled, (sh, sl), low in (
                (xst * tl, parts[2], True),
                (xst * ex, parts[3], True),
                (el * dy, parts[0], False),
                (eg * dy, parts[1], False),
            ):
                place = lambda v, low=low: jnp.concatenate([v, zero_state] if low else [zero_state, v], axis=0)
                two = stacked(scaled)
                acc_bc = acc_bc + halves_sum(nt(two, place(sh))) + nt(two[:SPAN], place(sl))
            dbc[b] = acc_bc

    def group_body(g, _):
        group_compute(g)
        halo_send(g, CHUNK)
        tick(pairs_n + 2 * g, 1)

        @pl.when(g >= 1)
        def _():
            conv_back(g - 1, CHUNK)
            first_in(X_CHUNK + g - 1)

        tick(pairs_n + 2 * g + 1, 1)

        @pl.when(g == 4)
        def _():
            for part in range(normed_parts):
                normed_part(INNER, 4 * CHUNK, part, False)

        return 0

    lax.fori_loop(0, X_CHUNK, group_body, 0)

    for b in range(blocks):
        at = slice(b * SPAN, (b + 1) * SPAN)
        bc = conv_low[at, INNER:].astype(F32)
        cb_lo, cb_hi = half_masks(pltpu.roll(bc, STATE, 1))
        qt = q_t[b] * twice
        d = dbc[b] + nn_split(qt, cb_lo.astype(BF16)) + nn_split(qt.T, cb_hi.astype(BF16))
        dpre[at, INNER:] = d * slope[at, INNER:]
    halo_send(X_CHUNK, LANES)
    conv_back(X_CHUNK - 1, CHUNK)
    first_in(2 * X_CHUNK - 1)
    tick(pairs_n + 2 * X_CHUNK, 2)
    for b in range(blocks):
        at = slice(b * SPAN, (b + 1) * SPAN)
        st = steps[at, :]
        rd = red[b]
        v_f = rd[0:SPAN] + at_f[b].T - back_f[b]
        v_g = rd[SPAN : 2 * SPAN] + at_g[b].T - back_g[b]
        da = precise(tri_high(), v_f) + precise(tri_low(), v_g) + cross[b, 0:1]
        dstep = rd[2 * SPAN : 3 * SPAN] + da * rates
        keep = jnp.logical_and(iota((SPAN, LANES), 0) + b * SPAN < left, iota((SPAN, LANES), 1) < HEADS)
        draw = jnp.where(keep, dstep * sigmoid(raw[at, :] + heads[0:1, :]), 0.0)
        pg[at, INNER + CONV_CH :] = draw.astype(BF16)
        dheads[0:1, :] += jnp.sum(draw, axis=0, keepdims=True)
        dheads[1:2, :] += jnp.sum(da * st, axis=0, keepdims=True) * rates
        dheads[2:3, :] += jnp.sum(rd[3 * SPAN :], axis=0, keepdims=True)
    conv_back(X_CHUNK, LANES)
    first_in(N_IN - 1)
    tick(pairs_n + 2 * X_CHUNK + 1, 2)
    for part in range(normed_parts):
        normed_part(INNER + 4 * CHUNK, 3 * CHUNK, part, False)
    tick(pairs_n + 2 * X_CHUNK + 2, 2)

    ngain[...] = jnp.zeros_like(ngain)

    def norm_body(i, _):
        at = pl.ds(pl.multiple_of(i * 16, 16), 16)
        v = x[at, :].astype(F32)
        r = lax.rsqrt(jnp.sum(v * v, axis=1, keepdims=True) * (1.0 / D) + EPS)
        unit = v * r
        g = ng[at, :]
        prod = g * unit
        ngain[...] += prod[0:8] + prod[8:16]
        gg = g * gain[...]
        mean = jnp.sum(gg * unit, axis=1, keepdims=True) * (1.0 / D)
        grad_x[at, :] = cot[at, :].astype(F32) + r * (gg - unit * mean)
        return 0

    lax.fori_loop(0, rows // 16, norm_body, 0, unroll=4)

    sends = []

    def start(buf, me, peers, along_z, snd, rcv):
        for j, p in enumerate(peers):
            c = remote(buf.at[me], buf.at[me], snd.at[j], rcv.at[me], (s, p) if along_z else (p, h))
            c.start()
            sends.append(c)

    def arrive(buf, peers, along_z, snd, rcv):
        for j, p in enumerate(peers):
            remote(buf.at[p], buf.at[p], snd.at[j], rcv.at[p], (s, p) if along_z else (p, h)).wait_recv()
        total = buf[0]
        for i in range(1, buf.shape[0]):
            total = total + buf[i]
        return total

    first = D // LANES
    gsum = ngain[...]
    if dp != D:
        gsum = sum(nn(p, piece_map(dp, rin, rp)) for p in split3(gsum))
    for i in range(first):
        sz[h, i : i + 1, :] = jnp.sum(gsum[:, i * LANES : (i + 1) * LANES], axis=0, keepdims=True)
    for k in range(CONV + 1):
        for i in range(TAPS_ROWS):
            t = first + k * TAPS_ROWS + i
            sz[h, t : t + 1, :] = dtaps[k : k + 1, i * LANES : (i + 1) * LANES]
    lane1 = iota((1, LANES), 1)
    turn = 3 * HEADS
    before = dheads[0:1, :]
    for n in range(1, 3):
        before = jnp.where(lane1 < n * HEADS, before, pltpu.roll(dheads[n : n + 1, :], n * HEADS, 1))
    for i in range(INNER // LANES):
        tile = jnp.sum(ogp[:, i * LANES : (i + 1) * LANES], axis=0, keepdims=True)
        tile = pltpu.roll(tile, turn, 1)
        sz[h, HEAD_ROW + i : HEAD_ROW + i + 1, :] = jnp.where(lane1 < turn, before, tile)
        before = tile
    t = HEAD_ROW + INNER // LANES
    sz[h, t : t + 1, :] = jnp.where(lane1 < turn, before, 0.0)
    sz[h, t + 1 :, :] = jnp.zeros((FLAT_ROWS - t - 1, LANES), F32)

    def tick_body(t, _):
        tick(t, 2)
        return 0

    lax.fori_loop(pairs_n + 2 * X_CHUNK + 3, last_tick + 1, tick_body, 0)
    share = FLAT_ROWS // n_h
    part = pl.ds(pl.multiple_of(share * h, 8), share)

    def share_out(j, q):
        rows_of = pl.ds(pl.multiple_of(share * q, 8), share)
        return remote(sz.at[h, rows_of], szin.at[h], szs.at[j], szr.at[h], (s, q))

    for j, q in enumerate(zpeer):
        share_out(j, q).start()
    szin[h] = sz[h, part]

    def window(slots, dst, wide, per, acc, rec, snd, rcv):
        c0 = (per * h) // wide
        c1 = (per * (h + 1) + wide - 1) // wide
        for c in range(slots):
            index = jnp.minimum(c0 + c, acc.shape[0] - 1)
            at = slice(c * wide, (c + 1) * wide)
            dst[:, at] = acc[index]
            n = jnp.where(owners(index, wide, per)[0] == h, 0, 1) if rec.shape[1] > 1 else 0
            held = jnp.minimum(index, rec.shape[0] - 1)
            for way, there in ((0, h > 0), (1, h < n_h - 1)):

                @pl.when(jnp.logical_and(jnp.logical_and(c0 + c < c1, index < rec.shape[0]), there))
                def _():
                    remote(acc.at[index], rec.at[held, n, way], snd.at[0, 0, 0], rcv.at[held, n, way], (s, up)).wait_recv()
                    dst[:, at] += rec[held, n, way]

            if rec.shape[0] == acc.shape[0]:
                continue
            late = jnp.maximum(index - X_CHUNK, 0)

            @pl.when(jnp.logical_and(c0 + c < c1, index >= X_CHUNK))
            def _():
                for z in zpeer:
                    remote(zb.at[late], r2b.at[z, late], zbs.at[0, 0], zbr.at[z, late], (s, z)).wait_recv()
                    dst[:, at] += r2b[z, late].astype(F32)

    wi = in_slots * CHUNK
    window(in_slots, win, *in_stream)
    g_in = pltpu.roll(win[...], lax.rem(wi - lax.rem(cph * h, CHUNK), wi), 1)[0:rin, :cph]
    window(1, win, *out_stream)
    g_out = win[0:rin, 0:OUT_CHUNK]
    if oph != OUT_CHUNK:
        g_out = pltpu.roll(g_out, lax.rem(OUT_CHUNK - lax.rem(oph * h, OUT_CHUNK), OUT_CHUNK), 1)[:, :oph]
    grad_in[...] = g_in
    grad_out[...] = g_out

    decay_keep = 1.0 - DECAY
    sq_in = g_in * g_in
    sq_out = g_out * g_out
    fill = jnp.zeros((LANES - rin, LANES), F32)
    line_in = jnp.concatenate(
        [jnp.broadcast_to(jnp.sum(sq_in, axis=1, keepdims=True), (rin, LANES)), fill], axis=0
    ).T[0:8]
    line_out = jnp.concatenate(
        [jnp.broadcast_to(jnp.sum(sq_out, axis=1, keepdims=True), (rin, LANES)), fill], axis=0
    ).T[0:8]
    z1[h] = jnp.where(iota((8, LANES), 0) == 0, line_in, line_out)
    start(z1, h, zpeer, True, z1s, z1r)
    cs_in = jnp.sum(sq_in, axis=0, keepdims=True)
    rs_out = jnp.sum(sq_out, axis=0, keepdims=True)
    n_ci = -(-cph // LANES)
    n_ro = -(-oph // LANES)
    line[...] = jnp.zeros_like(line)
    line[0:1, 0:cph] = cs_in
    line[0:1, n_ci * LANES : n_ci * LANES + oph] = rs_out
    p1[s] = jnp.zeros_like(p1[0])
    for i in range(n_ci + n_ro):
        p1[s, i : i + 1, :] = line[0:1, i * LANES : (i + 1) * LANES]
    start(p1, s, speer, False, p1s, p1r)
    spl[s] = arrive(szin, zpeer, True, szs, szr)
    start(spl, s, speer, False, sps, spr)
    sums = arrive(z1, zpeer, True, z1s, z1r)
    line_r = DECAY * row_in[...].reshape(1, rin) + decay_keep * (sums[0:1, 0:rin] / PROJ + EPS_SQUARE)
    line_c = DECAY * col_out[...].reshape(1, rin) + decay_keep * (sums[1:2, 0:rin] / INNER + EPS_SQUARE)
    row_in_new[...] = line_r.reshape(rin)
    col_out_new[...] = line_c.reshape(rin)
    fill_line = jnp.zeros((1, LANES - rin), F32)
    up_r = jnp.broadcast_to(jnp.concatenate([line_r, fill_line], axis=1), (LANES, LANES)).T[0:rin, 0:1]
    up_c = jnp.broadcast_to(jnp.concatenate([line_c, fill_line], axis=1), (LANES, LANES)).T[0:rin, 0:1]
    sums = arrive(p1, speer, False, p1s, p1r)
    for i in range(n_ci + n_ro):
        line[0:1, i * LANES : (i + 1) * LANES] = sums[i : i + 1]
    line_ci = DECAY * col_in[...].reshape(1, cph) + decay_keep * (line[0:1, 0:cph] / D + EPS_SQUARE)
    line_ro = DECAY * row_out[...].reshape(1, oph) + decay_keep * (
        line[0:1, n_ci * LANES : n_ci * LANES + oph] / D + EPS_SQUARE
    )
    col_in_new[...] = line_ci.reshape(cph)
    row_out_new[...] = line_ro.reshape(oph)
    u_in = g_in * lax.rsqrt(up_r * line_ci)
    u_out = g_out * lax.rsqrt(up_c * line_ro)
    lane = iota((8, LANES), 1)
    values = (
        jnp.sum(u_in * u_in, keepdims=True),
        jnp.sum(u_out * u_out, keepdims=True),
        jnp.sum(line_ro, axis=1, keepdims=True),
        jnp.sum(line_r, axis=1, keepdims=True) / n_h,
    )
    note = jnp.zeros((8, LANES), F32)
    for n, v in enumerate(values):
        note = jnp.where(lane == n, v, note)
    z2[h] = note
    start(z2, h, zpeer, True, z2s, z2r)

    sout[h] = arrive(spl, speer, False, sps, spr)
    start(sout, h, zpeer, True, sos, sor)
    p2[s] = arrive(z2, zpeer, True, z2s, z2r)
    start(p2, s, speer, False, p2s, p2r)
    mean_out = p2[s, 0:1, 2:3] / INNER
    for j, p in enumerate(zpeer):
        remote(sout.at[p], sout.at[p], sos.at[j], sor.at[p], (s, p)).wait_recv()
    g = jnp.concatenate([sout[q] for q in range(n_h)], axis=0)
    sec = DECAY * sec_rows[...] + decay_keep * (g * g + EPS_SQUARE)
    u = g * lax.rsqrt(sec)
    spread_small = jnp.sqrt(jnp.sum(u * u, keepdims=True) / SMALL)
    par = prm[...] - LEARN_SMALL * u / jnp.maximum(1.0, spread_small / CLIP_RMS)

    whole, rest = SMALL // LANES, SMALL % LANES
    for v, dst in ((g, small), (sec, second_new), (par, params_new)):
        for i in range(whole):
            dst[pl.ds(i * LANES, LANES)] = v[i : i + 1].reshape(LANES)
        dst[pl.ds(whole * LANES, rest)] = v[whole : whole + 1, 0:rest].reshape(rest)

    chain.finish()

    @pl.when(h > 0)
    def _():
        for g in range(X_CHUNK):
            halo_copy(g, CHUNK).wait_send()
        halo_copy(X_CHUNK, LANES).wait_send()

    for i in (N_IN - 2, N_IN - 1):
        over_in(i).wait_send()

    def drain_body(i, _):
        drain_in(i)

        @pl.when(i < N_OUT)
        def _():
            drain_out(i)

        return 0

    lax.fori_loop(0, N_IN, drain_body, 0)
    sums = arrive(p2, speer, False, p2s, p2r)
    mean_in = sums[0:1, 3:4] / D
    clip_in = jnp.maximum(1.0, jnp.sqrt(sums[0:1, 0:1] * mean_in / (D * PROJ)) / CLIP_RMS)
    clip_out = jnp.maximum(1.0, jnp.sqrt(sums[0:1, 1:2] * mean_out / (INNER * D)) / CLIP_RMS)
    w_in_new[...] = w_in[...] - u_in * (LEARN_RATE * jnp.sqrt(mean_in) / clip_in)
    w_out_new[...] = w_out_t[...] - u_out * (LEARN_RATE * jnp.sqrt(mean_out) / clip_out)
    for j, q in enumerate(zpeer):
        share_out(j, q).wait_send()
    for c in sends:
        c.wait_send()


def rear(n_s, n_h, rp, *args):
    x = args[0]
    w_in, w_out_t = args[22], args[23]
    rin, cph = w_in.shape
    oph = w_out_t.shape[1]
    rows, dp = x.shape
    n_c = n_s // 2
    half = n_c * rp
    blocks = rows // SPAN
    in_slots = max(-(-cph * (q + 1) // CHUNK) - cph * q // CHUNK for q in range(n_h))
    out_dup = 1 if oph % OUT_CHUNK == 0 else 2
    n_line = -(-cph // LANES) + -(-oph // LANES)
    n_rows = -(-(n_line + 1) // 8) * 8
    dma = pltpu.SemaphoreType.DMA
    vm = pl.BlockSpec(memory_space=pltpu.VMEM)
    sm = pl.BlockSpec(memory_space=pltpu.SMEM)
    hbm = pl.BlockSpec(memory_space=pl.ANY)
    sds = jax.ShapeDtypeStruct
    vf = lambda *shape: pltpu.VMEM(shape, F32)
    vb = lambda *shape: pltpu.VMEM(shape, BF16)
    tables = vf(blocks, SPAN, LANES)
    specs = [vm] * len(args)
    specs[3] = sm
    for i in (4, 6, 12, 13, 14, 15, 16, 17):
        specs[i] = hbm
    return pl.pallas_call(
        functools.partial(rear_kernel, n_s, n_h, cph, oph, rin, rp, in_slots),
        out_shape=(
            sds((rows, dp), F32),
            sds((rin, cph), F32),
            sds((rin,), F32),
            sds((cph,), F32),
            sds((rin, cph), F32),
            sds((rin, oph), F32),
            sds((oph,), F32),
            sds((rin,), F32),
            sds((rin, oph), F32),
            sds((SMALL,), F32),
            sds((SMALL,), F32),
            sds((SMALL,), F32),
        ),
        in_specs=specs,
        out_specs=(vm,) * 12,
        scratch_shapes=[
            vb(dp, WIDE),
            vf(rows, CONV_CH),
            vb(rows + HALO, CONV_CH),
            vf(blocks + 1, STATE, INNER),
            vf(blocks + 1, STATE, INNER),
            vf(blocks, STATE, INNER),
            vf(blocks, STATE, INNER),
            vf(FLAT_ROWS, LANES),
            vf(FLAT_ROWS, LANES),
            vf(1, dp),
            vf(8, CONV_CH),
            vf(8, LANES),
            vb(LANES, INNER),
            vf(2, STATE, INNER),
            vf(2, STATE, INNER),
            vb(2, half, rows),
            vb(2, half, rows),
            vb(rows, WIDE),
            vf(rows, dp),
            vf(rows, CONV_CH),
            vf(8, CONV_CH),
            vf(rows + 8, CHUNK),
            vf(rows + HALO, CHUNK),
            tables, tables, tables, tables, tables, tables, tables, tables, tables,
            vb(blocks, 2 * SPAN, 3 * LANES),
            vb(blocks, 2 * SPAN, LANES),
            vb(blocks, 10 * SPAN, LANES),
            vb(blocks, SPAN, LANES),
            vb(blocks, SPAN, LANES),
            vf(blocks, 4 * SPAN, LANES),
            vf(blocks, 8, LANES),
            tables,
            vf(8, LANES),
            vf(8, CONV_CH),
            vf(8, dp),
            tables,
            vf(2, half, OUT_CHUNK),
            vf(SLOTS, half, OUT_CHUNK),
            vf(n_c, rp, OUT_CHUNK),
            vb(N_IN, n_c - 1, rp, CHUNK),
            vb(N_IN, n_c - 1, rp, CHUNK),
            vf(N_IN, rp, CHUNK),
            vf(X_CHUNK, 2, 2, rp, CHUNK),
            vb(N_OUT, n_c - 1, rp, OUT_CHUNK),
            vb(N_OUT, n_c - 1, rp, OUT_CHUNK),
            vf(N_OUT, rp, OUT_CHUNK),
            vf(N_OUT, out_dup, 2, rp, OUT_CHUNK),
            vf(rp, in_slots * CHUNK),
            vb(N_IN - X_CHUNK, rp, CHUNK),
            vb(n_h, N_IN - X_CHUNK, rp, CHUNK),
            vf(n_h, FLAT_ROWS, LANES),
            vf(n_h, FLAT_ROWS // n_h, LANES),
            vf(n_s, FLAT_ROWS // n_h, LANES),
            vf(n_h, FLAT_ROWS // n_h, LANES),
            vf(n_h, 8, LANES),
            vf(n_s, n_rows, LANES),
            vf(n_h, 8, LANES),
            vf(n_s, 8, LANES),
            vf(8, n_line * LANES),
        ]
        + [dma((CHAIN_PARTS,))] * 4
        + [dma((X_CHUNK + 1,))] * 2
        + [dma((N_IN,)), dma((N_IN,)), dma((N_IN, n_c)), dma((N_IN, n_c)), dma((X_CHUNK, 2, 2)), dma((X_CHUNK, 2, 2))]
        + [dma((N_OUT,)), dma((N_OUT,)), dma((N_OUT, n_c)), dma((N_OUT, n_c)), dma((N_OUT, out_dup, 2)), dma((N_OUT, out_dup, 2))]
        + [dma((8,)), dma((N_IN - X_CHUNK, 2)), dma((n_h, N_IN - X_CHUNK)), dma((n_h,)), dma((n_h,))]
        + [dma((n_h,)), dma((n_h,)), dma((n_s,)), dma((n_s,))] * 3,
        compiler_params=pltpu.CompilerParams(
            collective_id=2, has_side_effects=True, vmem_limit_bytes=REAR_VMEM
        ),
        name="rear",
    )(*args)


REAR_VMEM = (63 << 20) + (1 << 19)


def results_kernel(*refs):
    count = len(refs) // 2
    for n in range(count):
        refs[count + n][...] = refs[n][...]


def results(*arrays):
    vm = pl.BlockSpec(memory_space=pltpu.VMEM)
    return pl.pallas_call(
        results_kernel,
        out_shape=tuple(jax.ShapeDtypeStruct(a.shape, a.dtype) for a in arrays),
        in_specs=[vm] * len(arrays),
        out_specs=(vm,) * len(arrays),
        compiler_params=pltpu.CompilerParams(vmem_limit_bytes=63 << 20),
        name="results",
    )(*arrays)


def on_device(
    x_in, lengths, cotangent, w_in, w_out, small_params, row_in, col_in, row_out, col_out, small_second
):
    n_s = lax.axis_size("seq")
    n_h = lax.axis_size("head")
    rin = w_in.shape[0]
    rp = -(-rin // 16) * 16
    dp = n_s * rp
    def pad(v, axis, fill=0):
        if rp == rin:
            return v
        shape = v.shape[:axis] + (n_s, rin) + v.shape[axis + 1 :]
        widths = [(0, 0)] * len(shape)
        widths[axis + 1] = (0, rp - rin)
        v = jnp.pad(v.reshape(shape), widths, constant_values=fill)
        return v.reshape(v.shape[:axis] + (dp,) + v.shape[axis + 2 :])

    def cut(v, axis):
        if rp == rin:
            return v
        shape = v.shape[:axis] + (n_s, rp) + v.shape[axis + 1 :]
        v = lax.slice_in_dim(v.reshape(shape), 0, rin, axis=axis + 1)
        return v.reshape(v.shape[:axis] + (D,) + v.shape[axis + 2 :])

    x = pad(x_in, 1)
    cot = pad(cotangent, 1)
    w_out_t = w_out.T
    (
        result, w_full, nlow, conv_in, conv_low, slope, raw, steps, decb, dec, dgate, hgrad, glow, og_part, lst, mst, dev2, hin,
        gin,
    ) = fore(n_s, n_h, rp, x, cot, w_in, w_out_t, small_params, lengths)
    (
        grad_x, grad_in, row_in_new, col_in_new, w_in_new, grad_out, row_out_new, col_out_new, w_out_new, small,
        second_new, params_new,
    ) = rear(
        n_s, n_h, rp,
        x, cot, small_params, lengths, w_full, nlow, dgate, glow, conv_low, hgrad, steps, raw, slope, conv_in, hin, gin, lst, mst,
        dev2, decb, dec, og_part, w_in, w_out_t, row_in, col_in, row_out, col_out, small_second,
    )
    (
        result, grad_x, grad_in, row_in_new, col_in_new, w_in_new, grad_out, row_out_new, col_out_new, w_out_new, small,
        second_new, params_new,
    ) = results(
        result, grad_x, grad_in, row_in_new, col_in_new, w_in_new, grad_out, row_out_new, col_out_new, w_out_new, small,
        second_new, params_new,
    )
    return (
        cut(result, 1), cut(grad_x, 1), grad_in, row_in_new, col_in_new, w_in_new, grad_out.T, row_out_new, col_out_new,
        w_out_new.T, small, second_new, params_new,
    )


def solution(mesh):
    both = P(("seq", "head"), None)
    factors = (P("seq", "head"), P("seq"), P("head"), P("seq", "head"))
    return jax.shard_map(
        on_device,
        mesh=mesh,
        in_specs=(
            both, P("seq"), both, P("seq", "head"), P("head", "seq"), P(), P("seq"), P("head"), P("head"), P("seq"), P(),
        ),
        out_specs=(
            both, both, P("seq", "head"), P("seq"), P("head"), P("seq", "head"), P("head", "seq"), P("head"), P("seq"),
            P("head", "seq"), P(), P(), P(),
        ),
        check_vma=False,
    )
```

```python
import functools

import jax
import jax.numpy as jnp
import numpy as np
from jax import lax
from jax.experimental import pallas as pl
from jax.experimental.pallas import tpu as pltpu
from jax.sharding import PartitionSpec as P

D = 768
HEADS = 24
HEAD_DIM = 64
STATE = 64
CONV = 4
SPAN = 128
STEP = 8
INNER = 1536
CONV_CH = 1664
PROJ = 3224
WIDE = 3328
LANES = 128
HALO = 16

EPS = 1e-05
EPS_SQUARE = 1e-30
LEARN_RATE = 0.3
LEARN_SMALL = 3.0
CLIP_RMS = 0.1
DECAY = 1.0 - STEP ** (-0.8)
F32 = jnp.float32
BF16 = jnp.bfloat16
HIGHEST = lax.Precision.HIGHEST
MESH = pl.DeviceIdType.MESH
VMEM_BYTES = 60 << 20


def nn(left, right):
    return lax.dot_general(left, right, (((1,), (0,)), ((), ())), preferred_element_type=F32)


def nt(left, right):
    return lax.dot_general(left, right, (((1,), (1,)), ((), ())), preferred_element_type=F32)


def split(value):
    high = value.astype(BF16)
    return high, (value - high.astype(F32)).astype(BF16)


def stacked(value):
    return jnp.concatenate(split(value), axis=0)


def halves_sum(value):
    rows = value.shape[0] // 2
    return value[:rows] + value[rows:]


def nn_split(value, exact):
    return halves_sum(nn(stacked(value), exact))


def expand(value, spread):
    return nn_split(value, spread)


def fold(value, spread):
    return halves_sum(nt(stacked(value), spread))


def iota(shape, dim):
    return lax.broadcasted_iota(jnp.int32, shape, dim)


def tri_low():
    return (iota((SPAN, SPAN), 0) >= iota((SPAN, SPAN), 1)).astype(F32)


def tri_high():
    return (iota((SPAN, SPAN), 0) <= iota((SPAN, SPAN), 1)).astype(F32)


def precise(left, right):
    return lax.dot_general(
        left, right, (((1,), (0,)), ((), ())), precision=HIGHEST, preferred_element_type=F32
    )


def sigmoid(value):
    return 1.0 / (1.0 + jnp.exp(-value))


def tiles_of(per_part, index):
    return (per_part * index) // LANES, -(-(per_part * (index + 1)) // LANES)


def tile_count(per_part, parts):
    return max(e - s for s, e in (tiles_of(per_part, i) for i in range(parts)))


def half_masks(value):
    low = iota(value.shape, 1) < HEAD_DIM
    zero = jnp.zeros_like(value)
    return jnp.where(low, value, zero), jnp.where(low, zero, value)


def head_terms(steps, rates):
    logs = steps * rates
    incl = precise(tri_low(), logs)
    return incl, incl - logs, incl[SPAN - 1 : SPAN]


CHAIN_PARTS = 6


class Chain:
    def __init__(self, n_h, s, h, dev, dec, out, snd, us, ur, ds, dr):
        self.n_h, self.s, self.h = n_h, s, h
        self.dev, self.dec, self.out, self.snd = dev, dec, out, snd
        self.sems = ((us, ur), (ds, dr))
        self.next = (lax.rem(h + 1, n_h), lax.rem(h + n_h - 1, n_h))
        self.inner = jnp.logical_and(h > 0, h < n_h - 1)
        self.first = (h == 0, h == n_h - 1)
        self.last = (h == n_h - 1, h == 0)

    def link(self, d, c):
        width = INNER // CHAIN_PARTS
        at = pl.ds(c * width, width)
        snd, rcv = self.sems[d]
        return remote(self.snd.at[d, :, at], self.out.at[d, :, at], snd.at[c], rcv.at[c], (self.s, self.next[d]))

    def begin(self, parts):
        width = INNER // CHAIN_PARTS
        for d in range(2):

            @pl.when(self.first[d])
            def _():
                for c in parts:
                    at = slice(c * width, (c + 1) * width)
                    self.out[d, :, at] = jnp.zeros((STATE, width), F32)
                    self.snd[d, :, at] = self.dev[d, :, at]
                    self.link(d, c).start()

    def step(self, d, c):
        width = INNER // CHAIN_PARTS
        at = slice(c * width, (c + 1) * width)

        @pl.when(jnp.logical_not(self.first[d]))
        def _():
            self.link(d, c).wait_recv()

        @pl.when(self.inner)
        def _():
            self.snd[d, :, at] = self.out[d, :, at] * self.dec[0:1, at] + self.dev[d, :, at]
            self.link(d, c).start()

    def at(self, k, stride=2):
        for c in range(CHAIN_PARTS):

            @pl.when(k == stride * self.h + c)
            def _():
                self.step(0, c)

            @pl.when(k == stride * (self.n_h - 1 - self.h) + c)
            def _():
                self.step(1, c)

    def steps(self, stride=2):
        return stride * (self.n_h - 1) + CHAIN_PARTS

    def finish(self):
        for d in range(2):

            @pl.when(jnp.logical_not(self.last[d]))
            def _():
                for c in range(CHAIN_PARTS):
                    self.link(d, c).wait_send()


def remote(src, dst, send, recv, dev):
    return pltpu.make_async_remote_copy(
        src_ref=src, dst_ref=dst, send_sem=send, recv_sem=recv, device_id=dev, device_id_type=MESH
    )


def split3(value):
    high = value.astype(BF16)
    rest = value - high.astype(F32)
    mid, low = split(rest)
    return high, mid, low


def flat_rows(flat, rows, fill):
    count = SMALL // LANES
    for i in range(count):
        rows[i : i + 1, :] = flat[pl.ds(i * LANES, LANES)].reshape(1, LANES)
    rows[count:, :] = jnp.full((rows.shape[0] - count, LANES), fill, F32)
    rest = SMALL - count * LANES
    rows[count : count + 1, 0:rest] = flat[pl.ds(count * LANES, rest)].reshape(1, rest)


def piece_map(dp, rin, rp):
    place = iota((dp, D), 0)
    return jnp.logical_and(place // rp * rin + place % rp == iota((dp, D), 1), place % rp < rin).astype(BF16)


def unpack_rows(rows, rin, rp, gain, taps, heads, out_gain):
    dp = gain.shape[1]
    first = D // LANES
    flat_gain = jnp.concatenate([rows[i : i + 1, :] for i in range(first)], axis=1)
    if dp == D:
        gain[...] = flat_gain
    else:
        parts = split3(jnp.broadcast_to(flat_gain, (8, D)))
        gain[...] = sum(nt(p, piece_map(dp, rin, rp)) for p in parts)[0:1]
    taps[...] = jnp.zeros_like(taps)
    for k in range(CONV + 1):
        for i in range(TAPS_ROWS):
            r = first + k * TAPS_ROWS + i
            taps[k : k + 1, i * LANES : (i + 1) * LANES] = rows[r : r + 1, :]
    r = HEAD_ROW
    lane = iota((1, LANES), 1)
    line = rows[r : r + 1, :]
    heads[...] = jnp.zeros_like(heads)
    for n in range(3):
        v = line if n == 0 else pltpu.roll(line, LANES - n * HEADS, 1)
        heads[n : n + 1, :] = jnp.where(lane < HEADS, v, 0.0)
    if out_gain is not None:
        turn = LANES - 3 * HEADS
        for i in range(INNER // LANES):
            here = pltpu.roll(rows[r + i : r + i + 1, :], turn, 1)
            after = pltpu.roll(rows[r + i + 1 : r + i + 2, :], turn, 1)
            out_gain[0:1, i * LANES : (i + 1) * LANES] = jnp.where(lane < turn, here, after)


def fill_spread(spread):
    spread[...] = (iota((LANES, INNER), 0) == iota((LANES, INNER), 1) // HEAD_DIM).astype(BF16)


def run_all(*steps):
    def run():
        for step in steps:
            step()

    return run


class Gather:
    def __init__(self, n_s, n_h, s, h, full, base, count, parts, sems, gap=3):
        self.gap = gap
        self.n_s, self.n_h, self.s, self.h, self.full = n_s, n_h, s, h, full
        self.base, self.count, self.parts = base, count, parts
        self.zs, self.zr, self.ps, self.pr, self.ds, self.dr, self.cs, self.cr = sems
        self.n_c = n_s // 2
        self.chip = s // 2
        self.core = lax.rem(s, 2)
        self.sib = self.chip * 2 + (1 - self.core)
        self.cpeer = [lax.rem(self.chip + j, self.n_c) for j in range(1, self.n_c)]
        self.square = self.n_c == 4
        self.xn = self.chip + 1 - 2 * lax.rem(self.chip, 2)
        self.yn = lax.rem(self.chip + self.n_c // 2, self.n_c)
        self.diag = 3 - self.chip
        place = jnp.clip(h - base, 0, count - 1)
        self.order = [base + place] + [base + self.nth(j, place, count) for j in range(1, count)]
        self.items = [(q, p) for q in self.order for p in range(len(parts))]

    def nth(self, j, place, count):
        below = jnp.where(j - 1 >= place, j, j - 1)
        mirror = count - 1 - place
        above = count - 1 - jnp.where(j - 1 >= mirror, j, j - 1)
        return jnp.where(2 * place < count, below, above)

    def when(self, item, work):
        q, p = item
        only = self.parts[p][1]
        if only is None:
            work()
        else:
            pl.when(q == only)(work)

    def blk(self, item, c, part=None, other=False):
        q, p = item
        core = 1 - self.core if other else self.core
        ref = self.full.at[q, c * 2 + core]
        rp = self.full.shape[2]
        lanes = self.parts[p][0]
        if part is None:
            return ref.at[:, lanes]
        mid = rp // 2 // 16 * 16
        return ref.at[pl.ds(0, mid) if part == 0 else pl.ds(mid, rp - mid), lanes]

    def along(self, item, way):
        ref = self.blk(item, self.chip)
        to = lax.rem(self.h + (1 if way == 0 else self.n_h - 1), self.n_h)
        q, p = item
        return remote(ref, ref, self.zs.at[q - self.base, p, way], self.zr.at[q - self.base, p], (self.s, to))

    def begin(self, chosen=None):
        for p in range(len(self.parts)) if chosen is None else chosen:
            item = (self.h, p)
            mine = jnp.logical_and(self.h >= self.base, self.h < self.base + self.count)
            if self.parts[p][1] is not None:
                mine = jnp.logical_and(mine, self.h == self.parts[p][1])
            for way, there in ((0, self.h < self.n_h - 1), (1, self.h > 0)):
                pl.when(jnp.logical_and(mine, there))(lambda item=item, way=way: self.along(item, way).start())

    def z_in(self, i):
        item = self.items[i]
        q = item[0]

        def take():
            self.along(item, 0).wait_recv()
            up = jnp.logical_and(q < self.h, self.h < self.n_h - 1)
            down = jnp.logical_and(q > self.h, self.h > 0)
            pl.when(up)(lambda: self.along(item, 0).start())
            pl.when(down)(lambda: self.along(item, 1).start())

        self.when(item, lambda: pl.when(q != self.h)(take))

    def z_done(self, i):
        item = self.items[i]
        q = item[0]
        up = jnp.logical_and(q <= self.h, self.h < self.n_h - 1)
        down = jnp.logical_and(q >= self.h, self.h > 0)
        self.when(item, lambda: pl.when(up)(lambda: self.along(item, 0).wait_send()))
        self.when(item, lambda: pl.when(down)(lambda: self.along(item, 1).wait_send()))

    def to_chip(self, i, m, part, c):
        item = self.items[i]
        q, p = item
        ref = self.blk(item, self.chip, part)
        n = 0 if part is None else part
        return remote(ref, ref, self.ps.at[q - self.base, p, m, n], self.pr.at[q - self.base, p, self.chip, n], (c * 2 + self.core, self.h))

    def to_chips(self, i):
        if self.square:
            near = ((0, self.xn), (1, self.yn))
            return [self.to_chip(i, m, (n + m) % 2, c) for n in range(2) for m, c in near]
        return [self.to_chip(i, j, None, c) for j, c in enumerate(self.cpeer)]

    def over(self, i, j, c):
        item = self.items[i]
        q, p = item
        ref = self.blk(item, c)
        return remote(ref, ref, self.cs.at[q - self.base, p, j], self.cr.at[q - self.base, p, c], (self.sib, self.h))

    def onward(self, i, n):
        item = self.items[i]
        q, p = item
        c, to = (self.xn, self.yn) if n == 0 else (self.yn, self.xn)
        ref = self.blk(item, c, n)
        return remote(ref, ref, self.ds.at[q - self.base, p, n], self.dr.at[q - self.base, p, n], (to * 2 + self.core, self.h))

    def spread_out(self, i):
        def work():
            for c in self.to_chips(i):
                c.start()
            self.over(i, 0, self.chip).start()

        self.when(self.items[i], work)

    def got(self, i, c, part):
        item = self.items[i]
        q, p = item
        ref = self.blk(item, c, part)
        n = 0 if part is None else part
        remote(ref, ref, self.ps.at[q - self.base, p, 0, 0], self.pr.at[q - self.base, p, c, n], (self.sib, self.h)).wait_recv()

    def pass_on(self, i):
        def work():
            if self.square:
                for n, c in ((0, self.xn), (1, self.yn)):
                    self.got(i, c, n)
                    self.onward(i, n).start()
                for n, c in ((1, self.xn), (0, self.yn)):
                    self.got(i, c, n)
                    self.over(i, 2 - n, c).start()
            else:
                for j, c in enumerate(self.cpeer):
                    self.got(i, c, None)
                    self.over(i, j + 1, c).start()

        self.when(self.items[i], work)

    def last_in(self, i):
        if not self.square:
            return
        item = self.items[i]
        q, p = item

        def work():
            for n in range(2):
                ref = self.blk(item, self.diag, n)
                remote(ref, ref, self.ds.at[q - self.base, p, 0], self.dr.at[q - self.base, p, n], (self.sib, self.h)).wait_recv()
            self.over(i, 3, self.diag).start()

        self.when(item, work)

    def complete(self, i):
        item = self.items[i]
        q, p = item

        def work():
            for c in [self.chip] + self.cpeer:
                ref = self.blk(item, c, other=True)
                remote(ref, ref, self.cs.at[q - self.base, p, 0], self.cr.at[q - self.base, p, c], (self.sib, self.h)).wait_recv()

        self.when(item, work)

    def plan(self, columns):
        count, parts = len(self.items), len(self.parts)
        gap = self.gap
        plan = []
        for i in range(count + 3 * gap):
            if i < count:
                plan.append(run_all(lambda i=i: self.z_in(i), lambda i=i: self.spread_out(i)))
            if gap <= i < count + gap:
                plan.append(lambda i=i: self.pass_on(i - gap))
            if 2 * gap <= i < count + 2 * gap:
                plan.append(lambda i=i: self.last_in(i - 2 * gap))
        for i in range(count):
            plan.append(lambda i=i: self.complete(i))
            if i % parts == parts - 1 and columns is not None:
                plan.append(lambda i=i: columns(self.order[i // parts]))
        return plan

    def finish(self):
        for i in range(len(self.items)):
            self.z_done(i)
            chips = [self.chip] + ([self.xn, self.yn, self.diag] if self.square else self.cpeer)

            def work():
                for c in self.to_chips(i):
                    c.wait_send()
                for j, c in enumerate(chips):
                    self.over(i, j, c).wait_send()
                if self.square:
                    for n in range(2):
                        self.onward(i, n).wait_send()

            self.when(self.items[i], work)


def gather_sems(n_s, count, parts):
    dma = pltpu.SemaphoreType.DMA
    n_c = n_s // 2
    n = 2 if n_c == 4 else 1
    return [
        dma((count, parts, 2)), dma((count, parts)), dma((count, parts, n_c, n)), dma((count, parts, n_c, n)),
        dma((count, parts, 2)), dma((count, parts, 2)), dma((count, parts, n_c)), dma((count, parts, n_c)),
    ]


def own_tiles(per_part, parts, width):
    return [(per_part * q) // LANES for q in range(parts)] + [width // LANES]


def payload_parts(per_part, parts, width):
    first = own_tiles(per_part, parts, width)
    counts = [first[q + 1] - first[q] for q in range(parts)]
    common = max(counts[:-1])
    mid = (common + 1) // 2
    ranges = [(slice(mid * LANES, common * LANES), None), (slice(0, mid * LANES), None)]
    if counts[-1] > common:
        ranges.append((slice(common * LANES, counts[-1] * LANES), parts - 1))
    return ranges, max(counts) * LANES


def fore_kernel(
    n_s, n_h, cph, oph, rin, rp, wi, wo, wide_in,
    x, cot, w_in, w_out_t, flat, lengths,
    result, w_full_o, nlow_o, conv_in_o, conv_low_o, slope_o, raw, steps, decb, dec, dgate, hgrad, glow, dgain, lst, mst,
    dev2, hin_o, gin_o,
    full, w_full, o_full, xh, shift_in, edge_out, edge_in, shift_out, nscr, conv_in, conv_low, slope, cf, gate, hst, gst, dev, into, csnd, incl_r,
    excl_r, incl_t, excl_t, steps_t, inter_s, yb, el, eg, gg_scr, hin, gin, prm, gain, taps, heads, out_gain, spread, logs3, el_eg, cc2, tot2, wfg, bts,
    xs_, xr_, es_, er_, us, ur, dws, dwr, outs, *gsems,
):
    s = lax.axis_index("seq")
    h = lax.axis_index("head")
    n_c = n_s // 2
    rows = x.shape[0]
    dp = x.shape[1]
    blocks = rows // SPAN
    chip = s // 2
    core = lax.rem(s, 2)
    sib = chip * 2 + (1 - core)
    cpeer = [lax.rem(chip + j, n_c) for j in range(1, n_c)]
    left = lengths[0] - h * rows
    parts, _ = payload_parts(cph, n_h, WIDE)
    sems = [gsems[8 * n : 8 * n + 8] for n in range(3)]
    half_h = n_h // 2
    g_high = Gather(n_s, n_h, s, h, full, half_h, n_h - half_h, parts, sems[0])
    g_low = Gather(n_s, n_h, s, h, full, 0, half_h, parts[:2], sems[1])
    g_out = Gather(n_s, n_h, s, h, full, 0, n_h, [(slice(wi, wi + wo), None)], sems[2])
    zpeer = [lax.rem(h + j, n_h) for j in range(1, n_h)]
    bar = pltpu.get_barrier_semaphore()
    for z in zpeer:
        pl.semaphore_signal(bar, inc=1, device_id=(s, z), device_id_type=MESH)
    for c in cpeer:
        pl.semaphore_signal(bar, inc=1, device_id=(c * 2 + core, h), device_id_type=MESH)
    pl.semaphore_signal(bar, inc=1, device_id=(sib, h), device_id_type=MESH)

    shift_in[...] = jnp.zeros_like(shift_in)
    shift_in[0:rin, 0:cph] = w_in[...]
    placed = pltpu.roll(shift_in[...], lax.rem(cph * h, LANES), 1)
    shift_in[...] = placed
    full[h, s, :, 0:wi] = placed[:, 0:wi].astype(BF16)
    first_tile = own_tiles(cph, n_h, WIDE)
    up = lax.rem(h + 1, n_h)
    for q in range(n_h - 1):
        at = (first_tile[q + 1] - first_tile[q]) * LANES

        @pl.when(h == q)
        def _():
            edge_out[...] = shift_in[:, at : at + LANES].astype(BF16)

    edge = remote(edge_out, edge_in, es_.at[0], er_.at[0], (s, up))
    shift_out[...] = jnp.zeros_like(shift_out)
    shift_out[0:rin, 0:oph] = w_out_t[...]
    turned = shift_out[...]
    if oph % LANES:
        turned = pltpu.roll(turned, lax.rem(oph * h, LANES), 1)
    full[h, s, :, wi:] = turned.astype(BF16)
    pl.semaphore_wait(bar, n_h + n_c - 1)


    @pl.when(h < n_h - 1)
    def _():
        edge.start()

    g_high.begin([0])

    @pl.when(h > 0)
    def _():
        edge.wait_recv()
        full[h, s, :, 0:LANES] += edge_in[...]

    g_high.begin(range(1, len(parts)))
    halo = remote(x.at[rows - HALO : rows], xh, xs_.at[0], xr_.at[0], (s, up))

    @pl.when(h < n_h - 1)
    def _():
        halo.start()

    high_plan = g_high.plan(lambda q: columns(q))
    high_plan[0]()

    flat_rows(flat, prm, 0.0)
    unpack_rows(prm, rin, rp, gain, taps, heads, out_gain)
    fill_spread(spread)

    def norm_rows(src, at, dst):
        v = src[at, :].astype(F32)
        n = v * lax.rsqrt(jnp.sum(v * v, axis=1, keepdims=True) * (1.0 / D) + EPS) * gain[...]
        nscr[dst, :] = n.astype(BF16)

    def norm_body(i, _):
        at = pl.multiple_of(i * 16, 16)
        norm_rows(x, pl.ds(at, 16), pl.ds(at + HALO, 16))
        return 0

    lax.fori_loop(0, rows // 16, norm_body, 0, unroll=4)

    @pl.when(h > 0)
    def _():
        halo.wait_recv()

    @pl.when(h == 0)
    def _():
        xh[...] = jnp.zeros_like(xh)

    norm_rows(xh, slice(0, HALO), slice(0, HALO))

    def leave(src, dst, n):
        return pltpu.make_async_copy(src, dst, outs.at[n])

    leaving = [leave(nscr.at[HALO:], nlow_o, 0)]
    leaving[0].start()

    def project(tile, weights):
        w_full[:, pl.ds(pl.multiple_of(tile * LANES, LANES), LANES)] = weights
        v = nn(nscr[...], weights).astype(BF16)
        first, last = INNER // LANES, WIDE // LANES - 1

        @pl.when(tile < first)
        def _():
            gate[:, pl.ds(pl.multiple_of(tile * LANES, LANES), LANES)] = v[HALO:]

        @pl.when(tile == last)
        def _():
            raw[...] = v[HALO:].astype(F32)

        @pl.when(jnp.logical_and(tile >= first, tile < last))
        def _():
            at = pl.ds(pl.multiple_of((tile - first) * LANES, LANES), LANES)
            conv_in[:, at] = v
            cf[...] = v.astype(F32)
            total = jnp.zeros((rows, LANES), F32) + taps[CONV : CONV + 1, at]
            for k in range(CONV):
                start = HALO - CONV + 1 + k
                total = total + taps[k : k + 1, at] * cf[start : start + rows, :]
            sg = sigmoid(total)
            conv_low[:, at] = (total * sg).astype(BF16)
            slope[:, at] = sg * (1.0 + total * (1.0 - sg))

    def tile_of(q, t):
        t0 = (cph * q) // LANES
        at = pl.ds(pl.multiple_of((t - t0) * LANES, LANES), LANES)
        project(t, full[q, :, :, at].reshape(dp, LANES))

    def columns(q):
        hi = jnp.where(q == n_h - 1, WIDE // LANES, (cph * (q + 1)) // LANES)

        def tile_body(t, _):
            tile_of(q, t)
            return 0

        lax.fori_loop((cph * q) // LANES, hi, tile_body, 0)

    for n, step in enumerate(high_plan[1:]):
        step()
        if n == 9:
            g_low.begin()
            g_out.begin()
    for n, (src, dst) in enumerate(((conv_in, conv_in_o), (conv_low, conv_low_o), (slope, slope_o))):
        leaving.append(leave(src, dst, n + 1))
        leaving[-1].start()

    biased = raw[...] + heads[0:1, :]
    soft = jnp.maximum(biased, 0.0) + jnp.log1p(jnp.exp(-jnp.abs(biased)))
    keep = jnp.logical_and(iota((rows, LANES), 0) < left, iota((rows, LANES), 1) < HEADS)
    steps[...] = jnp.where(keep, soft, 0.0)
    rates = -jnp.exp(heads[1:2, :])
    for b in range(blocks):
        at = slice(b * SPAN, (b + 1) * SPAN)
        st = steps[at, :]
        incl, excl, total = head_terms(st, rates)
        incl_r[b] = incl
        excl_r[b] = excl
        incl_t[b] = incl.T
        excl_t[b] = excl.T
        steps_t[b] = st.T
        logs3[b] = jnp.concatenate(split3(jnp.concatenate([incl, excl], axis=0)), axis=1)
        el_eg[b] = stacked(jnp.concatenate([jnp.exp(incl), jnp.exp(total - excl)], axis=0))
        wide = stacked(jnp.concatenate([jnp.exp(total - incl) * st, jnp.exp(excl) * st], axis=0))
        bc = conv_low[at, INNER:].astype(F32)
        bt = bc.T[:STATE].astype(BF16)
        bt2 = jnp.concatenate([bt, bt], axis=1)
        cb = pltpu.roll(bc, STATE, 1)
        c_low = half_masks(cb)[0].astype(BF16)
        inter_s[b] = nt(c_low, bc.astype(BF16)) * (1.0 + (iota((SPAN, SPAN), 0) == iota((SPAN, SPAN), 1)).astype(F32))
        cc = cb[:, :STATE].astype(BF16)
        cc2[b] = jnp.concatenate([cc, cc], axis=1)
        tot2[b] = stacked(jnp.broadcast_to(jnp.exp(total), (8, LANES)))
        wfg[b] = wide
        bts[b] = bt2
    chain = Chain(n_h, s, h, dev, dec, into, csnd, us, ur, dws, dwr)
    for g in range(CHAIN_PARTS):
        cols = slice(g * 256, (g + 1) * 256)
        sp = spread[:, cols]
        weights_all = nn(wfg[...].reshape(blocks * 4 * SPAN, LANES), sp)
        totals = nn(tot2[...].reshape(blocks * 16, LANES), sp)
        for b in range(blocks):
            at = slice(b * SPAN, (b + 1) * SPAN)
            xs = conv_low[at, cols].astype(F32)
            w = halves_sum(weights_all[b * 4 * SPAN : (b + 1) * 4 * SPAN])
            for n, dst in ((0, hst), (1, gst)):
                dst[b, :, cols] = nn(bts[b], stacked(w[n * SPAN : (n + 1) * SPAN] * xs))
            decb[b, :, cols] = halves_sum(totals[b * 16 : (b + 1) * 16])
        hv, gv, dv = hst[0, :, cols], gst[blocks - 1, :, cols], decb[0, :, cols]
        for b in range(1, blocks):
            hv = hv * decb[b, 0:1, cols] + hst[b, :, cols]
            dv = dv * decb[b, :, cols]
        for b in range(blocks - 2, -1, -1):
            gv = gv * decb[b, 0:1, cols] + gst[b, :, cols]
        dev[0, :, cols] = hv
        dev[1, :, cols] = gv
        dec[:, cols] = dv
        chain.begin([g])

    row = iota((SPAN, SPAN), 0)
    col = iota((SPAN, SPAN), 1)
    skip8 = jnp.broadcast_to(heads[2:3, :], (8, LANES))

    def pair_body(pair, _):
        cols = pl.ds(pl.multiple_of(pair * LANES, LANES), LANES)
        after = row >= col
        hot = (iota((LANES, 2 * LANES), 0) == 2 * pair + iota((LANES, 2 * LANES), 1) // LANES).astype(BF16)
        hot3 = jnp.concatenate([hot, hot, hot], axis=0)
        skip = expand(skip8, spread[:, cols])[0:1]
        wide_all = nn(logs3[...].reshape(blocks * 2 * SPAN, 3 * LANES), hot3)
        for b in range(blocks):
            at = slice(b * SPAN, (b + 1) * SPAN)
            wide = wide_all[b * 2 * SPAN : (b + 1) * 2 * SPAN]
            inter = inter_s[b]
            xs = conv_low[at, cols]
            mix = []
            for n in range(2):
                hd = 2 * pair + n
                lanes = slice(n * LANES, (n + 1) * LANES)
                gap = jnp.where(
                    after,
                    wide[0:SPAN, lanes] - incl_t[b, pl.ds(hd, 1), :],
                    excl_t[b, pl.ds(hd, 1), :] - wide[SPAN:, lanes],
                )
                mix.append(inter * jnp.exp(gap) * steps_t[b, pl.ds(hd, 1), :])
            x0, x1 = half_masks(xs)
            y = nn_split(jnp.concatenate(mix, axis=1), jnp.concatenate([x0, x1], axis=0))
            yb[at, cols] = y + skip * xs.astype(F32)
        chain.at(pair, 3)
        for n, step in enumerate(behind):
            pl.when(pair == n * pairs_n // len(behind))(step)
        return 0

    low_plan = g_low.plan(None)
    out_plan = g_out.plan(None)
    pairs_n = HEADS // 2
    gates_n = INNER // LANES
    behind = []
    for n in range(max(len(low_plan), len(out_plan))):
        behind += low_plan[n : n + 1] + out_plan[n : n + 1]
    out_plan = []
    lax.fori_loop(0, pairs_n, pair_body, 0)

    def gate_tiles(q):
        t0, t1 = (cph * q) // LANES, (cph * (q + 1)) // LANES

        def two_tiles(n, _):
            t = t0 + 2 * n
            here = pl.ds(pl.multiple_of(t * LANES, LANES), 2 * LANES)
            weights = full[q, :, :, pl.ds(pl.multiple_of(2 * n * LANES, LANES), 2 * LANES)].reshape(dp, 2 * LANES)
            w_full[:, here] = weights
            gate[:, here] = nn(nscr[HALO:, :], weights).astype(BF16)
            chain.at(pairs_n + t, 3)
            chain.at(pairs_n + t + 1, 3)
            return 0

        lax.fori_loop(0, (t1 - t0) // 2, two_tiles, 0)
        if (t1 - t0) % 2:
            tile_of(q, t1 - 1)
            chain.at(pairs_n + t1 - 1, 3)

    for q in range(half_h):
        gate_tiles(q)
    for t in range((cph * half_h) // LANES, max(chain.steps(3) - pairs_n, 0)):
        chain.at(pairs_n + t, 3)
    leaving.append(leave(w_full, w_full_o, 4))
    leaving[-1].start()

    for tile in range(INNER // LANES):
        parts = []
        for q in range(n_h):
            t0, t1 = tiles_of(oph, q)
            if t0 <= tile < t1:
                at = wi + (tile - t0) * LANES
                parts.append(full[q, :, :, at : at + LANES])
        v = parts[0] if len(parts) == 1 else parts[0] + parts[1]
        o_full[:, tile * LANES : (tile + 1) * LANES] = v.reshape(dp, LANES)

    hin[0] = into[0]
    gin[blocks] = into[1]
    for b in range(blocks):
        hin[b + 1] = hin[b] * decb[b, 0:1, :] + hst[b]
    for b in range(blocks - 1, -1, -1):
        gin[b] = gin[b + 1] * decb[b, 0:1, :] + gst[b]
    for src, dst, n in ((hin, hin_o, 5), (gin, gin_o, 6)):
        leaving.append(leave(src, dst, n))
        leaving[-1].start()
    keep_row = (iota((rows, 1), 0) < left).astype(F32)
    bgrad = (cot[...].astype(F32) * keep_row).astype(BF16)
    for g in range(INNER // 256):
        cols = slice(g * 256, (g + 1) * 256)
        sp = spread[:, cols]
        gg_scr[:, cols] = nn(bgrad, o_full[:, cols])
        wide_all = nn(el_eg[...].reshape(blocks * 4 * SPAN, LANES), sp)
        for b in range(blocks):
            at = slice(b * SPAN, (b + 1) * SPAN)
            wide = halves_sum(wide_all[b * 4 * SPAN : (b + 1) * 4 * SPAN])
            el[at, cols] = wide[0:SPAN]
            eg[at, cols] = wide[SPAN:]
            yf = nn(cc2[b], stacked(hin[b, :, cols]))
            yg = nn(cc2[b], stacked(gin[b + 1, :, cols]))
            yb[at, cols] += wide[0:SPAN] * yf + wide[SPAN:] * yg
    dgain[...] = jnp.zeros_like(dgain)

    def gate_body(i, _):
        at = pl.ds(pl.multiple_of(i * 16, 16), 16)
        z = gate[at, :].astype(F32)
        hv = yb[at, :].astype(BF16).astype(F32)
        sg = sigmoid(z)
        sl = z * sg
        gated = hv * sl
        r = lax.rsqrt(jnp.mean(gated * gated, axis=1, keepdims=True) + EPS)
        unit = gated * r
        glow[at, :] = (unit * out_gain[...]).astype(BF16)
        gr = gg_scr[at, :]
        prod = gr * unit
        dgain[...] += prod[0:8] + prod[8:16]
        gg = gr * out_gain[...]
        dg = r * (gg - unit * jnp.mean(gg * unit, axis=1, keepdims=True))
        hgrad[at, :] = (dg * sl).astype(BF16)
        dgate[at, :] = (dg * hv * (sg * (1.0 + z * (1.0 - sg)))).astype(BF16)
        return 0

    lax.fori_loop(0, rows // 16, gate_body, 0, unroll=4)
    for g in range(dp // 256):
        cols = slice(g * 256, (g + 1) * 256)
        branch = nt(glow[...], o_full[cols, :])
        result[:, cols] = (x[:, cols].astype(F32) + keep_row * branch).astype(BF16)

    def state_body(b, _):
        at = pl.ds(pl.multiple_of(b * SPAN, SPAN), SPAN)
        ct = conv_low[at, INNER:].astype(F32).T[STATE:].astype(BF16)
        ct2 = jnp.concatenate([ct, ct], axis=1)
        for g in range(INNER // 256):
            cols = slice(g * 256, (g + 1) * 256)
            dy = hgrad[at, cols].astype(F32)
            for scale, dst in ((el, lst), (eg, mst)):
                hi, lo = split(scale[at, cols] * dy)
                dst[b, :, cols] = nn(ct2, jnp.concatenate([hi, lo], axis=0))
        return 0

    lax.fori_loop(0, blocks, state_body, 0)
    mv, lv = mst[0], lst[blocks - 1]
    for b in range(1, blocks):
        mv = mv * decb[b, 0:1, :] + mst[b]
    for b in range(blocks - 2, -1, -1):
        lv = lv * decb[b, 0:1, :] + lst[b]
    dev2[0] = mv
    dev2[1] = lv
    chain.finish()

    @pl.when(h < n_h - 1)
    def _():
        halo.wait_send()

    g_high.finish()
    g_low.finish()
    g_out.finish()

    @pl.when(h < n_h - 1)
    def _():
        edge.wait_send()

    for c in leaving:
        c.wait()


def fore(n_s, n_h, rp, *args):
    x, _, w_in, w_out_t = args[:4]
    rin, cph = w_in.shape
    oph = w_out_t.shape[1]
    rows, dp = x.shape
    blocks = rows // SPAN
    parts, wi = payload_parts(cph, n_h, WIDE)
    wide_in = max(tile_count(cph, n_h) * LANES, wi)
    wo = tile_count(oph, n_h) * LANES
    dma = pltpu.SemaphoreType.DMA
    vm = pl.BlockSpec(memory_space=pltpu.VMEM)
    sm = pl.BlockSpec(memory_space=pltpu.SMEM)
    hbm = pl.BlockSpec(memory_space=pl.ANY)
    sds = jax.ShapeDtypeStruct
    vf = lambda *shape: pltpu.VMEM(shape, F32)
    vb = lambda *shape: pltpu.VMEM(shape, BF16)
    tables = vf(blocks, SPAN, LANES)
    act = sds((rows, INNER), BF16)
    states = sds((blocks, STATE, INNER), F32)
    entries = sds((blocks + 1, STATE, INNER), F32)
    outs = [
        (sds((rows, dp), BF16), vm),
        (sds((dp, WIDE), BF16), hbm),
        (sds((rows, dp), BF16), hbm),
        (sds((rows + HALO, CONV_CH), BF16), hbm),
        (sds((rows, CONV_CH), BF16), hbm),
        (sds((rows, CONV_CH), F32), hbm),
        (sds((rows, LANES), F32), vm),
        (sds((rows, LANES), F32), vm),
        (sds((blocks, 8, INNER), F32), vm),
        (sds((8, INNER), F32), vm),
        (act, vm),
        (act, vm),
        (act, vm),
        (sds((8, INNER), F32), vm),
        (states, vm),
        (states, vm),
        (sds((2, STATE, INNER), F32), vm),
        (entries, hbm),
        (entries, hbm),
    ]
    return pl.pallas_call(
        functools.partial(fore_kernel, n_s, n_h, cph, oph, rin, rp, wi, wo, wide_in),
        out_shape=tuple(o for o, _ in outs),
        in_specs=[vm, vm, vm, vm, vm, sm],
        out_specs=tuple(p for _, p in outs),
        scratch_shapes=[
            vb(n_h, n_s, rp, wi + wo),
            vb(dp, WIDE),
            vb(dp, INNER),
            vb(HALO, dp),
            vf(rp, wide_in),
            vb(rp, LANES),
            vb(rp, LANES),
            vf(rp, wo),
            vb(rows + HALO, dp),
            vb(rows + HALO, CONV_CH),
            vb(rows, CONV_CH),
            vf(rows, CONV_CH),
            vf(rows + HALO, LANES),
            vb(rows, INNER),
            vf(blocks, STATE, INNER),
            vf(blocks, STATE, INNER),
            vf(2, STATE, INNER),
            vf(2, STATE, INNER),
            vf(2, STATE, INNER),
            tables, tables, tables, tables, tables, tables,
            vf(rows, INNER),
            vf(rows, INNER),
            vf(rows, INNER),
            vf(rows, INNER),
            vf(blocks + 1, STATE, INNER),
            vf(blocks + 1, STATE, INNER),
            vf(FLAT_ROWS, LANES),
            vf(1, dp),
            vf(8, CONV_CH),
            vf(8, LANES),
            vf(1, INNER),
            vb(LANES, INNER),
            vb(blocks, 2 * SPAN, 3 * LANES),
            vb(blocks, 4 * SPAN, LANES),
            vb(blocks, SPAN, LANES),
            vb(blocks, 16, LANES),
            vb(blocks, 4 * SPAN, LANES),
            vb(blocks, STATE, 2 * SPAN),
            dma((1,)),
            dma((1,)),
            dma((1,)),
            dma((1,)),
        ]
        + [dma((CHAIN_PARTS,))] * 4
        + [dma((7,))]
        + gather_sems(n_s, n_h - n_h // 2, len(parts))
        + gather_sems(n_s, n_h // 2, 2)
        + gather_sems(n_s, n_h, 1),
        compiler_params=pltpu.CompilerParams(
            collective_id=1, has_side_effects=True, vmem_limit_bytes=FORE_VMEM
        ),
        name="fore",
    )(*args)


FORE_VMEM = 63 << 20
SMALL = 10696
FLAT_ROWS = 128
TAPS_ROWS = CONV_CH // LANES
HEAD_ROW = D // LANES + (CONV + 1) * TAPS_ROWS


CHUNK = 256
OUT_CHUNK = 384
N_IN = WIDE // CHUNK
N_OUT = INNER // OUT_CHUNK
X_CHUNK = INNER // CHUNK
SLOTS = 4
THIRD = 6
THIRD_LATE = 3
HOP = 4
EARLY = N_OUT + X_CHUNK
LATE = HEADS // 2 + 3


def rear_kernel(
    n_s, n_h, cph, oph, rin, rp, in_slots,
    x, cot, flat, lengths, w_full_i, nlow, dgate_i, glow, conv_low, hgrad, steps, raw, slope_i, conv_in_i,
    hin_i, gin_i, lst_i, mst_i, dev, decb, dec, ogp, w_in, w_out_t, row_in, col_in, row_out, col_out, second_i,
    grad_x, grad_in, row_in_new, col_in_new, w_in_new, grad_out, row_out_new, col_out_new, w_out_new, small, second_new,
    params_new,
    w_full, slope, conv_in, hin, gin, lst, mst, prm, sec_rows, gain, taps, heads, spread,
    adj, csnd, nt_p, bt_p, pg, ng, dpre, halo, dfs, cfs, incl_r, excl_r, incl_t, excl_t, q_t, at_f, at_g, back_f, back_g,
    logs3, steps2, terms2, bb2, cc2, red, cross, dbc, dheads, dtaps, ngain, inter_s,
    sb, r0, vs, pbi, r1i, acci, r2i, pbo, r1o, acco, r2o, win, zb, r2b,
    sz, szin, spl, sout, z1, p1, z2, p2, line,
    us, ur, ds, dr, hs, hr, s0s, s0r, s1s, s1r, s2s, s2r, o0s, o0r, o1s, o1r, o2s, o2r,
    load, zbs, zbr, sos, sor, szs, szr, sps, spr, z1s, z1r, p1s, p1r, z2s, z2r, p2s, p2r,
):
    s = lax.axis_index("seq")
    h = lax.axis_index("head")
    n_c = n_s // 2
    rows = x.shape[0]
    dp = x.shape[1]
    half = n_c * rp
    blocks = rows // SPAN
    chip = s // 2
    core = lax.rem(s, 2)
    sib = chip * 2 + (1 - core)
    up = lax.rem(h + 1, n_h)
    down = lax.rem(h + n_h - 1, n_h)
    zpeer = [lax.rem(h + j, n_h) for j in range(1, n_h)]
    cpeer = [lax.rem(chip + j, n_c) for j in range(1, n_c)]
    speer = [lax.rem(s + j, n_s) for j in range(1, n_s)]
    bar = pltpu.get_barrier_semaphore()
    for z in zpeer:
        pl.semaphore_signal(bar, inc=1, device_id=(s, z), device_id_type=MESH)
    for p in speer:
        pl.semaphore_signal(bar, inc=1, device_id=(p, h), device_id_type=MESH)
    chain = Chain(n_h, s, h, dev, dec, adj, csnd, us, ur, ds, dr)
    pairs_of = (
        (dgate_i, pg.at[:, 0:INNER]), (w_full_i, w_full), (slope_i, slope), (hin_i, hin), (gin_i, gin), (lst_i, lst), (mst_i, mst),
        (conv_in_i, conv_in),
    )
    loads = [pltpu.make_async_copy(src, dst, load.at[n]) for n, (src, dst) in enumerate(pairs_of)]
    for c in loads:
        c.start()
    left = lengths[0] - h * rows
    flat_rows(flat, prm, 0.0)
    flat_rows(second_i, sec_rows, 1.0)
    unpack_rows(prm, rin, rp, gain, taps, heads, None)
    fill_spread(spread)
    pl.semaphore_wait(bar, n_h + n_s - 2)
    chain.begin(range(CHAIN_PARTS))

    def over_in(i):
        own = pl.ds(0, CHUNK)
        return remote(
            sb.at[lax.rem(i, 2), :, own], r0.at[lax.rem(i, SLOTS), :, own], s0s.at[i], s0r.at[i], (sib, h)
        )

    def over_out(i):
        return remote(sb.at[lax.rem(i, 2)], r0.at[lax.rem(i, SLOTS)], o0s.at[i], o0r.at[i], (sib, h))

    def first_in(i):
        @pl.when(i >= 2)
        def _():
            over_in(i - 2).wait_send()

        @pl.when(i < 2)
        def _():
            over_out(i + N_OUT - 2).wait_send()

        cols = pl.ds(pl.multiple_of(i * CHUNK, CHUNK), CHUNK)
        part = pg[:, cols]
        sb[lax.rem(i, 2), :, 0:CHUNK] = nn(nt_p[1 - core], part)
        over_in(i).start()

    def normed_part(first, size, part, fresh):
        third = dp // 3 // LANES * LANES if dp % (3 * LANES) == 0 else dp // 4
        at = slice(part * third, (part + 1) * third)
        v = nt(pg[:, first : first + size], w_full[at, first : first + size])
        ng[:, at] = v if fresh else ng[:, at] + v

    normed_parts = 3 if dp % (3 * LANES) == 0 else 4

    def second_in(i):
        cols = pl.ds(pl.multiple_of(i * CHUNK, CHUNK), CHUNK)
        mine = nn(nt_p[core], pg[:, cols])
        over_in(i).wait_recv()
        vs[:, :, 0:CHUNK] = (mine + r0[lax.rem(i, SLOTS), :, 0:CHUNK]).reshape(n_c, rp, CHUNK)
        for j, k in enumerate(cpeer):
            pbi[i, j] = vs[k, :, 0:CHUNK].astype(BF16)
            remote(pbi.at[i, j], r1i.at[i, n_c - 2 - j], s1s.at[i, j], s1r.at[i, n_c - 2 - j], (2 * k + core, h)).start()
        acci[i] = vs[chip, :, 0:CHUNK]

    def owners(i, wide, per):
        one = (wide * i) // per
        two = (wide * i + wide - 1) // per
        return one, jnp.minimum(two, n_h - 1)

    def third_in(i):
        total = acci[i]
        for j, k in enumerate(cpeer):
            remote(pbi.at[i, j], r1i.at[i, j], s1s.at[i, j], s1r.at[i, j], (2 * k + core, h)).wait_recv()
            total = total + r1i[i, j].astype(F32)
        acci[i] = total

    def links(i, wide, per, acc, rec, snd, rcv):
        one, two = owners(i, wide, per)
        for n, q, real in ((0, one, None), (1, two, two != one))[: rec.shape[1]]:
            for way, to in ((0, up), (1, down)):
                sends_it = h < q if way == 0 else h > q
                if real is not None:
                    sends_it = jnp.logical_and(real, sends_it)
                begins = h == 0 if way == 0 else h == n_h - 1
                dst = rec.at[i, n, way]
                make = lambda src, n=n, way=way, to=to, dst=dst: remote(
                    src, dst, snd.at[i, n, way], rcv.at[i, n, way], (s, to)
                )
                yield way, sends_it, begins, make, n

    def along(i, way, *stream):
        acc, rec = stream[2], stream[3]
        for w, sends_it, begins, make, n in links(i, *stream):
            if w != way:
                continue

            @pl.when(jnp.logical_and(sends_it, begins))
            def _():
                make(acc.at[i]).start()

            @pl.when(jnp.logical_and(sends_it, jnp.logical_not(begins)))
            def _():
                make(acc.at[i]).wait_recv()
                rec[i, n, way] += acc[i]
                make(rec.at[i, n, way]).start()

    def straight(i):
        z = i - X_CHUNK
        zb[z] = acci[i].astype(BF16)
        for n, q, real in straight_to(i):
            pl.when(real)(lambda n=n, q=q: remote(zb.at[z], r2b.at[h, z], zbs.at[z, n], zbr.at[h, z], (s, q)).start())

    def straight_to(i):
        one, two = owners(i, CHUNK, cph)
        return ((0, one, one != h), (1, two, jnp.logical_and(two != one, two != h)))

    def drain_straight(i):
        z = i - X_CHUNK
        for n, q, real in straight_to(i):
            pl.when(real)(lambda n=n, q=q: remote(zb.at[z], r2b.at[h, z], zbs.at[z, n], zbr.at[h, z], (s, q)).wait_send())

    def drain_z(i, *stream):
        for _, sends_it, _, make, n in links(i, *stream):

            @pl.when(sends_it)
            def _():
                make(stream[2].at[i]).wait_send()

    in_stream = (CHUNK, cph, acci, r2i, s2s, s2r)
    out_stream = (OUT_CHUNK, oph, acco, r2o, o2s, o2r)

    def drain_in(i):
        for j, k in enumerate(cpeer):
            remote(pbi.at[i, j], r1i.at[i, n_c - 2 - j], s1s.at[i, j], s1r.at[i, n_c - 2 - j], (2 * k + core, h)).wait_send()
        pl.when(i < X_CHUNK)(lambda: drain_z(i, *in_stream))
        pl.when(i >= X_CHUNK)(lambda: drain_straight(i))

    def first_out(i):
        @pl.when(i >= 2)
        def _():
            over_out(i - 2).wait_send()

        cols = pl.ds(pl.multiple_of(i * OUT_CHUNK, LANES), OUT_CHUNK)
        sb[lax.rem(i, 2)] = nn(bt_p[1 - core], glow[:, cols])
        over_out(i).start()

    def second_out(i):
        cols = pl.ds(pl.multiple_of(i * OUT_CHUNK, LANES), OUT_CHUNK)
        mine = nn(bt_p[core], glow[:, cols])
        over_out(i).wait_recv()
        vs[...] = (mine + r0[lax.rem(i, SLOTS)]).reshape(n_c, rp, OUT_CHUNK)
        for j, k in enumerate(cpeer):
            pbo[i, j] = vs[k].astype(BF16)
            remote(pbo.at[i, j], r1o.at[i, n_c - 2 - j], o1s.at[i, j], o1r.at[i, n_c - 2 - j], (2 * k + core, h)).start()
        acco[i] = vs[chip]

    def third_out(i):
        total = acco[i]
        for j, k in enumerate(cpeer):
            remote(pbo.at[i, j], r1o.at[i, j], o1s.at[i, j], o1r.at[i, j], (2 * k + core, h)).wait_recv()
            total = total + r1o[i, j].astype(F32)
        acco[i] = total

    def drain_out(i):
        for j, k in enumerate(cpeer):
            remote(pbo.at[i, j], r1o.at[i, n_c - 2 - j], o1s.at[i, j], o1r.at[i, n_c - 2 - j], (2 * k + core, h)).wait_send()
        drain_z(i, *out_stream)

    def among(k, first, count):
        return jnp.logical_and(k >= first, k < first + count)

    def early_at(t):
        return among(t, 0, EARLY), t

    def late_at(t):
        spaced = LATE + 2 * (X_CHUNK - 2)
        last = t > spaced
        item = jnp.where(last, EARLY + X_CHUNK - 2 + t - spaced, EARLY + (t - LATE) // 2)
        ok = jnp.logical_or(last, (t - LATE) % 2 == 0)
        return jnp.logical_and(among(t, LATE, spaced + 3 - LATE), ok), item

    def tick(t, phase):
        def stage(at, lag, on_out, on_in):
            ok, item = at(t - lag)
            if on_out is not None:
                pl.when(jnp.logical_and(ok, item < N_OUT))(lambda: on_out(item))
                ok = jnp.logical_and(ok, item >= N_OUT)
            pl.when(ok)(lambda: on_in(item - N_OUT))

        if phase == 0:
            stage(early_at, 1, second_out, second_in)
        if phase < 2:
            stage(early_at, THIRD, third_out if phase == 0 else None, third_in)
        if phase > 0:
            stage(late_at, 1, None, second_in)
            stage(late_at, THIRD_LATE, None, lambda i: (third_in(i), straight(i))[0])
        for way, far in ((0, h), (1, n_h - 1 - h)):
            stage(
                early_at,
                THIRD + HOP * far,
                lambda i, way=way: along(i, way, *out_stream),
                lambda i, way=way: along(i, way, *in_stream),
            )

    last_tick = max(LATE + 2 * (X_CHUNK - 2) + 2 + THIRD_LATE, EARLY - 1 + THIRD + HOP * (n_h - 2))

    keep_row = (iota((rows, 1), 0) < left).astype(F32)
    for src, dst in ((nlow[...], nt_p), ((cot[...].astype(F32) * keep_row).astype(BF16), bt_p)):
        turned = src.T
        for q in range(n_s):
            dst[q % 2, (q // 2) * rp : (q // 2 + 1) * rp, :] = turned[q * rp : (q + 1) * rp]
    dheads[...] = jnp.zeros_like(dheads)
    dtaps[...] = jnp.zeros_like(dtaps)
    rates = -jnp.exp(heads[1:2, :])
    row = iota((SPAN, SPAN), 0)
    col = iota((SPAN, SPAN), 1)
    twice = 1.0 + (row == col).astype(F32)
    for ref in (q_t, at_f, at_g, back_f, back_g, red, cross, dbc):
        ref[...] = jnp.zeros_like(ref)
    for b in range(blocks):
        at = slice(b * SPAN, (b + 1) * SPAN)
        incl, excl, total = head_terms(steps[at, :], rates)
        incl_r[b] = incl
        excl_r[b] = excl
        incl_t[b] = incl.T
        excl_t[b] = excl.T
        logs3[b] = jnp.concatenate(split3(jnp.concatenate([incl, excl], axis=0)), axis=1)
        st = steps[at, :]
        steps2[b] = stacked(st)
        terms2[b] = stacked(
            jnp.concatenate([st, jnp.exp(incl), jnp.exp(total - excl), jnp.exp(total - incl), jnp.exp(excl)], axis=0)
        )
        bc = conv_low[at, INNER:].astype(F32)
        cb = pltpu.roll(bc, STATE, 1)
        inter_s[b] = nt(half_masks(bc)[0].astype(BF16), cb.astype(BF16))
        bb, cc = bc[:, :STATE].astype(BF16), cb[:, :STATE].astype(BF16)
        bb2[b] = jnp.concatenate([bb, bb], axis=1)
        cc2[b] = jnp.concatenate([cc, cc], axis=1)

    def pair_body(pair, _):
        cols = pl.ds(pl.multiple_of(pair * LANES, LANES), LANES)
        sp = spread[:, cols]
        later = col >= row
        hot = (iota((LANES, 2 * LANES), 0) == 2 * pair + iota((LANES, 2 * LANES), 1) // LANES).astype(BF16)
        hot3 = jnp.concatenate([hot, hot, hot], axis=0)
        wide_all = nn(logs3[...].reshape(blocks * 2 * SPAN, 3 * LANES), hot3)
        step_all = nn(steps2[...].reshape(blocks * 2 * SPAN, LANES), sp)
        for b in range(blocks):
            at = slice(b * SPAN, (b + 1) * SPAN)
            both = slice(b * 2 * SPAN, (b + 1) * 2 * SPAN)
            wide = wide_all[both]
            inter = inter_s[b]
            inter2 = inter * twice
            xs = conv_low[at, cols].astype(F32)
            dyl = hgrad[at, cols]
            xh, xl = split(halves_sum(step_all[both]) * xs)
            xhs = half_masks(xh)
            xls = half_masks(xl)
            dy2 = jnp.concatenate([dyl, dyl], axis=1)
            kern = []
            qt = q_t[b]
            for n in range(2):
                hd = 2 * pair + n
                lanes = slice(n * LANES, (n + 1) * LANES)
                gap = jnp.where(
                    later,
                    incl_t[b, pl.ds(hd, 1), :] - wide[0:SPAN, lanes],
                    wide[SPAN:, lanes] - excl_t[b, pl.ds(hd, 1), :],
                )
                decay = jnp.exp(gap)
                kern.append(inter2 * decay)
                weigh = nt(jnp.concatenate([xhs[n], xls[n]], axis=1), dy2) * decay
                qt = qt + weigh
                pairs = weigh * inter
                above = jnp.where(col > row, pairs, 0.0)
                below = jnp.where(col < row, pairs, 0.0)
                at_f[b, pl.ds(hd, 1), :] = jnp.sum(above, axis=0, keepdims=True)
                at_g[b, pl.ds(hd, 1), :] = jnp.sum(below, axis=0, keepdims=True)
                here = iota((SPAN, LANES), 1) == hd
                back_f[b] = jnp.where(here, jnp.sum(above, axis=1, keepdims=True), back_f[b])
                back_g[b] = jnp.where(here, jnp.sum(below, axis=1, keepdims=True), back_g[b])
            q_t[b] = qt
            dys = half_masks(dyl)
            dpre[at, cols] = nn_split(jnp.concatenate(kern, axis=1), jnp.concatenate(dys, axis=0))
        chain.at(pair)

        pl.when(pair < N_OUT)(lambda: first_out(pair))
        pl.when(among(pair, N_OUT, X_CHUNK))(lambda: first_in(pair - N_OUT))
        tick(pair, 0)
        for part in range(normed_parts):
            pl.when(pair == N_OUT + 2 + part)(lambda part=part: normed_part(0, INNER, part, True))
        return 0

    pairs_n = HEADS // 2
    for c in loads[:2]:
        c.wait()
    lax.fori_loop(0, pairs_n, pair_body, 0)
    for k in range(pairs_n, chain.steps()):
        chain.at(k)
    for c in loads[2:]:
        c.wait()

    @pl.when(h == n_h - 1)
    def _():
        halo[...] = jnp.zeros_like(halo)

    def halo_copy(g, size):
        cols = pl.ds(pl.multiple_of(g * CHUNK, CHUNK), size)
        return remote(dpre.at[0:8, cols], halo.at[:, cols], hs.at[g], hr.at[g], (s, down))

    def halo_send(g, size):
        @pl.when(h > 0)
        def _():
            halo_copy(g, size).start()

    def conv_back(g, size):
        cols = pl.ds(pl.multiple_of(g * CHUNK, CHUNK), size)
        own = slice(0, size)
        dp_ = dpre[:, cols]
        dfs[0:rows, own] = dp_
        cfs[:, own] = conv_in[:, cols].astype(F32)
        for k in range(CONV):
            first = HALO - CONV + 1 + k
            dtaps[k : k + 1, cols] = jnp.sum(dp_ * cfs[first : first + rows, own], axis=0, keepdims=True)
        dtaps[CONV : CONV + 1, cols] = jnp.sum(dp_, axis=0, keepdims=True)

        @pl.when(h < n_h - 1)
        def _():
            halo_copy(g, size).wait_recv()

        dfs[rows : rows + 8, own] = halo[:, cols]
        total = jnp.zeros((rows, size), F32)
        for k in range(CONV):
            first = CONV - 1 - k
            total = total + taps[k : k + 1, cols] * dfs[first : first + rows, own]
        pg[:, pl.ds(pl.multiple_of(INNER + g * CHUNK, CHUNK), size)] = total.astype(BF16)

    skip8 = jnp.broadcast_to(heads[2:3, :], (8, LANES))

    def group_compute(g):
        cols = pl.ds(pl.multiple_of(g * CHUNK, CHUNK), CHUNK)
        sp = spread[:, cols]
        skip = expand(skip8, sp)[0:1]
        ms, ls = [adj[0, :, cols]], [adj[1, :, cols]]
        for b in range(blocks - 1):
            ms.append(ms[-1] * decb[b, 0:1, cols] + mst[b, :, cols])
        for b in range(blocks - 1, 0, -1):
            ls.insert(0, ls[0] * decb[b, 0:1, cols] + lst[b, :, cols])
        zero_state = jnp.zeros((STATE, CHUNK), BF16)
        for b in range(blocks):
            at = slice(b * SPAN, (b + 1) * SPAN)
            wide = halves_sum(nn(terms2[b], sp))
            st_e, el, eg, tl, ex = [wide[n * SPAN : (n + 1) * SPAN] for n in range(5)]
            xs = conv_low[at, cols].astype(F32)
            dy = hgrad[at, cols].astype(F32)
            xst = st_e * xs
            parts = [split(v) for v in (hin[b, :, cols], gin[b + 1, :, cols], ls[b], ms[b])]
            into_f = el * nn(cc2[b], jnp.concatenate(parts[0], axis=0))
            into_g = eg * nn(cc2[b], jnp.concatenate(parts[1], axis=0))
            out_f = tl * nn(bb2[b], jnp.concatenate(parts[2], axis=0))
            out_g = ex * nn(bb2[b], jnp.concatenate(parts[3], axis=0))
            dxu = dpre[at, cols] + out_f + out_g
            dpre[at, cols] = (st_e * dxu + skip * dy) * slope[at, cols]
            stack = jnp.concatenate([dy * into_f - xst * out_f, dy * into_g - xst * out_g, xs * dxu, xs * dy], axis=0)
            red[b] += fold(stack, sp)
            pair_f = jnp.sum(ls[b] * hin[b + 1, :, cols], axis=0, keepdims=True)
            pair_g = jnp.sum(ms[b] * gin[b, :, cols], axis=0, keepdims=True)
            cross[b] += fold(jnp.broadcast_to(pair_f + pair_g, (8, CHUNK)), sp)
            acc_bc = dbc[b]
            for scaled, (sh, sl), low in (
                (xst * tl, parts[2], True),
                (xst * ex, parts[3], True),
                (el * dy, parts[0], False),
                (eg * dy, parts[1], False),
            ):
                place = lambda v, low=low: jnp.concatenate([v, zero_state] if low else [zero_state, v], axis=0)
                two = stacked(scaled)
                acc_bc = acc_bc + halves_sum(nt(two, place(sh))) + nt(two[:SPAN], place(sl))
            dbc[b] = acc_bc

    def group_body(g, _):
        group_compute(g)
        halo_send(g, CHUNK)
        tick(pairs_n + 2 * g, 1)

        @pl.when(g >= 1)
        def _():
            conv_back(g - 1, CHUNK)
            first_in(X_CHUNK + g - 1)

        tick(pairs_n + 2 * g + 1, 1)

        @pl.when(g == 4)
        def _():
            for part in range(normed_parts):
                normed_part(INNER, 4 * CHUNK, part, False)

        return 0

    lax.fori_loop(0, X_CHUNK, group_body, 0)

    for b in range(blocks):
        at = slice(b * SPAN, (b + 1) * SPAN)
        bc = conv_low[at, INNER:].astype(F32)
        cb_lo, cb_hi = half_masks(pltpu.roll(bc, STATE, 1))
        qt = q_t[b] * twice
        d = dbc[b] + nn_split(qt, cb_lo.astype(BF16)) + nn_split(qt.T, cb_hi.astype(BF16))
        dpre[at, INNER:] = d * slope[at, INNER:]
    halo_send(X_CHUNK, LANES)
    conv_back(X_CHUNK - 1, CHUNK)
    first_in(2 * X_CHUNK - 1)
    tick(pairs_n + 2 * X_CHUNK, 2)
    for b in range(blocks):
        at = slice(b * SPAN, (b + 1) * SPAN)
        st = steps[at, :]
        rd = red[b]
        v_f = rd[0:SPAN] + at_f[b].T - back_f[b]
        v_g = rd[SPAN : 2 * SPAN] + at_g[b].T - back_g[b]
        da = precise(tri_high(), v_f) + precise(tri_low(), v_g) + cross[b, 0:1]
        dstep = rd[2 * SPAN : 3 * SPAN] + da * rates
        keep = jnp.logical_and(iota((SPAN, LANES), 0) + b * SPAN < left, iota((SPAN, LANES), 1) < HEADS)
        draw = jnp.where(keep, dstep * sigmoid(raw[at, :] + heads[0:1, :]), 0.0)
        pg[at, INNER + CONV_CH :] = draw.astype(BF16)
        dheads[0:1, :] += jnp.sum(draw, axis=0, keepdims=True)
        dheads[1:2, :] += jnp.sum(da * st, axis=0, keepdims=True) * rates
        dheads[2:3, :] += jnp.sum(rd[3 * SPAN :], axis=0, keepdims=True)
    conv_back(X_CHUNK, LANES)
    first_in(N_IN - 1)
    tick(pairs_n + 2 * X_CHUNK + 1, 2)
    for part in range(normed_parts):
        normed_part(INNER + 4 * CHUNK, 3 * CHUNK, part, False)
    tick(pairs_n + 2 * X_CHUNK + 2, 2)

    ngain[...] = jnp.zeros_like(ngain)

    def norm_body(i, _):
        at = pl.ds(pl.multiple_of(i * 16, 16), 16)
        v = x[at, :].astype(F32)
        r = lax.rsqrt(jnp.sum(v * v, axis=1, keepdims=True) * (1.0 / D) + EPS)
        unit = v * r
        g = ng[at, :]
        prod = g * unit
        ngain[...] += prod[0:8] + prod[8:16]
        gg = g * gain[...]
        mean = jnp.sum(gg * unit, axis=1, keepdims=True) * (1.0 / D)
        grad_x[at, :] = cot[at, :].astype(F32) + r * (gg - unit * mean)
        return 0

    lax.fori_loop(0, rows // 16, norm_body, 0, unroll=4)

    sends = []

    def start(buf, me, peers, along_z, snd, rcv):
        for j, p in enumerate(peers):
            c = remote(buf.at[me], buf.at[me], snd.at[j], rcv.at[me], (s, p) if along_z else (p, h))
            c.start()
            sends.append(c)

    def arrive(buf, peers, along_z, snd, rcv):
        for j, p in enumerate(peers):
            remote(buf.at[p], buf.at[p], snd.at[j], rcv.at[p], (s, p) if along_z else (p, h)).wait_recv()
        total = buf[0]
        for i in range(1, buf.shape[0]):
            total = total + buf[i]
        return total

    first = D // LANES
    gsum = ngain[...]
    if dp != D:
        gsum = sum(nn(p, piece_map(dp, rin, rp)) for p in split3(gsum))
    for i in range(first):
        sz[h, i : i + 1, :] = jnp.sum(gsum[:, i * LANES : (i + 1) * LANES], axis=0, keepdims=True)
    for k in range(CONV + 1):
        for i in range(TAPS_ROWS):
            t = first + k * TAPS_ROWS + i
            sz[h, t : t + 1, :] = dtaps[k : k + 1, i * LANES : (i + 1) * LANES]
    lane1 = iota((1, LANES), 1)
    turn = 3 * HEADS
    before = dheads[0:1, :]
    for n in range(1, 3):
        before = jnp.where(lane1 < n * HEADS, before, pltpu.roll(dheads[n : n + 1, :], n * HEADS, 1))
    for i in range(INNER // LANES):
        tile = jnp.sum(ogp[:, i * LANES : (i + 1) * LANES], axis=0, keepdims=True)
        tile = pltpu.roll(tile, turn, 1)
        sz[h, HEAD_ROW + i : HEAD_ROW + i + 1, :] = jnp.where(lane1 < turn, before, tile)
        before = tile
    t = HEAD_ROW + INNER // LANES
    sz[h, t : t + 1, :] = jnp.where(lane1 < turn, before, 0.0)
    sz[h, t + 1 :, :] = jnp.zeros((FLAT_ROWS - t - 1, LANES), F32)

    share = FLAT_ROWS // n_h
    part = pl.ds(pl.multiple_of(share * h, 8), share)

    def share_out(j, q):
        rows_of = pl.ds(pl.multiple_of(share * q, 8), share)
        return remote(sz.at[h, rows_of], szin.at[h], szs.at[j], szr.at[h], (s, q))

    for j, q in enumerate(zpeer):
        share_out(j, q).start()
    szin[h] = sz[h, part]

    def window(slots, dst, wide, per, acc, rec, snd, rcv):
        c0 = (per * h) // wide
        c1 = (per * (h + 1) + wide - 1) // wide
        for c in range(slots):
            index = jnp.minimum(c0 + c, acc.shape[0] - 1)
            at = slice(c * wide, (c + 1) * wide)
            dst[:, at] = acc[index]
            n = jnp.where(owners(index, wide, per)[0] == h, 0, 1) if rec.shape[1] > 1 else 0
            held = jnp.minimum(index, rec.shape[0] - 1)
            for way, there in ((0, h > 0), (1, h < n_h - 1)):

                @pl.when(jnp.logical_and(jnp.logical_and(c0 + c < c1, index < rec.shape[0]), there))
                def _():
                    remote(acc.at[index], rec.at[held, n, way], snd.at[0, 0, 0], rcv.at[held, n, way], (s, up)).wait_recv()
                    dst[:, at] += rec[held, n, way]

            if rec.shape[0] == acc.shape[0]:
                continue
            late = jnp.maximum(index - X_CHUNK, 0)

            @pl.when(jnp.logical_and(c0 + c < c1, index >= X_CHUNK))
            def _():
                for z in zpeer:
                    remote(zb.at[late], r2b.at[z, late], zbs.at[0, 0], zbr.at[z, late], (s, z)).wait_recv()
                    dst[:, at] += r2b[z, late].astype(F32)

    def tick_body(t, _):
        tick(t, 2)
        return 0

    lax.fori_loop(pairs_n + 2 * X_CHUNK + 3, last_tick + 1, tick_body, 0)
    window(1, win, *out_stream)
    g_out = win[0:rin, 0:OUT_CHUNK]
    if oph != OUT_CHUNK:
        g_out = pltpu.roll(g_out, lax.rem(OUT_CHUNK - lax.rem(oph * h, OUT_CHUNK), OUT_CHUNK), 1)[:, :oph]
    grad_out[...] = g_out
    fill = jnp.zeros((LANES - rin, LANES), F32)

    def row_sums(squares):
        wide = jnp.broadcast_to(jnp.sum(squares, axis=1, keepdims=True), (rin, LANES))
        return jnp.concatenate([wide, fill], axis=0).T[0:8]

    sq_out = g_out * g_out
    line_out = row_sums(sq_out)
    rs_out = jnp.sum(sq_out, axis=0, keepdims=True)
    spl[s] = arrive(szin, zpeer, True, szs, szr)
    start(spl, s, speer, False, sps, spr)
    wi = in_slots * CHUNK
    window(in_slots, win, *in_stream)
    g_in = pltpu.roll(win[...], lax.rem(wi - lax.rem(cph * h, CHUNK), wi), 1)[0:rin, :cph]
    grad_in[...] = g_in

    decay_keep = 1.0 - DECAY
    sq_in = g_in * g_in
    line_in = row_sums(sq_in)
    z1[h] = jnp.where(iota((8, LANES), 0) == 0, line_in, line_out)
    start(z1, h, zpeer, True, z1s, z1r)
    cs_in = jnp.sum(sq_in, axis=0, keepdims=True)
    n_ci = -(-cph // LANES)
    n_ro = -(-oph // LANES)
    line[...] = jnp.zeros_like(line)
    line[0:1, 0:cph] = cs_in
    line[0:1, n_ci * LANES : n_ci * LANES + oph] = rs_out
    p1[s] = jnp.zeros_like(p1[0])
    for i in range(n_ci + n_ro):
        p1[s, i : i + 1, :] = line[0:1, i * LANES : (i + 1) * LANES]
    start(p1, s, speer, False, p1s, p1r)
    sums = arrive(z1, zpeer, True, z1s, z1r)
    line_r = DECAY * row_in[...].reshape(1, rin) + decay_keep * (sums[0:1, 0:rin] / PROJ + EPS_SQUARE)
    line_c = DECAY * col_out[...].reshape(1, rin) + decay_keep * (sums[1:2, 0:rin] / INNER + EPS_SQUARE)
    row_in_new[...] = line_r.reshape(rin)
    col_out_new[...] = line_c.reshape(rin)
    fill_line = jnp.zeros((1, LANES - rin), F32)
    up_r = jnp.broadcast_to(jnp.concatenate([line_r, fill_line], axis=1), (LANES, LANES)).T[0:rin, 0:1]
    up_c = jnp.broadcast_to(jnp.concatenate([line_c, fill_line], axis=1), (LANES, LANES)).T[0:rin, 0:1]
    sums = arrive(p1, speer, False, p1s, p1r)
    for i in range(n_ci + n_ro):
        line[0:1, i * LANES : (i + 1) * LANES] = sums[i : i + 1]
    line_ci = DECAY * col_in[...].reshape(1, cph) + decay_keep * (line[0:1, 0:cph] / D + EPS_SQUARE)
    line_ro = DECAY * row_out[...].reshape(1, oph) + decay_keep * (
        line[0:1, n_ci * LANES : n_ci * LANES + oph] / D + EPS_SQUARE
    )
    col_in_new[...] = line_ci.reshape(cph)
    row_out_new[...] = line_ro.reshape(oph)
    u_in = g_in * (lax.rsqrt(up_r) * lax.rsqrt(line_ci))
    u_out = g_out * (lax.rsqrt(up_c) * lax.rsqrt(line_ro))
    lane = iota((8, LANES), 1)
    values = (
        jnp.sum(u_in * u_in, keepdims=True),
        jnp.sum(u_out * u_out, keepdims=True),
        jnp.sum(line_ro, axis=1, keepdims=True),
        jnp.sum(line_r, axis=1, keepdims=True) / n_h,
    )
    note = jnp.zeros((8, LANES), F32)
    for n, v in enumerate(values):
        note = jnp.where(lane == n, v, note)
    z2[h] = note
    start(z2, h, zpeer, True, z2s, z2r)

    sout[h] = arrive(spl, speer, False, sps, spr)
    start(sout, h, zpeer, True, sos, sor)
    p2[s] = arrive(z2, zpeer, True, z2s, z2r)
    start(p2, s, speer, False, p2s, p2r)
    mean_out = p2[s, 0:1, 2:3] / INNER
    for j, p in enumerate(zpeer):
        remote(sout.at[p], sout.at[p], sos.at[j], sor.at[p], (s, p)).wait_recv()
    g = jnp.concatenate([sout[q] for q in range(n_h)], axis=0)
    sec = DECAY * sec_rows[...] + decay_keep * (g * g + EPS_SQUARE)
    u = g * lax.rsqrt(sec)
    spread_small = jnp.sqrt(jnp.sum(u * u, keepdims=True) / SMALL)
    par = prm[...] - LEARN_SMALL * u / jnp.maximum(1.0, spread_small / CLIP_RMS)

    whole, rest = SMALL // LANES, SMALL % LANES
    for v, dst in ((g, small), (sec, second_new), (par, params_new)):
        for i in range(whole):
            dst[pl.ds(i * LANES, LANES)] = v[i : i + 1].reshape(LANES)
        dst[pl.ds(whole * LANES, rest)] = v[whole : whole + 1, 0:rest].reshape(rest)

    chain.finish()

    @pl.when(h > 0)
    def _():
        for g in range(X_CHUNK):
            halo_copy(g, CHUNK).wait_send()
        halo_copy(X_CHUNK, LANES).wait_send()

    for i in (N_IN - 2, N_IN - 1):
        over_in(i).wait_send()

    def drain_body(i, _):
        drain_in(i)

        @pl.when(i < N_OUT)
        def _():
            drain_out(i)

        return 0

    lax.fori_loop(0, N_IN, drain_body, 0)
    sums = arrive(p2, speer, False, p2s, p2r)
    mean_in = sums[0:1, 3:4] / D
    clip_in = jnp.maximum(1.0, jnp.sqrt(sums[0:1, 0:1] * mean_in / (D * PROJ)) / CLIP_RMS)
    clip_out = jnp.maximum(1.0, jnp.sqrt(sums[0:1, 1:2] * mean_out / (INNER * D)) / CLIP_RMS)
    w_in_new[...] = w_in[...] - u_in * (LEARN_RATE * jnp.sqrt(mean_in) / clip_in)
    w_out_new[...] = w_out_t[...] - u_out * (LEARN_RATE * jnp.sqrt(mean_out) / clip_out)
    for j, q in enumerate(zpeer):
        share_out(j, q).wait_send()
    for c in sends:
        c.wait_send()


def rear(n_s, n_h, rp, *args):
    x = args[0]
    w_in, w_out_t = args[22], args[23]
    rin, cph = w_in.shape
    oph = w_out_t.shape[1]
    rows, dp = x.shape
    n_c = n_s // 2
    half = n_c * rp
    blocks = rows // SPAN
    in_slots = max(-(-cph * (q + 1) // CHUNK) - cph * q // CHUNK for q in range(n_h))
    out_dup = 1 if oph % OUT_CHUNK == 0 else 2
    n_line = -(-cph // LANES) + -(-oph // LANES)
    n_rows = -(-(n_line + 1) // 8) * 8
    dma = pltpu.SemaphoreType.DMA
    vm = pl.BlockSpec(memory_space=pltpu.VMEM)
    sm = pl.BlockSpec(memory_space=pltpu.SMEM)
    hbm = pl.BlockSpec(memory_space=pl.ANY)
    sds = jax.ShapeDtypeStruct
    vf = lambda *shape: pltpu.VMEM(shape, F32)
    vb = lambda *shape: pltpu.VMEM(shape, BF16)
    tables = vf(blocks, SPAN, LANES)
    specs = [vm] * len(args)
    specs[3] = sm
    for i in (4, 6, 12, 13, 14, 15, 16, 17):
        specs[i] = hbm
    return pl.pallas_call(
        functools.partial(rear_kernel, n_s, n_h, cph, oph, rin, rp, in_slots),
        out_shape=(
            sds((rows, dp), F32),
            sds((rin, cph), F32),
            sds((rin,), F32),
            sds((cph,), F32),
            sds((rin, cph), F32),
            sds((rin, oph), F32),
            sds((oph,), F32),
            sds((rin,), F32),
            sds((rin, oph), F32),
            sds((SMALL,), F32),
            sds((SMALL,), F32),
            sds((SMALL,), F32),
        ),
        in_specs=specs,
        out_specs=(vm,) * 12,
        scratch_shapes=[
            vb(dp, WIDE),
            vf(rows, CONV_CH),
            vb(rows + HALO, CONV_CH),
            vf(blocks + 1, STATE, INNER),
            vf(blocks + 1, STATE, INNER),
            vf(blocks, STATE, INNER),
            vf(blocks, STATE, INNER),
            vf(FLAT_ROWS, LANES),
            vf(FLAT_ROWS, LANES),
            vf(1, dp),
            vf(8, CONV_CH),
            vf(8, LANES),
            vb(LANES, INNER),
            vf(2, STATE, INNER),
            vf(2, STATE, INNER),
            vb(2, half, rows),
            vb(2, half, rows),
            vb(rows, WIDE),
            vf(rows, dp),
            vf(rows, CONV_CH),
            vf(8, CONV_CH),
            vf(rows + 8, CHUNK),
            vf(rows + HALO, CHUNK),
            tables, tables, tables, tables, tables, tables, tables, tables, tables,
            vb(blocks, 2 * SPAN, 3 * LANES),
            vb(blocks, 2 * SPAN, LANES),
            vb(blocks, 10 * SPAN, LANES),
            vb(blocks, SPAN, LANES),
            vb(blocks, SPAN, LANES),
            vf(blocks, 4 * SPAN, LANES),
            vf(blocks, 8, LANES),
            tables,
            vf(8, LANES),
            vf(8, CONV_CH),
            vf(8, dp),
            tables,
            vf(2, half, OUT_CHUNK),
            vf(SLOTS, half, OUT_CHUNK),
            vf(n_c, rp, OUT_CHUNK),
            vb(N_IN, n_c - 1, rp, CHUNK),
            vb(N_IN, n_c - 1, rp, CHUNK),
            vf(N_IN, rp, CHUNK),
            vf(X_CHUNK, 2, 2, rp, CHUNK),
            vb(N_OUT, n_c - 1, rp, OUT_CHUNK),
            vb(N_OUT, n_c - 1, rp, OUT_CHUNK),
            vf(N_OUT, rp, OUT_CHUNK),
            vf(N_OUT, out_dup, 2, rp, OUT_CHUNK),
            vf(rp, in_slots * CHUNK),
            vb(N_IN - X_CHUNK, rp, CHUNK),
            vb(n_h, N_IN - X_CHUNK, rp, CHUNK),
            vf(n_h, FLAT_ROWS, LANES),
            vf(n_h, FLAT_ROWS // n_h, LANES),
            vf(n_s, FLAT_ROWS // n_h, LANES),
            vf(n_h, FLAT_ROWS // n_h, LANES),
            vf(n_h, 8, LANES),
            vf(n_s, n_rows, LANES),
            vf(n_h, 8, LANES),
            vf(n_s, 8, LANES),
            vf(8, n_line * LANES),
        ]
        + [dma((CHAIN_PARTS,))] * 4
        + [dma((X_CHUNK + 1,))] * 2
        + [dma((N_IN,)), dma((N_IN,)), dma((N_IN, n_c)), dma((N_IN, n_c)), dma((X_CHUNK, 2, 2)), dma((X_CHUNK, 2, 2))]
        + [dma((N_OUT,)), dma((N_OUT,)), dma((N_OUT, n_c)), dma((N_OUT, n_c)), dma((N_OUT, out_dup, 2)), dma((N_OUT, out_dup, 2))]
        + [dma((8,)), dma((N_IN - X_CHUNK, 2)), dma((n_h, N_IN - X_CHUNK)), dma((n_h,)), dma((n_h,))]
        + [dma((n_h,)), dma((n_h,)), dma((n_s,)), dma((n_s,))] * 3,
        compiler_params=pltpu.CompilerParams(
            collective_id=2, has_side_effects=True, vmem_limit_bytes=REAR_VMEM
        ),
        name="rear",
    )(*args)


REAR_VMEM = (63 << 20) + (1 << 19)


def results_kernel(*refs):
    count = len(refs) // 2
    for n in range(count):
        refs[count + n][...] = refs[n][...]


def results(*arrays):
    vm = pl.BlockSpec(memory_space=pltpu.VMEM)
    return pl.pallas_call(
        results_kernel,
        out_shape=tuple(jax.ShapeDtypeStruct(a.shape, a.dtype) for a in arrays),
        in_specs=[vm] * len(arrays),
        out_specs=(vm,) * len(arrays),
        compiler_params=pltpu.CompilerParams(vmem_limit_bytes=63 << 20),
        name="results",
    )(*arrays)


def on_device(
    x_in, lengths, cotangent, w_in, w_out, small_params, row_in, col_in, row_out, col_out, small_second
):
    n_s = lax.axis_size("seq")
    n_h = lax.axis_size("head")
    rin = w_in.shape[0]
    rp = -(-rin // 16) * 16
    dp = n_s * rp
    def pad(v, axis, fill=0):
        if rp == rin:
            return v
        shape = v.shape[:axis] + (n_s, rin) + v.shape[axis + 1 :]
        widths = [(0, 0)] * len(shape)
        widths[axis + 1] = (0, rp - rin)
        v = jnp.pad(v.reshape(shape), widths, constant_values=fill)
        return v.reshape(v.shape[:axis] + (dp,) + v.shape[axis + 2 :])

    def cut(v, axis):
        if rp == rin:
            return v
        shape = v.shape[:axis] + (n_s, rp) + v.shape[axis + 1 :]
        v = lax.slice_in_dim(v.reshape(shape), 0, rin, axis=axis + 1)
        return v.reshape(v.shape[:axis] + (D,) + v.shape[axis + 2 :])

    x = pad(x_in, 1)
    cot = pad(cotangent, 1)
    w_out_t = w_out.T
    (
        result, w_full, nlow, conv_in, conv_low, slope, raw, steps, decb, dec, dgate, hgrad, glow, og_part, lst, mst, dev2, hin,
        gin,
    ) = fore(n_s, n_h, rp, x, cot, w_in, w_out_t, small_params, lengths)
    (
        grad_x, grad_in, row_in_new, col_in_new, w_in_new, grad_out, row_out_new, col_out_new, w_out_new, small,
        second_new, params_new,
    ) = rear(
        n_s, n_h, rp,
        x, cot, small_params, lengths, w_full, nlow, dgate, glow, conv_low, hgrad, steps, raw, slope, conv_in, hin, gin, lst, mst,
        dev2, decb, dec, og_part, w_in, w_out_t, row_in, col_in, row_out, col_out, small_second,
    )
    (
        result, grad_x, grad_in, row_in_new, col_in_new, w_in_new, grad_out, row_out_new, col_out_new, w_out_new, small,
        second_new, params_new,
    ) = results(
        result, grad_x, grad_in, row_in_new, col_in_new, w_in_new, grad_out, row_out_new, col_out_new, w_out_new, small,
        second_new, params_new,
    )
    return (
        cut(result, 1), cut(grad_x, 1), grad_in, row_in_new, col_in_new, w_in_new, grad_out.T, row_out_new, col_out_new,
        w_out_new.T, small, second_new, params_new,
    )


def solution(mesh):
    both = P(("seq", "head"), None)
    factors = (P("seq", "head"), P("seq"), P("head"), P("seq", "head"))
    return jax.shard_map(
        on_device,
        mesh=mesh,
        in_specs=(
            both, P("seq"), both, P("seq", "head"), P("head", "seq"), P(), P("seq"), P("head"), P("head"), P("seq"), P(),
        ),
        out_specs=(
            both, both, P("seq", "head"), P("seq"), P("head"), P("seq", "head"), P("head", "seq"), P("head"), P("seq"),
            P("head", "seq"), P(), P(), P(),
        ),
        check_vma=False,
    )
```
